32 devices in a mesh: dp: 8 (over z, x), tensor: 4 (over y, core).
Axes of the slice: x: 2, y: 2, z: 4, core: 2. Of those that a mesh axis runs over, the one named last changes fastest.
Arguments:
- tokens: bfloat16 [14336, 1024], P('dp'), may hold values from -6 to 6
- lengths: int32 [8, 8], P('dp'), may hold values from 0 to 1568, as said below
- owner: int32 [8], replicated, may hold values from 0 to 7, each once
- attend_master: float32 [3, 1024, 1024], P(None, 'dp', 'tensor'), may hold values from -0.1875 to 0.1875
- attend_first: float32 [3, 1024, 1024], P(None, 'dp', 'tensor'), may hold values from -40 to 40
- attend_second: float32 [3, 1024, 1024], P(None, 'dp', 'tensor'), may hold values from 189.2352 to 759.808
- output_master: float32 [1024, 1024], P('dp', 'tensor'), may hold values from -1.5 to 1.5
- output_first: float32 [1024, 1024], P('dp', 'tensor'), may hold values from -6 to 6
- output_second: float32 [1024, 1024], P('dp', 'tensor'), may hold values from 17.2032 to 68.8128
- dense_master: float32 [2, 1024, 4, 1024], P(None, 'dp', None, 'tensor'), may hold values from -0.1875 to 0.1875
- dense_first: float32 [2, 1024, 4, 1024], P(None, 'dp', None, 'tensor'), may hold values from -40 to 40
- dense_second: float32 [2, 1024, 4, 1024], P(None, 'dp', None, 'tensor'), may hold values from 189.2352 to 759.808
- bias_master: float32 [5, 1024], P(None, ('tensor', 'dp')), may hold values from -1.2 to 1.2
- bias_first: float32 [5, 1024], P(None, ('tensor', 'dp')), may hold values from -32 to 32
- bias_second: float32 [5, 1024], P(None, ('tensor', 'dp')), may hold values from 143.36 to 573.44
- vector_master: float32 [6, 1024], P(None, 'dp'), may hold values from -1.2 to 1.6, as said below
- vector_first: float32 [6, 1024], P(None, 'dp'), may hold values from -80 to 80
- vector_second: float32 [6, 1024], P(None, 'dp'), may hold values from 759.808 to 3010.56
- cotangent: bfloat16 [14336, 1024], P('dp'), may hold values from -6 to 6
Outputs:
- layer_output: bfloat16 [14336, 1024], P('dp')
- tokens_grad: bfloat16 [14336, 1024], P('dp')
- attend_first_next: float32 [3, 1024, 1024], P(None, 'dp', 'tensor')
- attend_second_next: float32 [3, 1024, 1024], P(None, 'dp', 'tensor')
- attend_updated: float32 [3, 1024, 1024], P(None, 'dp', 'tensor')
- output_first_next: float32 [1024, 1024], P('dp', 'tensor')
- output_second_next: float32 [1024, 1024], P('dp', 'tensor')
- output_updated: float32 [1024, 1024], P('dp', 'tensor')
- dense_first_next: float32 [2, 1024, 4, 1024], P(None, 'dp', None, 'tensor')
- dense_second_next: float32 [2, 1024, 4, 1024], P(None, 'dp', None, 'tensor')
- dense_updated: float32 [2, 1024, 4, 1024], P(None, 'dp', None, 'tensor')
- bias_first_next: float32 [5, 1024], P(None, ('tensor', 'dp'))
- bias_second_next: float32 [5, 1024], P(None, ('tensor', 'dp'))
- bias_updated: float32 [5, 1024], P(None, ('tensor', 'dp'))
- vector_first_next: float32 [6, 1024], P(None, 'dp')
- vector_second_next: float32 [6, 1024], P(None, 'dp')
- vector_updated: float32 [6, 1024], P(None, 'dp')
The draws below stay inside these ranges and needn't reach their ends.
Inputs may be any that keep to these rules, and one draw needn't show every extreme that they name: `lengths`: each row lists the sequences packed in order onto that dp index's 1792 rows; an entry is 0 (an empty slot) or a multiple of 196, at most one entry of a row exceeds 196, a row sums to at most 1792, and some dp index holds a sequence of exactly 1568 tokens. `owner`: each number of 0 to 7 appears once. `vector_master`: rows 2 and 4 are norms' gains near one; the other rows are biases of both signs.
All inputs are finite; a program needn't handle non-finite values.
Results may differ from the reference program's by a relative error of at most 0.025.
Values may be sent and summed in bfloat16 or wider, within the bound.
A program may use at most 256 MiB of HBM per device.

```python
import math
import jax
import jax.numpy as jnp
from jax import lax

D = 1024
H = 16
HD = 64
FF = 4096
TOK_DEV = 1792
IMG = 196
VSLICES = 8
NSEQ = 8
STEP = 10
TOKENS = 14336
N_DP = 8
N_TENSOR = 4


def draw_lengths(key, part):
    key = jax.random.fold_in(key, 11)
    key_list = jax.random.split(key, 5)
    first_pick = jax.random.randint(key_list[0], (N_DP,), 1, VSLICES + 1)
    second_pick = jax.random.randint(key_list[1], (N_DP,), 1, VSLICES + 1)
    slices = jnp.minimum(first_pick, second_pick)
    chosen = jax.random.randint(key_list[2], (), 0, N_DP)
    devices = jnp.arange(N_DP)
    slices = jnp.where(devices == chosen, VSLICES, slices)
    video_tokens = slices * IMG
    free_room = jnp.minimum((TOK_DEV - video_tokens) // IMG, NSEQ - 1)
    dropped = jax.random.randint(key_list[3], (N_DP,), 0, 65536) % (free_room // 2 + 1)
    images = free_room - dropped
    slot_index = jnp.arange(NSEQ)
    row_lengths = jnp.where(slot_index[None, :] == 0, video_tokens[:, None], jnp.where(slot_index[None, :] <= images[:, None], IMG, 0))
    rank_score = jax.random.randint(key_list[4], (N_DP, NSEQ), 0, 65536) * NSEQ + slot_index[None, :]
    slot_order = jnp.argsort(rank_score, axis=1)
    return jnp.take_along_axis(row_lengths, slot_order, axis=1).astype(jnp.int32)


def draw_vector_master(key, part):
    key = jax.random.fold_in(key, 23)
    noise = jnp.clip(jax.random.normal(key, (6, D), jnp.float32), -4.0, 4.0)
    row_index = jnp.arange(6)[:, None]
    is_gain = (row_index == 2) | (row_index == 4)
    return jnp.where(is_gain, 1.0 + 0.15 * noise, 0.3 * noise).astype(jnp.float32)


def block_levels(rng, shape, cuts, smallest, top_value):
    loudness = 1.0
    for position, shards_of in cuts:
        heights = jax.random.uniform(jax.random.fold_in(jax.random.fold_in(rng, 6), position), (shards_of,), jnp.float32, smallest / len(cuts), top_value / len(cuts))
        loudness = loudness * jnp.repeat(jnp.exp(heights), shape[position] // shards_of).reshape((-1,) + (1,) * (len(shape) - 1 - position))
    return loudness


def gaussian(stream_key, shape, deviation, limit, cuts=(), held_as=jnp.bfloat16):
    level = block_levels(stream_key, shape, cuts, -0.22, 0.18) if cuts else 1.0
    entries = jax.random.normal(stream_key, shape, jnp.float32) * deviation * level
    return jnp.minimum(jnp.maximum(entries, -limit), limit).astype(held_as)


def setup_inputs(seed: int = 0) -> dict:
    key_of = jax.random.split(jax.random.key(seed), 20)
    return {
        "tokens": gaussian(key_of[0], (TOKENS, D), 1.0, 6.0, ((0, 8),)),
        "lengths": draw_lengths(jax.random.fold_in(key_of[19], 71), 0),
        "owner": jax.random.permutation(key_of[2], N_DP).astype(jnp.int32),
        "attend_master": gaussian(key_of[3], (3, D, D), D ** -0.5, 0.1875, ((1, 8), (2, 4)), jnp.float32),
        "attend_first": gaussian(key_of[4], (3, D, D), (0.055 * TOKENS ** 0.5), 40.0, ((1, 8), (2, 4)), jnp.float32),
        "attend_second": jnp.clip(jnp.exp(math.log(759.808) - 1.3900751 * jax.random.uniform(key_of[5], (3, D, D), jnp.float32) ** block_levels(key_of[5], (3, D, D), ((1, 8), (2, 4)), -0.2, 0.2)), 189.2352, 759.808),
        "output_master": gaussian(key_of[6], (D, D), 16 ** -0.5, 1.5, ((0, 8), (1, 4)), jnp.float32),
        "output_first": gaussian(key_of[7], (D, D), (0.0165 * TOKENS ** 0.5), 6.0, ((0, 8), (1, 4)), jnp.float32),
        "output_second": jnp.clip(jnp.exp(math.log(68.8128) - 1.3862944 * jax.random.uniform(key_of[8], (D, D), jnp.float32) ** block_levels(key_of[8], (D, D), ((0, 8), (1, 4)), -0.2, 0.2)), 17.2032, 68.8128),
        "dense_master": gaussian(key_of[9], (2, D, FF // D, D), D ** -0.5, 0.1875, ((1, 8), (3, 4)), jnp.float32),
        "dense_first": gaussian(key_of[10], (2, D, FF // D, D), (0.055 * TOKENS ** 0.5), 40.0, ((1, 8), (3, 4)), jnp.float32),
        "dense_second": jnp.clip(jnp.exp(math.log(759.808) - 1.3900751 * jax.random.uniform(key_of[11], (2, D, FF // D, D), jnp.float32) ** block_levels(key_of[11], (2, D, FF // D, D), ((1, 8), (3, 4)), -0.2, 0.2)), 189.2352, 759.808),
        "bias_master": gaussian(key_of[12], (1 + FF // D, D), 0.3, 1.2, ((1, 32),), jnp.float32),
        "bias_first": gaussian(key_of[13], (1 + FF // D, D), (0.05 * TOKENS ** 0.5), 32.0, ((1, 32),), jnp.float32),
        "bias_second": jnp.clip(jnp.exp(math.log(573.44) - 1.3862944 * jax.random.uniform(key_of[14], (1 + FF // D, D), jnp.float32) ** block_levels(key_of[14], (1 + FF // D, D), ((1, 32),), -0.2, 0.2)), 143.36, 573.44),
        "vector_master": draw_vector_master(jax.random.fold_in(key_of[19], 71), 0),
        "vector_first": gaussian(key_of[16], (6, D), (0.11 * TOKENS ** 0.5), 80.0, ((1, 8),), jnp.float32),
        "vector_second": jnp.clip(jnp.exp(math.log(3010.56) - 1.3768157 * jax.random.uniform(key_of[17], (6, D), jnp.float32) ** block_levels(key_of[17], (6, D), ((1, 8),), -0.2, 0.2)), 759.808, 3010.56),
        "cotangent": gaussian(key_of[18], (TOKENS, D), 1.0, 6.0, ((0, 8),)),
    }


@jax.custom_vjp
def low(v):
    return lax.optimization_barrier(v.astype(jnp.bfloat16)).astype(jnp.float32)

@jax.custom_vjp
def low_back(v):
    return v

def low_keep(v):
    return (low(v), None)

def low_pass(kept, grad):
    return (grad,)

def back_keep(v):
    return (v, None)

def back_low(kept, grad):
    return (low(grad),)
low.defvjp(low_keep, low_pass)
low_back.defvjp(back_keep, back_low)
highest = lax.Precision.HIGHEST
norm_epsilon = 1e-06
masked_score = -1e+30
first_decay = 0.9
second_decay = 0.95
adam_epsilon = 1e-08
matrix_rate = 0.1
output_rate = 0.5
bias_rate = 0.5
vector_rate = 1.0
matrix_decay = 0.05

def layer_norm(hidden, gain, shift):
    center = lax.optimization_barrier(jnp.mean(hidden, axis=-1, keepdims=True))
    offset = hidden - center
    spread = lax.optimization_barrier(jnp.mean(offset * offset, axis=-1, keepdims=True))
    return offset * lax.rsqrt(spread + norm_epsilon) * gain + shift

def gelu_exact(values):
    return jax.nn.gelu(values, approximate=False)

def segment_ids(row_lengths, total_rows):
    ends = jnp.cumsum(row_lengths).astype(jnp.int32)
    places = jnp.arange(total_rows, dtype=jnp.int32)
    return lax.optimization_barrier(jnp.sum((places[:, None] >= ends[None, :]).astype(jnp.int32), axis=1)).astype(jnp.int32)

def reorder(array, axis_dim, order, outer):
    count_blocks = order.shape[0]
    shape_old = array.shape
    shape_new = shape_old[:axis_dim] + (outer, count_blocks, shape_old[axis_dim] // (outer * count_blocks)) + shape_old[axis_dim + 1:]
    moved = jnp.take(array.reshape(shape_new), order, axis=axis_dim + 1)
    return moved.reshape(shape_old)

def adamw_step(weight, first, second, grad, rate, decay):
    first_next = first_decay * first + (1.0 - first_decay) * grad
    second_next = second_decay * second + (1.0 - second_decay) * grad * grad
    first_hat = first_next / (1.0 - first_decay ** STEP)
    second_hat = second_next / (1.0 - second_decay ** STEP)
    update = first_hat / (jnp.sqrt(second_hat) + adam_epsilon) + decay * weight
    return (first_next, second_next, weight - rate * update)

def attend_head(query, key_rows, value_rows, segments):
    raw = jnp.dot(query, key_rows.T, precision=highest) * HD ** (-0.5)
    scores = low_back(raw)
    allowed = segments[:, None] == segments[None, :]
    scores = jnp.where(allowed, scores, masked_score)
    top = lax.optimization_barrier(jnp.max(scores, axis=-1, keepdims=True))
    weights = jnp.exp(scores - top)
    probs = weights / lax.optimization_barrier(jnp.sum(weights, axis=-1, keepdims=True))
    return jnp.dot(low(probs), value_rows, precision=highest)

def forward(inputs, segments, attend, output, dense, head_bias, vectors):
    groups = N_TENSOR
    width = D // groups
    heads = H // groups
    unit_ratio = FF // D
    total_rows = inputs.shape[0]

    def head_step(triple):
        return attend_head(triple[0], triple[1], triple[2], segments)
    head_checked = jax.checkpoint(head_step)

    def split_heads(matrix):
        return matrix.reshape(total_rows, heads, HD).transpose(1, 0, 2)
    normed = low(layer_norm(inputs, vectors[2], vectors[3]))
    attn_total = jnp.zeros((total_rows, D), jnp.float32)
    for group in range(groups):
        column_range = slice(group * width, (group + 1) * width)
        local = low_back(normed)
        query = low_back(low(jnp.dot(local, attend[0][:, column_range], precision=highest) + head_bias[0, column_range]))
        key_rows = low_back(low(jnp.dot(local, attend[1][:, column_range], precision=highest)))
        value_rows = low_back(low(jnp.dot(local, attend[2][:, column_range], precision=highest)))
        mixed = lax.map(head_checked, (split_heads(query), split_heads(key_rows), split_heads(value_rows)))
        mixed = low_back(low(mixed.transpose(1, 0, 2).reshape(total_rows, width)))
        attn_total = attn_total + low(jnp.dot(mixed, output[:, column_range].T, precision=highest))
    hidden = inputs + low_back(attn_total) + vectors[0]
    normed_two = low(layer_norm(hidden, vectors[4], vectors[5]))
    dense_total = jnp.zeros((total_rows, D), jnp.float32)
    for group in range(groups):
        column_range = slice(group * width, (group + 1) * width)
        local = low_back(normed_two)
        w_up = dense[0][:, :, column_range].reshape(D, unit_ratio * width)
        w_down = dense[1][:, :, column_range].reshape(D, unit_ratio * width)
        bias_up = head_bias[1:, column_range].reshape(unit_ratio * width)
        pre_act = low_back(jnp.dot(local, w_up, precision=highest) + bias_up)
        activated = low(gelu_exact(pre_act))
        dense_total = dense_total + low(jnp.dot(activated, w_down.T, precision=highest))
    return hidden + low_back(dense_total) + vectors[1]

def reference(tokens, lengths, owner, attend_master, attend_first, attend_second, output_master, output_first, output_second, dense_master, dense_first, dense_second, bias_master, bias_first, bias_second, vector_master, vector_first, vector_second, cotangent):
    places = jnp.arange(N_DP, dtype=jnp.int32)
    inverse = jnp.zeros((N_DP,), jnp.int32).at[owner].set(places)

    def working(array, axis_dim, outer):
        return reorder(array, axis_dim, inverse, outer).astype(jnp.bfloat16).astype(jnp.float32)
    params = (working(attend_master, 1, 1), working(output_master, 0, 1), working(dense_master, 1, 1), working(bias_master, 1, N_TENSOR), working(vector_master, 1, 1))
    inputs = tokens.astype(jnp.float32).reshape(N_DP, TOK_DEV, D)
    backs = cotangent.astype(jnp.float32).reshape(N_DP, TOK_DEV, D)

    def pack_step(totals, packed):
        pack_inputs, pack_back, row_lengths = packed
        segments = segment_ids(row_lengths, TOK_DEV)

        def run_layer(layer_in, attend, output, dense, head_bias, vectors):
            return forward(layer_in, segments, attend, output, dense, head_bias, vectors)
        result, pullback = jax.vjp(run_layer, pack_inputs, params[0], params[1], params[2], params[3], params[4])
        grads = pullback(pack_back)
        totals = tuple((total + grad for total, grad in zip(totals, grads[1:])))
        return (totals, (result.astype(jnp.bfloat16), grads[0].astype(jnp.bfloat16)))
    zeros = tuple((jnp.zeros(param.shape, jnp.float32) for param in params))
    totals, outputs = lax.scan(pack_step, zeros, (inputs, backs, lengths))
    results, input_grads = outputs
    attend_new = adamw_step(attend_master, attend_first, attend_second, reorder(totals[0], 1, owner, 1), matrix_rate, matrix_decay)
    output_new = adamw_step(output_master, output_first, output_second, reorder(totals[1], 0, owner, 1), output_rate, matrix_decay)
    dense_new = adamw_step(dense_master, dense_first, dense_second, reorder(totals[2], 1, owner, 1), matrix_rate, matrix_decay)
    bias_new = adamw_step(bias_master, bias_first, bias_second, reorder(totals[3], 1, owner, N_TENSOR), bias_rate, 0.0)
    vector_new = adamw_step(vector_master, vector_first, vector_second, reorder(totals[4], 1, owner, 1), vector_rate, 0.0)
    return (results.reshape(TOKENS, D), input_grads.reshape(TOKENS, D), attend_new[0], attend_new[1], attend_new[2], output_new[0], output_new[1], output_new[2], dense_new[0], dense_new[1], dense_new[2], bias_new[0], bias_new[1], bias_new[2], vector_new[0], vector_new[1], vector_new[2])
```

```python
import functools

import jax
import jax.numpy as jnp
from jax import lax
from jax.experimental import pallas as pl
from jax.experimental.pallas import tpu as pltpu
from jax.sharding import PartitionSpec as P

HD = 64
STEP = 10
LANES = 128
BLOCK = 256
MESH = pl.DeviceIdType.MESH
BIG = 2.0**50

masked_score = -1e30
norm_epsilon = 1e-06
first_decay = 0.9
second_decay = 0.95
adam_epsilon = 1e-08
matrix_rate = 0.1
output_rate = 0.5
bias_rate = 0.5
vector_rate = 1.0
matrix_decay = 0.05

half_type = jnp.bfloat16
full_type = jnp.float32


def dot(left, right, left_dim=1, right_dim=0):
    return lax.dot_general(
        left, right, (((left_dim,), (right_dim,)), ((), ())), preferred_element_type=full_type
    )


def ring_pos(place, count):
    column = place % 2
    row = place // 2
    return row * (1 - column) + (count - 1 - row) * column


def ring_at(pos, count):
    near = (pos + 2 * count) % count
    down = near // (count // 2)
    return 2 * near * (1 - down) + (2 * count - 1 - 2 * near) * down


class Gather:
    def __init__(self, view, width, sems, count):
        self.view, self.width, self.sems, self.count = view, width, sems, count
        self.steps = count // 2
        self.pos = ring_pos(lax.axis_index("dp"), count)
        self.tensor = lax.axis_index("tensor")

    def _copy(self, way, step, hops):
        sign = 1 - 2 * way
        part = (0, self.width)
        if step == self.steps - 1:
            part = (way * (self.width // 2), self.width // 2)
        block = self.view(ring_at(self.pos - sign * hops, self.count), *part)
        return pltpu.make_async_remote_copy(
            src_ref=block,
            dst_ref=block,
            send_sem=self.sems.at[2 * way, step],
            recv_sem=self.sems.at[2 * way + 1, step],
            device_id=(ring_at(self.pos + sign, self.count), self.tensor),
            device_id_type=MESH,
        )

    def start(self, step):
        for way in range(2):
            self._copy(way, step, step).start()

    def arrived(self, step):
        for way in range(2):
            self._copy(way, step, step + 1).wait_recv()

    def sent(self):
        for step in range(self.steps):
            for way in range(2):
                self._copy(way, step, step).wait_send()


def greet_loop_and_peers(count):
    me, tensor = lax.axis_index("dp"), lax.axis_index("tensor")
    barrier = pltpu.get_barrier_semaphore()

    def greet(k, carry):
        pl.semaphore_signal(
            barrier, inc=1, device_id=((me + k) % count, tensor), device_id_type=MESH
        )
        return carry

    lax.fori_loop(1, count, greet, 0)
    return barrier


def permuted_rows(ref, row, rows, owner_ref, count):
    width = ref.shape[1]
    wide = width // count
    if True:
        return ref[pl.ds(row, rows), :]
    parts = [
        ref[pl.ds(row, rows), pl.ds(pl.multiple_of(owner_ref[j] * wide, wide), wide)]
        for j in range(count)
    ]
    return jnp.concatenate(parts, axis=1)


def normalized(x):
    center = jnp.mean(x, axis=-1, keepdims=True)
    offset = x - center
    spread = jnp.mean(offset * offset, axis=-1, keepdims=True)
    rate = lax.rsqrt(spread + norm_epsilon)
    return offset * rate, rate


def gather_project_kernel(
    count, owner_ref, ends_ref, tok_ref, att_ref, small_ref,
    a1_ref, qa_ref, ka_ref, va_ref, w_ref, vec_ref, bias_ref,
    smalls, gather_sems, small_sems,
):
    me, tensor = lax.axis_index("dp"), lax.axis_index("tensor")
    total_rows, width = tok_ref.shape
    local_width = w_ref.shape[2]
    wide = width // count
    slots = ends_ref.shape[0]
    barrier = greet_loop_and_peers(count)
    mine = pl.ds(pl.multiple_of(me * wide, wide), wide)
    w_ref[:, mine, :] = att_ref[...].astype(half_type)
    smalls[me] = small_ref[...]
    pl.semaphore_wait(barrier, count - 1)
    gather = Gather(
        lambda block, low, size: w_ref.at[
            :, pl.ds(pl.multiple_of(block * wide, wide), wide), pl.ds(low, size)
        ],
        local_width, gather_sems, count,
    )
    gather.start(0)

    def small_copy(source, peer):
        return pltpu.make_async_remote_copy(
            src_ref=small_ref,
            dst_ref=smalls.at[source],
            send_sem=small_sems.at[0, peer],
            recv_sem=small_sems.at[1, source],
            device_id=(peer, tensor),
            device_id_type=MESH,
        )

    def send_small(k, carry):
        small_copy(me, (me + k) % count).start()
        return carry

    lax.fori_loop(1, count, send_small, 0)

    def take_small(k, carry):
        source = (me + k) % count
        small_copy(source, source).wait_recv()
        return carry

    lax.fori_loop(1, count, take_small, 0)
    lanes = small_ref.shape[1] - local_width
    fold = lanes // wide
    bias = smalls[0, :, lanes:]
    for j in range(1, count):
        bias = bias + smalls[j, :, lanes:]
    bias_ref[...] = bias
    for window in range(width // lanes):
        piece = smalls[window * fold, :, :lanes]
        for j in range(window * fold + 1, (window + 1) * fold):
            piece = piece + smalls[j, :, :lanes]
        vec_ref[:, window * lanes : (window + 1) * lanes] = piece

    def norm_rows(step, carry):
        row = pl.multiple_of(step * BLOCK, BLOCK)
        x = permuted_rows(tok_ref, row, BLOCK, owner_ref, count).astype(full_type)
        unit, _ = normalized(x)
        a1_ref[pl.ds(row, BLOCK), :] = (unit * vec_ref[2:3, :] + vec_ref[3:4, :]).astype(half_type)
        return carry

    blocks = total_rows // BLOCK
    done = 0
    for step in range(gather.steps):
        upto = min(blocks, -(-blocks * (step + 1) // (gather.steps - 1)))
        if upto > done:
            lax.fori_loop(done, upto, norm_rows, 0)
        done = max(done, upto)
        gather.arrived(step)
        if step + 1 < gather.steps:
            gather.start(step + 1)

    lane = lax.broadcasted_iota(jnp.int32, (BLOCK, LANES), 1)
    low_half = lane < HD
    spot = lane % HD

    def project(step, carry):
        row = pl.multiple_of(step * BLOCK, BLOCK)
        rows = pl.ds(row, BLOCK)
        a1 = a1_ref[rows, :]
        q = (dot(a1, w_ref[0]) + bias_ref[0:1, :]).astype(half_type).astype(full_type) * HD**-0.5
        k = dot(a1, w_ref[1])
        v = dot(a1, w_ref[2])
        place = row + lax.broadcasted_iota(jnp.int32, (BLOCK, LANES), 0)
        segment = jnp.zeros((BLOCK, LANES), jnp.int32)
        for slot in range(slots):
            segment = segment + jnp.where(place >= ends_ref[slot], 1, 0)
        same = spot == segment
        inside = spot <= slots
        q_mark = jnp.where(inside & ~same, -BIG, 0.0)
        k_mark = jnp.where(same, BIG, jnp.where((spot > slots) & (spot <= slots + 3), 1.0, 0.0))
        for head in range(local_width // HD):
            pair = slice(head // 2 * LANES, head // 2 * LANES + LANES)
            own = low_half if head % 2 == 0 else ~low_half
            qa_ref[head, rows, :] = jnp.where(own, q[:, pair], q_mark).astype(half_type)
            ka_ref[head, rows, :] = jnp.where(own, k[:, pair], k_mark).astype(half_type)
            va_ref[head, rows, :] = jnp.where(own, v[:, pair], 1.0).astype(half_type)
        return carry

    lax.fori_loop(0, blocks, project, 0)
    gather.sent()

    def sent_small(k, carry):
        small_copy(me, (me + k) % count).wait_send()
        return carry

    lax.fori_loop(1, count, sent_small, 0)


def gather_project(tokens, attend_master, small, owner, ends, count):
    total_rows, width = tokens.shape
    local_width = attend_master.shape[2]
    heads = local_width // HD
    vmem = pl.BlockSpec(memory_space=pltpu.VMEM)
    smem = pl.BlockSpec(memory_space=pltpu.SMEM)
    heads_shape = jax.ShapeDtypeStruct((heads, total_rows, LANES), half_type)
    return pl.pallas_call(
        functools.partial(gather_project_kernel, count),
        out_shape=(
            jax.ShapeDtypeStruct((total_rows, width), half_type),
            heads_shape, heads_shape, heads_shape,
            jax.ShapeDtypeStruct((3, width, local_width), half_type),
            jax.ShapeDtypeStruct((8, width), full_type),
            jax.ShapeDtypeStruct((8, local_width), full_type),
        ),
        in_specs=[smem, smem, vmem, vmem, vmem],
        out_specs=[vmem] * 7,
        scratch_shapes=[
            pltpu.VMEM((count,) + small.shape, full_type),
            pltpu.SemaphoreType.DMA((4, count // 2)),
            pltpu.SemaphoreType.DMA((2, count)),
        ],
        compiler_params=pltpu.CompilerParams(
            collective_id=0, has_side_effects=True, vmem_limit_bytes=56 * 2**20
        ),
    )(owner, ends, tokens, attend_master, small)


def pack_small(vector_master, bias_master, owner, count):
    me = lax.axis_index("dp")
    wide = vector_master.shape[1]
    lanes = max(LANES, wide)
    fold = lanes // wide
    lane = jnp.arange(lanes)
    vectors = jnp.where(lane // wide == me % fold, jnp.tile(vector_master, (1, fold)), 0.0)
    narrow = bias_master.shape[1]
    spot = jnp.arange(narrow * count)
    biases = jnp.where(spot // narrow == owner[me], jnp.tile(bias_master, (1, count)), 0.0)
    small = jnp.concatenate(
        [jnp.pad(vectors, ((0, 2), (0, 0))), jnp.pad(biases, ((0, 3), (0, 0)))], axis=1
    )
    return small.astype(half_type).astype(full_type)


def layer_norm(hidden, gain, shift):
    center = jnp.mean(hidden, axis=-1, keepdims=True)
    offset = hidden - center
    spread = jnp.mean(offset * offset, axis=-1, keepdims=True)
    return offset * lax.rsqrt(spread + norm_epsilon) * gain + shift


def gelu_exact(values):
    return jax.nn.gelu(values, approximate=False)


def segment_ids(row_lengths, total_rows):
    ends = jnp.cumsum(row_lengths)
    places = jnp.arange(total_rows, dtype=jnp.int32)
    return jnp.sum((places[:, None] >= ends[None, :]).astype(jnp.int32), axis=1)


def adamw_step(weight, first, second, grad, rate, decay):
    first_next = first_decay * first + (1.0 - first_decay) * grad
    second_next = second_decay * second + (1.0 - second_decay) * grad * grad
    first_hat = first_next / (1.0 - first_decay**STEP)
    second_hat = second_next / (1.0 - second_decay**STEP)
    update = first_hat / (jnp.sqrt(second_hat) + adam_epsilon) + decay * weight
    return (first_next, second_next, weight - rate * update)


def contract_rows(left, right):
    return lax.dot_general(
        left, right, (((0,), (0,)), ((), ())), preferred_element_type=jnp.float32
    )


def contract_cols(left, right):
    return lax.dot_general(
        left, right, (((1,), (1,)), ((), ())), preferred_element_type=jnp.float32
    )


def local(
    tokens,
    lengths,
    owner,
    attend_master,
    attend_first,
    attend_second,
    output_master,
    output_first,
    output_second,
    dense_master,
    dense_first,
    dense_second,
    bias_master,
    bias_first,
    bias_second,
    vector_master,
    vector_first,
    vector_second,
    cotangent,
):
    half_type = jnp.bfloat16
    full_type = jnp.float32
    owner_count = owner.shape[0]
    places = jnp.arange(owner_count, dtype=jnp.int32)
    inverse = jnp.sum(jnp.where(owner[None, :] == places[:, None], places[None, :], 0), axis=1)
    def unstored(array):
        return jnp.take(array.reshape(shape), inverse, axis=1).reshape(array.shape)
    attend_rows = owner_count
    if True:
        shape = (tokens.shape[0], owner_count, tokens.shape[1] // owner_count)
        tokens = jnp.take(tokens.reshape(shape), owner, axis=1).reshape(tokens.shape)
        cotangent = jnp.take(cotangent.reshape(shape), owner, axis=1).reshape(cotangent.shape)
    ends = jnp.cumsum(lengths[0])
    small = pack_small(vector_master, bias_master, owner, owner_count)
    act_one, qa, ka, va, attend_w, vectors, bias_w = gather_project(
        tokens, attend_master, small, owner, ends, owner_count
    )
    output_w = lax.all_gather(output_master.astype(half_type), "dp", axis=0, tiled=True)
    dense_w = lax.all_gather(dense_master.astype(half_type), "dp", axis=1, tiled=True)
    if False:
        shape = (tokens.shape[0], owner_count, tokens.shape[1] // owner_count)
        tokens = jnp.take(tokens.reshape(shape), owner, axis=1).reshape(tokens.shape)
        cotangent = jnp.take(cotangent.reshape(shape), owner, axis=1).reshape(cotangent.shape)
    D = tokens.shape[1]
    total_rows = tokens.shape[0]
    local_width = attend_w.shape[2]
    head_count = local_width // HD
    unit_ratio = dense_w.shape[2]
    hidden_width = unit_ratio * local_width
    score_scale = HD ** (-0.5)
    w_query = attend_w[0]
    w_key = attend_w[1]
    w_value = attend_w[2]
    w_up = dense_w[0].reshape(D, hidden_width)
    w_down = dense_w[1].reshape(D, hidden_width)
    bias_up = bias_w[1:5].reshape(hidden_width)
    segments = segment_ids(lengths[0], total_rows)
    block_count = max(1, total_rows // 896)
    block_rows = total_rows // block_count
    inputs = tokens.astype(full_type)
    def unpack(arr):
        return jnp.stack([arr[h][:, (h % 2) * HD:(h % 2) * HD + HD] for h in range(head_count)], axis=1).reshape(total_rows, local_width)
    query = unpack(qa) * 8.0
    key_rows = unpack(ka)
    value_rows = unpack(va)
    query_heads = query.reshape(total_rows, head_count, HD)
    key_heads = key_rows.reshape(total_rows, head_count, HD)
    value_heads = value_rows.reshape(total_rows, head_count, HD)

    def block_scores(block_index):
        row_start = block_index * block_rows
        query_block = lax.dynamic_slice_in_dim(query_heads, row_start, block_rows, 0)
        segment_block = lax.dynamic_slice_in_dim(segments, row_start, block_rows, 0)
        scores = (
            jnp.einsum("qhd,khd->hqk", query_block, key_heads, preferred_element_type=full_type)
            * score_scale
        )
        allowed = (segment_block[:, None] == segments[None, :])[None]
        return jnp.where(allowed, scores, masked_score)

    def forward_block(block_index):
        scores = block_scores(block_index)
        top = jnp.max(scores, axis=-1, keepdims=True)
        weights = jnp.exp(scores - top)
        row_totals = jnp.sum(weights, axis=-1, keepdims=True)
        probs = (weights / row_totals).astype(half_type)
        mixed_block = jnp.einsum(
            "hqk,khd->qhd", probs, value_heads, preferred_element_type=full_type
        )
        return (mixed_block.reshape(block_rows, local_width), (top + jnp.log(row_totals))[:, :, 0])

    mixed_parts, log_totals = lax.map(forward_block, jnp.arange(block_count))
    mixed = mixed_parts.reshape(total_rows, local_width).astype(half_type)
    attn_total = lax.psum(contract_cols(mixed, output_w).astype(jnp.bfloat16), "tensor").astype(
        jnp.float32
    )
    hidden = inputs + attn_total + vectors[0]
    act_two = layer_norm(hidden, vectors[4], vectors[5]).astype(half_type)
    pre_act = jnp.dot(act_two, w_up, preferred_element_type=full_type) + bias_up
    activated, gelu_back = jax.vjp(gelu_exact, pre_act)
    act_hidden = activated.astype(half_type)
    dense_total = lax.psum(contract_cols(act_hidden, w_down).astype(jnp.bfloat16), "tensor").astype(
        jnp.float32
    )
    layer_output = (hidden + dense_total + vectors[1]).astype(half_type)
    grad_out = cotangent.astype(full_type)
    grad_down = contract_rows(cotangent, act_hidden)
    grad_bias_two = jnp.sum(grad_out, axis=0)
    grad_act = jnp.dot(cotangent, w_down, preferred_element_type=full_type)
    grad_pre = gelu_back(grad_act)[0].astype(half_type)
    grad_bias_up = jnp.sum(grad_pre.astype(full_type), axis=0)
    grad_up = contract_rows(act_two, grad_pre)
    dense_grad = jnp.stack([grad_up, grad_down]).reshape(2, D, unit_ratio, local_width)
    grad_norm_two = lax.psum(contract_cols(grad_pre, w_up).astype(jnp.bfloat16), "tensor").astype(
        jnp.float32
    )
    norm_two_back = jax.vjp(layer_norm, hidden, vectors[4], vectors[5])[1]
    grad_hidden_norm, grad_gain_two, grad_shift_two = norm_two_back(grad_norm_two)
    grad_hidden = grad_out + grad_hidden_norm
    grad_bias_out = jnp.sum(grad_hidden, axis=0)
    grad_attn = grad_hidden.astype(half_type)
    grad_output = contract_rows(grad_attn, mixed)
    grad_mixed = jnp.dot(grad_attn, output_w, preferred_element_type=full_type).astype(half_type)
    grad_mixed_heads = grad_mixed.reshape(total_rows, head_count, HD)

    def backward_block(carry, block_index):
        grad_key, grad_value = carry
        row_start = block_index * block_rows
        query_block = lax.dynamic_slice_in_dim(query_heads, row_start, block_rows, 0)
        grad_block = lax.dynamic_slice_in_dim(grad_mixed_heads, row_start, block_rows, 0)
        scores = block_scores(block_index)
        probs = jnp.exp(scores - log_totals[block_index][:, :, None])
        probs_low = probs.astype(half_type)
        grad_value = grad_value + jnp.einsum(
            "hqk,qhd->khd", probs_low, grad_block, preferred_element_type=full_type
        )
        grad_probs = jnp.einsum(
            "qhd,khd->hqk", grad_block, value_heads, preferred_element_type=full_type
        )
        row_dot = jnp.sum(probs * grad_probs, axis=-1, keepdims=True)
        grad_scores = (probs * (grad_probs - row_dot)).astype(half_type)
        grad_query_block = (
            jnp.einsum("hqk,khd->qhd", grad_scores, key_heads, preferred_element_type=full_type)
            * score_scale
        )
        grad_key = (
            grad_key
            + jnp.einsum("hqk,qhd->khd", grad_scores, query_block, preferred_element_type=full_type)
            * score_scale
        )
        return ((grad_key, grad_value), grad_query_block)

    empty = jnp.zeros((total_rows, head_count, HD), full_type)
    carried, grad_query_parts = lax.scan(backward_block, (empty, empty), jnp.arange(block_count))
    grad_query = grad_query_parts.reshape(total_rows, local_width).astype(half_type)
    grad_key_low = carried[0].reshape(total_rows, local_width).astype(half_type)
    grad_value_low = carried[1].reshape(total_rows, local_width).astype(half_type)
    grad_bias_query = jnp.sum(grad_query.astype(full_type), axis=0)
    attend_grad = jnp.stack(
        [
            contract_rows(act_one, grad_query),
            contract_rows(act_one, grad_key_low),
            contract_rows(act_one, grad_value_low),
        ]
    )
    norm_one_part = (
        contract_cols(grad_query, w_query)
        + contract_cols(grad_key_low, w_key)
        + contract_cols(grad_value_low, w_value)
    )
    grad_norm_one = lax.psum(norm_one_part.astype(jnp.bfloat16), "tensor").astype(jnp.float32)
    norm_one_back = jax.vjp(layer_norm, inputs, vectors[2], vectors[3])[1]
    grad_input_norm, grad_gain_one, grad_shift_one = norm_one_back(grad_norm_one)
    tokens_grad = (grad_hidden + grad_input_norm).astype(half_type)
    bias_grad = jnp.concatenate(
        [grad_bias_query[None], grad_bias_up.reshape(unit_ratio, local_width)], axis=0
    )
    vector_grad = jnp.stack(
        [grad_bias_out, grad_bias_two, grad_gain_one, grad_shift_one, grad_gain_two, grad_shift_two]
    )
    bias_stored = jnp.take(bias_grad.reshape(bias_grad.shape[0], owner_count, -1), owner, axis=1).reshape(bias_grad.shape)
    attend_sum, output_sum, dense_sum, bias_sum, vector_sum = (
        lax.psum_scatter(attend_grad, "dp", scatter_dimension=1, tiled=True),
        lax.psum_scatter(grad_output, "dp", scatter_dimension=0, tiled=True),
        lax.psum_scatter(dense_grad, "dp", scatter_dimension=1, tiled=True),
        lax.psum_scatter(bias_stored, "dp", scatter_dimension=1, tiled=True),
        lax.psum_scatter(vector_grad, "dp", scatter_dimension=1, tiled=True),
    )
    attend_new = adamw_step(
        attend_master, attend_first, attend_second, attend_sum, matrix_rate, matrix_decay
    )
    output_new = adamw_step(
        output_master, output_first, output_second, output_sum, output_rate, matrix_decay
    )
    dense_new = adamw_step(
        dense_master, dense_first, dense_second, dense_sum, matrix_rate, matrix_decay
    )
    bias_new = adamw_step(bias_master, bias_first, bias_second, bias_sum, bias_rate, 0.0)
    vector_new = adamw_step(
        vector_master, vector_first, vector_second, vector_sum, vector_rate, 0.0
    )
    return (
        unstored(layer_output),
        unstored(tokens_grad),
        attend_new[0],
        attend_new[1],
        attend_new[2],
        output_new[0],
        output_new[1],
        output_new[2],
        dense_new[0],
        dense_new[1],
        dense_new[2],
        bias_new[0],
        bias_new[1],
        bias_new[2],
        vector_new[0],
        vector_new[1],
        vector_new[2],
    )


def solution(mesh):
    return jax.shard_map(
        local,
        mesh=mesh,
        in_specs=(
            P("dp", None),
            P("dp", None),
            P(),
            P(None, "dp", "tensor"),
            P(None, "dp", "tensor"),
            P(None, "dp", "tensor"),
            P("dp", "tensor"),
            P("dp", "tensor"),
            P("dp", "tensor"),
            P(None, "dp", None, "tensor"),
            P(None, "dp", None, "tensor"),
            P(None, "dp", None, "tensor"),
            P(None, ("tensor", "dp")),
            P(None, ("tensor", "dp")),
            P(None, ("tensor", "dp")),
            P(None, "dp"),
            P(None, "dp"),
            P(None, "dp"),
            P("dp", None),
        ),
        out_specs=(
            P("dp", None),
            P("dp", None),
            P(None, "dp", "tensor"),
            P(None, "dp", "tensor"),
            P(None, "dp", "tensor"),
            P("dp", "tensor"),
            P("dp", "tensor"),
            P("dp", "tensor"),
            P(None, "dp", None, "tensor"),
            P(None, "dp", None, "tensor"),
            P(None, "dp", None, "tensor"),
            P(None, ("tensor", "dp")),
            P(None, ("tensor", "dp")),
            P(None, ("tensor", "dp")),
            P(None, "dp"),
            P(None, "dp"),
            P(None, "dp"),
        ),
        check_vma=False,
    )
```

```python
import functools

import jax
import jax.numpy as jnp
from jax import lax
from jax.experimental import pallas as pl
from jax.experimental.pallas import tpu as pltpu
from jax.sharding import PartitionSpec as P

HD = 64
STEP = 10
LANES = 128
BLOCK = 256
MESH = pl.DeviceIdType.MESH
BIG = 2.0**50

norm_epsilon = 1e-06
first_decay = 0.9
second_decay = 0.95
adam_epsilon = 1e-08
matrix_rate = 0.1
output_rate = 0.5
bias_rate = 0.5
vector_rate = 1.0
matrix_decay = 0.05

half_type = jnp.bfloat16
full_type = jnp.float32


def dot(left, right, left_dim=1, right_dim=0):
    return lax.dot_general(
        left, right, (((left_dim,), (right_dim,)), ((), ())), preferred_element_type=full_type
    )


def ring_pos(place, count):
    column = place % 2
    row = place // 2
    return row * (1 - column) + (count - 1 - row) * column


def ring_at(pos, count):
    near = (pos + 2 * count) % count
    down = near // (count // 2)
    return 2 * near * (1 - down) + (2 * count - 1 - 2 * near) * down


def normalized(x):
    center = jnp.mean(x, axis=-1, keepdims=True)
    offset = x - center
    spread = jnp.mean(offset * offset, axis=-1, keepdims=True)
    rate = lax.rsqrt(spread + norm_epsilon)
    return offset * rate, rate


class Gather:
    def __init__(self, view, width, sems, count):
        self.view, self.width, self.sems, self.count = view, width, sems, count
        self.steps = count // 2
        self.pos = ring_pos(lax.axis_index("dp"), count)
        self.tensor = lax.axis_index("tensor")

    def _copy(self, way, step, hops):
        sign = 1 - 2 * way
        part = (0, self.width)
        if step == self.steps - 1:
            part = (way * (self.width // 2), self.width // 2)
        block = self.view(ring_at(self.pos - sign * hops, self.count), *part)
        return pltpu.make_async_remote_copy(
            src_ref=block,
            dst_ref=block,
            send_sem=self.sems.at[2 * way, step],
            recv_sem=self.sems.at[2 * way + 1, step],
            device_id=(ring_at(self.pos + sign, self.count), self.tensor),
            device_id_type=MESH,
        )

    def advance(self, step):
        if step:
            for way in range(2):
                self._copy(way, step - 1, step).wait_recv()
        if step < self.steps:
            for way in range(2):
                self._copy(way, step, step).start()

    def sent(self):
        for step in range(self.steps):
            for way in range(2):
                self._copy(way, step, step).wait_send()


class RowSum:
    def __init__(self, term, given, sent, crossed, sems):
        self.term, self.given, self.sent_ref, self.crossed = term, given, sent, crossed
        self.sems = sems
        self.half = given.shape[1]
        self.dp, tensor = lax.axis_index("dp"), lax.axis_index("tensor")
        self.core = tensor % 2
        self.mate = tensor - tensor % 2 + (tensor + 1) % 2
        self.other = (tensor + 2) % 4

    def rows(self, core):
        return pl.ds(pl.multiple_of(core * self.half, self.half), self.half)

    def _give(self, i):
        return pltpu.make_async_remote_copy(
            src_ref=self.term.at[i, self.rows(1 - self.core), :],
            dst_ref=self.given.at[i],
            send_sem=self.sems.at[0, i],
            recv_sem=self.sems.at[1, i],
            device_id=(self.dp, self.mate),
            device_id_type=MESH,
        )

    def _cross(self, i):
        return pltpu.make_async_remote_copy(
            src_ref=self.sent_ref.at[i],
            dst_ref=self.crossed.at[i],
            send_sem=self.sems.at[2, i],
            recv_sem=self.sems.at[3, i],
            device_id=(self.dp, self.other),
            device_id_type=MESH,
        )

    def give(self, i):
        self._give(i).start()

    def cross(self, i):
        self._give(i).wait_recv()
        mine = self.term[i, self.rows(self.core), :].astype(full_type)
        self.sent_ref[i] = (mine + self.given[i].astype(full_type)).astype(half_type)
        self._cross(i).start()

    def total(self, i):
        self._cross(i).wait_recv()
        return self.sent_ref[i].astype(full_type) + self.crossed[i].astype(full_type)

    def finish(self, blocks):
        def done(i, carry):
            self._give(i).wait_send()
            self._cross(i).wait_send()
            return carry

        lax.fori_loop(0, blocks, done, 0)


class Share:
    def __init__(self, ref, sems):
        self.ref, self.sems = ref, sems
        self.dp, tensor = lax.axis_index("dp"), lax.axis_index("tensor")
        self.core = tensor % 2
        self.mate = tensor - tensor % 2 + (tensor + 1) % 2

    def rows(self, i, core):
        half = BLOCK // 2
        return pl.ds(pl.multiple_of(i * BLOCK + core * half, half), half)

    def _copy(self, i, core):
        piece = self.ref.at[self.rows(i, core), :]
        return pltpu.make_async_remote_copy(
            src_ref=piece,
            dst_ref=piece,
            send_sem=self.sems.at[0, i],
            recv_sem=self.sems.at[1, i],
            device_id=(self.dp, self.mate),
            device_id_type=MESH,
        )

    def put(self, i, value):
        self.ref[self.rows(i, self.core), :] = value
        self._copy(i, self.core).start()

    def arrived(self, i):
        self._copy(i, 1 - self.core).wait_recv()

    def finish(self, blocks):
        def done(i, carry):
            self._copy(i, self.core).wait_send()
            return carry

        lax.fori_loop(0, blocks, done, 0)


def greet(peers):
    barrier = pltpu.get_barrier_semaphore()
    for peer in peers:
        pl.semaphore_signal(barrier, inc=1, device_id=peer, device_id_type=MESH)
    return lambda: pl.semaphore_wait(barrier, len(peers))


def tensor_peers():
    dp, tensor = lax.axis_index("dp"), lax.axis_index("tensor")
    return [(dp, tensor - tensor % 2 + (tensor + 1) % 2), (dp, (tensor + 2) % 4)]


def ring_peers(count):
    dp, tensor = lax.axis_index("dp"), lax.axis_index("tensor")
    pos = ring_pos(dp, count)
    return [(ring_at(pos + 1, count), tensor), (ring_at(pos - 1, count), tensor)]


def dp_peers(count):
    dp, tensor = lax.axis_index("dp"), lax.axis_index("tensor")
    return [((dp + k) % count, tensor) for k in range(1, count)]


def three_parts(x):
    high = x.astype(half_type).astype(full_type)
    middle = (x - high).astype(half_type).astype(full_type)
    return high, middle, x - high - middle


def front_kernel(
    count, ends_ref, tok_ref, att_ref, out_ref, dense_ref, small_ref,
    a1_ref, qb_ref, ka_ref, va_ref, o_ref, a2_ref, h2_ref, w_ref, wo_ref, wd_ref, vec_ref, bias_ref,
    qa_ref, smalls, term, given, sent, crossed,
    gather_sems, small_sems, sum_sems, share_sems,
):
    me, tensor = lax.axis_index("dp"), lax.axis_index("tensor")
    total_rows, width = tok_ref.shape
    local_width = wo_ref.shape[1]
    ratio = dense_ref.shape[2]
    wide = width // count
    slots = ends_ref.shape[0]
    heads = local_width // HD
    blocks = total_rows // BLOCK
    half = BLOCK // 2
    greeted = greet(tensor_peers() + dp_peers(count))
    mine = pl.ds(pl.multiple_of(me * wide, wide), wide)
    smalls[me] = small_ref[...]
    for row in range(3):
        w_ref[mine, row * local_width : (row + 1) * local_width] = att_ref[row].astype(half_type)
    wo_ref[mine, :] = out_ref[...].astype(half_type)
    greeted()

    def place(block):
        return pl.ds(pl.multiple_of(block * wide, wide), wide)

    def small_copy(source, peer):
        return pltpu.make_async_remote_copy(
            src_ref=small_ref,
            dst_ref=smalls.at[source],
            send_sem=small_sems.at[0, peer],
            recv_sem=small_sems.at[1, source],
            device_id=(peer, tensor),
            device_id_type=MESH,
        )

    def send_small(k, carry):
        small_copy(me, (me + k) % count).start()
        return carry

    lax.fori_loop(1, count, send_small, 0)

    def attend_view(row):
        return lambda block, low, size: w_ref.at[
            place(block), pl.ds(row * local_width + low, size)
        ]

    def dense_view(row):
        return lambda block, low, size: wd_ref.at[row, place(block), pl.ds(low, size)]

    attend = [Gather(attend_view(row), local_width, gather_sems.at[row], count) for row in range(3)]
    attend.append(
        Gather(
            lambda block, low, size: wo_ref.at[place(block), pl.ds(low, size)],
            local_width, gather_sems.at[3], count,
        )
    )
    dense = [
        Gather(dense_view(row), ratio * local_width, gather_sems.at[4 + row], count)
        for row in range(2)
    ]
    for piece in attend:
        piece.advance(0)
    for row in range(2):
        for r in range(ratio):
            wd_ref[row, mine, r * local_width : (r + 1) * local_width] = dense_ref[
                row, :, r, :
            ].astype(half_type)

    def take_small(k, carry):
        source = (me + k) % count
        small_copy(source, source).wait_recv()
        return carry

    lax.fori_loop(1, count, take_small, 0)
    lanes = small_ref.shape[1] - local_width
    fold = lanes // wide
    bias = smalls[0, :, lanes:]
    for j in range(1, count):
        bias = bias + smalls[j, :, lanes:]
    bias_ref[...] = bias
    for window in range(width // lanes):
        piece = smalls[window * fold, :, :lanes]
        for j in range(window * fold + 1, (window + 1) * fold):
            piece = piece + smalls[j, :, :lanes]
        vec_ref[:, window * lanes : (window + 1) * lanes] = piece

    def norm_rows(i, carry):
        rows = pl.ds(pl.multiple_of(i * BLOCK, BLOCK), BLOCK)
        unit, _ = normalized(tok_ref[rows, :].astype(full_type))
        a1_ref[rows, :] = (unit * vec_ref[2:3, :] + vec_ref[3:4, :]).astype(half_type)
        return carry

    steps = count // 2
    done = 0
    for step in range(1, steps + 1):
        upto = min(blocks, -(-blocks * step // (steps - 1)))
        if upto > done:
            lax.fori_loop(done, upto, norm_rows, 0)
        done = max(done, upto)
        for piece in attend[: 3 if step == steps else 4]:
            piece.advance(step)
        if step == steps - 1:
            for piece in dense:
                piece.advance(0)

    lane = lax.broadcasted_iota(jnp.int32, (BLOCK, LANES), 1)
    low_half = lane < HD
    spot = lane % HD

    def project(i, carry):
        row = pl.multiple_of(i * BLOCK, BLOCK)
        rows = pl.ds(row, BLOCK)
        a1 = a1_ref[rows, :]
        qkv = dot(a1, w_ref[...])
        q, k, v = (qkv[:, part * local_width : (part + 1) * local_width] for part in range(3))
        q = (q + bias_ref[0:1, :]).astype(half_type).astype(full_type) * HD**-0.5
        index = row + lax.broadcasted_iota(jnp.int32, (BLOCK, LANES), 0)
        segment = jnp.zeros((BLOCK, LANES), jnp.int32)
        for slot in range(slots):
            segment = segment + jnp.where(index >= ends_ref[slot], 1, 0)
        same = spot == segment
        inside = spot <= slots
        q_mark = jnp.where(inside & ~same, -BIG, 0.0)
        k_mark = jnp.where(same, BIG, jnp.where((spot > slots) & (spot <= slots + 3), 1.0, 0.0))
        for head in range(heads):
            pair = slice(head // 2 * LANES, head // 2 * LANES + LANES)
            own = low_half if head % 2 == 0 else ~low_half
            qa_ref[head, rows, :] = jnp.where(own, q[:, pair], q_mark).astype(half_type)
            ka_ref[head, rows, :] = jnp.where(own, k[:, pair], k_mark).astype(half_type)
            va_ref[head, rows, :] = jnp.where(own, v[:, pair], 1.0).astype(half_type)
        return carry

    lax.fori_loop(0, blocks, project, 0)
    attend[3].advance(steps)

    rowsum = RowSum(term, given, sent, crossed, sum_sems)
    share = Share(a2_ref, share_sems)

    def attend_block(i):
        rows = pl.ds(pl.multiple_of(i * BLOCK, BLOCK), BLOCK)
        for head in range(heads):
            query = qa_ref[head, rows, :]
            scores = dot(query, ka_ref[head], 1, 1)
            top = jnp.max(scores, axis=1, keepdims=True)
            weights = jnp.exp(scores - top).astype(half_type)
            mixed = dot(weights, va_ref[head])
            turned = pltpu.roll(mixed, HD, 1)
            own = low_half if head % 2 == 0 else ~low_half
            log_total = three_parts(top + jnp.log(jnp.where(own, turned, mixed)))
            marked = query.astype(full_type)
            for part in range(3):
                marked = jnp.where(~own & (spot == slots + 1 + part), -log_total[part], marked)
            qb_ref[head, rows, :] = marked.astype(half_type)
            out = mixed / turned
            if head % 2 == 0:
                before = out
            else:
                pair = slice(head // 2 * LANES, head // 2 * LANES + LANES)
                o_ref[rows, pair] = jnp.where(low_half, before, out).astype(half_type)
        term[i] = dot(o_ref[rows, :], wo_ref[...], 1, 1).astype(half_type)

    def norm_block(i):
        x = tok_ref[share.rows(i, share.core), :].astype(full_type)
        hidden = x + rowsum.total(i) + vec_ref[0:1, :]
        h2_ref[pl.ds(pl.multiple_of(i * half, half), half), :] = hidden
        unit, _ = normalized(hidden)
        share.put(i, (unit * vec_ref[4:5, :] + vec_ref[5:6, :]).astype(half_type))

    def attend_step(i, carry):
        attend_block(i)
        rowsum.give(i)
        for step in range(1, steps):

            @pl.when(i == (step - 1) * blocks // steps)
            def _(step=step):
                for piece in dense:
                    piece.advance(step)

        @pl.when(i >= 1)
        def _():
            rowsum.cross(i - 1)

        @pl.when(i >= 2)
        def _():
            norm_block(i - 2)

        return carry

    lax.fori_loop(0, blocks, attend_step, 0)
    rowsum.cross(blocks - 1)
    norm_block(blocks - 2)
    norm_block(blocks - 1)
    for piece in dense:
        piece.advance(steps)

    def arrived(i, carry):
        share.arrived(i)
        return carry

    lax.fori_loop(0, blocks, arrived, 0)
    for piece in attend + dense:
        piece.sent()
    rowsum.finish(blocks)
    share.finish(blocks)

    def sent_small(k, carry):
        small_copy(me, (me + k) % count).wait_send()
        return carry

    lax.fori_loop(1, count, sent_small, 0)


def gelu_parts(z):
    phi = 0.5 + 0.5 * lax.erf(z * (0.5**0.5))
    slope = phi + z * (jnp.exp(-0.5 * z * z) * (2.0 * 3.141592653589793) ** -0.5)
    return z * phi, slope


def mlp_kernel(
    a2_ref, cot_ref, h2_ref, w_ref, vec_ref, bias_ref,
    down_ref, ga_ref, gh2_ref, grad_ref, gbias_ref, gvec_ref,
    term, given, sent, crossed, up_sum, down_sum,
    sum_sems, share_sems,
):
    total_rows, width = a2_ref.shape
    blocks = total_rows // BLOCK
    half = BLOCK // 2
    greeted = greet(tensor_peers())
    gbias_ref[...] = jnp.zeros_like(gbias_ref)
    gvec_ref[...] = jnp.zeros_like(gvec_ref)
    greeted()
    rowsum = RowSum(term, given, sent, crossed, sum_sems)
    share = Share(ga_ref, share_sems)

    def mlp_block(i):
        rows = pl.ds(pl.multiple_of(i * BLOCK, BLOCK), BLOCK)
        a2 = a2_ref[rows, :]
        gy = cot_ref[rows, :]
        u, slope = gelu_parts(dot(a2, w_ref[0]) + bias_ref[0:1, :])
        ul = u.astype(half_type)
        gz = (dot(gy, w_ref[1]) * slope).astype(half_type)
        term[i] = dot(gz, w_ref[0], 1, 1).astype(half_type)
        rowsum.give(i)
        gbias_ref[0:1, :] += jnp.sum(gz.astype(full_type), axis=0, keepdims=True)
        down_ref[rows, :] = dot(ul, w_ref[1], 1, 1).astype(half_type)
        up = dot(a2, gz, 0, 0)
        down = dot(gy, ul, 0, 0)

        @pl.when(i == 0)
        def _():
            up_sum[...] = up
            down_sum[...] = down

        @pl.when(i > 0)
        def _():
            up_sum[...] += up
            down_sum[...] += down

    def back_block(i):
        own = pl.ds(pl.multiple_of(i * half, half), half)
        gn = rowsum.total(i)
        unit, rate = normalized(h2_ref[own, :])
        e = gn * vec_ref[4:5, :]
        inner = e - jnp.mean(e, axis=-1, keepdims=True)
        inner = inner - unit * jnp.mean(e * unit, axis=-1, keepdims=True)
        gy = cot_ref[share.rows(i, share.core), :].astype(full_type)
        gh = gy + rate * inner
        gh2_ref[own, :] = gh
        share.put(i, gh.astype(half_type))
        gvec_ref[0:1, :] += jnp.sum(gh, axis=0, keepdims=True)
        gvec_ref[1:2, :] += jnp.sum(gy, axis=0, keepdims=True)
        gvec_ref[4:5, :] += jnp.sum(gn * unit, axis=0, keepdims=True)
        gvec_ref[5:6, :] += jnp.sum(gn, axis=0, keepdims=True)

    def step(i, carry):
        mlp_block(i)

        @pl.when(i >= 1)
        def _():
            rowsum.cross(i - 1)

        @pl.when(i >= 2)
        def _():
            back_block(i - 2)

        return carry

    lax.fori_loop(0, blocks, step, 0)
    rowsum.cross(blocks - 1)
    grad_ref[0] = up_sum[...].astype(half_type)
    grad_ref[1] = down_sum[...].astype(half_type)
    back_block(blocks - 2)
    back_block(blocks - 1)

    def arrived(i, carry):
        share.arrived(i)
        return carry

    lax.fori_loop(0, blocks, arrived, 0)
    rowsum.finish(blocks)
    share.finish(blocks)


class Scatter:
    def __init__(self, view, stage, taken, sems, count):
        self.view, self.stage, self.taken = view, stage, taken
        self.sems, self.count = sems, count
        self.pos = ring_pos(lax.axis_index("dp"), count)
        self.tensor = lax.axis_index("tensor")

    def _copy(self, way, step):
        sign = 1 - 2 * way
        return pltpu.make_async_remote_copy(
            src_ref=self.stage.at[way, step],
            dst_ref=self.taken.at[way, step],
            send_sem=self.sems.at[2 * way, step],
            recv_sem=self.sems.at[2 * way + 1, step],
            device_id=(ring_at(self.pos + sign, self.count), self.tensor),
            device_id_type=MESH,
        )

    def begin(self):
        for way in range(2):
            block = ring_at(self.pos - (1 - 2 * way), self.count)
            self.stage[way, 0] = self.view(way, block).astype(half_type)
            self._copy(way, 0).start()

    def advance(self, step):
        for way in range(2):
            block = ring_at(self.pos - (1 - 2 * way) * (1 + step), self.count)
            self._copy(way, step - 1).wait_recv()
            own = self.view(way, block).astype(full_type)
            total = self.taken[way, step - 1].astype(full_type) + own
            self.stage[way, step] = total.astype(half_type)
            self._copy(way, step).start()

    def total(self, way):
        last = self.count - 2
        self._copy(way, last).wait_recv()
        own = self.view(way, lax.axis_index("dp")).astype(full_type)
        return self.taken[way, last].astype(full_type) + own

    def finish(self):
        def done(step, carry):
            for way in range(2):
                self._copy(way, step).wait_send()
            return carry

        lax.fori_loop(0, self.count - 1, done, 0)


def attention_back_kernel(
    count, ga_ref, o_ref, qb_ref, ka_ref, va_ref, wo_ref, grad_ref, down_ref, h2_ref, vec_ref,
    gqkv_ref, sum_ref, out_ref,
    goa_ref, kt_ref, gqt_ref, given, sent, crossed, stage, taken,
    sum_sems, share_sems, scatter_sems,
):
    total_rows, width = ga_ref.shape
    local_width = wo_ref.shape[1]
    heads = local_width // HD
    blocks = total_rows // BLOCK
    half = BLOCK // 2
    wide = width // count
    greeted = greet(tensor_peers() + ring_peers(count))
    greeted()

    def view(way, block):
        return grad_ref[way, pl.ds(pl.multiple_of(block * wide, wide), wide), :]

    scatter = Scatter(view, stage, taken, scatter_sems, count)
    scatter.begin()
    rowsum = RowSum(down_ref, given, sent, crossed, sum_sems)
    share = Share(out_ref, share_sems)
    rowsum.give(0)
    lane = lax.broadcasted_iota(jnp.int32, (BLOCK, LANES), 1)
    low_half = lane < HD
    spot = lane % HD

    def prepare(i, carry):
        rows = pl.ds(pl.multiple_of(i * BLOCK, BLOCK), BLOCK)
        go = dot(ga_ref[rows, :], wo_ref[...]).astype(half_type).astype(full_type)
        both = go * o_ref[rows, :].astype(full_type)
        for head in range(heads):
            pair = slice(head // 2 * LANES, head // 2 * LANES + LANES)
            own = low_half if head % 2 == 0 else ~low_half
            inner = jnp.sum(jnp.where(own, both[:, pair], 0.0), axis=1, keepdims=True)
            high, middle, low = three_parts(inner)
            filled = jnp.where(own, go[:, pair], 0.0)
            for part, value in enumerate((high, middle, low)):
                filled = jnp.where(~own & (spot == part), -value, filled)
            goa_ref[head, rows, :] = filled.astype(half_type)
            if head % 2 == 0:
                before = ka_ref[head, rows, :].astype(full_type)
            else:
                k = jnp.where(low_half, before, ka_ref[head, rows, :].astype(full_type))
                kt_ref[pair, rows] = k.T.astype(half_type)
        return carry

    lax.fori_loop(0, blocks, prepare, 0)
    rowsum.give(1)

    def keys_block(j):
        rows = pl.ds(pl.multiple_of(j * BLOCK, BLOCK), BLOCK)
        for head in range(heads):
            scores = dot(ka_ref[head, rows, :], qb_ref[head], 1, 1)
            probs = jnp.exp(scores)
            gp = dot(va_ref[head, rows, :], goa_ref[head], 1, 1)
            gs = (probs * gp).astype(half_type)
            gv = dot(probs.astype(half_type), goa_ref[head])
            gk = dot(gs, qb_ref[head])
            own = slice(head * HD, head * HD + HD)
            gqt = dot(kt_ref[own, rows], gs)

            @pl.when(j == 0)
            def _():
                gqt_ref[own, :] = gqt

            @pl.when(j > 0)
            def _():
                gqt_ref[own, :] += gqt

            if head % 2 == 0:
                gk_even, gv_even = gk, gv
            else:
                pair = slice(head // 2 * LANES, head // 2 * LANES + LANES)
                for part, value in ((1, (gk_even, gk)), (2, (gv_even, gv))):
                    base = part * local_width + head // 2 * LANES
                    gqkv_ref[rows, base : base + LANES] = jnp.where(low_half, *value).astype(
                        half_type
                    )

    def output_block(i):
        own = pl.ds(pl.multiple_of(i * half, half), half)
        total = h2_ref[own, :] + rowsum.total(i) + vec_ref[1:2, :]
        share.put(i, total.astype(half_type))

    def step(j, carry):
        keys_block(j)

        hops = count - 1
        per = -(-hops // blocks)
        for t in range(per):
            hop = j * per + t

            @pl.when((hop >= 1) & (hop < hops))
            def _(hop=hop):
                scatter.advance(hop)

        @pl.when(j < blocks - 2)
        def _():
            rowsum.give(j + 2)

        rowsum.cross(j)

        @pl.when(j >= 1)
        def _():
            output_block(j - 1)

        return carry

    lax.fori_loop(0, blocks, step, 0)
    output_block(blocks - 1)

    def turn(i, carry):
        rows = pl.ds(pl.multiple_of(i * BLOCK, BLOCK), BLOCK)
        gqkv_ref[rows, :local_width] = (gqt_ref[:, rows].T * HD**-0.5).astype(half_type)
        return carry

    lax.fori_loop(0, blocks, turn, 0)
    for way in range(2):
        sum_ref[way] = scatter.total(way)

    def arrived(i, carry):
        share.arrived(i)
        return carry

    lax.fori_loop(0, blocks, arrived, 0)
    scatter.finish()
    rowsum.finish(blocks)
    share.finish(blocks)


def end_kernel(
    count, gqkv_ref, w_ref, a1_ref, ga_ref, o_ref, gh2_ref, tok_ref, vec_ref, gbias_ref, gvec_ref,
    tg_ref, sum_ref, small_ref,
    term, given, sent, crossed, grads, stage, taken, small_mine, small_taken, small_mate,
    sum_sems, share_sems, scatter_sems, small_sems, mate_sems,
):
    total_rows, width = a1_ref.shape
    local_width = w_ref.shape[1] // 3
    blocks = total_rows // BLOCK
    half = BLOCK // 2
    wide = width // count
    lanes = small_ref.shape[1] - local_width
    fold = lanes // wide
    me, tensor = lax.axis_index("dp"), lax.axis_index("tensor")
    mate = tensor - tensor % 2 + (tensor + 1) % 2
    greeted = greet(tensor_peers() + dp_peers(count))
    small_mine[:, :width] = gvec_ref[...]
    ones = jnp.ones((8, total_rows), half_type)
    bias_query = dot(ones, gqkv_ref[:, :local_width])
    small_mine[0:1, width:] = bias_query[0:1, :]
    ratio = gbias_ref.shape[1] // local_width
    for r in range(ratio):
        small_mine[1 + r : 2 + r, width:] = gbias_ref[0:1, r * local_width : (r + 1) * local_width]
    small_mine[1 + ratio :, width:] = jnp.zeros((7 - ratio, local_width), full_type)
    greeted()

    def small_copy(part, source, peer):
        window = pl.ds(pl.multiple_of(peer // fold * lanes, lanes), lanes)
        return pltpu.make_async_remote_copy(
            src_ref=small_mine.at[:, pl.ds(width, local_width) if part else window],
            dst_ref=small_taken.at[source, :, pl.ds(lanes, local_width) if part else pl.ds(0, lanes)],
            send_sem=small_sems.at[2 * part, peer],
            recv_sem=small_sems.at[2 * part + 1, source],
            device_id=(peer, tensor),
            device_id_type=MESH,
        )

    def send_small(part):
        def send(k, carry):
            small_copy(part, me, (me + k) % count).start()
            return carry

        lax.fori_loop(1, count, send, 0)

    send_small(1)
    rowsum = RowSum(term, given, sent, crossed, sum_sems)
    share = Share(tg_ref, share_sems)

    def view(way, block):
        rows = pl.ds(pl.multiple_of(block * wide, wide), wide)
        return jnp.stack([grads[2 * way, rows, :], grads[2 * way + 1, rows, :]])

    scatter = Scatter(view, stage, taken, scatter_sems, count)

    def norm_term(i):
        rows = pl.ds(pl.multiple_of(i * BLOCK, BLOCK), BLOCK)
        term[i] = dot(gqkv_ref[rows, :], w_ref[...], 1, 1).astype(half_type)
        rowsum.give(i)

    def norm_block(i):
        own = pl.ds(pl.multiple_of(i * half, half), half)
        gn = rowsum.total(i)
        unit, rate = normalized(tok_ref[share.rows(i, share.core), :].astype(full_type))
        e = gn * vec_ref[2:3, :]
        inner = e - jnp.mean(e, axis=-1, keepdims=True)
        inner = inner - unit * jnp.mean(e * unit, axis=-1, keepdims=True)
        share.put(i, (gh2_ref[own, :] + rate * inner).astype(half_type))
        small_mine[2:3, :width] += jnp.sum(gn * unit, axis=0, keepdims=True)
        small_mine[3:4, :width] += jnp.sum(gn, axis=0, keepdims=True)

    def weight_grads(c, carry):
        columns = pl.ds(pl.multiple_of(c * BLOCK, BLOCK), BLOCK)
        three = dot(a1_ref[:, columns], gqkv_ref[...], 0, 0)
        for row in range(3):
            grads[row, columns, :] = three[:, row * local_width : (row + 1) * local_width]
        grads[3, columns, :] = dot(ga_ref[:, columns], o_ref[...], 0, 0)
        return carry

    norm_term(0)
    norm_term(1)
    lax.fori_loop(0, 1, weight_grads, 0)
    rowsum.cross(0)
    lax.fori_loop(1, width // BLOCK, weight_grads, 0)
    scatter.begin()
    hops = count - 1
    per = -(-hops // blocks)

    def step(i, carry):
        @pl.when(i < blocks - 2)
        def _():
            norm_term(i + 2)

        @pl.when(i < blocks - 1)
        def _():
            rowsum.cross(i + 1)

        norm_block(i)
        for t in range(per):
            hop = i * per + t

            @pl.when((hop >= 1) & (hop < hops))
            def _(hop=hop):
                scatter.advance(hop)

        return carry

    lax.fori_loop(0, blocks, step, 0)
    send_small(0)
    for way in range(2):
        total = scatter.total(way)
        sum_ref[2 * way] = total[0]
        sum_ref[2 * way + 1] = total[1]
    for part in range(2):
        window = pl.ds(pl.multiple_of(me // fold * lanes, lanes), lanes)
        here = slice(lanes, lanes + local_width) if part else slice(0, lanes)
        small_taken[me, :, here] = small_mine[:, width:] if part else small_mine[:, window]

        def take(k, carry, part=part):
            source = (me + k) % count
            small_copy(part, source, source).wait_recv()
            return carry

        lax.fori_loop(1, count, take, 0)
    total = small_taken[0]
    for j in range(1, count):
        total = total + small_taken[j]
    small_ref[...] = total
    pair = pltpu.make_async_remote_copy(
        src_ref=small_ref.at[:, pl.ds(0, lanes)],
        dst_ref=small_mate,
        send_sem=mate_sems.at[0],
        recv_sem=mate_sems.at[1],
        device_id=(me, mate),
        device_id_type=MESH,
    )
    pair.start()
    pair.wait()
    small_ref[:, :lanes] = total[:, :lanes] + small_mate[...]

    def arrived(i, carry):
        share.arrived(i)
        return carry

    lax.fori_loop(0, blocks, arrived, 0)
    scatter.finish()
    rowsum.finish(blocks)
    share.finish(blocks)
    for part in range(2):

        def done(k, carry, part=part):
            small_copy(part, me, (me + k) % count).wait_send()
            return carry

        lax.fori_loop(1, count, done, 0)


def permute_kernel(back, owner_ref, *refs):
    for x_ref, y_ref in zip(refs[: len(refs) // 2], refs[len(refs) // 2 :]):
        count = owner_ref.shape[0]
        wide = x_ref.shape[1] // count
        for j in range(count):
            natural = pl.ds(pl.multiple_of(owner_ref[j] * wide, wide), wide)
            stored = slice(j * wide, (j + 1) * wide)
            if back:
                y_ref[:, natural] = x_ref[:, stored]
            else:
                y_ref[:, stored] = x_ref[:, natural]


def permuted(arrays, owner, back):
    rows, width = arrays[0].shape
    count = owner.shape[0]
    wide = width // count
    if wide % LANES:
        order = jnp.argsort(owner) if back else owner
        shape = (rows, count, wide)
        return [jnp.take(x.reshape(shape), order, axis=1).reshape(rows, width) for x in arrays]
    spec = pl.BlockSpec((BLOCK, width), lambda i, *_: (i, 0))
    return pl.pallas_call(
        functools.partial(permute_kernel, back),
        out_shape=[jax.ShapeDtypeStruct(x.shape, x.dtype) for x in arrays],
        grid_spec=pltpu.PrefetchScalarGridSpec(
            num_scalar_prefetch=1,
            grid=(rows // BLOCK,),
            in_specs=[spec] * len(arrays),
            out_specs=[spec] * len(arrays),
        ),
        compiler_params=pltpu.CompilerParams(vmem_limit_bytes=32 * 2**20),
    )(owner, *arrays)


def adamw_step(weight, first, second, grad, rate, decay):
    first_next = first_decay * first + (1.0 - first_decay) * grad
    second_next = second_decay * second + (1.0 - second_decay) * grad * grad
    first_hat = first_next / (1.0 - first_decay**STEP)
    second_hat = second_next / (1.0 - second_decay**STEP)
    update = first_hat / (jnp.sqrt(second_hat) + adam_epsilon) + decay * weight
    return (first_next, second_next, weight - rate * update)


def pack_small(vector_master, bias_master, owner, count):
    me = lax.axis_index("dp")
    wide = vector_master.shape[1]
    lanes = max(LANES, wide)
    fold = lanes // wide
    lane = jnp.arange(lanes)
    vectors = jnp.where(lane // wide == me % fold, jnp.tile(vector_master, (1, fold)), 0.0)
    narrow = bias_master.shape[1]
    spot = jnp.arange(narrow * count)
    biases = jnp.where(spot // narrow == owner[me], jnp.tile(bias_master, (1, count)), 0.0)
    small = jnp.concatenate(
        [jnp.pad(vectors, ((0, 2), (0, 0))), jnp.pad(biases, ((0, 3), (0, 0)))], axis=1
    )
    return small.astype(half_type).astype(full_type)


def call(kernel, collective, outs, scratch, operands, scalars=0, limit=58):
    vmem = pl.BlockSpec(memory_space=pltpu.VMEM)
    smem = pl.BlockSpec(memory_space=pltpu.SMEM)
    return pl.pallas_call(
        kernel,
        out_shape=[jax.ShapeDtypeStruct(shape, dtype) for shape, dtype in outs],
        in_specs=[smem] * scalars + [vmem] * (len(operands) - scalars),
        out_specs=[vmem] * len(outs),
        scratch_shapes=scratch,
        compiler_params=pltpu.CompilerParams(
            collective_id=collective, has_side_effects=True, vmem_limit_bytes=limit * 2**20
        ),
    )(*operands)


def dma(*shape):
    return pltpu.SemaphoreType.DMA(shape)


def local(
    tokens,
    lengths,
    owner,
    attend_master,
    attend_first,
    attend_second,
    output_master,
    output_first,
    output_second,
    dense_master,
    dense_first,
    dense_second,
    bias_master,
    bias_first,
    bias_second,
    vector_master,
    vector_first,
    vector_second,
    cotangent,
):
    count = owner.shape[0]
    rows, width = tokens.shape
    local_width = output_master.shape[1]
    ratio = dense_master.shape[2]
    hidden = ratio * local_width
    heads = local_width // HD
    blocks = rows // BLOCK
    half = BLOCK // 2
    wide = width // count
    lanes = max(LANES, wide)
    me = lax.axis_index("dp")

    tok, cot = permuted([tokens, cotangent], owner, False)
    small = pack_small(vector_master, bias_master, owner, count)
    ends = jnp.cumsum(lengths[0])
    row_sum = [pltpu.VMEM((blocks, half, width), half_type)] * 3
    heads_shape = (heads, rows, LANES)
    a1, qb, ka, va, o, a2, h2, w, wo, wd, vec, bias = call(
        functools.partial(front_kernel, count),
        0,
        [
            ((rows, width), half_type),
            (heads_shape, half_type),
            (heads_shape, half_type),
            (heads_shape, half_type),
            ((rows, local_width), half_type),
            ((rows, width), half_type),
            ((rows // 2, width), full_type),
            ((width, 3 * local_width), half_type),
            ((width, local_width), half_type),
            ((2, width, hidden), half_type),
            ((8, width), full_type),
            ((8, local_width), full_type),
        ],
        [
            pltpu.VMEM(heads_shape, half_type),
            pltpu.VMEM((count,) + small.shape, full_type),
            pltpu.VMEM((blocks, BLOCK, width), half_type),
            *row_sum,
            dma(6, 4, count // 2),
            dma(2, count),
            dma(4, blocks),
            dma(2, blocks),
        ],
        (ends, tok, attend_master, output_master, dense_master, small),
        scalars=1,
    )
    bias_up = bias[1 : 1 + ratio].reshape(1, hidden)
    down, ga, gh2, grad, gbias, gvec = call(
        mlp_kernel,
        1,
        [
            ((rows, width), half_type),
            ((rows, width), half_type),
            ((rows // 2, width), full_type),
            ((2, width, hidden), half_type),
            ((8, hidden), full_type),
            ((8, width), full_type),
        ],
        [
            pltpu.VMEM((blocks, BLOCK, width), half_type),
            *row_sum,
            pltpu.VMEM((width, hidden), full_type),
            pltpu.VMEM((width, hidden), full_type),
            dma(4, blocks),
            dma(2, blocks),
        ],
        (a2, cot, h2, wd, vec, bias_up),
    )
    gqkv, dense_sum, layer_output = call(
        functools.partial(attention_back_kernel, count),
        2,
        [
            ((rows, 3 * local_width), half_type),
            ((2, wide, hidden), full_type),
            ((rows, width), half_type),
        ],
        [
            pltpu.VMEM(heads_shape, half_type),
            pltpu.VMEM((local_width, rows), half_type),
            pltpu.VMEM((local_width, rows), full_type),
            *row_sum,
            pltpu.VMEM((2, count - 1, wide, hidden), half_type),
            pltpu.VMEM((2, count - 1, wide, hidden), half_type),
            dma(4, blocks),
            dma(2, blocks),
            dma(4, count - 1),
        ],
        (ga, o, qb, ka, va, wo, grad, down.reshape(blocks, BLOCK, width), h2, vec),
    )
    tokens_grad, weight_sum, small_sum = call(
        functools.partial(end_kernel, count),
        3,
        [
            ((rows, width), half_type),
            ((4, wide, local_width), full_type),
            ((8, lanes + local_width), full_type),
        ],
        [
            pltpu.VMEM((blocks, BLOCK, width), half_type),
            *row_sum,
            pltpu.VMEM((4, width, local_width), full_type),
            pltpu.VMEM((2, count - 1, 2, wide, local_width), half_type),
            pltpu.VMEM((2, count - 1, 2, wide, local_width), half_type),
            pltpu.VMEM((8, width + local_width), full_type),
            pltpu.VMEM((count, 8, lanes + local_width), full_type),
            pltpu.VMEM((8, lanes), full_type),
            dma(4, blocks),
            dma(2, blocks),
            dma(4, count - 1),
            dma(4, count),
            dma(2),
        ],
        (gqkv, w, a1, ga, o, gh2, tok, vec, gbias, gvec),
    )
    layer_output, tokens_grad = permuted([layer_output, tokens_grad], owner, True)
    dense_sum = dense_sum.reshape(dense_master.shape)
    vector_sum = lax.dynamic_slice_in_dim(
        small_sum[:6, :lanes], me % (lanes // wide) * wide, wide, axis=1
    )
    narrow = bias_master.shape[1]
    bias_sum = lax.dynamic_slice_in_dim(
        small_sum[: 1 + ratio, lanes:], owner[me] * narrow, narrow, axis=1
    )
    attend_new = adamw_step(
        attend_master, attend_first, attend_second, weight_sum[:3], matrix_rate, matrix_decay
    )
    output_new = adamw_step(
        output_master, output_first, output_second, weight_sum[3], output_rate, matrix_decay
    )
    dense_new = adamw_step(
        dense_master, dense_first, dense_second, dense_sum, matrix_rate, matrix_decay
    )
    bias_new = adamw_step(bias_master, bias_first, bias_second, bias_sum, bias_rate, 0.0)
    vector_new = adamw_step(
        vector_master, vector_first, vector_second, vector_sum, vector_rate, 0.0
    )
    return (
        layer_output,
        tokens_grad,
        *attend_new,
        *output_new,
        *dense_new,
        *bias_new,
        *vector_new,
    )


def solution(mesh):
    return jax.shard_map(
        local,
        mesh=mesh,
        in_specs=(
            P("dp", None),
            P("dp", None),
            P(),
            P(None, "dp", "tensor"),
            P(None, "dp", "tensor"),
            P(None, "dp", "tensor"),
            P("dp", "tensor"),
            P("dp", "tensor"),
            P("dp", "tensor"),
            P(None, "dp", None, "tensor"),
            P(None, "dp", None, "tensor"),
            P(None, "dp", None, "tensor"),
            P(None, ("tensor", "dp")),
            P(None, ("tensor", "dp")),
            P(None, ("tensor", "dp")),
            P(None, "dp"),
            P(None, "dp"),
            P(None, "dp"),
            P("dp", None),
        ),
        out_specs=(
            P("dp", None),
            P("dp", None),
            P(None, "dp", "tensor"),
            P(None, "dp", "tensor"),
            P(None, "dp", "tensor"),
            P("dp", "tensor"),
            P("dp", "tensor"),
            P("dp", "tensor"),
            P(None, "dp", None, "tensor"),
            P(None, "dp", None, "tensor"),
            P(None, "dp", None, "tensor"),
            P(None, ("tensor", "dp")),
            P(None, ("tensor", "dp")),
            P(None, ("tensor", "dp")),
            P(None, "dp"),
            P(None, "dp"),
            P(None, "dp"),
        ),
        check_vma=False,
    )
```

```python
import functools

import jax
import jax.numpy as jnp
from jax import lax
from jax.experimental import pallas as pl
from jax.experimental.pallas import tpu as pltpu
from jax.sharding import PartitionSpec as P

HD = 64
STEP = 10
LANES = 128
BLOCK = 256
MESH = pl.DeviceIdType.MESH
BIG = 2.0**50

norm_epsilon = 1e-06
first_decay = 0.9
second_decay = 0.95
adam_epsilon = 1e-08
matrix_rate = 0.1
output_rate = 0.5
bias_rate = 0.5
vector_rate = 1.0
matrix_decay = 0.05

half_type = jnp.bfloat16
full_type = jnp.float32


def dot(left, right, left_dim=1, right_dim=0):
    return lax.dot_general(
        left, right, (((left_dim,), (right_dim,)), ((), ())), preferred_element_type=full_type
    )


def ring_pos(place, count):
    column = place % 2
    row = place // 2
    return row * (1 - column) + (count - 1 - row) * column


def ring_at(pos, count):
    near = (pos + 2 * count) % count
    down = near // (count // 2)
    return 2 * near * (1 - down) + (2 * count - 1 - 2 * near) * down


def normalized(x):
    center = jnp.mean(x, axis=-1, keepdims=True)
    offset = x - center
    spread = jnp.mean(offset * offset, axis=-1, keepdims=True)
    rate = lax.rsqrt(spread + norm_epsilon)
    return offset * rate, rate


class Gather:
    def __init__(self, view, width, sems, count):
        self.view, self.width, self.sems, self.count = view, width, sems, count
        self.steps = count // 2
        self.pos = ring_pos(lax.axis_index("dp"), count)
        self.tensor = lax.axis_index("tensor")

    def _copy(self, way, step, hops):
        sign = 1 - 2 * way
        part = (0, self.width)
        if step == self.steps - 1:
            part = (way * (self.width // 2), self.width // 2)
        block = self.view(ring_at(self.pos - sign * hops, self.count), *part)
        return pltpu.make_async_remote_copy(
            src_ref=block,
            dst_ref=block,
            send_sem=self.sems.at[2 * way, step],
            recv_sem=self.sems.at[2 * way + 1, step],
            device_id=(ring_at(self.pos + sign, self.count), self.tensor),
            device_id_type=MESH,
        )

    def advance(self, step):
        if step:
            for way in range(2):
                self._copy(way, step - 1, step).wait_recv()
        if step < self.steps:
            for way in range(2):
                self._copy(way, step, step).start()

    def sent(self):
        for step in range(self.steps):
            for way in range(2):
                self._copy(way, step, step).wait_send()


class RowSum:
    def __init__(self, term, given, sent, crossed, sems):
        self.term, self.given, self.sent_ref, self.crossed = term, given, sent, crossed
        self.slots, self.blocks = term.shape[0], given.shape[0]
        self.sems = sems
        self.half = given.shape[1]
        self.dp, tensor = lax.axis_index("dp"), lax.axis_index("tensor")
        self.core = tensor % 2
        self.mate = tensor - tensor % 2 + (tensor + 1) % 2
        self.other = (tensor + 2) % 4

    def rows(self, core):
        return pl.ds(pl.multiple_of(core * self.half, self.half), self.half)

    def _give(self, i):
        return pltpu.make_async_remote_copy(
            src_ref=self.term.at[i % self.slots, self.rows(1 - self.core), :],
            dst_ref=self.given.at[i],
            send_sem=self.sems.at[0, i],
            recv_sem=self.sems.at[1, i],
            device_id=(self.dp, self.mate),
            device_id_type=MESH,
        )

    def _cross(self, i):
        return pltpu.make_async_remote_copy(
            src_ref=self.sent_ref.at[i],
            dst_ref=self.crossed.at[i],
            send_sem=self.sems.at[2, i],
            recv_sem=self.sems.at[3, i],
            device_id=(self.dp, self.other),
            device_id_type=MESH,
        )

    def free(self, i):
        if self.slots < self.blocks:

            @pl.when(i >= self.slots)
            def _():
                self._give(i - self.slots).wait_send()

    def give(self, i):
        self._give(i).start()

    def cross(self, i):
        self._give(i).wait_recv()
        mine = self.term[i % self.slots, self.rows(self.core), :].astype(full_type)
        self.sent_ref[i] = (mine + self.given[i].astype(full_type)).astype(half_type)
        self._cross(i).start()

    def total(self, i):
        self._cross(i).wait_recv()
        return self.sent_ref[i].astype(full_type) + self.crossed[i].astype(full_type)

    def finish(self):
        def given(i, carry):
            self._give(i).wait_send()
            return carry

        def crossed(i, carry):
            self._cross(i).wait_send()
            return carry

        lax.fori_loop(max(self.blocks - self.slots, 0), self.blocks, given, 0)
        lax.fori_loop(0, self.blocks, crossed, 0)


class Share:
    def __init__(self, ref, sems):
        self.ref, self.sems = ref, sems
        self.dp, tensor = lax.axis_index("dp"), lax.axis_index("tensor")
        self.core = tensor % 2
        self.mate = tensor - tensor % 2 + (tensor + 1) % 2

    def rows(self, i, core):
        half = BLOCK // 2
        return pl.ds(pl.multiple_of(i * BLOCK + core * half, half), half)

    def _copy(self, i, core):
        piece = self.ref.at[self.rows(i, core), :]
        return pltpu.make_async_remote_copy(
            src_ref=piece,
            dst_ref=piece,
            send_sem=self.sems.at[0, i],
            recv_sem=self.sems.at[1, i],
            device_id=(self.dp, self.mate),
            device_id_type=MESH,
        )

    def put(self, i, value):
        self.ref[self.rows(i, self.core), :] = value
        self._copy(i, self.core).start()

    def arrived(self, i):
        self._copy(i, 1 - self.core).wait_recv()

    def finish(self, blocks):
        def done(i, carry):
            self._copy(i, self.core).wait_send()
            return carry

        lax.fori_loop(0, blocks, done, 0)


def greet(peers):
    barrier = pltpu.get_barrier_semaphore()
    for peer in peers:
        pl.semaphore_signal(barrier, inc=1, device_id=peer, device_id_type=MESH)
    return lambda: pl.semaphore_wait(barrier, len(peers))


def tensor_peers():
    dp, tensor = lax.axis_index("dp"), lax.axis_index("tensor")
    return [(dp, tensor - tensor % 2 + (tensor + 1) % 2), (dp, (tensor + 2) % 4)]


def ring_peers(count):
    dp, tensor = lax.axis_index("dp"), lax.axis_index("tensor")
    pos = ring_pos(dp, count)
    return [(ring_at(pos + 1, count), tensor), (ring_at(pos - 1, count), tensor)]


def dp_peers(count):
    dp, tensor = lax.axis_index("dp"), lax.axis_index("tensor")
    return [((dp + k) % count, tensor) for k in range(1, count)]


def three_parts(x):
    high = x.astype(half_type).astype(full_type)
    middle = (x - high).astype(half_type).astype(full_type)
    return high, middle, x - high - middle


def gelu_parts(z):
    phi = 0.5 + 0.5 * lax.erf(z * (0.5**0.5))
    slope = phi + z * (jnp.exp(-0.5 * z * z) * (2.0 * 3.141592653589793) ** -0.5)
    return z * phi, slope


def fetch(source, target, sems):
    def copy(i):
        rows = pl.ds(pl.multiple_of(i * BLOCK, BLOCK), BLOCK)
        return pltpu.make_async_copy(source.at[rows, :], target.at[rows, :], sems.at[i])

    return copy


def stored_order(x, owner_ref):
    count = owner_ref.shape[0]
    wide = x.shape[1] // count
    if wide % LANES:
        return x
    parts = []
    for j in range(count):
        total = None
        for n in range(count):
            term = x[:, n * wide : (n + 1) * wide] * jnp.where(owner_ref[j] == n, 1.0, 0.0)
            total = term if total is None else total + term
        parts.append(total)
    return jnp.concatenate(parts, axis=1)


def front_kernel(
    count, len_ref, owner_ref, tok_hbm, cot_hbm, att_ref, out_ref, dense_ref, vector_ref, split_ref,
    a1_hbm, ga_hbm, h2_hbm, own_hbm, qa_hbm, ka_hbm, va_hbm, o_hbm, w_hbm, wo_hbm, gh2_hbm, down_hbm,
    up_hbm, dn_hbm, vec_ref, gbias_ref, gvec_ref,
    own_ref, qa_ref, ka_ref, va_ref, o_ref, w_ref, wo_ref, gh2_ref, down_ref, up_ref, dn_ref,
    norm_ref, cot_ref, wd_ref, ga_ref, bias_ref, b1_ref, small_ref, smalls,
    term, given, sent, crossed, term2, given2, sent2, crossed2,
    gather_sems, small_sems, sum_sems, sum2_sems, share_sems, put_sems, local_sems, whole_sems,
):
    me, tensor = lax.axis_index("dp"), lax.axis_index("tensor")
    total_rows, width = norm_ref.shape
    local_width = wo_ref.shape[1]
    ratio = dense_ref.shape[2]
    wide = width // count
    slots = len_ref.shape[1]
    heads = local_width // HD
    blocks = total_rows // BLOCK
    half = BLOCK // 2
    lanes = small_ref.shape[1] - local_width
    fold = lanes // wide
    steps = count // 2
    core = tensor % 2

    greeted = greet(tensor_peers() + dp_peers(count))
    tokens_in = fetch(tok_hbm, norm_ref, local_sems.at[0])
    cot_in = fetch(cot_hbm, cot_ref, local_sems.at[1])
    a1_out = fetch(norm_ref, a1_hbm, local_sems.at[2])
    for i in range(blocks):
        tokens_in(i).start()
    for i in range(blocks):
        cot_in(i).start()
    mine = pl.ds(pl.multiple_of(me * wide, wide), wide)
    for row in range(3):
        w_ref[mine, row * local_width : (row + 1) * local_width] = att_ref[row].astype(half_type)
    wo_ref[mine, :] = out_ref[...].astype(half_type)

    small_ref[...] = jnp.zeros_like(small_ref)
    vectors = vector_ref[...].astype(half_type)
    if fold == 1:
        small_ref[0:6, :lanes] = vectors.astype(full_type)
    else:
        row = lax.broadcasted_iota(jnp.int32, (wide, lanes), 0)
        column = lax.broadcasted_iota(jnp.int32, (wide, lanes), 1)
        spread = jnp.where(column == row + me % fold * wide, 1.0, 0.0).astype(half_type)
        small_ref[0:6, :lanes] = dot(vectors, spread)
    narrow = split_ref.shape[1]
    row = lax.broadcasted_iota(jnp.int32, (narrow, local_width), 0)
    column = lax.broadcasted_iota(jnp.int32, (narrow, local_width), 1)
    spread = jnp.where(column == row + owner_ref[me] * narrow, 1.0, 0.0).astype(half_type)
    small_ref[0 : 1 + ratio, lanes:] = dot(split_ref[...].astype(half_type), spread)
    smalls[me] = small_ref[...]
    greeted()

    def place(block):
        return pl.ds(pl.multiple_of(block * wide, wide), wide)

    def small_copy(source, peer):
        return pltpu.make_async_remote_copy(
            src_ref=small_ref,
            dst_ref=smalls.at[source],
            send_sem=small_sems.at[0, peer],
            recv_sem=small_sems.at[1, source],
            device_id=(peer, tensor),
            device_id_type=MESH,
        )

    def send_small(k, carry):
        small_copy(me, (me + k) % count).start()
        return carry

    lax.fori_loop(1, count, send_small, 0)

    def attend_view(row):
        return lambda block, low, size: w_ref.at[
            place(block), pl.ds(row * local_width + low, size)
        ]

    def dense_view(row):
        return lambda block, low, size: wd_ref.at[row, place(block), pl.ds(low, size)]

    attend = [Gather(attend_view(row), local_width, gather_sems.at[row], count) for row in range(3)]
    attend.append(
        Gather(
            lambda block, low, size: wo_ref.at[place(block), pl.ds(low, size)],
            local_width, gather_sems.at[3], count,
        )
    )
    dense = [
        Gather(dense_view(row), ratio * local_width, gather_sems.at[4 + row], count)
        for row in range(2)
    ]
    for piece in attend:
        piece.advance(0)
    for row in range(2):
        for r in range(ratio):
            wd_ref[row, mine, r * local_width : (r + 1) * local_width] = dense_ref[
                row, :, r, :
            ].astype(half_type)

    def take_small(k, carry):
        source = (me + k) % count
        small_copy(source, source).wait_recv()
        return carry

    lax.fori_loop(1, count, take_small, 0)
    bias = smalls[0, :, lanes:]
    for j in range(1, count):
        bias = bias + smalls[j, :, lanes:]
    bias_ref[...] = bias
    for r in range(ratio):
        b1_ref[:, r * local_width : (r + 1) * local_width] = bias[1 + r : 2 + r, :]
    for window in range(width // lanes):
        piece = smalls[window * fold, :, :lanes]
        for j in range(window * fold + 1, (window + 1) * fold):
            piece = piece + smalls[j, :, :lanes]
        vec_ref[:, window * lanes : (window + 1) * lanes] = piece

    def norm_rows(i, carry):
        tokens_in(i).wait()
        rows = pl.ds(pl.multiple_of(i * BLOCK, BLOCK), BLOCK)
        x = stored_order(norm_ref[rows, :].astype(full_type), owner_ref)
        norm_ref[rows, :] = x.astype(half_type)
        here = pl.ds(pl.multiple_of(i * BLOCK + core * half, half), half)
        own_ref[pl.ds(pl.multiple_of(i * half, half), half), :] = norm_ref[here, :]
        unit, _ = normalized(x)
        norm_ref[rows, :] = (unit * vec_ref[2:3, :] + vec_ref[3:4, :]).astype(half_type)
        a1_out(i).start()
        cot_in(i).wait()
        cot_ref[rows, :] = stored_order(cot_ref[rows, :].astype(full_type), owner_ref).astype(
            half_type
        )
        return carry

    done = 0
    for step in range(1, steps + 1):
        upto = min(blocks, -(-blocks * step // (steps - 1)))
        if upto > done:
            lax.fori_loop(done, upto, norm_rows, 0)
        done = max(done, upto)
        for piece in attend[: 3 if step == steps else 4]:
            piece.advance(step)
        if step == steps - 1:
            for piece in dense:
                piece.advance(0)

    pumps = [(piece, step) for step in range(1, steps + 1) for piece in dense]

    def pump(slot):
        first, last = (len(pumps) * s // (blocks + 1) for s in (slot, slot + 1))
        for piece, step in pumps[first:last]:
            piece.advance(step)

    lane = lax.broadcasted_iota(jnp.int32, (BLOCK, LANES), 1)
    low_half = lane < HD
    spot = lane % HD

    def project(i, carry):
        row = pl.multiple_of(i * BLOCK, BLOCK)
        rows = pl.ds(row, BLOCK)
        a1 = norm_ref[rows, :]
        qkv = dot(a1, w_ref[...])
        q, k, v = (qkv[:, part * local_width : (part + 1) * local_width] for part in range(3))
        q = (q + bias_ref[0:1, :]).astype(half_type).astype(full_type) * HD**-0.5
        index = row + lax.broadcasted_iota(jnp.int32, (BLOCK, LANES), 0)
        segment = jnp.zeros((BLOCK, LANES), jnp.int32)
        end = 0
        for slot in range(slots):
            end = end + len_ref[0, slot]
            segment = segment + jnp.where(index >= end, 1, 0)
        same = spot == segment
        inside = spot <= slots
        q_mark = jnp.where(inside & ~same, -BIG, 0.0)
        k_mark = jnp.where(same, BIG, jnp.where((spot > slots) & (spot <= slots + 3), 1.0, 0.0))
        for head in range(heads):
            pair = slice(head // 2 * LANES, head // 2 * LANES + LANES)
            own = low_half if head % 2 == 0 else ~low_half
            qa_ref[head, rows, :] = jnp.where(own, q[:, pair], q_mark).astype(half_type)
            ka_ref[head, rows, :] = jnp.where(own, k[:, pair], k_mark).astype(half_type)
            va_ref[head, rows, :] = jnp.where(own, v[:, pair], 1.0).astype(half_type)
        return carry

    lax.fori_loop(0, blocks, project, 0)
    attend[3].advance(steps)
    pump(0)

    def a1_left(i, carry):
        a1_out(i).wait()
        return carry

    lax.fori_loop(0, blocks, a1_left, 0)
    gbias_ref[...] = jnp.zeros_like(gbias_ref)
    gvec_ref[...] = jnp.zeros_like(gvec_ref)

    rowsum = RowSum(term, given, sent, crossed, sum_sems)
    share = Share(norm_ref, share_sems)

    def h2_out(i):
        own = pl.ds(pl.multiple_of(i * half, half), half)
        return pltpu.make_async_copy(gh2_ref.at[own, :], h2_hbm.at[own, :], local_sems.at[3, i])

    def attend_block(i):
        rows = pl.ds(pl.multiple_of(i * BLOCK, BLOCK), BLOCK)
        for head in range(heads):
            query = qa_ref[head, rows, :]
            scores = dot(query, ka_ref[head], 1, 1)
            top = jnp.max(scores, axis=1, keepdims=True)
            weights = jnp.exp(scores - top).astype(half_type)
            mixed = dot(weights, va_ref[head])
            turned = pltpu.roll(mixed, HD, 1)
            own = low_half if head % 2 == 0 else ~low_half
            log_total = three_parts(top + jnp.log(jnp.where(own, turned, mixed)))
            marked = query.astype(full_type)
            for part in range(3):
                marked = jnp.where(~own & (spot == slots + 1 + part), -log_total[part], marked)
            qa_ref[head, rows, :] = marked.astype(half_type)
            out = mixed / turned
            if head % 2 == 0:
                before = out
            else:
                pair = slice(head // 2 * LANES, head // 2 * LANES + LANES)
                o_ref[rows, pair] = jnp.where(low_half, before, out).astype(half_type)
            if head == 1:

                @pl.when(i >= 1)
                def _():
                    rowsum.cross(i - 1)

        rowsum.free(i)
        term[i % term.shape[0]] = dot(o_ref[rows, :], wo_ref[...], 1, 1).astype(half_type)
        rowsum.give(i)

    def norm_block(i):
        own = pl.ds(pl.multiple_of(i * half, half), half)
        hidden = own_ref[own, :].astype(full_type) + rowsum.total(i) + vec_ref[0:1, :]
        gh2_ref[own, :] = hidden
        h2_out(i).start()
        unit, _ = normalized(hidden)
        share.put(i, (unit * vec_ref[4:5, :] + vec_ref[5:6, :]).astype(half_type))

    behind = min(3, blocks)

    def attend_step(i, carry):
        attend_block(i)
        for slot in range(1, blocks + 1):

            @pl.when(i == slot - 1)
            def _(slot=slot):
                pump(slot)

        @pl.when(i >= behind)
        def _():
            norm_block(i - behind)

        return carry

    lax.fori_loop(0, blocks, attend_step, 0)
    rowsum.cross(blocks - 1)
    norm_block(blocks - 3)

    whole = [
        pltpu.make_async_copy(source, target, whole_sems.at[k])
        for k, (source, target) in enumerate(
            (
                (own_ref, own_hbm), (qa_ref, qa_hbm), (ka_ref, ka_hbm), (va_ref, va_hbm),
                (o_ref, o_hbm), (w_ref, w_hbm), (wo_ref, wo_hbm), (up_ref, up_hbm), (dn_ref, dn_hbm),
            )
        )
    ]
    for copy in whole[:-2]:
        copy.start()
    down_out = fetch(down_ref, down_hbm, local_sems.at[5])

    def gh2_out(i):
        own = pl.ds(pl.multiple_of(i * half, half), half)
        return pltpu.make_async_copy(gh2_ref.at[own, :], gh2_hbm.at[own, :], local_sems.at[6, i])

    rowsum2 = RowSum(term2, given2, sent2, crossed2, sum2_sems)

    def ga_copies(i):
        there = share.rows(i, core)
        here = ga_ref.at[pl.ds(pl.multiple_of(i * half, half), half), :]
        return (
            pltpu.make_async_copy(here, ga_hbm.at[there, :], local_sems.at[4, i]),
            pltpu.make_async_remote_copy(
                src_ref=here,
                dst_ref=ga_hbm.at[there, :],
                send_sem=put_sems.at[0, i],
                recv_sem=put_sems.at[1, i],
                device_id=(me, share.mate),
                device_id_type=MESH,
            ),
        )

    def mlp_block(i):
        rows = pl.ds(pl.multiple_of(i * BLOCK, BLOCK), BLOCK)
        share.arrived(i)
        a2 = norm_ref[rows, :]
        gy = cot_ref[rows, :]
        u, slope = gelu_parts(dot(a2, wd_ref[0]) + b1_ref[...])
        ul = u.astype(half_type)
        gz = (dot(gy, wd_ref[1]) * slope).astype(half_type)
        rowsum2.free(i)
        term2[i % term2.shape[0]] = dot(gz, wd_ref[0], 1, 1).astype(half_type)
        rowsum2.give(i)
        gbias_ref[0:1, :] += jnp.sum(gz.astype(full_type), axis=0, keepdims=True)
        down_ref[rows, :] = dot(ul, wd_ref[1], 1, 1).astype(half_type)
        down_out(i).start()
        up = dot(a2, gz, 0, 0)

        @pl.when(i == 0)
        def _():
            up_ref[...] = up

        @pl.when(i > 0)
        def _():
            up_ref[...] += up

        rowsum2.cross(i)
        dn = dot(gy, ul, 0, 0)

        @pl.when(i == 0)
        def _():
            dn_ref[...] = dn

        @pl.when(i > 0)
        def _():
            dn_ref[...] += dn

    def back_block(i):
        own = pl.ds(pl.multiple_of(i * half, half), half)
        gn = rowsum2.total(i)
        h2_out(i).wait()
        unit, rate = normalized(gh2_ref[own, :])
        e = gn * vec_ref[4:5, :]
        inner = e - jnp.mean(e, axis=-1, keepdims=True)
        inner = inner - unit * jnp.mean(e * unit, axis=-1, keepdims=True)
        gy = cot_ref[share.rows(i, core), :].astype(full_type)
        gh = gy + rate * inner
        gh2_ref[own, :] = gh
        gh2_out(i).start()
        ga_ref[own, :] = gh.astype(half_type)
        for copy in ga_copies(i):
            copy.start()
        gvec_ref[0:1, :] += jnp.sum(gh, axis=0, keepdims=True)
        gvec_ref[1:2, :] += jnp.sum(gy, axis=0, keepdims=True)
        gvec_ref[4:5, :] += jnp.sum(gn * unit, axis=0, keepdims=True)
        gvec_ref[5:6, :] += jnp.sum(gn, axis=0, keepdims=True)

    def mlp_step(i, carry):
        mlp_block(i)

        @pl.when(i < 2)
        def _():
            norm_block(blocks - 2 + i)

        @pl.when(i >= 2)
        def _():
            back_block(i - 2)

        return carry

    lax.fori_loop(0, blocks, mlp_step, 0)
    for copy in whole[-2:]:
        copy.start()
    back_block(blocks - 2)
    back_block(blocks - 1)

    def copied(i, carry):
        down_out(i).wait()
        gh2_out(i).wait()
        here, there = ga_copies(i)
        here.wait()
        there.wait_send()
        piece = ga_hbm.at[share.rows(i, 1 - core), :]
        pltpu.make_async_remote_copy(
            src_ref=piece,
            dst_ref=piece,
            send_sem=put_sems.at[0, i],
            recv_sem=put_sems.at[1, i],
            device_id=(me, share.mate),
            device_id_type=MESH,
        ).wait_recv()
        return carry

    lax.fori_loop(0, blocks, copied, 0)
    for copy in whole:
        copy.wait()
    for piece in attend + dense:
        piece.sent()
    rowsum.finish()
    rowsum2.finish()
    share.finish(blocks)

    def sent_small(k, carry):
        small_copy(me, (me + k) % count).wait_send()
        return carry

    lax.fori_loop(1, count, sent_small, 0)


class Scatter:
    def __init__(self, view, stage, taken, sems, count):
        self.view, self.stage, self.taken = view, stage, taken
        self.sems, self.count = sems, count
        self.pos = ring_pos(lax.axis_index("dp"), count)
        self.tensor = lax.axis_index("tensor")

    def _copy(self, way, step):
        sign = 1 - 2 * way
        return pltpu.make_async_remote_copy(
            src_ref=self.stage.at[way, step],
            dst_ref=self.taken.at[way, step],
            send_sem=self.sems.at[2 * way, step],
            recv_sem=self.sems.at[2 * way + 1, step],
            device_id=(ring_at(self.pos + sign, self.count), self.tensor),
            device_id_type=MESH,
        )

    def begin(self):
        for way in range(2):
            block = ring_at(self.pos - (1 - 2 * way), self.count)
            self.stage[way, 0] = self.view(way, block).astype(half_type)
            self._copy(way, 0).start()

    def advance(self, step):
        for way in range(2):
            block = ring_at(self.pos - (1 - 2 * way) * (1 + step), self.count)
            self._copy(way, step - 1).wait_recv()
            own = self.view(way, block).astype(full_type)
            total = self.taken[way, step - 1].astype(full_type) + own
            self.stage[way, step] = total.astype(half_type)
            self._copy(way, step).start()

    def total(self, way):
        last = self.count - 2
        self._copy(way, last).wait_recv()
        own = self.view(way, lax.axis_index("dp")).astype(full_type)
        return self.taken[way, last].astype(full_type) + own

    def finish(self):
        def done(step, carry):
            for way in range(2):
                self._copy(way, step).wait_send()
            return carry

        lax.fori_loop(0, self.count - 1, done, 0)


def attention_back_kernel(
    count, ga_ref, o_ref, qb_ref, ka_ref, va_ref, wo_ref, up_ref, dn_ref, down_ref, h2_ref, vec_ref,
    gqkv_ref, sum_ref, out_ref,
    goa_ref, kt_ref, gqt_ref, given, sent, crossed, stage, taken,
    sum_sems, share_sems, scatter_sems,
):
    total_rows, width = ga_ref.shape
    local_width = wo_ref.shape[1]
    heads = local_width // HD
    blocks = total_rows // BLOCK
    half = BLOCK // 2
    wide = width // count
    greeted = greet(tensor_peers() + ring_peers(count))
    greeted()

    def view(way, block):
        return (up_ref, dn_ref)[way][pl.ds(pl.multiple_of(block * wide, wide), wide), :]

    scatter = Scatter(view, stage, taken, scatter_sems, count)
    scatter.begin()
    rowsum = RowSum(down_ref, given, sent, crossed, sum_sems)
    share = Share(out_ref, share_sems)
    rowsum.give(0)
    lane = lax.broadcasted_iota(jnp.int32, (BLOCK, LANES), 1)
    low_half = lane < HD
    spot = lane % HD

    def prepare(i, carry):
        rows = pl.ds(pl.multiple_of(i * BLOCK, BLOCK), BLOCK)
        go = dot(ga_ref[rows, :], wo_ref[...]).astype(half_type).astype(full_type)
        both = go * o_ref[rows, :].astype(full_type)
        for head in range(heads):
            pair = slice(head // 2 * LANES, head // 2 * LANES + LANES)
            own = low_half if head % 2 == 0 else ~low_half
            inner = jnp.sum(jnp.where(own, both[:, pair], 0.0), axis=1, keepdims=True)
            high, middle, low = three_parts(inner)
            filled = jnp.where(own, go[:, pair], 0.0)
            for part, value in enumerate((high, middle, low)):
                filled = jnp.where(~own & (spot == part), -value, filled)
            goa_ref[head, rows, :] = filled.astype(half_type)
            if head % 2 == 0:
                before = ka_ref[head, rows, :].astype(full_type)
            else:
                k = jnp.where(low_half, before, ka_ref[head, rows, :].astype(full_type))
                kt_ref[pair, rows] = k.T.astype(half_type)
        return carry

    lax.fori_loop(0, blocks, prepare, 0)
    rowsum.give(1)

    def keys_block(j):
        rows = pl.ds(pl.multiple_of(j * BLOCK, BLOCK), BLOCK)
        for head in range(heads):
            scores = dot(ka_ref[head, rows, :], qb_ref[head], 1, 1)
            probs = jnp.exp(scores)
            gp = dot(va_ref[head, rows, :], goa_ref[head], 1, 1)
            gs = (probs * gp).astype(half_type)
            gv = dot(probs.astype(half_type), goa_ref[head])
            gk = dot(gs, qb_ref[head])
            own = slice(head * HD, head * HD + HD)
            gqt = dot(kt_ref[own, rows], gs)

            @pl.when(j == 0)
            def _():
                gqt_ref[own, :] = gqt

            @pl.when(j > 0)
            def _():
                gqt_ref[own, :] += gqt

            if head % 2 == 0:
                gk_even, gv_even = gk, gv
            else:
                pair = slice(head // 2 * LANES, head // 2 * LANES + LANES)
                for part, value in ((1, (gk_even, gk)), (2, (gv_even, gv))):
                    base = part * local_width + head // 2 * LANES
                    gqkv_ref[rows, base : base + LANES] = jnp.where(low_half, *value).astype(
                        half_type
                    )

    def output_block(i):
        own = pl.ds(pl.multiple_of(i * half, half), half)
        total = h2_ref[own, :] + rowsum.total(i) + vec_ref[1:2, :]
        share.put(i, total.astype(half_type))

    def step(j, carry):
        keys_block(j)

        hops = count - 1
        per = -(-hops // blocks)
        for t in range(per):
            hop = j * per + t

            @pl.when((hop >= 1) & (hop < hops))
            def _(hop=hop):
                scatter.advance(hop)

        @pl.when(j < blocks - 2)
        def _():
            rowsum.give(j + 2)

        rowsum.cross(j)

        @pl.when(j >= 1)
        def _():
            output_block(j - 1)

        return carry

    lax.fori_loop(0, blocks, step, 0)
    output_block(blocks - 1)

    def turn(i, carry):
        rows = pl.ds(pl.multiple_of(i * BLOCK, BLOCK), BLOCK)
        gqkv_ref[rows, :local_width] = (gqt_ref[:, rows].T * HD**-0.5).astype(half_type)
        return carry

    lax.fori_loop(0, blocks, turn, 0)
    for way in range(2):
        sum_ref[way] = scatter.total(way)

    def arrived(i, carry):
        share.arrived(i)
        return carry

    lax.fori_loop(0, blocks, arrived, 0)
    scatter.finish()
    rowsum.finish()
    share.finish(blocks)


def end_kernel(
    count, gqkv_ref, w_ref, a1_ref, ga_ref, o_ref, gh2_ref, tok_ref, vec_ref, gbias_ref, gvec_ref,
    tg_ref, sum_ref, small_ref,
    term, given, sent, crossed, grads, stage, taken, small_mine, small_taken, small_mate,
    sum_sems, share_sems, scatter_sems, small_sems, mate_sems,
):
    total_rows, width = a1_ref.shape
    local_width = w_ref.shape[1] // 3
    blocks = total_rows // BLOCK
    half = BLOCK // 2
    wide = width // count
    lanes = small_ref.shape[1] - local_width
    fold = lanes // wide
    me, tensor = lax.axis_index("dp"), lax.axis_index("tensor")
    mate = tensor - tensor % 2 + (tensor + 1) % 2
    greeted = greet(tensor_peers() + dp_peers(count))
    small_mine[:, :width] = gvec_ref[...]
    ones = jnp.ones((8, total_rows), half_type)
    bias_query = dot(ones, gqkv_ref[:, :local_width])
    small_mine[0:1, width:] = bias_query[0:1, :]
    ratio = gbias_ref.shape[1] // local_width
    for r in range(ratio):
        small_mine[1 + r : 2 + r, width:] = gbias_ref[0:1, r * local_width : (r + 1) * local_width]
    small_mine[1 + ratio :, width:] = jnp.zeros((7 - ratio, local_width), full_type)
    greeted()

    def small_copy(part, source, peer):
        window = pl.ds(pl.multiple_of(peer // fold * lanes, lanes), lanes)
        return pltpu.make_async_remote_copy(
            src_ref=small_mine.at[:, pl.ds(width, local_width) if part else window],
            dst_ref=small_taken.at[source, :, pl.ds(lanes, local_width) if part else pl.ds(0, lanes)],
            send_sem=small_sems.at[2 * part, peer],
            recv_sem=small_sems.at[2 * part + 1, source],
            device_id=(peer, tensor),
            device_id_type=MESH,
        )

    def send_small(part):
        def send(k, carry):
            small_copy(part, me, (me + k) % count).start()
            return carry

        lax.fori_loop(1, count, send, 0)

    send_small(1)
    rowsum = RowSum(term, given, sent, crossed, sum_sems)
    share = Share(tg_ref, share_sems)

    def view(way, block):
        rows = pl.ds(pl.multiple_of(block * wide, wide), wide)
        return jnp.stack([grads[2 * way, rows, :], grads[2 * way + 1, rows, :]])

    scatter = Scatter(view, stage, taken, scatter_sems, count)

    def norm_term(i):
        rows = pl.ds(pl.multiple_of(i * BLOCK, BLOCK), BLOCK)
        term[i] = dot(gqkv_ref[rows, :], w_ref[...], 1, 1).astype(half_type)
        rowsum.give(i)

    def norm_block(i):
        own = pl.ds(pl.multiple_of(i * half, half), half)
        gn = rowsum.total(i)
        unit, rate = normalized(tok_ref[own, :].astype(full_type))
        e = gn * vec_ref[2:3, :]
        inner = e - jnp.mean(e, axis=-1, keepdims=True)
        inner = inner - unit * jnp.mean(e * unit, axis=-1, keepdims=True)
        share.put(i, (gh2_ref[own, :] + rate * inner).astype(half_type))
        small_mine[2:3, :width] += jnp.sum(gn * unit, axis=0, keepdims=True)
        small_mine[3:4, :width] += jnp.sum(gn, axis=0, keepdims=True)

    def weight_grads(c, carry):
        columns = pl.ds(pl.multiple_of(c * BLOCK, BLOCK), BLOCK)
        three = dot(a1_ref[:, columns], gqkv_ref[...], 0, 0)
        for row in range(3):
            grads[row, columns, :] = three[:, row * local_width : (row + 1) * local_width]
        grads[3, columns, :] = dot(ga_ref[:, columns], o_ref[...], 0, 0)
        return carry

    norm_term(0)
    norm_term(1)
    lax.fori_loop(0, 1, weight_grads, 0)
    rowsum.cross(0)
    lax.fori_loop(1, width // BLOCK, weight_grads, 0)
    scatter.begin()
    hops = count - 1
    per = -(-hops // blocks)

    def step(i, carry):
        @pl.when(i < blocks - 2)
        def _():
            norm_term(i + 2)

        @pl.when(i < blocks - 1)
        def _():
            rowsum.cross(i + 1)

        norm_block(i)
        for t in range(per):
            hop = i * per + t

            @pl.when((hop >= 1) & (hop < hops))
            def _(hop=hop):
                scatter.advance(hop)

        return carry

    lax.fori_loop(0, blocks, step, 0)
    send_small(0)
    for way in range(2):
        total = scatter.total(way)
        sum_ref[2 * way] = total[0]
        sum_ref[2 * way + 1] = total[1]
    for part in range(2):
        window = pl.ds(pl.multiple_of(me // fold * lanes, lanes), lanes)
        here = slice(lanes, lanes + local_width) if part else slice(0, lanes)
        small_taken[me, :, here] = small_mine[:, width:] if part else small_mine[:, window]

        def take(k, carry, part=part):
            source = (me + k) % count
            small_copy(part, source, source).wait_recv()
            return carry

        lax.fori_loop(1, count, take, 0)
    total = small_taken[0]
    for j in range(1, count):
        total = total + small_taken[j]
    small_ref[...] = total
    pair = pltpu.make_async_remote_copy(
        src_ref=small_ref.at[:, pl.ds(0, lanes)],
        dst_ref=small_mate,
        send_sem=mate_sems.at[0],
        recv_sem=mate_sems.at[1],
        device_id=(me, mate),
        device_id_type=MESH,
    )
    pair.start()
    pair.wait()
    small_ref[:, :lanes] = total[:, :lanes] + small_mate[...]

    def arrived(i, carry):
        share.arrived(i)
        return carry

    lax.fori_loop(0, blocks, arrived, 0)
    scatter.finish()
    rowsum.finish()
    share.finish(blocks)
    for part in range(2):

        def done(k, carry, part=part):
            small_copy(part, me, (me + k) % count).wait_send()
            return carry

        lax.fori_loop(1, count, done, 0)


def permuted(x, owner, back):
    rows, width = x.shape
    count = owner.shape[0]
    order = jnp.argsort(owner) if back else owner
    return jnp.take(x.reshape(rows, count, -1), order, axis=1).reshape(rows, width)


def adamw_step(weight, first, second, grad, rate, decay):
    first_next = first_decay * first + (1.0 - first_decay) * grad
    second_next = second_decay * second + (1.0 - second_decay) * grad * grad
    first_hat = first_next / (1.0 - first_decay**STEP)
    second_hat = second_next / (1.0 - second_decay**STEP)
    update = first_hat / (jnp.sqrt(second_hat) + adam_epsilon) + decay * weight
    return (first_next, second_next, weight - rate * update)


def last_kernel(rates, owner_ref, *refs):
    count = owner_ref.shape[0]
    given, refs = refs[:5], refs[5:]
    layer, grad, weight_sum, dense_sum, small = given
    state, refs = refs[:15], refs[15:]
    results, outs = refs[:2], refs[2:]

    def step(k, grad, at=(Ellipsis,)):
        new = adamw_step(*(ref[at] for ref in state[3 * k : 3 * k + 3]), grad, *rates[k])
        for ref, value in zip(outs[3 * k : 3 * k + 3], new):
            ref[at] = value

    wide = layer.shape[1] // count
    if wide % LANES == 0:
        for j in range(count):
            natural = pl.ds(pl.multiple_of(owner_ref[j] * wide, wide), wide)
            for x, y in zip((layer, grad), results):
                y[:, natural] = x[:, j * wide : (j + 1) * wide]
    else:
        for x, y in zip((layer, grad), results):
            y[...] = x[...]
    step(0, weight_sum[0:3])
    step(1, weight_sum[3])
    ratio, local_width = state[6].shape[2:]
    for r in range(ratio):
        step(
            2,
            dense_sum[:, :, r * local_width : (r + 1) * local_width],
            (slice(None), slice(None), r, slice(None)),
        )
    me = lax.axis_index("dp")
    lanes = small.shape[1] - local_width

    def chosen(x, start, size):
        row = lax.broadcasted_iota(jnp.int32, (x.shape[1], size), 0)
        column = lax.broadcasted_iota(jnp.int32, (x.shape[1], size), 1)
        pick = jnp.where(row == column + start, 1.0, 0.0).astype(half_type)
        return sum(dot(part.astype(half_type), pick) for part in three_parts(x))

    narrow, wide = state[9].shape[1], state[12].shape[1]
    step(3, chosen(small[:, lanes:], owner_ref[me] * narrow, narrow)[: 1 + ratio])
    step(4, chosen(small[:, :lanes], me % (lanes // wide) * wide, wide)[:6])


def last(owner, layer_output, tokens_grad, weight_sum, dense_sum, small_sum, *state):
    steps = 8 if dense_sum.shape[1] % 128 == 0 else 1
    rates = (
        (matrix_rate, matrix_decay),
        (output_rate, matrix_decay),
        (matrix_rate, matrix_decay),
        (bias_rate, 0.0),
        (vector_rate, 0.0),
    )

    def spec(x, dim):
        shape = tuple(n // steps if k == dim else n for k, n in enumerate(x.shape))
        return pl.BlockSpec(shape, lambda i, *_: tuple(i if k == dim else 0 for k in range(x.ndim)))

    dims = [0, 0, 1, 1, None] + [1] * 3 + [0] * 3 + [1] * 3 + [None] * 6
    operands = (layer_output, tokens_grad, weight_sum, dense_sum, small_sum) + state
    specs = [spec(x, dim) for x, dim in zip(operands, dims)]
    outs = operands[:2] + state
    return pl.pallas_call(
        functools.partial(last_kernel, rates),
        out_shape=[jax.ShapeDtypeStruct(x.shape, x.dtype) for x in outs],
        grid_spec=pltpu.PrefetchScalarGridSpec(
            num_scalar_prefetch=1, grid=(steps,), in_specs=specs, out_specs=specs[:2] + specs[5:]
        ),
        compiler_params=pltpu.CompilerParams(vmem_limit_bytes=60 * 2**20),
    )(owner, *operands)


def call(kernel, collective, outs, scratch, operands, spaces, limit=62):
    spec = {
        "s": pl.BlockSpec(memory_space=pltpu.SMEM),
        "v": pl.BlockSpec(memory_space=pltpu.VMEM),
        "h": pl.BlockSpec(memory_space=pl.ANY),
    }
    return pl.pallas_call(
        kernel,
        out_shape=[jax.ShapeDtypeStruct(shape, dtype) for shape, dtype in outs],
        in_specs=[spec[c] for c in spaces[0]],
        out_specs=[spec[c] for c in spaces[1]],
        scratch_shapes=scratch,
        compiler_params=pltpu.CompilerParams(
            collective_id=collective, has_side_effects=True, vmem_limit_bytes=limit * 2**20
        ),
    )(*operands)


def dma(*shape):
    return pltpu.SemaphoreType.DMA(shape)


def local(
    tokens,
    lengths,
    owner,
    attend_master,
    attend_first,
    attend_second,
    output_master,
    output_first,
    output_second,
    dense_master,
    dense_first,
    dense_second,
    bias_master,
    bias_first,
    bias_second,
    vector_master,
    vector_first,
    vector_second,
    cotangent,
):
    count = owner.shape[0]
    rows, width = tokens.shape
    local_width = output_master.shape[1]
    ratio = dense_master.shape[2]
    hidden = ratio * local_width
    heads = local_width // HD
    blocks = rows // BLOCK
    half = BLOCK // 2
    wide = width // count
    lanes = max(LANES, wide)
    tok, cot = tokens, cotangent
    if wide % LANES:
        tok, cot = (permuted(x, owner, False) for x in (tokens, cotangent))
    row_sum = [pltpu.VMEM((blocks, half, width), half_type)] * 3
    two_terms = pltpu.VMEM((2, BLOCK, width), half_type)
    heads_shape = (heads, rows, LANES)
    small = (8, lanes + local_width)
    a1, ga, h2, own, qb, ka, va, o, w, wo, gh2, down, up, dn, vec, gbias, gvec = call(
        functools.partial(front_kernel, count),
        0,
        [
            ((rows, width), half_type),
            ((rows, width), half_type),
            ((rows // 2, width), full_type),
            ((rows // 2, width), half_type),
            (heads_shape, half_type),
            (heads_shape, half_type),
            (heads_shape, half_type),
            ((rows, local_width), half_type),
            ((width, 3 * local_width), half_type),
            ((width, local_width), half_type),
            ((rows // 2, width), full_type),
            ((rows, width), half_type),
            ((width, hidden), full_type),
            ((width, hidden), full_type),
            ((8, width), full_type),
            ((8, hidden), full_type),
            ((8, width), full_type),
        ],
        [
            pltpu.VMEM((rows // 2, width), half_type),
            *[pltpu.VMEM(heads_shape, half_type)] * 3,
            pltpu.VMEM((rows, local_width), half_type),
            pltpu.VMEM((width, 3 * local_width), half_type),
            pltpu.VMEM((width, local_width), half_type),
            pltpu.VMEM((rows // 2, width), full_type),
            pltpu.VMEM((rows, width), half_type),
            *[pltpu.VMEM((width, hidden), full_type)] * 2,
            *[pltpu.VMEM((rows, width), half_type)] * 2,
            pltpu.VMEM((2, width, hidden), half_type),
            pltpu.VMEM((rows // 2, width), half_type),
            pltpu.VMEM((8, local_width), full_type),
            pltpu.VMEM((1, hidden), full_type),
            pltpu.VMEM(small, full_type),
            pltpu.VMEM((count,) + small, full_type),
            two_terms,
            *row_sum,
            two_terms,
            *row_sum,
            dma(6, 4, count // 2),
            dma(2, count),
            dma(4, blocks),
            dma(4, blocks),
            dma(2, blocks),
            dma(2, blocks),
            dma(7, blocks),
            dma(9),
        ],
        (
            lengths, owner, tok, cot, attend_master, output_master, dense_master, vector_master,
            bias_master,
        ),
        ("sshhvvvvv", "h" * 14 + "vvv"),
    )
    gqkv, dense_sum, layer_output = call(
        functools.partial(attention_back_kernel, count),
        1,
        [
            ((rows, 3 * local_width), half_type),
            ((2, wide, hidden), full_type),
            ((rows, width), half_type),
        ],
        [
            pltpu.VMEM(heads_shape, half_type),
            pltpu.VMEM((local_width, rows), half_type),
            pltpu.VMEM((local_width, rows), full_type),
            *row_sum,
            pltpu.VMEM((2, count - 1, wide, hidden), half_type),
            pltpu.VMEM((2, count - 1, wide, hidden), half_type),
            dma(4, blocks),
            dma(2, blocks),
            dma(4, count - 1),
        ],
        (ga, o, qb, ka, va, wo, up, dn, down.reshape(blocks, BLOCK, width), h2, vec),
        ("v" * 11, "v" * 3),
    )
    tokens_grad, weight_sum, small_sum = call(
        functools.partial(end_kernel, count),
        2,
        [
            ((rows, width), half_type),
            ((4, wide, local_width), full_type),
            ((8, lanes + local_width), full_type),
        ],
        [
            pltpu.VMEM((blocks, BLOCK, width), half_type),
            *row_sum,
            pltpu.VMEM((4, width, local_width), full_type),
            pltpu.VMEM((2, count - 1, 2, wide, local_width), half_type),
            pltpu.VMEM((2, count - 1, 2, wide, local_width), half_type),
            pltpu.VMEM((8, width + local_width), full_type),
            pltpu.VMEM((count, 8, lanes + local_width), full_type),
            pltpu.VMEM((8, lanes), full_type),
            dma(4, blocks),
            dma(2, blocks),
            dma(4, count - 1),
            dma(4, count),
            dma(2),
        ],
        (gqkv, w, a1, ga, o, gh2, own, vec, gbias, gvec),
        ("v" * 10, "v" * 3),
    )
    if wide % LANES:
        layer_output, tokens_grad = (permuted(x, owner, True) for x in (layer_output, tokens_grad))
    return tuple(
        last(
            owner, layer_output, tokens_grad, weight_sum, dense_sum, small_sum,
            attend_master, attend_first, attend_second,
            output_master, output_first, output_second,
            dense_master, dense_first, dense_second,
            bias_master, bias_first, bias_second,
            vector_master, vector_first, vector_second,
        )
    )


def solution(mesh):
    return jax.shard_map(
        local,
        mesh=mesh,
        in_specs=(
            P("dp", None),
            P("dp", None),
            P(),
            P(None, "dp", "tensor"),
            P(None, "dp", "tensor"),
            P(None, "dp", "tensor"),
            P("dp", "tensor"),
            P("dp", "tensor"),
            P("dp", "tensor"),
            P(None, "dp", None, "tensor"),
            P(None, "dp", None, "tensor"),
            P(None, "dp", None, "tensor"),
            P(None, ("tensor", "dp")),
            P(None, ("tensor", "dp")),
            P(None, ("tensor", "dp")),
            P(None, "dp"),
            P(None, "dp"),
            P(None, "dp"),
            P("dp", None),
        ),
        out_specs=(
            P("dp", None),
            P("dp", None),
            P(None, "dp", "tensor"),
            P(None, "dp", "tensor"),
            P(None, "dp", "tensor"),
            P("dp", "tensor"),
            P("dp", "tensor"),
            P("dp", "tensor"),
            P(None, "dp", None, "tensor"),
            P(None, "dp", None, "tensor"),
            P(None, "dp", None, "tensor"),
            P(None, ("tensor", "dp")),
            P(None, ("tensor", "dp")),
            P(None, ("tensor", "dp")),
            P(None, "dp"),
            P(None, "dp"),
            P(None, "dp"),
        ),
        check_vma=False,
    )
```

```python
import functools

import jax
import jax.numpy as jnp
from jax import lax
from jax.experimental import pallas as pl
from jax.experimental.pallas import tpu as pltpu
from jax.sharding import PartitionSpec as P

HD = 64
STEP = 10
LANES = 128
BLOCK = 256
MESH = pl.DeviceIdType.MESH
BIG = 2.0**50

norm_epsilon = 1e-06
first_decay = 0.9
second_decay = 0.95
adam_epsilon = 1e-08
matrix_rate = 0.1
output_rate = 0.5
bias_rate = 0.5
vector_rate = 1.0
matrix_decay = 0.05

half_type = jnp.bfloat16
full_type = jnp.float32


def dot(left, right, left_dim=1, right_dim=0):
    return lax.dot_general(
        left, right, (((left_dim,), (right_dim,)), ((), ())), preferred_element_type=full_type
    )


def ring_pos(place, count):
    column = place % 2
    row = place // 2
    return row * (1 - column) + (count - 1 - row) * column


def ring_at(pos, count):
    near = (pos + 2 * count) % count
    down = near // (count // 2)
    return 2 * near * (1 - down) + (2 * count - 1 - 2 * near) * down


def normalized(x):
    center = jnp.mean(x, axis=-1, keepdims=True)
    offset = x - center
    spread = jnp.mean(offset * offset, axis=-1, keepdims=True)
    rate = lax.rsqrt(spread + norm_epsilon)
    return offset * rate, rate


class Gather:
    def __init__(self, view, width, sems, count):
        self.view, self.width, self.sems, self.count = view, width, sems, count
        self.steps = count // 2
        self.pos = ring_pos(lax.axis_index("dp"), count)
        self.tensor = lax.axis_index("tensor")

    def _copy(self, way, step, hops):
        sign = 1 - 2 * way
        part = (0, self.width)
        if step == self.steps - 1:
            part = (way * (self.width // 2), self.width // 2)
        block = self.view(ring_at(self.pos - sign * hops, self.count), *part)
        return pltpu.make_async_remote_copy(
            src_ref=block,
            dst_ref=block,
            send_sem=self.sems.at[2 * way, step],
            recv_sem=self.sems.at[2 * way + 1, step],
            device_id=(ring_at(self.pos + sign, self.count), self.tensor),
            device_id_type=MESH,
        )

    def advance(self, step):
        if step:
            for way in range(2):
                self._copy(way, step - 1, step).wait_recv()
        if step < self.steps:
            for way in range(2):
                self._copy(way, step, step).start()

    def sent(self):
        for step in range(self.steps):
            for way in range(2):
                self._copy(way, step, step).wait_send()


class RowSum:
    def __init__(self, term, given, sent, crossed, sems):
        self.term, self.given, self.sent_ref, self.crossed = term, given, sent, crossed
        self.slots, self.sent_slots, self.blocks = term.shape[0], sent.shape[0], given.shape[0]
        self.sems = sems
        self.half = given.shape[1]
        self.dp, tensor = lax.axis_index("dp"), lax.axis_index("tensor")
        self.core = tensor % 2
        self.mate = tensor - tensor % 2 + (tensor + 1) % 2
        self.other = (tensor + 2) % 4

    def rows(self, core):
        return pl.ds(pl.multiple_of(core * self.half, self.half), self.half)

    def _give(self, i):
        return pltpu.make_async_remote_copy(
            src_ref=self.term.at[i % self.slots, self.rows(1 - self.core), :],
            dst_ref=self.given.at[i],
            send_sem=self.sems.at[0, i],
            recv_sem=self.sems.at[1, i],
            device_id=(self.dp, self.mate),
            device_id_type=MESH,
        )

    def _cross(self, i):
        return pltpu.make_async_remote_copy(
            src_ref=self.sent_ref.at[i % self.sent_slots],
            dst_ref=self.crossed.at[i],
            send_sem=self.sems.at[2, i],
            recv_sem=self.sems.at[3, i],
            device_id=(self.dp, self.other),
            device_id_type=MESH,
        )

    def free(self, i):
        if self.slots < self.blocks:

            @pl.when(i >= self.slots)
            def _():
                self._give(i - self.slots).wait_send()

    def give(self, i):
        self._give(i).start()

    def cross(self, i):
        self._give(i).wait_recv()
        mine = self.term[i % self.slots, self.rows(self.core), :].astype(full_type)
        if self.sent_slots < self.blocks:

            @pl.when(i >= self.sent_slots)
            def _():
                self._cross(i - self.sent_slots).wait_send()

        total = mine + self.given[i].astype(full_type)
        self.sent_ref[i % self.sent_slots] = total.astype(half_type)
        self._cross(i).start()

    def total(self, i):
        self._cross(i).wait_recv()
        mine = self.sent_ref[i % self.sent_slots].astype(full_type)
        return mine + self.crossed[i].astype(full_type)

    def gone(self):
        def given(i, carry):
            self._give(i).wait_send()
            return carry

        lax.fori_loop(max(self.blocks - self.slots, 0), self.blocks, given, 0)

    def finish(self, given=True):
        if given:
            self.gone()

        def crossed(i, carry):
            self._cross(i).wait_send()
            return carry

        lax.fori_loop(max(self.blocks - self.sent_slots, 0), self.blocks, crossed, 0)


class Share:
    def __init__(self, ref, sems):
        self.ref, self.sems = ref, sems
        self.dp, tensor = lax.axis_index("dp"), lax.axis_index("tensor")
        self.core = tensor % 2
        self.mate = tensor - tensor % 2 + (tensor + 1) % 2

    def rows(self, i, core):
        half = BLOCK // 2
        return pl.ds(pl.multiple_of(i * BLOCK + core * half, half), half)

    def _copy(self, i, core):
        piece = self.ref.at[self.rows(i, core), :]
        return pltpu.make_async_remote_copy(
            src_ref=piece,
            dst_ref=piece,
            send_sem=self.sems.at[0, i],
            recv_sem=self.sems.at[1, i],
            device_id=(self.dp, self.mate),
            device_id_type=MESH,
        )

    def put(self, i, value):
        self.ref[self.rows(i, self.core), :] = value
        self._copy(i, self.core).start()

    def arrived(self, i):
        self._copy(i, 1 - self.core).wait_recv()

    def finish(self, blocks):
        def done(i, carry):
            self._copy(i, self.core).wait_send()
            return carry

        lax.fori_loop(0, blocks, done, 0)


def greet(peers):
    barrier = pltpu.get_barrier_semaphore()
    for peer in peers:
        pl.semaphore_signal(barrier, inc=1, device_id=peer, device_id_type=MESH)
    return lambda: pl.semaphore_wait(barrier, len(peers))


def tensor_peers():
    dp, tensor = lax.axis_index("dp"), lax.axis_index("tensor")
    return [(dp, tensor - tensor % 2 + (tensor + 1) % 2), (dp, (tensor + 2) % 4)]


def ring_peers(count):
    dp, tensor = lax.axis_index("dp"), lax.axis_index("tensor")
    pos = ring_pos(dp, count)
    return [(ring_at(pos + 1, count), tensor), (ring_at(pos - 1, count), tensor)]


def dp_peers(count):
    dp, tensor = lax.axis_index("dp"), lax.axis_index("tensor")
    return [((dp + k) % count, tensor) for k in range(1, count)]


def three_parts(x):
    high = x.astype(half_type).astype(full_type)
    middle = (x - high).astype(half_type).astype(full_type)
    return high, middle, x - high - middle


def gelu_parts(z):
    phi = 0.5 + 0.5 * lax.erf(z * (0.5**0.5))
    slope = phi + z * (jnp.exp(-0.5 * z * z) * (2.0 * 3.141592653589793) ** -0.5)
    return z * phi, slope


def fetch(source, target, sems):
    def copy(i):
        rows = pl.ds(pl.multiple_of(i * BLOCK, BLOCK), BLOCK)
        return pltpu.make_async_copy(source.at[rows, :], target.at[rows, :], sems.at[i])

    return copy


def stored_order(x, owner_ref):
    count = owner_ref.shape[0]
    wide = x.shape[1] // count
    if wide % LANES:
        return x
    parts = []
    for j in range(count):
        total = None
        for n in range(count):
            term = x[:, n * wide : (n + 1) * wide] * jnp.where(owner_ref[j] == n, 1.0, 0.0)
            total = term if total is None else total + term
        parts.append(total)
    return jnp.concatenate(parts, axis=1)


def front_kernel(
    count, len_ref, owner_ref, tok_hbm, cot_hbm, att_ref, out_ref, dense_ref, vector_ref, split_ref,
    a1_hbm, ga_hbm, h2_hbm, own_hbm, qa_hbm, ka_hbm, va_hbm, o_hbm, w_hbm, wo_hbm, gh2_hbm, down_hbm,
    up_hbm, dn_hbm, vec_ref, gbias_ref, gvec_ref,
    own_ref, qa_ref, ka_ref, va_ref, o_ref, w_ref, wo_ref, gh2_ref, down_ref, up_ref, dn_ref,
    norm_ref, cot_ref, wd_ref, ga_ref, bias_ref, b1_ref, small_ref, smalls,
    term, given, sent, crossed, term2, given2, sent2, crossed2,
    gather_sems, small_sems, sum_sems, sum2_sems, share_sems, put_sems, local_sems, whole_sems,
):
    me, tensor = lax.axis_index("dp"), lax.axis_index("tensor")
    total_rows, width = norm_ref.shape
    local_width = wo_ref.shape[1]
    ratio = dense_ref.shape[2]
    wide = width // count
    slots = len_ref.shape[1]
    heads = local_width // HD
    blocks = total_rows // BLOCK
    half = BLOCK // 2
    lanes = small_ref.shape[1] - local_width
    fold = lanes // wide
    steps = count // 2
    core = tensor % 2

    greeted = greet(tensor_peers() + dp_peers(count))
    tokens_in = fetch(tok_hbm, norm_ref, local_sems.at[0])
    cot_in = fetch(cot_hbm, cot_ref, local_sems.at[1])
    a1_out = fetch(norm_ref, a1_hbm, local_sems.at[2])
    for i in range(blocks):
        tokens_in(i).start()
    for i in range(blocks):
        cot_in(i).start()
    mine = pl.ds(pl.multiple_of(me * wide, wide), wide)
    for row in range(3):
        w_ref[mine, row * local_width : (row + 1) * local_width] = att_ref[row].astype(half_type)
    wo_ref[mine, :] = out_ref[...].astype(half_type)

    small_ref[...] = jnp.zeros_like(small_ref)
    vectors = vector_ref[...].astype(half_type)
    if fold == 1:
        small_ref[0:6, :lanes] = vectors.astype(full_type)
    else:
        row = lax.broadcasted_iota(jnp.int32, (wide, lanes), 0)
        column = lax.broadcasted_iota(jnp.int32, (wide, lanes), 1)
        spread = jnp.where(column == row + me % fold * wide, 1.0, 0.0).astype(half_type)
        small_ref[0:6, :lanes] = dot(vectors, spread)
    narrow = split_ref.shape[1]
    row = lax.broadcasted_iota(jnp.int32, (narrow, local_width), 0)
    column = lax.broadcasted_iota(jnp.int32, (narrow, local_width), 1)
    spread = jnp.where(column == row + owner_ref[me] * narrow, 1.0, 0.0).astype(half_type)
    small_ref[0 : 1 + ratio, lanes:] = dot(split_ref[...].astype(half_type), spread)
    smalls[me] = small_ref[...]
    greeted()

    def place(block):
        return pl.ds(pl.multiple_of(block * wide, wide), wide)

    def small_copy(source, peer):
        return pltpu.make_async_remote_copy(
            src_ref=small_ref,
            dst_ref=smalls.at[source],
            send_sem=small_sems.at[0, peer],
            recv_sem=small_sems.at[1, source],
            device_id=(peer, tensor),
            device_id_type=MESH,
        )

    def send_small(k, carry):
        small_copy(me, (me + k) % count).start()
        return carry

    lax.fori_loop(1, count, send_small, 0)

    def attend_view(row):
        return lambda block, low, size: w_ref.at[
            place(block), pl.ds(row * local_width + low, size)
        ]

    def dense_view(row):
        return lambda block, low, size: wd_ref.at[row, place(block), pl.ds(low, size)]

    attend = [Gather(attend_view(row), local_width, gather_sems.at[row], count) for row in range(3)]
    attend.append(
        Gather(
            lambda block, low, size: wo_ref.at[place(block), pl.ds(low, size)],
            local_width, gather_sems.at[3], count,
        )
    )
    dense = [
        Gather(dense_view(row), ratio * local_width, gather_sems.at[4 + row], count)
        for row in range(2)
    ]
    for piece in attend:
        piece.advance(0)
    for row in range(2):
        for r in range(ratio):
            wd_ref[row, mine, r * local_width : (r + 1) * local_width] = dense_ref[
                row, :, r, :
            ].astype(half_type)

    def take_small(k, carry):
        source = (me + k) % count
        small_copy(source, source).wait_recv()
        return carry

    lax.fori_loop(1, count, take_small, 0)
    bias = smalls[0, :, lanes:]
    for j in range(1, count):
        bias = bias + smalls[j, :, lanes:]
    bias_ref[...] = bias
    for r in range(ratio):
        b1_ref[:, r * local_width : (r + 1) * local_width] = bias[1 + r : 2 + r, :]
    for window in range(width // lanes):
        piece = smalls[window * fold, :, :lanes]
        for j in range(window * fold + 1, (window + 1) * fold):
            piece = piece + smalls[j, :, :lanes]
        vec_ref[:, window * lanes : (window + 1) * lanes] = piece

    def norm_rows(i, carry):
        tokens_in(i).wait()
        rows = pl.ds(pl.multiple_of(i * BLOCK, BLOCK), BLOCK)
        x = stored_order(norm_ref[rows, :].astype(full_type), owner_ref)
        norm_ref[rows, :] = x.astype(half_type)
        here = pl.ds(pl.multiple_of(i * BLOCK + core * half, half), half)
        own_ref[pl.ds(pl.multiple_of(i * half, half), half), :] = norm_ref[here, :]
        unit, _ = normalized(x)
        norm_ref[rows, :] = (unit * vec_ref[2:3, :] + vec_ref[3:4, :]).astype(half_type)
        a1_out(i).start()
        cot_in(i).wait()
        cot_ref[rows, :] = stored_order(cot_ref[rows, :].astype(full_type), owner_ref).astype(
            half_type
        )
        return carry

    done = 0
    for step in range(1, steps + 1):
        upto = min(blocks, -(-blocks * step // (steps - 1)))
        if upto > done:
            lax.fori_loop(done, upto, norm_rows, 0)
        done = max(done, upto)
        for piece in attend[: 3 if step == steps else 4]:
            piece.advance(step)
        if step == steps - 1:
            for piece in dense:
                piece.advance(0)

    pumps = [(piece, step) for step in range(1, steps + 1) for piece in dense]

    def pump(slot):
        first, last = (len(pumps) * s // (blocks + 1) for s in (slot, slot + 1))
        for piece, step in pumps[first:last]:
            piece.advance(step)

    lane = lax.broadcasted_iota(jnp.int32, (BLOCK, LANES), 1)
    low_half = lane < HD
    spot = lane % HD

    def project(i, carry):
        row = pl.multiple_of(i * BLOCK, BLOCK)
        rows = pl.ds(row, BLOCK)
        a1 = norm_ref[rows, :]
        qkv = dot(a1, w_ref[...])
        q, k, v = (qkv[:, part * local_width : (part + 1) * local_width] for part in range(3))
        q = (q + bias_ref[0:1, :]).astype(half_type).astype(full_type) * HD**-0.5
        index = row + lax.broadcasted_iota(jnp.int32, (BLOCK, LANES), 0)
        segment = jnp.zeros((BLOCK, LANES), jnp.int32)
        end = 0
        for slot in range(slots):
            end = end + len_ref[0, slot]
            segment = segment + jnp.where(index >= end, 1, 0)
        same = spot == segment
        inside = spot <= slots
        q_mark = jnp.where(inside & ~same, -BIG, 0.0)
        k_mark = jnp.where(same, BIG, jnp.where((spot > slots) & (spot <= slots + 3), 1.0, 0.0))
        for head in range(heads):
            pair = slice(head // 2 * LANES, head // 2 * LANES + LANES)
            own = low_half if head % 2 == 0 else ~low_half
            qa_ref[head, rows, :] = jnp.where(own, q[:, pair], q_mark).astype(half_type)
            ka_ref[head, rows, :] = jnp.where(own, k[:, pair], k_mark).astype(half_type)
            va_ref[head, rows, :] = jnp.where(own, v[:, pair], 1.0).astype(half_type)
        return carry

    lax.fori_loop(0, blocks, project, 0)
    attend[3].advance(steps)
    pump(0)

    def a1_left(i, carry):
        a1_out(i).wait()
        return carry

    lax.fori_loop(0, blocks, a1_left, 0)
    gbias_ref[...] = jnp.zeros_like(gbias_ref)
    gvec_ref[...] = jnp.zeros_like(gvec_ref)

    rowsum = RowSum(term, given, sent, crossed, sum_sems)
    share = Share(norm_ref, share_sems)

    def h2_out(i):
        own = pl.ds(pl.multiple_of(i * half, half), half)
        return pltpu.make_async_copy(gh2_ref.at[own, :], h2_hbm.at[own, :], local_sems.at[3, i])

    def attend_block(i):
        rows = pl.ds(pl.multiple_of(i * BLOCK, BLOCK), BLOCK)
        for head in range(heads):
            query = qa_ref[head, rows, :]
            scores = dot(query, ka_ref[head], 1, 1)
            top = jnp.max(scores, axis=1, keepdims=True)
            weights = jnp.exp(scores - top).astype(half_type)
            mixed = dot(weights, va_ref[head])
            turned = pltpu.roll(mixed, HD, 1)
            own = low_half if head % 2 == 0 else ~low_half
            log_total = three_parts(top + jnp.log(jnp.where(own, turned, mixed)))
            marked = query.astype(full_type)
            for part in range(3):
                marked = jnp.where(~own & (spot == slots + 1 + part), -log_total[part], marked)
            qa_ref[head, rows, :] = marked.astype(half_type)
            out = mixed / turned
            if head % 2 == 0:
                before = out
            else:
                pair = slice(head // 2 * LANES, head // 2 * LANES + LANES)
                o_ref[rows, pair] = jnp.where(low_half, before, out).astype(half_type)
            if head == 1:

                @pl.when(i >= 1)
                def _():
                    rowsum.cross(i - 1)

        rowsum.free(i)
        term[i % term.shape[0]] = dot(o_ref[rows, :], wo_ref[...], 1, 1).astype(half_type)
        rowsum.give(i)

    def norm_block(i):
        own = pl.ds(pl.multiple_of(i * half, half), half)
        hidden = own_ref[own, :].astype(full_type) + rowsum.total(i) + vec_ref[0:1, :]
        gh2_ref[own, :] = hidden
        h2_out(i).start()
        unit, _ = normalized(hidden)
        share.put(i, (unit * vec_ref[4:5, :] + vec_ref[5:6, :]).astype(half_type))

    behind = min(3, blocks)

    def attend_step(i, carry):
        attend_block(i)
        for slot in range(1, blocks + 1):

            @pl.when(i == slot - 1)
            def _(slot=slot):
                pump(slot)

        @pl.when(i >= behind)
        def _():
            norm_block(i - behind)

        return carry

    lax.fori_loop(0, blocks, attend_step, 0)
    rowsum.cross(blocks - 1)
    norm_block(blocks - 3)

    whole = [
        pltpu.make_async_copy(source, target, whole_sems.at[k])
        for k, (source, target) in enumerate(
            (
                (own_ref, own_hbm), (qa_ref, qa_hbm), (ka_ref, ka_hbm), (va_ref, va_hbm),
                (o_ref, o_hbm), (w_ref, w_hbm), (wo_ref, wo_hbm), (up_ref, up_hbm), (dn_ref, dn_hbm),
            )
        )
    ]
    for copy in whole[:-2]:
        copy.start()
    down_out = fetch(down_ref, down_hbm, local_sems.at[5])

    def gh2_out(i):
        own = pl.ds(pl.multiple_of(i * half, half), half)
        return pltpu.make_async_copy(gh2_ref.at[own, :], gh2_hbm.at[own, :], local_sems.at[6, i])

    rowsum2 = RowSum(term2, given2, sent2, crossed2, sum2_sems)

    def ga_copies(i):
        there = share.rows(i, core)
        here = ga_ref.at[pl.ds(pl.multiple_of(i * half, half), half), :]
        return (
            pltpu.make_async_copy(here, ga_hbm.at[there, :], local_sems.at[4, i]),
            pltpu.make_async_remote_copy(
                src_ref=here,
                dst_ref=ga_hbm.at[there, :],
                send_sem=put_sems.at[0, i],
                recv_sem=put_sems.at[1, i],
                device_id=(me, share.mate),
                device_id_type=MESH,
            ),
        )

    def mlp_block(i):
        rows = pl.ds(pl.multiple_of(i * BLOCK, BLOCK), BLOCK)
        share.arrived(i)
        a2 = norm_ref[rows, :]
        gy = cot_ref[rows, :]
        u, slope = gelu_parts(dot(a2, wd_ref[0]) + b1_ref[...])
        ul = u.astype(half_type)
        gz = (dot(gy, wd_ref[1]) * slope).astype(half_type)
        rowsum2.free(i)
        term2[i % term2.shape[0]] = dot(gz, wd_ref[0], 1, 1).astype(half_type)
        rowsum2.give(i)
        gbias_ref[0:1, :] += jnp.sum(gz.astype(full_type), axis=0, keepdims=True)
        down_ref[rows, :] = dot(ul, wd_ref[1], 1, 1).astype(half_type)
        down_out(i).start()
        up = dot(a2, gz, 0, 0)

        @pl.when(i == 0)
        def _():
            up_ref[...] = up

        @pl.when(i > 0)
        def _():
            up_ref[...] += up

        rowsum2.cross(i)
        dn = dot(gy, ul, 0, 0)

        @pl.when(i == 0)
        def _():
            dn_ref[...] = dn

        @pl.when(i > 0)
        def _():
            dn_ref[...] += dn

    def back_block(i):
        own = pl.ds(pl.multiple_of(i * half, half), half)
        gn = rowsum2.total(i)
        h2_out(i).wait()
        unit, rate = normalized(gh2_ref[own, :])
        e = gn * vec_ref[4:5, :]
        inner = e - jnp.mean(e, axis=-1, keepdims=True)
        inner = inner - unit * jnp.mean(e * unit, axis=-1, keepdims=True)
        gy = cot_ref[share.rows(i, core), :].astype(full_type)
        gh = gy + rate * inner
        gh2_ref[own, :] = gh
        gh2_out(i).start()
        ga_ref[own, :] = gh.astype(half_type)
        for copy in ga_copies(i):
            copy.start()
        gvec_ref[0:1, :] += jnp.sum(gh, axis=0, keepdims=True)
        gvec_ref[1:2, :] += jnp.sum(gy, axis=0, keepdims=True)
        gvec_ref[4:5, :] += jnp.sum(gn * unit, axis=0, keepdims=True)
        gvec_ref[5:6, :] += jnp.sum(gn, axis=0, keepdims=True)

    def mlp_step(i, carry):
        mlp_block(i)

        @pl.when(i < 2)
        def _():
            norm_block(blocks - 2 + i)

        @pl.when(i >= 2)
        def _():
            back_block(i - 2)

        return carry

    lax.fori_loop(0, blocks, mlp_step, 0)
    for copy in whole[-2:]:
        copy.start()
    back_block(blocks - 2)
    back_block(blocks - 1)

    def copied(i, carry):
        down_out(i).wait()
        gh2_out(i).wait()
        here, there = ga_copies(i)
        here.wait()
        there.wait_send()
        piece = ga_hbm.at[share.rows(i, 1 - core), :]
        pltpu.make_async_remote_copy(
            src_ref=piece,
            dst_ref=piece,
            send_sem=put_sems.at[0, i],
            recv_sem=put_sems.at[1, i],
            device_id=(me, share.mate),
            device_id_type=MESH,
        ).wait_recv()
        return carry

    lax.fori_loop(0, blocks, copied, 0)
    for copy in whole:
        copy.wait()
    for piece in attend + dense:
        piece.sent()
    rowsum.finish()
    rowsum2.finish()
    share.finish(blocks)

    def sent_small(k, carry):
        small_copy(me, (me + k) % count).wait_send()
        return carry

    lax.fori_loop(1, count, sent_small, 0)


class Scatter:
    def __init__(self, view, stage, taken, sems, count):
        self.view, self.stage, self.taken = view, stage, taken
        self.sems, self.count = sems, count
        self.slots = stage.shape[1]
        self.pos = ring_pos(lax.axis_index("dp"), count)
        self.tensor = lax.axis_index("tensor")

    def _copy(self, way, step):
        sign = 1 - 2 * way
        return pltpu.make_async_remote_copy(
            src_ref=self.stage.at[way, step % self.slots],
            dst_ref=self.taken.at[way, step],
            send_sem=self.sems.at[2 * way, step],
            recv_sem=self.sems.at[2 * way + 1, step],
            device_id=(ring_at(self.pos + sign, self.count), self.tensor),
            device_id_type=MESH,
        )

    def begin(self):
        for way in range(2):
            self.stage[way, 0] = self.view(way, 0).astype(half_type)
            self._copy(way, 0).start()

    def advance(self, step):
        for way in range(2):
            self._copy(way, step - 1).wait_recv()
            total = self.taken[way, step - 1].astype(full_type) + self.view(way, step)

            @pl.when(step >= self.slots)
            def _(way=way):
                self._copy(way, step - self.slots).wait_send()

            self.stage[way, step % self.slots] = total.astype(half_type)
            self._copy(way, step).start()

    def total(self, way):
        last = self.count - 2
        self._copy(way, last).wait_recv()
        return self.taken[way, last].astype(full_type) + self.view(way, last + 1)

    def finish(self):
        for step in range(max(self.count - 1 - self.slots, 0), self.count - 1):
            for way in range(2):
                self._copy(way, step).wait_send()


def sent_block(pos, way, step, count):
    return ring_at(pos - (1 - 2 * way) * (1 + step), count)


class Put:
    def __init__(self, held, result, sems):
        self.held, self.result, self.sems = held, result, sems
        self.half = held.shape[0] // sems.shape[1]
        self.dp, tensor = lax.axis_index("dp"), lax.axis_index("tensor")
        self.core = tensor % 2
        self.mate = tensor - tensor % 2 + (tensor + 1) % 2

    def own(self, i):
        return pl.ds(pl.multiple_of(i * self.half, self.half), self.half)

    def _rows(self, i, core):
        return pl.ds(pl.multiple_of((2 * i + core) * self.half, self.half), self.half)

    def _here(self, i):
        target = self.result.at[self._rows(i, self.core), :]
        return pltpu.make_async_copy(self.held.at[self.own(i), :], target, self.sems.at[0, i])

    def _there(self, i, core):
        return pltpu.make_async_remote_copy(
            src_ref=self.held.at[self.own(i), :],
            dst_ref=self.result.at[self._rows(i, core), :],
            send_sem=self.sems.at[1, i],
            recv_sem=self.sems.at[2, i],
            device_id=(self.dp, self.mate),
            device_id_type=MESH,
        )

    def put(self, i, value):
        self.held[self.own(i), :] = value
        self._here(i).start()
        self._there(i, self.core).start()

    def left(self, i):
        self._here(i).wait()
        self._there(i, self.core).wait_send()

    def arrived(self, i):
        self._there(i, 1 - self.core).wait_recv()


def back_kernel(
    count, ga_hbm, o_ref, qb_ref, ka_ref, va_ref, wo_ref, w_ref, up_hbm, dn_hbm, down_hbm, h2_hbm,
    gh2_hbm, own_hbm, a1_hbm, vec_ref, gbias_ref, gvec_ref,
    layer_hbm, tg_hbm, dense_ref, sum_ref, small_ref,
    ga_ref, wide_ref, gh_ref, own_ref, goa_ref, kt_ref, gqt_ref, gqkv_ref, put_ref,
    given, sent, crossed, term2, given2, sent2, crossed2,
    terms, stage, taken, grads, stage2, taken2, small_mine, small_taken, small_mate,
    sum_sems, sum2_sems, put_sems, put2_sems, scatter_sems, scatter2_sems, small_sems, mate_sems,
    local_sems, terms_sems,
):
    total_rows, width = ga_ref.shape
    local_width = wo_ref.shape[1]
    heads = local_width // HD
    blocks = total_rows // BLOCK
    half = BLOCK // 2
    wide = width // count
    hops = count - 1
    lanes = small_ref.shape[1] - local_width
    fold = lanes // wide
    me, tensor = lax.axis_index("dp"), lax.axis_index("tensor")
    mate = tensor - tensor % 2 + (tensor + 1) % 2
    pos = ring_pos(me, count)
    greeted = greet(tensor_peers() + dp_peers(count))

    def own_rows(i):
        return pl.ds(pl.multiple_of(i * half, half), half)

    def place(block):
        return pl.ds(pl.multiple_of(block * wide, wide), wide)

    def own_fetch(source, target, sems):
        return lambda i: pltpu.make_async_copy(
            source.at[own_rows(i), :], target.at[own_rows(i), :], sems.at[i]
        )

    ga_in = fetch(ga_hbm, ga_ref, local_sems.at[0])
    down_in = fetch(down_hbm, wide_ref, local_sems.at[1])
    a1_in = fetch(a1_hbm, wide_ref, local_sems.at[2])
    h2_in = own_fetch(h2_hbm, gh_ref, local_sems.at[3])
    gh2_in = own_fetch(gh2_hbm, gh_ref, local_sems.at[4])
    own_in = own_fetch(own_hbm, own_ref, local_sems.at[5])

    def term_in(way, step):
        rows = place(sent_block(pos, way, step, count))
        source = (up_hbm, dn_hbm)[way].at[rows, :]
        return pltpu.make_async_copy(
            source, terms.at[way, step % 2], terms_sems.at[way, step % 2]
        )

    def each(copy):
        def start(i, carry):
            copy(i).start()
            return carry

        lax.fori_loop(0, blocks, start, 0)

    for step in range(2):
        for way in range(2):
            term_in(way, step).start()
    each(ga_in)
    each(down_in)
    each(h2_in)
    each(own_in)
    small_mine[:, :width] = gvec_ref[...]
    ratio = gbias_ref.shape[1] // local_width
    for r in range(ratio):
        small_mine[1 + r : 2 + r, width:] = gbias_ref[0:1, r * local_width : (r + 1) * local_width]
    small_mine[1 + ratio :, width:] = jnp.zeros((7 - ratio, local_width), full_type)
    greeted()

    pieces = stage.shape[0]
    part = terms.shape[3] // pieces

    def term_view(piece):
        columns = slice(piece * part, (piece + 1) * part)
        return lambda way, step: terms[way, step % 2, :, columns]

    scatters = [
        Scatter(term_view(p), stage.at[p], taken.at[p], scatter_sems.at[p], count)
        for p in range(pieces)
    ]

    def terms_ready(step):
        for way in range(2):
            term_in(way, step).wait()

    def terms_next(step):
        @pl.when(step <= hops)
        def _():
            for way in range(2):
                term_in(way, step).start()

    terms_ready(0)
    for scatter in scatters:
        scatter.begin()
    terms_next(2)

    rowsum = RowSum(wide_ref.reshape(blocks, BLOCK, width), given, sent, crossed, sum_sems)
    layer = Put(put_ref, layer_hbm, put_sems)
    down_in(0).wait()
    rowsum.give(0)
    lane = lax.broadcasted_iota(jnp.int32, (BLOCK, LANES), 1)
    low_half = lane < HD
    spot = lane % HD

    def prepare(i, carry):
        ga_in(i).wait()
        rows = pl.ds(pl.multiple_of(i * BLOCK, BLOCK), BLOCK)
        go = dot(ga_ref[rows, :], wo_ref[...]).astype(half_type).astype(full_type)
        both = go * o_ref[rows, :].astype(full_type)
        for head in range(heads):
            pair = slice(head // 2 * LANES, head // 2 * LANES + LANES)
            own = low_half if head % 2 == 0 else ~low_half
            inner = jnp.sum(jnp.where(own, both[:, pair], 0.0), axis=1, keepdims=True)
            filled = jnp.where(own, go[:, pair], 0.0)
            for k, value in enumerate(three_parts(inner)):
                filled = jnp.where(~own & (spot == k), -value, filled)
            goa_ref[head, rows, :] = filled.astype(half_type)
            if head % 2 == 0:
                before = ka_ref[head, rows, :].astype(full_type)
            else:
                k = jnp.where(low_half, before, ka_ref[head, rows, :].astype(full_type))
                kt_ref[pair, rows] = k.T.astype(half_type)
        return carry

    lax.fori_loop(0, blocks, prepare, 0)
    down_in(1).wait()
    rowsum.give(1)

    def output_block(i):
        h2_in(i).wait()
        total = gh_ref[own_rows(i), :] + rowsum.total(i) + vec_ref[1:2, :]
        layer.put(i, total.astype(half_type))
        gh2_in(i).start()

    per = -(-hops // blocks)

    def between(j, head):
        if head == 0:
            rowsum.cross(j)
        for t in range(per):
            hop = j * per + t

            @pl.when((hop >= 1) & (hop < hops))
            def _(hop=hop):
                if head == 0:
                    terms_ready(hop)
                for p, scatter in enumerate(scatters):
                    if p * heads // pieces == head:
                        scatter.advance(hop)
                if (pieces - 1) * heads // pieces == head:
                    terms_next(hop + 2)

        if head == 1:

            @pl.when(j < blocks - 2)
            def _():
                down_in(j + 2).wait()
                rowsum.give(j + 2)

        if head == heads - 1:

            @pl.when(j >= 1)
            def _():
                output_block(j - 1)

    def keys_block(j, carry):
        rows = pl.ds(pl.multiple_of(j * BLOCK, BLOCK), BLOCK)
        for head in range(heads):
            scores = dot(ka_ref[head, rows, :], qb_ref[head], 1, 1)
            probs = jnp.exp(scores)
            gp = dot(va_ref[head, rows, :], goa_ref[head], 1, 1)
            gs = (probs * gp).astype(half_type)
            gv = dot(probs.astype(half_type), goa_ref[head])
            gk = dot(gs, qb_ref[head])
            own = slice(head * HD, head * HD + HD)
            gqt = dot(kt_ref[own, rows], gs)

            @pl.when(j == 0)
            def _():
                gqt_ref[own, :] = gqt

            @pl.when(j > 0)
            def _():
                gqt_ref[own, :] += gqt

            if head % 2 == 0:
                gk_even, gv_even = gk, gv
            else:
                for k, value in ((1, (gk_even, gk)), (2, (gv_even, gv))):
                    base = k * local_width + head // 2 * LANES
                    gqkv_ref[rows, base : base + LANES] = jnp.where(low_half, *value).astype(
                        half_type
                    )
            between(j, head)
        return carry

    lax.fori_loop(0, blocks, keys_block, 0)

    def turn(i, carry):
        rows = pl.ds(pl.multiple_of(i * BLOCK, BLOCK), BLOCK)
        gqkv_ref[rows, :local_width] = (gqt_ref[:, rows].T * HD**-0.5).astype(half_type)
        return carry

    rowsum2 = RowSum(term2, given2, sent2, crossed2, sum2_sems)

    def norm_term(i):
        rows = pl.ds(pl.multiple_of(i * BLOCK, BLOCK), BLOCK)
        rowsum2.free(i)
        term2[i % term2.shape[0]] = dot(gqkv_ref[rows, :], w_ref[...], 1, 1).astype(half_type)
        rowsum2.give(i)

    lax.fori_loop(0, 2, turn, 0)
    norm_term(0)
    norm_term(1)
    rowsum.gone()
    each(a1_in)
    lax.fori_loop(2, blocks, turn, 0)
    rowsum2.cross(0)
    ones = jnp.ones((8, total_rows), half_type)
    bias_query = dot(ones, gqkv_ref[:, :local_width])
    small_mine[0:1, width:] = bias_query[0:1, :]

    def small_copy(kind, source, peer):
        window = pl.ds(pl.multiple_of(peer // fold * lanes, lanes), lanes)
        return pltpu.make_async_remote_copy(
            src_ref=small_mine.at[:, pl.ds(width, local_width) if kind else window],
            dst_ref=small_taken.at[source, :, pl.ds(lanes, local_width) if kind else pl.ds(0, lanes)],
            send_sem=small_sems.at[2 * kind, peer],
            recv_sem=small_sems.at[2 * kind + 1, source],
            device_id=(peer, tensor),
            device_id_type=MESH,
        )

    def send_small(kind):
        def send(k, carry):
            small_copy(kind, me, (me + k) % count).start()
            return carry

        lax.fori_loop(1, count, send, 0)

    send_small(1)

    def arrived_a1(i, carry):
        a1_in(i).wait()
        return carry

    lax.fori_loop(0, blocks, arrived_a1, 0)

    def weight_grads(c, carry):
        columns = pl.ds(pl.multiple_of(c * BLOCK, BLOCK), BLOCK)
        grads[columns, : 3 * local_width] = dot(wide_ref[:, columns], gqkv_ref[...], 0, 0)
        grads[columns, 3 * local_width :] = dot(ga_ref[:, columns], o_ref[...], 0, 0)
        return carry

    chunks = width // BLOCK
    lax.fori_loop(0, chunks // 2, weight_grads, 0)
    rowsum2.cross(1)
    output_block(blocks - 1)
    lax.fori_loop(chunks // 2, chunks, weight_grads, 0)
    side = grads.shape[1] // 2

    def grads_view(way, step):
        return grads[
            place(sent_block(pos, way, step, count)), way * side : (way + 1) * side
        ]

    scatter2 = Scatter(grads_view, stage2, taken2, scatter2_sems, count)
    scatter2.begin()

    def layer_left(i, carry):
        layer.left(i)
        layer.arrived(i)
        return carry

    lax.fori_loop(0, blocks, layer_left, 0)
    result = Put(put_ref, tg_hbm, put2_sems)

    def norm_block(i):
        gn = rowsum2.total(i)
        own_in(i).wait()
        gh2_in(i).wait()
        unit, rate = normalized(own_ref[own_rows(i), :].astype(full_type))
        e = gn * vec_ref[2:3, :]
        inner = e - jnp.mean(e, axis=-1, keepdims=True)
        inner = inner - unit * jnp.mean(e * unit, axis=-1, keepdims=True)
        result.put(i, (gh_ref[own_rows(i), :] + rate * inner).astype(half_type))
        small_mine[2:3, :width] += jnp.sum(gn * unit, axis=0, keepdims=True)
        small_mine[3:4, :width] += jnp.sum(gn, axis=0, keepdims=True)

    def end_step(i, carry):
        @pl.when(i < blocks - 2)
        def _():
            norm_term(i + 2)

        norm_block(i)

        @pl.when(i < blocks - 2)
        def _():
            rowsum2.cross(i + 2)

        for t in range(per):
            hop = i * per + t + 1

            @pl.when(hop < hops)
            def _(hop=hop):
                scatter2.advance(hop)

        return carry

    lax.fori_loop(0, blocks, end_step, 0)
    send_small(0)
    terms_ready(hops)
    for way in range(2):
        for p, scatter in enumerate(scatters):
            dense_ref[way, :, p * part : (p + 1) * part] = scatter.total(way)
        total = scatter2.total(way)
        for k in range(2):
            sum_ref[2 * way + k] = total[:, k * local_width : (k + 1) * local_width]
    for kind in range(2):
        window = pl.ds(pl.multiple_of(me // fold * lanes, lanes), lanes)
        here = slice(lanes, lanes + local_width) if kind else slice(0, lanes)
        small_taken[me, :, here] = small_mine[:, width:] if kind else small_mine[:, window]

        def take(k, carry, kind=kind):
            source = (me + k) % count
            small_copy(kind, source, source).wait_recv()
            return carry

        lax.fori_loop(1, count, take, 0)
    total = small_taken[0]
    for j in range(1, count):
        total = total + small_taken[j]
    small_ref[...] = total
    pair = pltpu.make_async_remote_copy(
        src_ref=small_ref.at[:, pl.ds(0, lanes)],
        dst_ref=small_mate,
        send_sem=mate_sems.at[0],
        recv_sem=mate_sems.at[1],
        device_id=(me, mate),
        device_id_type=MESH,
    )
    pair.start()
    pair.wait()
    small_ref[:, :lanes] = total[:, :lanes] + small_mate[...]

    def result_left(i, carry):
        result.left(i)
        result.arrived(i)
        return carry

    lax.fori_loop(0, blocks, result_left, 0)
    for scatter in scatters + [scatter2]:
        scatter.finish()
    rowsum.finish(given=False)
    rowsum2.finish()
    for kind in range(2):

        def done(k, carry, kind=kind):
            small_copy(kind, me, (me + k) % count).wait_send()
            return carry

        lax.fori_loop(1, count, done, 0)


def permuted(x, owner, back):
    rows, width = x.shape
    count = owner.shape[0]
    order = jnp.argsort(owner) if back else owner
    return jnp.take(x.reshape(rows, count, -1), order, axis=1).reshape(rows, width)


def adamw_step(weight, first, second, grad, rate, decay):
    first_next = first_decay * first + (1.0 - first_decay) * grad
    second_next = second_decay * second + (1.0 - second_decay) * grad * grad
    first_hat = first_next / (1.0 - first_decay**STEP)
    second_hat = second_next / (1.0 - second_decay**STEP)
    update = first_hat / (jnp.sqrt(second_hat) + adam_epsilon) + decay * weight
    return (first_next, second_next, weight - rate * update)


def last_kernel(rates, owner_ref, *refs):
    count = owner_ref.shape[0]
    given, refs = refs[:5], refs[5:]
    layer, grad, weight_sum, dense_sum, small = given
    state, refs = refs[:15], refs[15:]
    results, outs = refs[:2], refs[2:]

    def step(k, grad, at=(Ellipsis,)):
        new = adamw_step(*(ref[at] for ref in state[3 * k : 3 * k + 3]), grad, *rates[k])
        for ref, value in zip(outs[3 * k : 3 * k + 3], new):
            ref[at] = value

    wide = layer.shape[1] // count
    if wide % LANES == 0:
        for j in range(count):
            natural = pl.ds(pl.multiple_of(owner_ref[j] * wide, wide), wide)
            for x, y in zip((layer, grad), results):
                y[:, natural] = x[:, j * wide : (j + 1) * wide]
    else:
        for x, y in zip((layer, grad), results):
            y[...] = x[...]
    step(0, weight_sum[0:3])
    step(1, weight_sum[3])
    ratio, local_width = state[6].shape[2:]
    for r in range(ratio):
        step(
            2,
            dense_sum[:, :, r * local_width : (r + 1) * local_width],
            (slice(None), slice(None), r, slice(None)),
        )
    me = lax.axis_index("dp")
    lanes = small.shape[1] - local_width

    def chosen(x, start, size):
        row = lax.broadcasted_iota(jnp.int32, (x.shape[1], size), 0)
        column = lax.broadcasted_iota(jnp.int32, (x.shape[1], size), 1)
        pick = jnp.where(row == column + start, 1.0, 0.0).astype(half_type)
        return sum(dot(part.astype(half_type), pick) for part in three_parts(x))

    narrow, wide = state[9].shape[1], state[12].shape[1]
    step(3, chosen(small[:, lanes:], owner_ref[me] * narrow, narrow)[: 1 + ratio])
    step(4, chosen(small[:, :lanes], me % (lanes // wide) * wide, wide)[:6])


def last(owner, layer_output, tokens_grad, weight_sum, dense_sum, small_sum, *state):
    steps = 8 if dense_sum.shape[1] % 128 == 0 else 1
    rates = (
        (matrix_rate, matrix_decay),
        (output_rate, matrix_decay),
        (matrix_rate, matrix_decay),
        (bias_rate, 0.0),
        (vector_rate, 0.0),
    )

    def spec(x, dim):
        shape = tuple(n // steps if k == dim else n for k, n in enumerate(x.shape))
        return pl.BlockSpec(shape, lambda i, *_: tuple(i if k == dim else 0 for k in range(x.ndim)))

    dims = [0, 0, 1, 1, None] + [1] * 3 + [0] * 3 + [1] * 3 + [None] * 6
    operands = (layer_output, tokens_grad, weight_sum, dense_sum, small_sum) + state
    specs = [spec(x, dim) for x, dim in zip(operands, dims)]
    outs = operands[:2] + state
    return pl.pallas_call(
        functools.partial(last_kernel, rates),
        out_shape=[jax.ShapeDtypeStruct(x.shape, x.dtype) for x in outs],
        grid_spec=pltpu.PrefetchScalarGridSpec(
            num_scalar_prefetch=1, grid=(steps,), in_specs=specs, out_specs=specs[:2] + specs[5:]
        ),
        compiler_params=pltpu.CompilerParams(vmem_limit_bytes=60 * 2**20),
    )(owner, *operands)


def call(kernel, collective, outs, scratch, operands, spaces, limit=62):
    spec = {
        "s": pl.BlockSpec(memory_space=pltpu.SMEM),
        "v": pl.BlockSpec(memory_space=pltpu.VMEM),
        "h": pl.BlockSpec(memory_space=pl.ANY),
    }
    return pl.pallas_call(
        kernel,
        out_shape=[jax.ShapeDtypeStruct(shape, dtype) for shape, dtype in outs],
        in_specs=[spec[c] for c in spaces[0]],
        out_specs=[spec[c] for c in spaces[1]],
        scratch_shapes=scratch,
        compiler_params=pltpu.CompilerParams(
            collective_id=collective, has_side_effects=True, vmem_limit_bytes=limit * 2**20
        ),
    )(*operands)


def dma(*shape):
    return pltpu.SemaphoreType.DMA(shape)


def local(
    tokens,
    lengths,
    owner,
    attend_master,
    attend_first,
    attend_second,
    output_master,
    output_first,
    output_second,
    dense_master,
    dense_first,
    dense_second,
    bias_master,
    bias_first,
    bias_second,
    vector_master,
    vector_first,
    vector_second,
    cotangent,
):
    count = owner.shape[0]
    rows, width = tokens.shape
    local_width = output_master.shape[1]
    ratio = dense_master.shape[2]
    hidden = ratio * local_width
    heads = local_width // HD
    blocks = rows // BLOCK
    half = BLOCK // 2
    wide = width // count
    lanes = max(LANES, wide)
    tok, cot = tokens, cotangent
    if wide % LANES:
        tok, cot = (permuted(x, owner, False) for x in (tokens, cotangent))
    row_sum = [pltpu.VMEM((blocks, half, width), half_type)] * 3
    two_terms = pltpu.VMEM((2, BLOCK, width), half_type)
    heads_shape = (heads, rows, LANES)
    small = (8, lanes + local_width)
    a1, ga, h2, own, qb, ka, va, o, w, wo, gh2, down, up, dn, vec, gbias, gvec = call(
        functools.partial(front_kernel, count),
        0,
        [
            ((rows, width), half_type),
            ((rows, width), half_type),
            ((rows // 2, width), full_type),
            ((rows // 2, width), half_type),
            (heads_shape, half_type),
            (heads_shape, half_type),
            (heads_shape, half_type),
            ((rows, local_width), half_type),
            ((width, 3 * local_width), half_type),
            ((width, local_width), half_type),
            ((rows // 2, width), full_type),
            ((rows, width), half_type),
            ((width, hidden), full_type),
            ((width, hidden), full_type),
            ((8, width), full_type),
            ((8, hidden), full_type),
            ((8, width), full_type),
        ],
        [
            pltpu.VMEM((rows // 2, width), half_type),
            *[pltpu.VMEM(heads_shape, half_type)] * 3,
            pltpu.VMEM((rows, local_width), half_type),
            pltpu.VMEM((width, 3 * local_width), half_type),
            pltpu.VMEM((width, local_width), half_type),
            pltpu.VMEM((rows // 2, width), full_type),
            pltpu.VMEM((rows, width), half_type),
            *[pltpu.VMEM((width, hidden), full_type)] * 2,
            *[pltpu.VMEM((rows, width), half_type)] * 2,
            pltpu.VMEM((2, width, hidden), half_type),
            pltpu.VMEM((rows // 2, width), half_type),
            pltpu.VMEM((8, local_width), full_type),
            pltpu.VMEM((1, hidden), full_type),
            pltpu.VMEM(small, full_type),
            pltpu.VMEM((count,) + small, full_type),
            two_terms,
            *row_sum,
            two_terms,
            *row_sum,
            dma(6, 4, count // 2),
            dma(2, count),
            dma(4, blocks),
            dma(4, blocks),
            dma(2, blocks),
            dma(2, blocks),
            dma(7, blocks),
            dma(9),
        ],
        (
            lengths, owner, tok, cot, attend_master, output_master, dense_master, vector_master,
            bias_master,
        ),
        ("sshhvvvvv", "h" * 14 + "vvv"),
    )
    pieces = 2
    row_blocks = pltpu.VMEM((blocks, half, width), half_type)
    row_slots = pltpu.VMEM((min(3, blocks), half, width), half_type)
    part, side = hidden // pieces, 2 * local_width
    layer_output, tokens_grad, dense_sum, weight_sum, small_sum = call(
        functools.partial(back_kernel, count),
        1,
        [
            ((rows, width), half_type),
            ((rows, width), half_type),
            ((2, wide, hidden), full_type),
            ((4, wide, local_width), full_type),
            ((8, lanes + local_width), full_type),
        ],
        [
            pltpu.VMEM((rows, width), half_type),
            pltpu.VMEM((rows, width), half_type),
            pltpu.VMEM((rows // 2, width), full_type),
            pltpu.VMEM((rows // 2, width), half_type),
            pltpu.VMEM(heads_shape, half_type),
            pltpu.VMEM((local_width, rows), half_type),
            pltpu.VMEM((local_width, rows), full_type),
            pltpu.VMEM((rows, 3 * local_width), half_type),
            pltpu.VMEM((rows // 2, width), half_type),
            row_blocks,
            row_slots,
            row_blocks,
            two_terms,
            row_blocks,
            row_slots,
            row_blocks,
            pltpu.VMEM((2, 2, wide, hidden), full_type),
            pltpu.VMEM((pieces, 2, 2, wide, part), half_type),
            pltpu.VMEM((pieces, 2, count - 1, wide, part), half_type),
            pltpu.VMEM((width, 4 * local_width), full_type),
            pltpu.VMEM((2, 2, wide, side), half_type),
            pltpu.VMEM((2, count - 1, wide, side), half_type),
            pltpu.VMEM((8, width + local_width), full_type),
            pltpu.VMEM((count, 8, lanes + local_width), full_type),
            pltpu.VMEM((8, lanes), full_type),
            dma(4, blocks),
            dma(4, blocks),
            dma(3, blocks),
            dma(3, blocks),
            dma(pieces, 4, count - 1),
            dma(4, count - 1),
            dma(4, count),
            dma(2),
            dma(6, blocks),
            dma(2, 2),
        ],
        (ga, o, qb, ka, va, wo, w, up, dn, down, h2, gh2, own, a1, vec, gbias, gvec),
        ("hvvvvvvhhhhhhhvvv", "hhvvv"),
    )
    if wide % LANES:
        layer_output, tokens_grad = (permuted(x, owner, True) for x in (layer_output, tokens_grad))
    return tuple(
        last(
            owner, layer_output, tokens_grad, weight_sum, dense_sum, small_sum,
            attend_master, attend_first, attend_second,
            output_master, output_first, output_second,
            dense_master, dense_first, dense_second,
            bias_master, bias_first, bias_second,
            vector_master, vector_first, vector_second,
        )
    )


def solution(mesh):
    return jax.shard_map(
        local,
        mesh=mesh,
        in_specs=(
            P("dp", None),
            P("dp", None),
            P(),
            P(None, "dp", "tensor"),
            P(None, "dp", "tensor"),
            P(None, "dp", "tensor"),
            P("dp", "tensor"),
            P("dp", "tensor"),
            P("dp", "tensor"),
            P(None, "dp", None, "tensor"),
            P(None, "dp", None, "tensor"),
            P(None, "dp", None, "tensor"),
            P(None, ("tensor", "dp")),
            P(None, ("tensor", "dp")),
            P(None, ("tensor", "dp")),
            P(None, "dp"),
            P(None, "dp"),
            P(None, "dp"),
            P("dp", None),
        ),
        out_specs=(
            P("dp", None),
            P("dp", None),
            P(None, "dp", "tensor"),
            P(None, "dp", "tensor"),
            P(None, "dp", "tensor"),
            P("dp", "tensor"),
            P("dp", "tensor"),
            P("dp", "tensor"),
            P(None, "dp", None, "tensor"),
            P(None, "dp", None, "tensor"),
            P(None, "dp", None, "tensor"),
            P(None, ("tensor", "dp")),
            P(None, ("tensor", "dp")),
            P(None, ("tensor", "dp")),
            P(None, "dp"),
            P(None, "dp"),
            P(None, "dp"),
        ),
        check_vma=False,
    )
```

```python
import functools

import jax
import jax.numpy as jnp
from jax import lax
from jax.experimental import pallas as pl
from jax.experimental.pallas import tpu as pltpu
from jax.sharding import PartitionSpec as P

HD = 64
STEP = 10
LANES = 128
BLOCK = 256
MESH = pl.DeviceIdType.MESH
BIG = 2.0**50

norm_epsilon = 1e-06
first_decay = 0.9
second_decay = 0.95
adam_epsilon = 1e-08
matrix_rate = 0.1
output_rate = 0.5
bias_rate = 0.5
vector_rate = 1.0
matrix_decay = 0.05

half_type = jnp.bfloat16
full_type = jnp.float32


def dot(left, right, left_dim=1, right_dim=0):
    return lax.dot_general(
        left, right, (((left_dim,), (right_dim,)), ((), ())), preferred_element_type=full_type
    )


def ring_pos(place, count):
    column = place % 2
    row = place // 2
    return row * (1 - column) + (count - 1 - row) * column


def ring_at(pos, count):
    near = (pos + 2 * count) % count
    down = near // (count // 2)
    return 2 * near * (1 - down) + (2 * count - 1 - 2 * near) * down


def normalized(x):
    center = jnp.mean(x, axis=-1, keepdims=True)
    offset = x - center
    spread = jnp.mean(offset * offset, axis=-1, keepdims=True)
    rate = lax.rsqrt(spread + norm_epsilon)
    return offset * rate, rate


class Gather:
    def __init__(self, view, width, sems, count):
        self.view, self.width, self.sems, self.count = view, width, sems, count
        self.steps = count // 2
        self.pos = ring_pos(lax.axis_index("dp"), count)
        self.tensor = lax.axis_index("tensor")

    def _copy(self, way, step, hops):
        sign = 1 - 2 * way
        part = (0, self.width)
        if step == self.steps - 1:
            part = (way * (self.width // 2), self.width // 2)
        block = self.view(ring_at(self.pos - sign * hops, self.count), *part)
        return pltpu.make_async_remote_copy(
            src_ref=block,
            dst_ref=block,
            send_sem=self.sems.at[2 * way, step],
            recv_sem=self.sems.at[2 * way + 1, step],
            device_id=(ring_at(self.pos + sign, self.count), self.tensor),
            device_id_type=MESH,
        )

    def advance(self, step):
        if step:
            for way in range(2):
                self._copy(way, step - 1, step).wait_recv()
        if step < self.steps:
            for way in range(2):
                self._copy(way, step, step).start()

    def sent(self):
        for step in range(self.steps):
            for way in range(2):
                self._copy(way, step, step).wait_send()


class RowSum:
    def __init__(self, term, given, sent, crossed, sems):
        self.term, self.given, self.sent_ref, self.crossed = term, given, sent, crossed
        self.slots, self.sent_slots, self.blocks = term.shape[0], sent.shape[0], given.shape[0]
        self.sems = sems
        self.half = given.shape[1]
        self.dp, tensor = lax.axis_index("dp"), lax.axis_index("tensor")
        self.core = tensor % 2
        self.mate = tensor - tensor % 2 + (tensor + 1) % 2
        self.other = (tensor + 2) % 4

    def rows(self, core):
        return pl.ds(pl.multiple_of(core * self.half, self.half), self.half)

    def _give(self, i):
        return pltpu.make_async_remote_copy(
            src_ref=self.term.at[i % self.slots, self.rows(1 - self.core), :],
            dst_ref=self.given.at[i],
            send_sem=self.sems.at[0, i],
            recv_sem=self.sems.at[1, i],
            device_id=(self.dp, self.mate),
            device_id_type=MESH,
        )

    def _cross(self, i):
        return pltpu.make_async_remote_copy(
            src_ref=self.sent_ref.at[i % self.sent_slots],
            dst_ref=self.crossed.at[i],
            send_sem=self.sems.at[2, i],
            recv_sem=self.sems.at[3, i],
            device_id=(self.dp, self.other),
            device_id_type=MESH,
        )

    def free(self, i):
        if self.slots < self.blocks:

            @pl.when(i >= self.slots)
            def _():
                self._give(i - self.slots).wait_send()

    def give(self, i):
        self._give(i).start()

    def cross(self, i):
        self._give(i).wait_recv()
        mine = self.term[i % self.slots, self.rows(self.core), :].astype(full_type)
        if self.sent_slots < self.blocks:

            @pl.when(i >= self.sent_slots)
            def _():
                self._cross(i - self.sent_slots).wait_send()

        total = mine + self.given[i].astype(full_type)
        self.sent_ref[i % self.sent_slots] = total.astype(half_type)
        self._cross(i).start()

    def total(self, i):
        self._cross(i).wait_recv()
        mine = self.sent_ref[i % self.sent_slots].astype(full_type)
        return mine + self.crossed[i].astype(full_type)

    def gone(self):
        def given(i, carry):
            self._give(i).wait_send()
            return carry

        lax.fori_loop(max(self.blocks - self.slots, 0), self.blocks, given, 0)

    def finish(self, given=True):
        if given:
            self.gone()

        def crossed(i, carry):
            self._cross(i).wait_send()
            return carry

        lax.fori_loop(max(self.blocks - self.sent_slots, 0), self.blocks, crossed, 0)


class Share:
    def __init__(self, ref, sems):
        self.ref, self.sems = ref, sems
        self.dp, tensor = lax.axis_index("dp"), lax.axis_index("tensor")
        self.core = tensor % 2
        self.mate = tensor - tensor % 2 + (tensor + 1) % 2

    def rows(self, i, core):
        half = BLOCK // 2
        return pl.ds(pl.multiple_of(i * BLOCK + core * half, half), half)

    def _copy(self, i, core):
        piece = self.ref.at[self.rows(i, core), :]
        return pltpu.make_async_remote_copy(
            src_ref=piece,
            dst_ref=piece,
            send_sem=self.sems.at[0, i],
            recv_sem=self.sems.at[1, i],
            device_id=(self.dp, self.mate),
            device_id_type=MESH,
        )

    def put(self, i, value):
        self.ref[self.rows(i, self.core), :] = value
        self._copy(i, self.core).start()

    def arrived(self, i):
        self._copy(i, 1 - self.core).wait_recv()

    def finish(self, blocks):
        def done(i, carry):
            self._copy(i, self.core).wait_send()
            return carry

        lax.fori_loop(0, blocks, done, 0)


def greet(peers):
    barrier = pltpu.get_barrier_semaphore()
    for peer in peers:
        pl.semaphore_signal(barrier, inc=1, device_id=peer, device_id_type=MESH)
    return lambda: pl.semaphore_wait(barrier, len(peers))


def tensor_peers():
    dp, tensor = lax.axis_index("dp"), lax.axis_index("tensor")
    return [(dp, tensor - tensor % 2 + (tensor + 1) % 2), (dp, (tensor + 2) % 4)]


def ring_peers(count):
    dp, tensor = lax.axis_index("dp"), lax.axis_index("tensor")
    pos = ring_pos(dp, count)
    return [(ring_at(pos + 1, count), tensor), (ring_at(pos - 1, count), tensor)]


def dp_peers(count):
    dp, tensor = lax.axis_index("dp"), lax.axis_index("tensor")
    return [((dp + k) % count, tensor) for k in range(1, count)]


def three_parts(x):
    high = x.astype(half_type).astype(full_type)
    middle = (x - high).astype(half_type).astype(full_type)
    return high, middle, x - high - middle


def gelu_parts(z):
    phi = 0.5 + 0.5 * lax.erf(z * (0.5**0.5))
    slope = phi + z * (jnp.exp(-0.5 * z * z) * (2.0 * 3.141592653589793) ** -0.5)
    return z * phi, slope


def fetch(source, target, sems):
    def copy(i):
        rows = pl.ds(pl.multiple_of(i * BLOCK, BLOCK), BLOCK)
        return pltpu.make_async_copy(source.at[rows, :], target.at[rows, :], sems.at[i])

    return copy


def stored_order(x, owner_ref):
    count = owner_ref.shape[0]
    wide = x.shape[1] // count
    if wide % LANES:
        return x
    parts = []
    for j in range(count):
        total = None
        for n in range(count):
            term = x[:, n * wide : (n + 1) * wide] * jnp.where(owner_ref[j] == n, 1.0, 0.0)
            total = term if total is None else total + term
        parts.append(total)
    return jnp.concatenate(parts, axis=1)


def front_kernel(
    count, len_ref, owner_ref, tok_hbm, cot_hbm, att_ref, out_ref, dense_ref, vector_ref, split_ref,
    a1_hbm, ga_hbm, h2_hbm, own_hbm, qa_hbm, ka_hbm, va_hbm, o_hbm, w_hbm, gh2_hbm, down_hbm,
    up_hbm, dn_hbm, goa_hbm, kt_hbm, vec_ref, gbias_ref, gvec_ref,
    own_ref, qa_ref, ka_ref, va_ref, o_ref, w_ref, wo_ref, gh2_ref, down_ref, ul_ref, gz_ref, made,
    norm_ref, cot_ref, wd_ref, ga_ref, goa_ref, kt_ref, bias_ref, b1_ref, small_ref, smalls,
    mixed_ref, term2, given2, sent2, crossed2,
    gather_sems, small_sems, spread_sems, mixed_sems, sum2_sems, share_sems, put_sems, local_sems,
    whole_sems, made_sems,
):
    me, tensor = lax.axis_index("dp"), lax.axis_index("tensor")
    total_rows, width = norm_ref.shape
    local_width = out_ref.shape[1]
    ratio = dense_ref.shape[2]
    wide = width // count
    slots = len_ref.shape[1]
    heads = local_width // HD
    blocks = total_rows // BLOCK
    half = BLOCK // 2
    lanes = small_ref.shape[1] - local_width
    fold = lanes // wide
    steps = count // 2
    core = tensor % 2
    mate = tensor - core + 1 - core
    other, across = (tensor + 2) % 4, (mate + 2) % 4

    greeted = greet(tensor_peers() + [(me, across)] + dp_peers(count))
    tokens_in = fetch(tok_hbm, norm_ref, local_sems.at[0])
    cot_in = fetch(cot_hbm, cot_ref, local_sems.at[1])
    a1_out = fetch(norm_ref, a1_hbm, local_sems.at[2])
    for i in range(blocks):
        tokens_in(i).start()
    for i in range(blocks):
        cot_in(i).start()
    mine = pl.ds(pl.multiple_of(me * wide, wide), wide)
    for row in range(3):
        w_ref[mine, row * local_width : (row + 1) * local_width] = att_ref[row].astype(half_type)

    def columns_of(index, low=0, size=local_width):
        return pl.ds(pl.multiple_of(index * local_width + low, LANES), size)

    wo_ref[mine, columns_of(tensor)] = out_ref[...].astype(half_type)

    small_ref[...] = jnp.zeros_like(small_ref)
    vectors = vector_ref[...].astype(half_type)
    if fold == 1:
        small_ref[0:6, :lanes] = vectors.astype(full_type)
    else:
        row = lax.broadcasted_iota(jnp.int32, (wide, lanes), 0)
        column = lax.broadcasted_iota(jnp.int32, (wide, lanes), 1)
        spread = jnp.where(column == row + me % fold * wide, 1.0, 0.0).astype(half_type)
        small_ref[0:6, :lanes] = dot(vectors, spread)
    narrow = split_ref.shape[1]
    row = lax.broadcasted_iota(jnp.int32, (narrow, local_width), 0)
    column = lax.broadcasted_iota(jnp.int32, (narrow, local_width), 1)
    spread = jnp.where(column == row + owner_ref[me] * narrow, 1.0, 0.0).astype(half_type)
    small_ref[0 : 1 + ratio, lanes:] = dot(split_ref[...].astype(half_type), spread)
    smalls[me] = small_ref[...]
    greeted()

    def place(block):
        return pl.ds(pl.multiple_of(block * wide, wide), wide)

    def small_copy(source, peer):
        return pltpu.make_async_remote_copy(
            src_ref=small_ref,
            dst_ref=smalls.at[source],
            send_sem=small_sems.at[0, peer],
            recv_sem=small_sems.at[1, source],
            device_id=(peer, tensor),
            device_id_type=MESH,
        )

    def send_small(k, carry):
        small_copy(me, (me + k) % count).start()
        return carry

    lax.fori_loop(1, count, send_small, 0)

    def attend_view(row):
        return lambda block, low, size: w_ref.at[
            place(block), pl.ds(row * local_width + low, size)
        ]

    def dense_view(row):
        return lambda block, low, size: wd_ref.at[row, place(block), pl.ds(low, size)]

    attend = [Gather(attend_view(row), local_width, gather_sems.at[row], count) for row in range(3)]
    attend.append(
        Gather(
            lambda block, low, size: wo_ref.at[place(block), columns_of(tensor, low, size)],
            local_width, gather_sems.at[3], count,
        )
    )
    dense = [
        Gather(dense_view(row), ratio * local_width, gather_sems.at[4 + row], count)
        for row in range(2)
    ]
    for piece in attend:
        piece.advance(0)

    def spread(kind, block, source, target):
        piece = wo_ref.at[place(block), columns_of(source)]
        return pltpu.make_async_remote_copy(
            src_ref=piece,
            dst_ref=piece,
            send_sem=spread_sems.at[2 * kind, block],
            recv_sem=spread_sems.at[2 * kind + 1, block],
            device_id=(me, target),
            device_id_type=MESH,
        )

    def spread_step(step):
        pos = attend[3].pos
        hops = {0: [0], steps: [steps]}.get(step, [step, -step])
        for hop in hops:
            block = ring_at(pos - hop, count)
            spread(0, block, tensor, mate).start()
            spread(1, block, tensor, other).start()

    spread_step(0)
    for row in range(2):
        for r in range(ratio):
            wd_ref[row, mine, r * local_width : (r + 1) * local_width] = dense_ref[
                row, :, r, :
            ].astype(half_type)

    def take_small(k, carry):
        source = (me + k) % count
        small_copy(source, source).wait_recv()
        return carry

    lax.fori_loop(1, count, take_small, 0)
    bias = smalls[0, :, lanes:]
    for j in range(1, count):
        bias = bias + smalls[j, :, lanes:]
    bias_ref[...] = bias
    for r in range(ratio):
        b1_ref[:, r * local_width : (r + 1) * local_width] = bias[1 + r : 2 + r, :]
    for window in range(width // lanes):
        piece = smalls[window * fold, :, :lanes]
        for j in range(window * fold + 1, (window + 1) * fold):
            piece = piece + smalls[j, :, :lanes]
        vec_ref[:, window * lanes : (window + 1) * lanes] = piece

    def norm_rows(i, carry):
        tokens_in(i).wait()
        rows = pl.ds(pl.multiple_of(i * BLOCK, BLOCK), BLOCK)
        x = stored_order(norm_ref[rows, :].astype(full_type), owner_ref)
        norm_ref[rows, :] = x.astype(half_type)
        here = pl.ds(pl.multiple_of(i * BLOCK + core * half, half), half)
        own_ref[pl.ds(pl.multiple_of(i * half, half), half), :] = norm_ref[here, :]
        unit, _ = normalized(x)
        norm_ref[rows, :] = (unit * vec_ref[2:3, :] + vec_ref[3:4, :]).astype(half_type)
        a1_out(i).start()
        cot_in(i).wait()
        cot_ref[rows, :] = stored_order(cot_ref[rows, :].astype(full_type), owner_ref).astype(
            half_type
        )
        return carry

    done = 0
    for step in range(1, steps + 1):
        for piece in attend:
            piece.advance(step)
        spread_step(step)
        if step == steps - 1:
            for piece in dense:
                piece.advance(0)
        upto = min(blocks, -(-blocks * step // (steps - 1)))
        if upto > done:
            lax.fori_loop(done, upto, norm_rows, 0)
        done = max(done, upto)

    pumps = [(piece, step) for step in range(1, steps + 1) for piece in dense]

    def pump(slot):
        for k, (piece, step) in enumerate(pumps):
            if min(blocks + 1, (13 * k + 2) // 10 * 8 // len(pumps)) == slot:
                piece.advance(step)

    lane = lax.broadcasted_iota(jnp.int32, (BLOCK, LANES), 1)
    low_half = lane < HD
    spot = lane % HD

    def project(i, carry):
        row = pl.multiple_of(i * BLOCK, BLOCK)
        rows = pl.ds(row, BLOCK)
        a1 = norm_ref[rows, :]
        qkv = dot(a1, w_ref[...])
        q, k, v = (qkv[:, part * local_width : (part + 1) * local_width] for part in range(3))
        q = (q + bias_ref[0:1, :]).astype(half_type).astype(full_type) * HD**-0.5
        index = row + lax.broadcasted_iota(jnp.int32, (BLOCK, LANES), 0)
        segment = jnp.zeros((BLOCK, LANES), jnp.int32)
        end = 0
        for slot in range(slots):
            end = end + len_ref[0, slot]
            segment = segment + jnp.where(index >= end, 1, 0)
        same = spot == segment
        inside = spot <= slots
        q_mark = jnp.where(inside & ~same, -BIG, 0.0)
        k_mark = jnp.where(same, BIG, jnp.where((spot > slots) & (spot <= slots + 3), 1.0, 0.0))
        for head in range(heads):
            pair = slice(head // 2 * LANES, head // 2 * LANES + LANES)
            own = low_half if head % 2 == 0 else ~low_half
            qa_ref[head, rows, :] = jnp.where(own, q[:, pair], q_mark).astype(half_type)
            ka_ref[head, rows, :] = jnp.where(own, k[:, pair], k_mark).astype(half_type)
            va_ref[head, rows, :] = jnp.where(own, v[:, pair], 1.0).astype(half_type)
        return carry

    lax.fori_loop(0, blocks, project, 0)
    pump(0)

    def forward(block, carry):
        spread(1, block, other, other).wait_recv()
        spread(2, block, other, mate).start()
        return carry

    lax.fori_loop(0, count, forward, 0)

    def a1_left(i, carry):
        a1_out(i).wait()
        return carry

    lax.fori_loop(0, blocks, a1_left, 0)
    gbias_ref[...] = jnp.zeros_like(gbias_ref)
    gvec_ref[...] = jnp.zeros_like(gvec_ref)

    share = Share(norm_ref, share_sems)

    def mixed_copy(kind, i, source, target, half_rows):
        rows = pl.ds(pl.multiple_of(i * BLOCK + half_rows * half, half), half)
        return pltpu.make_async_remote_copy(
            src_ref=o_ref.at[rows, :],
            dst_ref=mixed_ref.at[i, :, columns_of(source)],
            send_sem=mixed_sems.at[2 * kind, i],
            recv_sem=mixed_sems.at[2 * kind + 1, i],
            device_id=(me, target),
            device_id_type=MESH,
        )

    peers = ((0, mate, 1 - core), (1, other, core), (2, across, 1 - core))

    def h2_out(i):
        own = pl.ds(pl.multiple_of(i * half, half), half)
        return pltpu.make_async_copy(gh2_ref.at[own, :], h2_hbm.at[own, :], local_sems.at[3, i])

    def attend_block(i):
        rows = pl.ds(pl.multiple_of(i * BLOCK, BLOCK), BLOCK)
        for head in range(heads):
            query = qa_ref[head, rows, :]
            scores = dot(query, ka_ref[head], 1, 1)
            top = jnp.max(scores, axis=1, keepdims=True)
            weights = jnp.exp(scores - top).astype(half_type)
            mixed = dot(weights, va_ref[head])
            turned = pltpu.roll(mixed, HD, 1)
            own = low_half if head % 2 == 0 else ~low_half
            log_total = three_parts(top + jnp.log(jnp.where(own, turned, mixed)))
            marked = query.astype(full_type)
            for part in range(3):
                marked = jnp.where(~own & (spot == slots + 1 + part), -log_total[part], marked)
            qa_ref[head, rows, :] = marked.astype(half_type)
            out = mixed / turned
            if head % 2 == 0:
                before = out
            else:
                pair = slice(head // 2 * LANES, head // 2 * LANES + LANES)
                o_ref[rows, pair] = jnp.where(low_half, before, out).astype(half_type)
        for kind, peer, half_rows in peers[1:] + peers[:1]:
            mixed_copy(kind, i, tensor, peer, half_rows).start()
        here = pl.ds(pl.multiple_of(i * BLOCK + core * half, half), half)
        mixed_ref[i, :, columns_of(tensor)] = o_ref[here, :]

    def norm_block(i):
        own = pl.ds(pl.multiple_of(i * half, half), half)
        for kind, peer, _ in peers:
            mixed_copy(kind, i, peer, peer, 0).wait_recv()
        attn = dot(mixed_ref[i], wo_ref[...], 1, 1)
        hidden = own_ref[own, :].astype(full_type) + attn + vec_ref[0:1, :]
        gh2_ref[own, :] = hidden
        h2_out(i).start()
        unit, _ = normalized(hidden)
        share.put(i, (unit * vec_ref[4:5, :] + vec_ref[5:6, :]).astype(half_type))

    behind = min(2, blocks)

    def attend_step(i, carry):
        attend_block(i)
        for slot in range(1, blocks + 1):

            @pl.when(i == slot - 1)
            def _(slot=slot):
                pump(slot)

        @pl.when(i == behind)
        def _():
            def spread_in(block, carry):
                spread(0, block, mate, mate).wait_recv()
                spread(2, block, across, mate).wait_recv()
                return carry

            lax.fori_loop(0, count, spread_in, 0)

        @pl.when(i >= behind)
        def _():
            norm_block(i - behind)

        return carry

    lax.fori_loop(0, blocks, attend_step, 0)
    for i in range(blocks - behind, blocks):
        norm_block(i)
    pump(blocks + 1)

    whole = [
        pltpu.make_async_copy(source, target, whole_sems.at[k])
        for k, (source, target) in enumerate(
            (
                (own_ref, own_hbm), (qa_ref, qa_hbm), (ka_ref, ka_hbm), (va_ref, va_hbm),
                (o_ref, o_hbm), (w_ref, w_hbm),
            )
        )
    ]
    for copy in whole:
        copy.start()
    down_out = fetch(down_ref, down_hbm, local_sems.at[5])

    def gh2_out(i):
        own = pl.ds(pl.multiple_of(i * half, half), half)
        return pltpu.make_async_copy(gh2_ref.at[own, :], gh2_hbm.at[own, :], local_sems.at[6, i])

    rowsum2 = RowSum(term2, given2, sent2, crossed2, sum2_sems)

    share2 = Share(ga_ref, put_sems)
    ga_out = fetch(ga_ref, ga_hbm, local_sems.at[4])

    def goa_out(i):
        rows = pl.ds(pl.multiple_of(i * BLOCK, BLOCK), BLOCK)
        return pltpu.make_async_copy(
            goa_ref.at[:, rows, :], goa_hbm.at[:, rows, :], local_sems.at[7, i]
        )

    def prepare(i):
        share2.arrived(i)
        ga_out(i).start()
        rows = pl.ds(i * BLOCK, BLOCK)
        go = dot(ga_ref[rows, :], wo_ref[:, columns_of(tensor)]).astype(half_type).astype(full_type)
        both = go * o_ref[rows, :].astype(full_type)
        for head in range(heads):
            pair = slice(head // 2 * LANES, head // 2 * LANES + LANES)
            own = low_half if head % 2 == 0 else ~low_half
            inner = jnp.sum(jnp.where(own, both[:, pair], 0.0), axis=1, keepdims=True)
            filled = jnp.where(own, go[:, pair], 0.0)
            for k, value in enumerate(three_parts(inner)):
                filled = jnp.where(~own & (spot == k), -value, filled)
            goa_ref[head, rows, :] = filled.astype(half_type)
            if head % 2 == 0:
                before = ka_ref[head, rows, :].astype(full_type)
            else:
                k = jnp.where(low_half, before, ka_ref[head, rows, :].astype(full_type))
                kt_ref[pair, rows] = k.T.astype(half_type)
        goa_out(i).start()

    def mlp_block(i):
        rows = pl.ds(pl.multiple_of(i * BLOCK, BLOCK), BLOCK)
        share.arrived(i)
        a2 = norm_ref[rows, :]
        gy = cot_ref[rows, :]
        u, slope = gelu_parts(dot(a2, wd_ref[0]) + b1_ref[...])
        ul = u.astype(half_type)
        gz = (dot(gy, wd_ref[1]) * slope).astype(half_type)
        rowsum2.free(i)
        term2[i % term2.shape[0]] = dot(gz, wd_ref[0], 1, 1).astype(half_type)
        rowsum2.give(i)
        gbias_ref[0:1, :] += jnp.sum(gz.astype(full_type), axis=0, keepdims=True)
        ul_ref[rows, :] = ul
        gz_ref[rows, :] = gz
        down_ref[rows, :] = dot(ul, wd_ref[1], 1, 1).astype(half_type)
        down_out(i).start()
        rowsum2.cross(i)

    chunks = width // BLOCK

    def made_out(c):
        rows = pl.ds(c % chunks * BLOCK, BLOCK)
        target = (up_hbm, dn_hbm)[c // chunks].at[rows, :]
        return pltpu.make_async_copy(made.at[c % 2], target, made_sems.at[c])

    def weight_grads(c):
        left, right = ((norm_ref, gz_ref), (cot_ref, ul_ref))[c // chunks]
        if c >= 2:
            made_out(c - 2).wait()
        columns = slice(c % chunks * BLOCK, (c % chunks + 1) * BLOCK)
        made[c % 2] = dot(left[:, columns], right[...], 0, 0)
        made_out(c).start()

    def back_block(i):
        own = pl.ds(pl.multiple_of(i * half, half), half)
        gn = rowsum2.total(i)
        h2_out(i).wait()
        unit, rate = normalized(gh2_ref[own, :])
        e = gn * vec_ref[4:5, :]
        inner = e - jnp.mean(e, axis=-1, keepdims=True)
        inner = inner - unit * jnp.mean(e * unit, axis=-1, keepdims=True)
        gy = cot_ref[share.rows(i, core), :].astype(full_type)
        gh = gy + rate * inner
        gh2_ref[own, :] = gh
        gh2_out(i).start()
        share2.put(i, gh.astype(half_type))
        gvec_ref[0:1, :] += jnp.sum(gh, axis=0, keepdims=True)
        gvec_ref[1:2, :] += jnp.sum(gy, axis=0, keepdims=True)
        gvec_ref[4:5, :] += jnp.sum(gn * unit, axis=0, keepdims=True)
        gvec_ref[5:6, :] += jnp.sum(gn, axis=0, keepdims=True)

    def mlp_step(i, carry):
        mlp_block(i)
        return carry

    lax.fori_loop(0, blocks, mlp_step, 0)
    chunk = 0
    for i in range(blocks):
        back_block(i)
        if i >= 2:
            prepare(i - 2)
        upto = 2 * chunks if i == blocks - 1 else max(0, min(3, i) * 2 * chunks // 3)
        for c in range(chunk, upto):
            weight_grads(c)
        chunk = max(chunk, upto)
    prepare(blocks - 2)
    prepare(blocks - 1)
    kt_out = pltpu.make_async_copy(kt_ref, kt_hbm, whole_sems.at[len(whole)])
    kt_out.start()
    made_out(2 * chunks - 2).wait()
    made_out(2 * chunks - 1).wait()

    def copied(i, carry):
        down_out(i).wait()
        gh2_out(i).wait()
        ga_out(i).wait()
        goa_out(i).wait()
        return carry

    lax.fori_loop(0, blocks, copied, 0)
    for copy in whole + [kt_out]:
        copy.wait()
    for piece in attend + dense:
        piece.sent()
    rowsum2.finish()
    share.finish(blocks)
    share2.finish(blocks)

    def spread_out(block, carry):
        spread(0, block, tensor, mate).wait_send()
        spread(1, block, tensor, other).wait_send()
        spread(2, block, other, mate).wait_send()
        return carry

    lax.fori_loop(0, count, spread_out, 0)

    def mixed_out(i, carry):
        for kind, peer, half_rows in peers:
            mixed_copy(kind, i, tensor, peer, half_rows).wait_send()
        return carry

    lax.fori_loop(0, blocks, mixed_out, 0)

    def sent_small(k, carry):
        small_copy(me, (me + k) % count).wait_send()
        return carry

    lax.fori_loop(1, count, sent_small, 0)


class Scatter:
    def __init__(self, view, stage, taken, sems, count):
        self.view, self.stage, self.taken = view, stage, taken
        self.sems, self.count = sems, count
        self.slots = stage.shape[1]
        self.pos = ring_pos(lax.axis_index("dp"), count)
        self.tensor = lax.axis_index("tensor")

    def _copy(self, way, step):
        sign = 1 - 2 * way
        return pltpu.make_async_remote_copy(
            src_ref=self.stage.at[way, step % self.slots],
            dst_ref=self.taken.at[way, step],
            send_sem=self.sems.at[2 * way, step],
            recv_sem=self.sems.at[2 * way + 1, step],
            device_id=(ring_at(self.pos + sign, self.count), self.tensor),
            device_id_type=MESH,
        )

    def begin(self):
        for way in range(2):
            self.stage[way, 0] = self.view(way, 0).astype(half_type)
            self._copy(way, 0).start()

    def advance(self, step):
        for way in range(2):
            self._copy(way, step - 1).wait_recv()
            total = self.taken[way, step - 1].astype(full_type) + self.view(way, step)

            @pl.when(step >= self.slots)
            def _(way=way):
                self._copy(way, step - self.slots).wait_send()

            self.stage[way, step % self.slots] = total.astype(half_type)
            self._copy(way, step).start()

    def total(self, way):
        last = self.count - 2
        self._copy(way, last).wait_recv()
        return self.taken[way, last].astype(full_type) + self.view(way, last + 1)

    def finish(self):
        for step in range(max(self.count - 1 - self.slots, 0), self.count - 1):
            for way in range(2):
                self._copy(way, step).wait_send()


def sent_block(pos, way, step, count):
    return ring_at(pos - (1 - 2 * way) * (1 + step), count)


class Put:
    def __init__(self, held, result, sems):
        self.held, self.result, self.sems = held, result, sems
        self.half = held.shape[0] // sems.shape[1]
        self.dp, tensor = lax.axis_index("dp"), lax.axis_index("tensor")
        self.core = tensor % 2
        self.mate = tensor - tensor % 2 + (tensor + 1) % 2

    def own(self, i):
        return pl.ds(pl.multiple_of(i * self.half, self.half), self.half)

    def _rows(self, i, core):
        return pl.ds(pl.multiple_of((2 * i + core) * self.half, self.half), self.half)

    def _here(self, i):
        target = self.result.at[self._rows(i, self.core), :]
        return pltpu.make_async_copy(self.held.at[self.own(i), :], target, self.sems.at[0, i])

    def _there(self, i, core):
        return pltpu.make_async_remote_copy(
            src_ref=self.held.at[self.own(i), :],
            dst_ref=self.result.at[self._rows(i, core), :],
            send_sem=self.sems.at[1, i],
            recv_sem=self.sems.at[2, i],
            device_id=(self.dp, self.mate),
            device_id_type=MESH,
        )

    def put(self, i, value):
        self.held[self.own(i), :] = value
        self._here(i).start()
        self._there(i, self.core).start()

    def left(self, i):
        self._here(i).wait()
        self._there(i, self.core).wait_send()

    def arrived(self, i):
        self._there(i, 1 - self.core).wait_recv()


def back_kernel(
    count, ga_hbm, o_hbm, qb_hbm, ka_hbm, va_hbm, goa_hbm, kt_hbm, w_hbm, up_hbm, dn_hbm, down_hbm,
    h2_hbm, gh2_hbm, own_hbm, a1_hbm, vec_ref, gbias_ref, gvec_ref,
    layer_hbm, tg_hbm, dense_ref, sum_ref, small_ref,
    ga_ref, o_ref, qb_ref, ka_ref, va_ref, w_ref, wide_ref, gh_ref, own_ref, goa_ref, kt_ref, gqt_ref, gqkv_ref, put_ref,
    given, sent, crossed, term2, given2, sent2, crossed2,
    terms, stage, taken, grads, stage2, taken2, small_mine, small_taken, small_mate,
    sum_sems, sum2_sems, put_sems, put2_sems, scatter_sems, scatter2_sems, small_sems, mate_sems,
    local_sems, terms_sems, whole_sems,
):
    total_rows, width = ga_ref.shape
    local_width = o_ref.shape[1]
    heads = local_width // HD
    blocks = total_rows // BLOCK
    half = BLOCK // 2
    wide = width // count
    hops = count - 1
    lanes = small_ref.shape[1] - local_width
    fold = lanes // wide
    me, tensor = lax.axis_index("dp"), lax.axis_index("tensor")
    mate = tensor - tensor % 2 + (tensor + 1) % 2
    pos = ring_pos(me, count)
    greeted = greet(tensor_peers() + dp_peers(count))

    def own_rows(i):
        return pl.ds(pl.multiple_of(i * half, half), half)

    def place(block):
        return pl.ds(pl.multiple_of(block * wide, wide), wide)

    def own_fetch(source, target, sems):
        return lambda i: pltpu.make_async_copy(
            source.at[own_rows(i), :], target.at[own_rows(i), :], sems.at[i]
        )

    ga_in = fetch(ga_hbm, ga_ref, local_sems.at[0])
    down_in = fetch(down_hbm, wide_ref, local_sems.at[1])
    a1_in = fetch(a1_hbm, wide_ref, local_sems.at[2])
    h2_in = own_fetch(h2_hbm, gh_ref, local_sems.at[3])
    gh2_in = own_fetch(gh2_hbm, gh_ref, local_sems.at[4])
    own_in = own_fetch(own_hbm, own_ref, local_sems.at[5])

    def term_in(way, step):
        rows = place(sent_block(pos, way, step, count))
        source = (up_hbm, dn_hbm)[way].at[rows, :]
        return pltpu.make_async_copy(
            source, terms.at[way, step % 2], terms_sems.at[way, step % 2]
        )

    def each(copy):
        def start(i, carry):
            copy(i).start()
            return carry

        lax.fori_loop(0, blocks, start, 0)

    for step in range(2):
        for way in range(2):
            term_in(way, step).start()
    whole = [
        pltpu.make_async_copy(source, target, whole_sems.at[k])
        for k, (source, target) in enumerate(
            (
                (qb_hbm, qb_ref), (ka_hbm, ka_ref), (va_hbm, va_ref), (goa_hbm, goa_ref),
                (kt_hbm, kt_ref), (o_hbm, o_ref), (w_hbm, w_ref),
            )
        )
    ]
    for copy in whole[:-2]:
        copy.start()
    each(down_in)
    each(h2_in)
    for copy in whole[-2:]:
        copy.start()
    each(ga_in)
    each(own_in)
    small_mine[:, :width] = gvec_ref[...]
    ratio = gbias_ref.shape[1] // local_width
    for r in range(ratio):
        small_mine[1 + r : 2 + r, width:] = gbias_ref[0:1, r * local_width : (r + 1) * local_width]
    small_mine[1 + ratio :, width:] = jnp.zeros((7 - ratio, local_width), full_type)
    greeted()

    pieces = stage.shape[0]
    part = terms.shape[3] // pieces

    def term_view(piece):
        columns = slice(piece * part, (piece + 1) * part)
        return lambda way, step: terms[way, step % 2, :, columns]

    scatters = [
        Scatter(term_view(p), stage.at[p], taken.at[p], scatter_sems.at[p], count)
        for p in range(pieces)
    ]

    def terms_ready(step):
        for way in range(2):
            term_in(way, step).wait()

    def terms_next(step):
        @pl.when(step <= hops)
        def _():
            for way in range(2):
                term_in(way, step).start()

    rowsum = RowSum(wide_ref.reshape(blocks, BLOCK, width), given, sent, crossed, sum_sems)
    layer = Put(put_ref, layer_hbm, put_sems)
    def give_all(i, carry):
        down_in(i).wait()
        rowsum.give(i)
        return carry

    lax.fori_loop(0, blocks, give_all, 0)
    terms_ready(0)
    for scatter in scatters:
        scatter.begin()
    terms_next(2)

    lane = lax.broadcasted_iota(jnp.int32, (BLOCK, LANES), 1)
    low_half = lane < HD
    gqt_ref[...] = jnp.zeros_like(gqt_ref)
    rowsum.cross(0)
    for copy in whole[:-2]:
        copy.wait()

    def output_block(i):
        h2_in(i).wait()
        total = gh_ref[own_rows(i), :] + rowsum.total(i) + vec_ref[1:2, :]
        layer.put(i, total.astype(half_type))
        gh2_in(i).start()

    per = -(-hops // blocks)

    def between(j, piece):
        if piece == 0:

            @pl.when(j >= 1)
            def _():
                output_block(j - 1)

            @pl.when(j < blocks - 1)
            def _():
                rowsum.cross(j + 1)

        for t in range(per):
            hop = j * per + t

            @pl.when((hop >= 1) & (hop < hops))
            def _(hop=hop):
                if piece == 0:
                    terms_ready(hop)
                scatters[piece].advance(hop)
                if piece == pieces - 1:
                    terms_next(hop + 2)

    def keys_block(j, carry):
        rows = pl.ds(pl.multiple_of(j * BLOCK, BLOCK), BLOCK)
        for head in range(heads):
            scores = dot(ka_ref[head, rows, :], qb_ref[head], 1, 1)
            probs = jnp.exp(scores)
            gp = dot(va_ref[head, rows, :], goa_ref[head], 1, 1)
            gs = (probs * gp).astype(half_type)
            gv = dot(probs.astype(half_type), goa_ref[head])
            gk = dot(gs, qb_ref[head])
            own = slice(head * HD, head * HD + HD)
            gqt_ref[own, :] += dot(kt_ref[own, rows], gs)
            if head % 2 == 0:
                gk_even, gv_even = gk, gv
            else:
                for k, value in ((1, (gk_even, gk)), (2, (gv_even, gv))):
                    base = k * local_width + head // 2 * LANES
                    gqkv_ref[rows, base : base + LANES] = jnp.where(low_half, *value).astype(
                        half_type
                    )
            if (head + 1) * pieces % heads == 0:
                between(j, (head + 1) * pieces // heads - 1)
        return carry

    lax.fori_loop(0, blocks, keys_block, 0)

    def turn(i, carry):
        rows = pl.ds(pl.multiple_of(i * BLOCK, BLOCK), BLOCK)
        gqkv_ref[rows, :local_width] = (gqt_ref[:, rows].T * HD**-0.5).astype(half_type)
        return carry

    rowsum2 = RowSum(term2, given2, sent2, crossed2, sum2_sems)

    def norm_term(i):
        rows = pl.ds(pl.multiple_of(i * BLOCK, BLOCK), BLOCK)
        rowsum2.free(i)
        term2[i % term2.shape[0]] = dot(gqkv_ref[rows, :], w_ref[...], 1, 1).astype(half_type)
        rowsum2.give(i)

    lax.fori_loop(0, 2, turn, 0)
    whole[-1].wait()
    norm_term(0)
    norm_term(1)
    rowsum.gone()
    each(a1_in)
    lax.fori_loop(2, blocks, turn, 0)
    rowsum2.cross(0)
    ones = jnp.ones((8, total_rows), half_type)
    bias_query = dot(ones, gqkv_ref[:, :local_width])
    small_mine[0:1, width:] = bias_query[0:1, :]

    def small_copy(kind, source, peer):
        window = pl.ds(pl.multiple_of(peer // fold * lanes, lanes), lanes)
        return pltpu.make_async_remote_copy(
            src_ref=small_mine.at[:, pl.ds(width, local_width) if kind else window],
            dst_ref=small_taken.at[source, :, pl.ds(lanes, local_width) if kind else pl.ds(0, lanes)],
            send_sem=small_sems.at[2 * kind, peer],
            recv_sem=small_sems.at[2 * kind + 1, source],
            device_id=(peer, tensor),
            device_id_type=MESH,
        )

    def send_small(kind):
        def send(k, carry):
            small_copy(kind, me, (me + k) % count).start()
            return carry

        lax.fori_loop(1, count, send, 0)

    send_small(1)

    def arrived_a1(i, carry):
        a1_in(i).wait()
        ga_in(i).wait()
        return carry

    lax.fori_loop(0, blocks, arrived_a1, 0)

    def weight_grads(c, carry):
        columns = pl.ds(pl.multiple_of(c * BLOCK, BLOCK), BLOCK)
        grads[columns, : 3 * local_width] = dot(wide_ref[:, columns], gqkv_ref[...], 0, 0)
        grads[columns, 3 * local_width :] = dot(ga_ref[:, columns], o_ref[...], 0, 0)
        return carry

    chunks = width // BLOCK
    whole[-2].wait()
    lax.fori_loop(0, chunks // 2, weight_grads, 0)
    rowsum2.cross(1)
    output_block(blocks - 1)
    lax.fori_loop(chunks // 2, chunks, weight_grads, 0)
    side = grads.shape[1] // 2

    def grads_view(way, step):
        return grads[
            place(sent_block(pos, way, step, count)), way * side : (way + 1) * side
        ]

    scatter2 = Scatter(grads_view, stage2, taken2, scatter2_sems, count)
    scatter2.begin()

    def layer_left(i, carry):
        layer.left(i)
        layer.arrived(i)
        return carry

    lax.fori_loop(0, blocks, layer_left, 0)
    result = Put(put_ref, tg_hbm, put2_sems)

    def norm_block(i):
        gn = rowsum2.total(i)
        own_in(i).wait()
        gh2_in(i).wait()
        unit, rate = normalized(own_ref[own_rows(i), :].astype(full_type))
        e = gn * vec_ref[2:3, :]
        inner = e - jnp.mean(e, axis=-1, keepdims=True)
        inner = inner - unit * jnp.mean(e * unit, axis=-1, keepdims=True)
        result.put(i, (gh_ref[own_rows(i), :] + rate * inner).astype(half_type))
        small_mine[2:3, :width] += jnp.sum(gn * unit, axis=0, keepdims=True)
        small_mine[3:4, :width] += jnp.sum(gn, axis=0, keepdims=True)

    def end_step(i, carry):
        @pl.when(i < blocks - 2)
        def _():
            norm_term(i + 2)

        norm_block(i)

        @pl.when(i < blocks - 2)
        def _():
            rowsum2.cross(i + 2)

        for t in range(per):
            hop = i * per + t + 1

            @pl.when(hop < hops)
            def _(hop=hop):
                scatter2.advance(hop)

        return carry

    lax.fori_loop(0, blocks, end_step, 0)
    send_small(0)
    terms_ready(hops)
    for way in range(2):
        for p, scatter in enumerate(scatters):
            dense_ref[way, :, p * part : (p + 1) * part] = scatter.total(way)
        total = scatter2.total(way)
        for k in range(2):
            sum_ref[2 * way + k] = total[:, k * local_width : (k + 1) * local_width]
    for kind in range(2):
        window = pl.ds(pl.multiple_of(me // fold * lanes, lanes), lanes)
        here = slice(lanes, lanes + local_width) if kind else slice(0, lanes)
        small_taken[me, :, here] = small_mine[:, width:] if kind else small_mine[:, window]

        def take(k, carry, kind=kind):
            source = (me + k) % count
            small_copy(kind, source, source).wait_recv()
            return carry

        lax.fori_loop(1, count, take, 0)
    total = small_taken[0]
    for j in range(1, count):
        total = total + small_taken[j]
    small_ref[...] = total
    pair = pltpu.make_async_remote_copy(
        src_ref=small_ref.at[:, pl.ds(0, lanes)],
        dst_ref=small_mate,
        send_sem=mate_sems.at[0],
        recv_sem=mate_sems.at[1],
        device_id=(me, mate),
        device_id_type=MESH,
    )
    pair.start()
    pair.wait()
    small_ref[:, :lanes] = total[:, :lanes] + small_mate[...]

    def result_left(i, carry):
        result.left(i)
        result.arrived(i)
        return carry

    lax.fori_loop(0, blocks, result_left, 0)
    for scatter in scatters + [scatter2]:
        scatter.finish()
    rowsum.finish(given=False)
    rowsum2.finish()
    for kind in range(2):

        def done(k, carry, kind=kind):
            small_copy(kind, me, (me + k) % count).wait_send()
            return carry

        lax.fori_loop(1, count, done, 0)


def permuted(x, owner, back):
    rows, width = x.shape
    count = owner.shape[0]
    order = jnp.argsort(owner) if back else owner
    return jnp.take(x.reshape(rows, count, -1), order, axis=1).reshape(rows, width)


def adamw_step(weight, first, second, grad, rate, decay):
    first_next = first_decay * first + (1.0 - first_decay) * grad
    second_next = second_decay * second + (1.0 - second_decay) * grad * grad
    first_hat = first_next / (1.0 - first_decay**STEP)
    second_hat = second_next / (1.0 - second_decay**STEP)
    update = first_hat / (jnp.sqrt(second_hat) + adam_epsilon) + decay * weight
    return (first_next, second_next, weight - rate * update)


def last_kernel(rates, owner_ref, *refs):
    count = owner_ref.shape[0]
    given, refs = refs[:5], refs[5:]
    layer, grad, weight_sum, dense_sum, small = given
    state, refs = refs[:15], refs[15:]
    results, outs = refs[:2], refs[2:]

    def step(k, grad, at=(Ellipsis,)):
        new = adamw_step(*(ref[at] for ref in state[3 * k : 3 * k + 3]), grad, *rates[k])
        for ref, value in zip(outs[3 * k : 3 * k + 3], new):
            ref[at] = value

    wide = layer.shape[1] // count
    if wide % LANES == 0:
        for j in range(count):
            natural = pl.ds(pl.multiple_of(owner_ref[j] * wide, wide), wide)
            for x, y in zip((layer, grad), results):
                y[:, natural] = x[:, j * wide : (j + 1) * wide]
    else:
        for x, y in zip((layer, grad), results):
            y[...] = x[...]
    step(0, weight_sum[0:3])
    step(1, weight_sum[3])
    ratio, local_width = state[6].shape[2:]
    for r in range(ratio):
        step(
            2,
            dense_sum[:, :, r * local_width : (r + 1) * local_width],
            (slice(None), slice(None), r, slice(None)),
        )
    me = lax.axis_index("dp")
    lanes = small.shape[1] - local_width

    def chosen(x, start, size):
        row = lax.broadcasted_iota(jnp.int32, (x.shape[1], size), 0)
        column = lax.broadcasted_iota(jnp.int32, (x.shape[1], size), 1)
        pick = jnp.where(row == column + start, 1.0, 0.0).astype(half_type)
        return sum(dot(part.astype(half_type), pick) for part in three_parts(x))

    narrow, wide = state[9].shape[1], state[12].shape[1]
    step(3, chosen(small[:, lanes:], owner_ref[me] * narrow, narrow)[: 1 + ratio])
    step(4, chosen(small[:, :lanes], me % (lanes // wide) * wide, wide)[:6])


def last(owner, layer_output, tokens_grad, weight_sum, dense_sum, small_sum, *state):
    steps = 4 if dense_sum.shape[1] % 128 == 0 else 1
    rates = (
        (matrix_rate, matrix_decay),
        (output_rate, matrix_decay),
        (matrix_rate, matrix_decay),
        (bias_rate, 0.0),
        (vector_rate, 0.0),
    )

    def spec(x, dim):
        shape = tuple(n // steps if k == dim else n for k, n in enumerate(x.shape))
        return pl.BlockSpec(shape, lambda i, *_: tuple(i if k == dim else 0 for k in range(x.ndim)))

    dims = [0, 0, 1, 1, None] + [1] * 3 + [0] * 3 + [1] * 3 + [None] * 6
    operands = (layer_output, tokens_grad, weight_sum, dense_sum, small_sum) + state
    specs = [spec(x, dim) for x, dim in zip(operands, dims)]
    outs = operands[:2] + state
    return pl.pallas_call(
        functools.partial(last_kernel, rates),
        out_shape=[jax.ShapeDtypeStruct(x.shape, x.dtype) for x in outs],
        grid_spec=pltpu.PrefetchScalarGridSpec(
            num_scalar_prefetch=1, grid=(steps,), in_specs=specs, out_specs=specs[:2] + specs[5:]
        ),
        compiler_params=pltpu.CompilerParams(vmem_limit_bytes=60 * 2**20),
    )(owner, *operands)


def call(kernel, collective, outs, scratch, operands, spaces, limit=62):
    spec = {
        "s": pl.BlockSpec(memory_space=pltpu.SMEM),
        "v": pl.BlockSpec(memory_space=pltpu.VMEM),
        "h": pl.BlockSpec(memory_space=pl.ANY),
    }
    return pl.pallas_call(
        kernel,
        out_shape=[jax.ShapeDtypeStruct(shape, dtype) for shape, dtype in outs],
        in_specs=[spec[c] for c in spaces[0]],
        out_specs=[spec[c] for c in spaces[1]],
        scratch_shapes=scratch,
        compiler_params=pltpu.CompilerParams(
            collective_id=collective, has_side_effects=True, vmem_limit_bytes=limit * 2**20
        ),
    )(*operands)


def dma(*shape):
    return pltpu.SemaphoreType.DMA(shape)


def local(
    tokens,
    lengths,
    owner,
    attend_master,
    attend_first,
    attend_second,
    output_master,
    output_first,
    output_second,
    dense_master,
    dense_first,
    dense_second,
    bias_master,
    bias_first,
    bias_second,
    vector_master,
    vector_first,
    vector_second,
    cotangent,
):
    count = owner.shape[0]
    rows, width = tokens.shape
    local_width = output_master.shape[1]
    ratio = dense_master.shape[2]
    hidden = ratio * local_width
    heads = local_width // HD
    blocks = rows // BLOCK
    half = BLOCK // 2
    wide = width // count
    lanes = max(LANES, wide)
    tok, cot = tokens, cotangent
    if wide % LANES:
        tok, cot = (permuted(x, owner, False) for x in (tokens, cotangent))
    row_sum = [pltpu.VMEM((blocks, half, width), half_type)] * 3
    two_terms = pltpu.VMEM((2, BLOCK, width), half_type)
    heads_shape = (heads, rows, LANES)
    small = (8, lanes + local_width)
    a1, ga, h2, own, qb, ka, va, o, w, gh2, down, up, dn, goa, kt, vec, gbias, gvec = call(
        functools.partial(front_kernel, count),
        0,
        [
            ((rows, width), half_type),
            ((rows, width), half_type),
            ((rows // 2, width), full_type),
            ((rows // 2, width), half_type),
            (heads_shape, half_type),
            (heads_shape, half_type),
            (heads_shape, half_type),
            ((rows, local_width), half_type),
            ((width, 3 * local_width), half_type),
            ((rows // 2, width), full_type),
            ((rows, width), half_type),
            ((width, hidden), full_type),
            ((width, hidden), full_type),
            (heads_shape, half_type),
            ((local_width, rows), half_type),
            ((8, width), full_type),
            ((8, hidden), full_type),
            ((8, width), full_type),
        ],
        [
            pltpu.VMEM((rows // 2, width), half_type),
            *[pltpu.VMEM(heads_shape, half_type)] * 3,
            pltpu.VMEM((rows, local_width), half_type),
            pltpu.VMEM((width, 3 * local_width), half_type),
            pltpu.VMEM((width, width), half_type),
            pltpu.VMEM((rows // 2, width), full_type),
            pltpu.VMEM((rows, width), half_type),
            *[pltpu.VMEM((rows, hidden), half_type)] * 2,
            pltpu.VMEM((2, BLOCK, hidden), full_type),
            *[pltpu.VMEM((rows, width), half_type)] * 2,
            pltpu.VMEM((2, width, hidden), half_type),
            pltpu.VMEM((rows, width), half_type),
            pltpu.VMEM(heads_shape, half_type),
            pltpu.VMEM((local_width, rows), half_type),
            pltpu.VMEM((8, local_width), full_type),
            pltpu.VMEM((1, hidden), full_type),
            pltpu.VMEM(small, full_type),
            pltpu.VMEM((count,) + small, full_type),
            pltpu.VMEM((blocks, half, width), half_type),
            two_terms,
            *row_sum,
            dma(6, 4, count // 2),
            dma(2, count),
            dma(6, count),
            dma(6, blocks),
            dma(4, blocks),
            dma(2, blocks),
            dma(2, blocks),
            dma(8, blocks),
            dma(7),
            dma(2 * (width // BLOCK)),
        ],
        (
            lengths, owner, tok, cot, attend_master, output_master, dense_master, vector_master,
            bias_master,
        ),
        ("sshhvvvvv", "h" * 15 + "vvv"),
    )
    pieces = 2
    row_blocks = pltpu.VMEM((blocks, half, width), half_type)
    row_slots = pltpu.VMEM((min(3, blocks), half, width), half_type)
    part, side = hidden // pieces, 2 * local_width
    layer_output, tokens_grad, dense_sum, weight_sum, small_sum = call(
        functools.partial(back_kernel, count),
        1,
        [
            ((rows, width), half_type),
            ((rows, width), half_type),
            ((2, wide, hidden), full_type),
            ((4, wide, local_width), full_type),
            ((8, lanes + local_width), full_type),
        ],
        [
            pltpu.VMEM((rows, width), half_type),
            pltpu.VMEM((rows, local_width), half_type),
            *[pltpu.VMEM(heads_shape, half_type)] * 3,
            pltpu.VMEM((width, 3 * local_width), half_type),
            pltpu.VMEM((rows, width), half_type),
            pltpu.VMEM((rows // 2, width), full_type),
            pltpu.VMEM((rows // 2, width), half_type),
            pltpu.VMEM(heads_shape, half_type),
            pltpu.VMEM((local_width, rows), half_type),
            pltpu.VMEM((local_width, rows), full_type),
            pltpu.VMEM((rows, 3 * local_width), half_type),
            pltpu.VMEM((rows // 2, width), half_type),
            row_blocks,
            row_slots,
            row_blocks,
            two_terms,
            row_blocks,
            row_slots,
            row_blocks,
            pltpu.VMEM((2, 2, wide, hidden), full_type),
            pltpu.VMEM((pieces, 2, 2, wide, part), half_type),
            pltpu.VMEM((pieces, 2, count - 1, wide, part), half_type),
            pltpu.VMEM((width, 4 * local_width), full_type),
            pltpu.VMEM((2, 2, wide, side), half_type),
            pltpu.VMEM((2, count - 1, wide, side), half_type),
            pltpu.VMEM((8, width + local_width), full_type),
            pltpu.VMEM((count, 8, lanes + local_width), full_type),
            pltpu.VMEM((8, lanes), full_type),
            dma(4, blocks),
            dma(4, blocks),
            dma(3, blocks),
            dma(3, blocks),
            dma(pieces, 4, count - 1),
            dma(4, count - 1),
            dma(4, count),
            dma(2),
            dma(6, blocks),
            dma(2, 2),
            dma(7),
        ],
        (ga, o, qb, ka, va, goa, kt, w, up, dn, down, h2, gh2, own, a1, vec, gbias, gvec),
        ("h" * 15 + "vvv", "hhvvv"),
    )
    if wide % LANES:
        layer_output, tokens_grad = (permuted(x, owner, True) for x in (layer_output, tokens_grad))
    return tuple(
        last(
            owner, layer_output, tokens_grad, weight_sum, dense_sum, small_sum,
            attend_master, attend_first, attend_second,
            output_master, output_first, output_second,
            dense_master, dense_first, dense_second,
            bias_master, bias_first, bias_second,
            vector_master, vector_first, vector_second,
        )
    )


def solution(mesh):
    return jax.shard_map(
        local,
        mesh=mesh,
        in_specs=(
            P("dp", None),
            P("dp", None),
            P(),
            P(None, "dp", "tensor"),
            P(None, "dp", "tensor"),
            P(None, "dp", "tensor"),
            P("dp", "tensor"),
            P("dp", "tensor"),
            P("dp", "tensor"),
            P(None, "dp", None, "tensor"),
            P(None, "dp", None, "tensor"),
            P(None, "dp", None, "tensor"),
            P(None, ("tensor", "dp")),
            P(None, ("tensor", "dp")),
            P(None, ("tensor", "dp")),
            P(None, "dp"),
            P(None, "dp"),
            P(None, "dp"),
            P("dp", None),
        ),
        out_specs=(
            P("dp", None),
            P("dp", None),
            P(None, "dp", "tensor"),
            P(None, "dp", "tensor"),
            P(None, "dp", "tensor"),
            P("dp", "tensor"),
            P("dp", "tensor"),
            P("dp", "tensor"),
            P(None, "dp", None, "tensor"),
            P(None, "dp", None, "tensor"),
            P(None, "dp", None, "tensor"),
            P(None, ("tensor", "dp")),
            P(None, ("tensor", "dp")),
            P(None, ("tensor", "dp")),
            P(None, "dp"),
            P(None, "dp"),
            P(None, "dp"),
        ),
        check_vma=False,
    )
```

```python
import functools

import jax
import jax.numpy as jnp
from jax import lax
from jax.experimental import pallas as pl
from jax.experimental.pallas import tpu as pltpu
from jax.sharding import PartitionSpec as P

HD = 64
STEP = 10
LANES = 128
BLOCK = 256
MESH = pl.DeviceIdType.MESH
BIG = 2.0**50

norm_epsilon = 1e-06
first_decay = 0.9
second_decay = 0.95
adam_epsilon = 1e-08
matrix_rate = 0.1
output_rate = 0.5
bias_rate = 0.5
vector_rate = 1.0
matrix_decay = 0.05

half_type = jnp.bfloat16
full_type = jnp.float32


def dot(left, right, left_dim=1, right_dim=0):
    return lax.dot_general(
        left, right, (((left_dim,), (right_dim,)), ((), ())), preferred_element_type=full_type
    )


def ring_pos(place, count):
    column = place % 2
    row = place // 2
    return row * (1 - column) + (count - 1 - row) * column


def ring_at(pos, count):
    near = (pos + 2 * count) % count
    down = near // (count // 2)
    return 2 * near * (1 - down) + (2 * count - 1 - 2 * near) * down


def normalized(x):
    center = jnp.mean(x, axis=-1, keepdims=True)
    offset = x - center
    spread = jnp.mean(offset * offset, axis=-1, keepdims=True)
    rate = lax.rsqrt(spread + norm_epsilon)
    return offset * rate, rate


class Gather:
    def __init__(self, view, width, sems, count):
        self.view, self.width, self.sems, self.count = view, width, sems, count
        self.steps = count // 2
        self.pos = ring_pos(lax.axis_index("dp"), count)
        self.tensor = lax.axis_index("tensor")

    def _copy(self, way, step, hops):
        sign = 1 - 2 * way
        part = (0, self.width)
        if step == self.steps - 1:
            part = (way * (self.width // 2), self.width // 2)
        block = self.view(ring_at(self.pos - sign * hops, self.count), *part)
        return pltpu.make_async_remote_copy(
            src_ref=block,
            dst_ref=block,
            send_sem=self.sems.at[2 * way, step],
            recv_sem=self.sems.at[2 * way + 1, step],
            device_id=(ring_at(self.pos + sign, self.count), self.tensor),
            device_id_type=MESH,
        )

    def advance(self, step):
        if step:
            for way in range(2):
                self._copy(way, step - 1, step).wait_recv()
        if step < self.steps:
            for way in range(2):
                self._copy(way, step, step).start()

    def sent(self):
        for step in range(self.steps):
            for way in range(2):
                self._copy(way, step, step).wait_send()


class RowSum:
    def __init__(self, term, given, sent, crossed, sems):
        self.term, self.given, self.sent_ref, self.crossed = term, given, sent, crossed
        self.slots, self.sent_slots, self.blocks = term.shape[0], sent.shape[0], given.shape[0]
        self.sems = sems
        self.half = given.shape[1]
        self.dp, tensor = lax.axis_index("dp"), lax.axis_index("tensor")
        self.core = tensor % 2
        self.mate = tensor - tensor % 2 + (tensor + 1) % 2
        self.other = (tensor + 2) % 4

    def rows(self, core):
        return pl.ds(pl.multiple_of(core * self.half, self.half), self.half)

    def _give(self, i):
        return pltpu.make_async_remote_copy(
            src_ref=self.term.at[i % self.slots, self.rows(1 - self.core), :],
            dst_ref=self.given.at[i],
            send_sem=self.sems.at[0, i],
            recv_sem=self.sems.at[1, i],
            device_id=(self.dp, self.mate),
            device_id_type=MESH,
        )

    def _cross(self, i):
        return pltpu.make_async_remote_copy(
            src_ref=self.sent_ref.at[i % self.sent_slots],
            dst_ref=self.crossed.at[i],
            send_sem=self.sems.at[2, i],
            recv_sem=self.sems.at[3, i],
            device_id=(self.dp, self.other),
            device_id_type=MESH,
        )

    def free(self, i):
        if self.slots < self.blocks:

            @pl.when(i >= self.slots)
            def _():
                self._give(i - self.slots).wait_send()

    def give(self, i):
        self._give(i).start()

    def cross(self, i):
        self._give(i).wait_recv()
        mine = self.term[i % self.slots, self.rows(self.core), :].astype(full_type)
        if self.sent_slots < self.blocks:

            @pl.when(i >= self.sent_slots)
            def _():
                self._cross(i - self.sent_slots).wait_send()

        total = mine + self.given[i].astype(full_type)
        self.sent_ref[i % self.sent_slots] = total.astype(half_type)
        self._cross(i).start()

    def total(self, i):
        self._cross(i).wait_recv()
        mine = self.sent_ref[i % self.sent_slots].astype(full_type)
        return mine + self.crossed[i].astype(full_type)

    def gone(self):
        def given(i, carry):
            self._give(i).wait_send()
            return carry

        lax.fori_loop(max(self.blocks - self.slots, 0), self.blocks, given, 0)

    def finish(self, given=True):
        if given:
            self.gone()

        def crossed(i, carry):
            self._cross(i).wait_send()
            return carry

        lax.fori_loop(max(self.blocks - self.sent_slots, 0), self.blocks, crossed, 0)


class Share:
    def __init__(self, ref, sems):
        self.ref, self.sems = ref, sems
        self.dp, tensor = lax.axis_index("dp"), lax.axis_index("tensor")
        self.core = tensor % 2
        self.mate = tensor - tensor % 2 + (tensor + 1) % 2

    def rows(self, i, core):
        half = BLOCK // 2
        return pl.ds(pl.multiple_of(i * BLOCK + core * half, half), half)

    def _copy(self, i, core):
        piece = self.ref.at[self.rows(i, core), :]
        return pltpu.make_async_remote_copy(
            src_ref=piece,
            dst_ref=piece,
            send_sem=self.sems.at[0, i],
            recv_sem=self.sems.at[1, i],
            device_id=(self.dp, self.mate),
            device_id_type=MESH,
        )

    def put(self, i, value):
        self.ref[self.rows(i, self.core), :] = value
        self._copy(i, self.core).start()

    def arrived(self, i):
        self._copy(i, 1 - self.core).wait_recv()

    def finish(self, blocks):
        def done(i, carry):
            self._copy(i, self.core).wait_send()
            return carry

        lax.fori_loop(0, blocks, done, 0)


def greet(peers):
    barrier = pltpu.get_barrier_semaphore()
    for peer in peers:
        pl.semaphore_signal(barrier, inc=1, device_id=peer, device_id_type=MESH)
    return lambda: pl.semaphore_wait(barrier, len(peers))


def tensor_peers():
    dp, tensor = lax.axis_index("dp"), lax.axis_index("tensor")
    return [(dp, tensor - tensor % 2 + (tensor + 1) % 2), (dp, (tensor + 2) % 4)]


def ring_peers(count):
    dp, tensor = lax.axis_index("dp"), lax.axis_index("tensor")
    pos = ring_pos(dp, count)
    return [(ring_at(pos + 1, count), tensor), (ring_at(pos - 1, count), tensor)]


def dp_peers(count):
    dp, tensor = lax.axis_index("dp"), lax.axis_index("tensor")
    return [((dp + k) % count, tensor) for k in range(1, count)]


def three_parts(x):
    high = x.astype(half_type).astype(full_type)
    middle = (x - high).astype(half_type).astype(full_type)
    return high, middle, x - high - middle


def gelu_parts(z):
    phi = 0.5 + 0.5 * lax.erf(z * (0.5**0.5))
    slope = phi + z * (jnp.exp(-0.5 * z * z) * (2.0 * 3.141592653589793) ** -0.5)
    return z * phi, slope


def fetch(source, target, sems):
    def copy(i):
        rows = pl.ds(pl.multiple_of(i * BLOCK, BLOCK), BLOCK)
        return pltpu.make_async_copy(source.at[rows, :], target.at[rows, :], sems.at[i])

    return copy


def stored_order(x, owner_ref):
    count = owner_ref.shape[0]
    wide = x.shape[1] // count
    if wide % LANES:
        return x
    parts = []
    for j in range(count):
        total = None
        for n in range(count):
            term = x[:, n * wide : (n + 1) * wide] * jnp.where(owner_ref[j] == n, 1.0, 0.0)
            total = term if total is None else total + term
        parts.append(total)
    return jnp.concatenate(parts, axis=1)


def front_kernel(
    count, len_ref, owner_ref, tok_hbm, cot_hbm, att_ref, out_ref, dense_ref, vector_ref, split_ref,
    a1_hbm, ga_hbm, h2_hbm, own_hbm, qa_hbm, ka_hbm, va_hbm, o_hbm, w_hbm, gh2_hbm, down_hbm,
    up_hbm, dn_hbm, goa_hbm, kt_hbm, vec_ref, gbias_ref, gvec_ref,
    own_ref, qa_ref, ka_ref, va_ref, o_ref, w_ref, wo_ref, gh2_ref, down_ref, ul_ref, gz_ref, made,
    norm_ref, cot_ref, wd_ref, ga_ref, goa_ref, kt_ref, bias_ref, b1_ref, small_ref, smalls,
    mixed_ref, term2, given2, sent2, crossed2,
    gather_sems, small_sems, spread_sems, mixed_sems, sum2_sems, share_sems, put_sems, local_sems,
    whole_sems, made_sems,
):
    me, tensor = lax.axis_index("dp"), lax.axis_index("tensor")
    total_rows, width = norm_ref.shape
    local_width = out_ref.shape[1]
    ratio = dense_ref.shape[2]
    wide = width // count
    slots = len_ref.shape[1]
    heads = local_width // HD
    blocks = total_rows // BLOCK
    half = BLOCK // 2
    lanes = small_ref.shape[1] - local_width
    fold = lanes // wide
    steps = count // 2
    core = tensor % 2
    mate = tensor - core + 1 - core
    other, across = (tensor + 2) % 4, (mate + 2) % 4

    greeted = greet(tensor_peers() + [(me, across)] + dp_peers(count))
    tokens_in = fetch(tok_hbm, norm_ref, local_sems.at[0])
    cot_in = fetch(cot_hbm, cot_ref, local_sems.at[1])
    a1_out = fetch(norm_ref, a1_hbm, local_sems.at[2])
    for i in range(blocks):
        tokens_in(i).start()
    for i in range(blocks):
        cot_in(i).start()
    mine = pl.ds(pl.multiple_of(me * wide, wide), wide)
    for row in range(3):
        w_ref[mine, row * local_width : (row + 1) * local_width] = att_ref[row].astype(half_type)

    def columns_of(index, low=0, size=local_width):
        return pl.ds(pl.multiple_of(index * local_width + low, LANES), size)

    wo_ref[mine, columns_of(tensor)] = out_ref[...].astype(half_type)

    small_ref[...] = jnp.zeros_like(small_ref)
    vectors = vector_ref[...].astype(half_type)
    if fold == 1:
        small_ref[0:6, :lanes] = vectors.astype(full_type)
    else:
        row = lax.broadcasted_iota(jnp.int32, (wide, lanes), 0)
        column = lax.broadcasted_iota(jnp.int32, (wide, lanes), 1)
        spread = jnp.where(column == row + me % fold * wide, 1.0, 0.0).astype(half_type)
        small_ref[0:6, :lanes] = dot(vectors, spread)
    narrow = split_ref.shape[1]
    row = lax.broadcasted_iota(jnp.int32, (narrow, local_width), 0)
    column = lax.broadcasted_iota(jnp.int32, (narrow, local_width), 1)
    spread = jnp.where(column == row + owner_ref[me] * narrow, 1.0, 0.0).astype(half_type)
    small_ref[0 : 1 + ratio, lanes:] = dot(split_ref[...].astype(half_type), spread)
    smalls[me] = small_ref[...]
    greeted()

    def place(block):
        return pl.ds(pl.multiple_of(block * wide, wide), wide)

    def small_copy(source, peer):
        return pltpu.make_async_remote_copy(
            src_ref=small_ref,
            dst_ref=smalls.at[source],
            send_sem=small_sems.at[0, peer],
            recv_sem=small_sems.at[1, source],
            device_id=(peer, tensor),
            device_id_type=MESH,
        )

    def send_small(k, carry):
        small_copy(me, (me + k) % count).start()
        return carry

    lax.fori_loop(1, count, send_small, 0)

    def attend_view(row):
        return lambda block, low, size: w_ref.at[
            place(block), pl.ds(row * local_width + low, size)
        ]

    def dense_view(row):
        return lambda block, low, size: wd_ref.at[row, place(block), pl.ds(low, size)]

    attend = [Gather(attend_view(row), local_width, gather_sems.at[row], count) for row in range(3)]
    attend.append(
        Gather(
            lambda block, low, size: wo_ref.at[place(block), columns_of(tensor, low, size)],
            local_width, gather_sems.at[3], count,
        )
    )
    dense = [
        Gather(dense_view(row), ratio * local_width, gather_sems.at[4 + row], count)
        for row in range(2)
    ]
    for piece in attend:
        piece.advance(0)

    def spread(kind, block, source, target):
        piece = wo_ref.at[place(block), columns_of(source)]
        return pltpu.make_async_remote_copy(
            src_ref=piece,
            dst_ref=piece,
            send_sem=spread_sems.at[2 * kind, block],
            recv_sem=spread_sems.at[2 * kind + 1, block],
            device_id=(me, target),
            device_id_type=MESH,
        )

    def spread_step(step):
        pos = attend[3].pos
        hops = {0: [0], steps: [steps]}.get(step, [step, -step])
        for hop in hops:
            block = ring_at(pos - hop, count)
            spread(0, block, tensor, mate).start()
            spread(1, block, tensor, other).start()

    spread_step(0)
    for row in range(2):
        for r in range(ratio):
            wd_ref[row, mine, r * local_width : (r + 1) * local_width] = dense_ref[
                row, :, r, :
            ].astype(half_type)

    def take_small(k, carry):
        source = (me + k) % count
        small_copy(source, source).wait_recv()
        return carry

    lax.fori_loop(1, count, take_small, 0)
    bias = smalls[0, :, lanes:]
    for j in range(1, count):
        bias = bias + smalls[j, :, lanes:]
    bias_ref[...] = bias
    for r in range(ratio):
        b1_ref[:, r * local_width : (r + 1) * local_width] = bias[1 + r : 2 + r, :]
    for window in range(width // lanes):
        piece = smalls[window * fold, :, :lanes]
        for j in range(window * fold + 1, (window + 1) * fold):
            piece = piece + smalls[j, :, :lanes]
        vec_ref[:, window * lanes : (window + 1) * lanes] = piece

    def norm_rows(i, carry):
        tokens_in(i).wait()
        rows = pl.ds(pl.multiple_of(i * BLOCK, BLOCK), BLOCK)
        x = stored_order(norm_ref[rows, :].astype(full_type), owner_ref)
        norm_ref[rows, :] = x.astype(half_type)
        here = pl.ds(pl.multiple_of(i * BLOCK + core * half, half), half)
        own_ref[pl.ds(pl.multiple_of(i * half, half), half), :] = norm_ref[here, :]
        unit, _ = normalized(x)
        norm_ref[rows, :] = (unit * vec_ref[2:3, :] + vec_ref[3:4, :]).astype(half_type)
        a1_out(i).start()
        cot_in(i).wait()
        cot_ref[rows, :] = stored_order(cot_ref[rows, :].astype(full_type), owner_ref).astype(
            half_type
        )
        return carry

    done = 0
    for step in range(1, steps + 1):
        for piece in attend:
            piece.advance(step)
        spread_step(step)
        if step == steps - 1:
            for piece in dense:
                piece.advance(0)
        upto = min(blocks, -(-blocks * step // (steps - 1)))
        if upto > done:
            lax.fori_loop(done, upto, norm_rows, 0)
        done = max(done, upto)

    pumps = [(piece, step) for step in range(1, steps + 1) for piece in dense]

    def pump(slot):
        for k, (piece, step) in enumerate(pumps):
            if min(blocks + 1, (13 * k + 2) // 10 * 8 // len(pumps)) == slot:
                piece.advance(step)

    lane = lax.broadcasted_iota(jnp.int32, (BLOCK, LANES), 1)
    low_half = lane < HD
    spot = lane % HD

    def project(i, carry):
        row = pl.multiple_of(i * BLOCK, BLOCK)
        rows = pl.ds(row, BLOCK)
        a1 = norm_ref[rows, :]
        qkv = dot(a1, w_ref[...])
        q, k, v = (qkv[:, part * local_width : (part + 1) * local_width] for part in range(3))
        q = (q + bias_ref[0:1, :]).astype(half_type).astype(full_type) * HD**-0.5
        index = row + lax.broadcasted_iota(jnp.int32, (BLOCK, LANES), 0)
        segment = jnp.zeros((BLOCK, LANES), jnp.int32)
        end = 0
        for slot in range(slots):
            end = end + len_ref[0, slot]
            segment = segment + jnp.where(index >= end, 1, 0)
        same = spot == segment
        inside = spot <= slots
        q_mark = jnp.where(inside & ~same, -BIG, 0.0)
        k_mark = jnp.where(same, BIG, jnp.where((spot > slots) & (spot <= slots + 3), 1.0, 0.0))
        for head in range(heads):
            pair = slice(head // 2 * LANES, head // 2 * LANES + LANES)
            own = low_half if head % 2 == 0 else ~low_half
            qa_ref[head, rows, :] = jnp.where(own, q[:, pair], q_mark).astype(half_type)
            ka_ref[head, rows, :] = jnp.where(own, k[:, pair], k_mark).astype(half_type)
            va_ref[head, rows, :] = jnp.where(own, v[:, pair], 1.0).astype(half_type)
        return carry

    lax.fori_loop(0, blocks, project, 0)
    pump(0)

    def forward(block, carry):
        spread(1, block, other, other).wait_recv()
        spread(2, block, other, mate).start()
        return carry

    lax.fori_loop(0, count, forward, 0)

    def a1_left(i, carry):
        a1_out(i).wait()
        return carry

    lax.fori_loop(0, blocks, a1_left, 0)
    gbias_ref[...] = jnp.zeros_like(gbias_ref)
    gvec_ref[...] = jnp.zeros_like(gvec_ref)

    share = Share(norm_ref, share_sems)

    def mixed_copy(kind, i, source, target, half_rows):
        rows = pl.ds(pl.multiple_of(i * BLOCK + half_rows * half, half), half)
        return pltpu.make_async_remote_copy(
            src_ref=o_ref.at[rows, :],
            dst_ref=mixed_ref.at[i, :, columns_of(source)],
            send_sem=mixed_sems.at[2 * kind, i],
            recv_sem=mixed_sems.at[2 * kind + 1, i],
            device_id=(me, target),
            device_id_type=MESH,
        )

    peers = ((0, mate, 1 - core), (1, other, core), (2, across, 1 - core))

    def h2_out(i):
        own = pl.ds(pl.multiple_of(i * half, half), half)
        return pltpu.make_async_copy(gh2_ref.at[own, :], h2_hbm.at[own, :], local_sems.at[3, i])

    def attend_block(i):
        rows = pl.ds(pl.multiple_of(i * BLOCK, BLOCK), BLOCK)
        for head in range(heads):
            query = qa_ref[head, rows, :]
            scores = dot(query, ka_ref[head], 1, 1)
            top = jnp.max(scores, axis=1, keepdims=True)
            weights = jnp.exp(scores - top).astype(half_type)
            mixed = dot(weights, va_ref[head])
            turned = pltpu.roll(mixed, HD, 1)
            own = low_half if head % 2 == 0 else ~low_half
            log_total = three_parts(top + jnp.log(jnp.where(own, turned, mixed)))
            marked = query.astype(full_type)
            for part in range(3):
                marked = jnp.where(~own & (spot == slots + 1 + part), -log_total[part], marked)
            qa_ref[head, rows, :] = marked.astype(half_type)
            out = mixed / turned
            if head % 2 == 0:
                before = out
            else:
                pair = slice(head // 2 * LANES, head // 2 * LANES + LANES)
                o_ref[rows, pair] = jnp.where(low_half, before, out).astype(half_type)
        for kind, peer, half_rows in peers[1:] + peers[:1]:
            mixed_copy(kind, i, tensor, peer, half_rows).start()
        here = pl.ds(pl.multiple_of(i * BLOCK + core * half, half), half)
        mixed_ref[i, :, columns_of(tensor)] = o_ref[here, :]

    def norm_block(i):
        own = pl.ds(pl.multiple_of(i * half, half), half)
        for kind, peer, _ in peers:
            mixed_copy(kind, i, peer, peer, 0).wait_recv()
        attn = dot(mixed_ref[i], wo_ref[...], 1, 1)
        hidden = own_ref[own, :].astype(full_type) + attn + vec_ref[0:1, :]
        gh2_ref[own, :] = hidden
        h2_out(i).start()
        unit, _ = normalized(hidden)
        share.put(i, (unit * vec_ref[4:5, :] + vec_ref[5:6, :]).astype(half_type))

    behind = min(2, blocks)

    def attend_step(i, carry):
        attend_block(i)
        for slot in range(1, blocks + 1):

            @pl.when(i == slot - 1)
            def _(slot=slot):
                pump(slot)

        @pl.when(i == behind)
        def _():
            def spread_in(block, carry):
                spread(0, block, mate, mate).wait_recv()
                spread(2, block, across, mate).wait_recv()
                return carry

            lax.fori_loop(0, count, spread_in, 0)

        @pl.when(i >= behind)
        def _():
            norm_block(i - behind)

        return carry

    lax.fori_loop(0, blocks, attend_step, 0)

    def norm_step(i, carry):
        norm_block(i)
        return carry

    lax.fori_loop(blocks - behind, blocks, norm_step, 0)
    pump(blocks + 1)

    whole = [
        pltpu.make_async_copy(source, target, whole_sems.at[k])
        for k, (source, target) in enumerate(
            (
                (own_ref, own_hbm), (qa_ref, qa_hbm), (ka_ref, ka_hbm), (va_ref, va_hbm),
                (o_ref, o_hbm), (w_ref, w_hbm),
            )
        )
    ]
    for copy in whole:
        copy.start()
    down_out = fetch(down_ref, down_hbm, local_sems.at[5])

    def gh2_out(i):
        own = pl.ds(pl.multiple_of(i * half, half), half)
        return pltpu.make_async_copy(gh2_ref.at[own, :], gh2_hbm.at[own, :], local_sems.at[6, i])

    rowsum2 = RowSum(term2, given2, sent2, crossed2, sum2_sems)

    share2 = Share(ga_ref, put_sems)
    ga_out = fetch(ga_ref, ga_hbm, local_sems.at[4])

    def goa_out(i):
        rows = pl.ds(pl.multiple_of(i * BLOCK, BLOCK), BLOCK)
        return pltpu.make_async_copy(
            goa_ref.at[:, rows, :], goa_hbm.at[:, rows, :], local_sems.at[7, i]
        )

    def prepare(i):
        share2.arrived(i)
        ga_out(i).start()
        rows = pl.ds(pl.multiple_of(i * BLOCK, BLOCK), BLOCK)
        go = dot(ga_ref[rows, :], wo_ref[:, columns_of(tensor)]).astype(half_type).astype(full_type)
        both = go * o_ref[rows, :].astype(full_type)
        for head in range(heads):
            pair = slice(head // 2 * LANES, head // 2 * LANES + LANES)
            own = low_half if head % 2 == 0 else ~low_half
            inner = jnp.sum(jnp.where(own, both[:, pair], 0.0), axis=1, keepdims=True)
            filled = jnp.where(own, go[:, pair], 0.0)
            for k, value in enumerate(three_parts(inner)):
                filled = jnp.where(~own & (spot == k), -value, filled)
            goa_ref[head, rows, :] = filled.astype(half_type)
            if head % 2 == 0:
                before = ka_ref[head, rows, :].astype(full_type)
            else:
                k = jnp.where(low_half, before, ka_ref[head, rows, :].astype(full_type))
                kt_ref[pair, rows] = k.T.astype(half_type)
        goa_out(i).start()

    def mlp_block(i):
        rows = pl.ds(pl.multiple_of(i * BLOCK, BLOCK), BLOCK)
        share.arrived(i)
        a2 = norm_ref[rows, :]
        gy = cot_ref[rows, :]
        u, slope = gelu_parts(dot(a2, wd_ref[0]) + b1_ref[...])
        ul = u.astype(half_type)
        gz = (dot(gy, wd_ref[1]) * slope).astype(half_type)
        rowsum2.free(i)
        term2[i % term2.shape[0]] = dot(gz, wd_ref[0], 1, 1).astype(half_type)
        rowsum2.give(i)
        gbias_ref[0:1, :] += jnp.sum(gz.astype(full_type), axis=0, keepdims=True)
        ul_ref[rows, :] = ul
        gz_ref[rows, :] = gz
        down_ref[rows, :] = dot(ul, wd_ref[1], 1, 1).astype(half_type)
        down_out(i).start()
        rowsum2.cross(i)

    chunks = width // BLOCK

    def made_out(kind, c):
        rows = pl.ds(pl.multiple_of(c * BLOCK, BLOCK), BLOCK)
        target = (up_hbm, dn_hbm)[kind].at[rows, :]
        return pltpu.make_async_copy(made.at[kind], target, made_sems.at[kind, c])

    def weight_grads(c):
        columns = pl.ds(pl.multiple_of(c * BLOCK, BLOCK), BLOCK)
        for kind, (left, right) in enumerate(((norm_ref, gz_ref), (cot_ref, ul_ref))):

            @pl.when(c >= 1)
            def _(kind=kind):
                made_out(kind, c - 1).wait()

            made[kind] = dot(left[:, columns], right[...], 0, 0)
            made_out(kind, c).start()

    def back_block(i):
        own = pl.ds(pl.multiple_of(i * half, half), half)
        gn = rowsum2.total(i)
        h2_out(i).wait()
        unit, rate = normalized(gh2_ref[own, :])
        e = gn * vec_ref[4:5, :]
        inner = e - jnp.mean(e, axis=-1, keepdims=True)
        inner = inner - unit * jnp.mean(e * unit, axis=-1, keepdims=True)
        gy = cot_ref[share.rows(i, core), :].astype(full_type)
        gh = gy + rate * inner
        gh2_ref[own, :] = gh
        gh2_out(i).start()
        share2.put(i, gh.astype(half_type))
        gvec_ref[0:1, :] += jnp.sum(gh, axis=0, keepdims=True)
        gvec_ref[1:2, :] += jnp.sum(gy, axis=0, keepdims=True)
        gvec_ref[4:5, :] += jnp.sum(gn * unit, axis=0, keepdims=True)
        gvec_ref[5:6, :] += jnp.sum(gn, axis=0, keepdims=True)

    def mlp_step(i, carry):
        mlp_block(i)
        return carry

    lax.fori_loop(0, blocks, mlp_step, 0)
    late = max(blocks + 2, chunks)

    def tail_step(i, carry):
        @pl.when(i < blocks)
        def _():
            back_block(i)

        @pl.when((i >= 2) & (i < blocks + 2))
        def _():
            prepare(i - 2)

        @pl.when(i < chunks)
        def _():
            weight_grads(i)

        return carry

    lax.fori_loop(0, late, tail_step, 0)
    kt_out = pltpu.make_async_copy(kt_ref, kt_hbm, whole_sems.at[len(whole)])
    kt_out.start()
    for kind in range(2):
        made_out(kind, chunks - 1).wait()

    def copied(i, carry):
        down_out(i).wait()
        gh2_out(i).wait()
        ga_out(i).wait()
        goa_out(i).wait()
        return carry

    lax.fori_loop(0, blocks, copied, 0)
    for copy in whole + [kt_out]:
        copy.wait()
    for piece in attend + dense:
        piece.sent()
    rowsum2.finish()
    share.finish(blocks)
    share2.finish(blocks)

    def spread_out(block, carry):
        spread(0, block, tensor, mate).wait_send()
        spread(1, block, tensor, other).wait_send()
        spread(2, block, other, mate).wait_send()
        return carry

    lax.fori_loop(0, count, spread_out, 0)

    def mixed_out(i, carry):
        for kind, peer, half_rows in peers:
            mixed_copy(kind, i, tensor, peer, half_rows).wait_send()
        return carry

    lax.fori_loop(0, blocks, mixed_out, 0)

    def sent_small(k, carry):
        small_copy(me, (me + k) % count).wait_send()
        return carry

    lax.fori_loop(1, count, sent_small, 0)


class Scatter:
    def __init__(self, view, stage, taken, sems, count):
        self.view, self.stage, self.taken = view, stage, taken
        self.sems, self.count = sems, count
        self.slots = stage.shape[1]
        self.pos = ring_pos(lax.axis_index("dp"), count)
        self.tensor = lax.axis_index("tensor")

    def _copy(self, way, step):
        sign = 1 - 2 * way
        return pltpu.make_async_remote_copy(
            src_ref=self.stage.at[way, step % self.slots],
            dst_ref=self.taken.at[way, step],
            send_sem=self.sems.at[2 * way, step],
            recv_sem=self.sems.at[2 * way + 1, step],
            device_id=(ring_at(self.pos + sign, self.count), self.tensor),
            device_id_type=MESH,
        )

    def begin(self):
        for way in range(2):
            self.stage[way, 0] = self.view(way, 0).astype(half_type)
            self._copy(way, 0).start()

    def advance(self, step):
        for way in range(2):
            self._copy(way, step - 1).wait_recv()
            total = self.taken[way, step - 1].astype(full_type) + self.view(way, step)

            @pl.when(step >= self.slots)
            def _(way=way):
                self._copy(way, step - self.slots).wait_send()

            self.stage[way, step % self.slots] = total.astype(half_type)
            self._copy(way, step).start()

    def total(self, way):
        last = self.count - 2
        self._copy(way, last).wait_recv()
        return self.taken[way, last].astype(full_type) + self.view(way, last + 1)

    def finish(self):
        for step in range(max(self.count - 1 - self.slots, 0), self.count - 1):
            for way in range(2):
                self._copy(way, step).wait_send()


def sent_block(pos, way, step, count):
    return ring_at(pos - (1 - 2 * way) * (1 + step), count)


class Put:
    def __init__(self, held, result, sems):
        self.held, self.result, self.sems = held, result, sems
        self.half = held.shape[0] // sems.shape[1]
        self.dp, tensor = lax.axis_index("dp"), lax.axis_index("tensor")
        self.core = tensor % 2
        self.mate = tensor - tensor % 2 + (tensor + 1) % 2

    def own(self, i):
        return pl.ds(pl.multiple_of(i * self.half, self.half), self.half)

    def _rows(self, i, core):
        return pl.ds(pl.multiple_of((2 * i + core) * self.half, self.half), self.half)

    def _here(self, i):
        target = self.result.at[self._rows(i, self.core), :]
        return pltpu.make_async_copy(self.held.at[self.own(i), :], target, self.sems.at[0, i])

    def _there(self, i, core):
        return pltpu.make_async_remote_copy(
            src_ref=self.held.at[self.own(i), :],
            dst_ref=self.result.at[self._rows(i, core), :],
            send_sem=self.sems.at[1, i],
            recv_sem=self.sems.at[2, i],
            device_id=(self.dp, self.mate),
            device_id_type=MESH,
        )

    def put(self, i, value):
        self.held[self.own(i), :] = value
        self._here(i).start()
        self._there(i, self.core).start()

    def left(self, i):
        self._here(i).wait()
        self._there(i, self.core).wait_send()

    def arrived(self, i):
        self._there(i, 1 - self.core).wait_recv()


def back_kernel(
    count, ga_hbm, o_hbm, qb_hbm, ka_hbm, va_hbm, goa_hbm, kt_hbm, w_hbm, up_hbm, dn_hbm, down_hbm,
    h2_hbm, gh2_hbm, own_hbm, a1_hbm, vec_ref, gbias_ref, gvec_ref,
    layer_hbm, tg_hbm, dense_ref, sum_ref, small_ref,
    ga_ref, o_ref, qb_ref, ka_ref, va_ref, w_ref, wide_ref, gh_ref, own_ref, goa_ref, kt_ref, gqt_ref, gqkv_ref, put_ref,
    given, sent, crossed, term2, given2, sent2, crossed2,
    terms, stage, taken, grads, stage2, taken2, small_mine, small_taken, small_mate,
    sum_sems, sum2_sems, put_sems, put2_sems, scatter_sems, scatter2_sems, small_sems, mate_sems,
    local_sems, terms_sems, whole_sems,
):
    total_rows, width = ga_ref.shape
    local_width = o_ref.shape[1]
    heads = local_width // HD
    blocks = total_rows // BLOCK
    half = BLOCK // 2
    wide = width // count
    hops = count - 1
    lanes = small_ref.shape[1] - local_width
    fold = lanes // wide
    me, tensor = lax.axis_index("dp"), lax.axis_index("tensor")
    mate = tensor - tensor % 2 + (tensor + 1) % 2
    pos = ring_pos(me, count)
    greeted = greet(tensor_peers() + dp_peers(count))

    def own_rows(i):
        return pl.ds(pl.multiple_of(i * half, half), half)

    def place(block):
        return pl.ds(pl.multiple_of(block * wide, wide), wide)

    def own_fetch(source, target, sems):
        return lambda i: pltpu.make_async_copy(
            source.at[own_rows(i), :], target.at[own_rows(i), :], sems.at[i]
        )

    ga_in = fetch(ga_hbm, ga_ref, local_sems.at[0])
    down_in = fetch(down_hbm, wide_ref, local_sems.at[1])
    a1_in = fetch(a1_hbm, wide_ref, local_sems.at[2])
    h2_in = own_fetch(h2_hbm, gh_ref, local_sems.at[3])
    gh2_in = own_fetch(gh2_hbm, gh_ref, local_sems.at[4])
    own_in = own_fetch(own_hbm, own_ref, local_sems.at[5])

    def term_in(way, step):
        rows = place(sent_block(pos, way, step, count))
        source = (up_hbm, dn_hbm)[way].at[rows, :]
        return pltpu.make_async_copy(
            source, terms.at[way, step % 2], terms_sems.at[way, step % 2]
        )

    def each(copy):
        def start(i, carry):
            copy(i).start()
            return carry

        lax.fori_loop(0, blocks, start, 0)

    for step in range(2):
        for way in range(2):
            term_in(way, step).start()
    whole = [
        pltpu.make_async_copy(source, target, whole_sems.at[k])
        for k, (source, target) in enumerate(
            (
                (qb_hbm, qb_ref), (ka_hbm, ka_ref), (va_hbm, va_ref), (goa_hbm, goa_ref),
                (kt_hbm, kt_ref), (o_hbm, o_ref), (w_hbm, w_ref),
            )
        )
    ]
    for copy in whole[:-2]:
        copy.start()
    each(down_in)
    each(h2_in)
    for copy in whole[-2:]:
        copy.start()
    each(ga_in)
    each(own_in)
    small_mine[:, :width] = gvec_ref[...]
    ratio = gbias_ref.shape[1] // local_width
    for r in range(ratio):
        small_mine[1 + r : 2 + r, width:] = gbias_ref[0:1, r * local_width : (r + 1) * local_width]
    small_mine[1 + ratio :, width:] = jnp.zeros((7 - ratio, local_width), full_type)
    greeted()

    pieces = stage.shape[0]
    part = terms.shape[3] // pieces

    def term_view(piece):
        columns = slice(piece * part, (piece + 1) * part)
        return lambda way, step: terms[way, step % 2, :, columns]

    scatters = [
        Scatter(term_view(p), stage.at[p], taken.at[p], scatter_sems.at[p], count)
        for p in range(pieces)
    ]

    def terms_ready(step):
        for way in range(2):
            term_in(way, step).wait()

    def terms_next(step):
        @pl.when(step <= hops)
        def _():
            for way in range(2):
                term_in(way, step).start()

    rowsum = RowSum(wide_ref.reshape(blocks, BLOCK, width), given, sent, crossed, sum_sems)
    layer = Put(put_ref, layer_hbm, put_sems)
    def give_all(i, carry):
        down_in(i).wait()
        rowsum.give(i)
        return carry

    lax.fori_loop(0, blocks, give_all, 0)
    terms_ready(0)
    for scatter in scatters:
        scatter.begin()
    terms_next(2)

    lane = lax.broadcasted_iota(jnp.int32, (BLOCK, LANES), 1)
    low_half = lane < HD
    gqt_ref[...] = jnp.zeros_like(gqt_ref)
    rowsum.cross(0)
    for copy in whole[:-2]:
        copy.wait()

    def output_block(i):
        h2_in(i).wait()
        total = gh_ref[own_rows(i), :] + rowsum.total(i) + vec_ref[1:2, :]
        layer.put(i, total.astype(half_type))
        gh2_in(i).start()

    per = -(-hops // blocks)

    def between(j, piece):
        if piece == 0:

            @pl.when(j >= 1)
            def _():
                output_block(j - 1)

            @pl.when(j < blocks - 1)
            def _():
                rowsum.cross(j + 1)

        for t in range(per):
            hop = j * per + t

            @pl.when((hop >= 1) & (hop < hops))
            def _(hop=hop):
                if piece == 0:
                    terms_ready(hop)
                scatters[piece].advance(hop)
                if piece == pieces - 1:
                    terms_next(hop + 2)

    def keys_block(j, carry):
        rows = pl.ds(pl.multiple_of(j * BLOCK, BLOCK), BLOCK)
        for head in range(heads):
            scores = dot(ka_ref[head, rows, :], qb_ref[head], 1, 1)
            probs = jnp.exp(scores)
            gp = dot(va_ref[head, rows, :], goa_ref[head], 1, 1)
            gs = (probs * gp).astype(half_type)
            gv = dot(probs.astype(half_type), goa_ref[head])
            gk = dot(gs, qb_ref[head])
            own = slice(head * HD, head * HD + HD)
            gqt_ref[own, :] += dot(kt_ref[own, rows], gs)
            if head % 2 == 0:
                gk_even, gv_even = gk, gv
            else:
                for k, value in ((1, (gk_even, gk)), (2, (gv_even, gv))):
                    base = k * local_width + head // 2 * LANES
                    gqkv_ref[rows, base : base + LANES] = jnp.where(low_half, *value).astype(
                        half_type
                    )
            if (head + 1) * pieces % heads == 0:
                between(j, (head + 1) * pieces // heads - 1)
        return carry

    lax.fori_loop(0, blocks, keys_block, 0)

    def turn(i, carry):
        rows = pl.ds(pl.multiple_of(i * BLOCK, BLOCK), BLOCK)
        gqkv_ref[rows, :local_width] = (gqt_ref[:, rows].T * HD**-0.5).astype(half_type)
        return carry

    rowsum2 = RowSum(term2, given2, sent2, crossed2, sum2_sems)

    def norm_term(i):
        rows = pl.ds(pl.multiple_of(i * BLOCK, BLOCK), BLOCK)
        rowsum2.free(i)
        term2[i % term2.shape[0]] = dot(gqkv_ref[rows, :], w_ref[...], 1, 1).astype(half_type)
        rowsum2.give(i)

    lax.fori_loop(0, 2, turn, 0)
    whole[-1].wait()
    norm_term(0)
    norm_term(1)
    rowsum.gone()
    each(a1_in)
    lax.fori_loop(2, blocks, turn, 0)
    rowsum2.cross(0)
    ones = jnp.ones((8, total_rows), half_type)
    bias_query = dot(ones, gqkv_ref[:, :local_width])
    small_mine[0:1, width:] = bias_query[0:1, :]

    def small_copy(kind, source, peer):
        window = pl.ds(pl.multiple_of(peer // fold * lanes, lanes), lanes)
        return pltpu.make_async_remote_copy(
            src_ref=small_mine.at[:, pl.ds(width, local_width) if kind else window],
            dst_ref=small_taken.at[source, :, pl.ds(lanes, local_width) if kind else pl.ds(0, lanes)],
            send_sem=small_sems.at[2 * kind, peer],
            recv_sem=small_sems.at[2 * kind + 1, source],
            device_id=(peer, tensor),
            device_id_type=MESH,
        )

    def send_small(kind):
        def send(k, carry):
            small_copy(kind, me, (me + k) % count).start()
            return carry

        lax.fori_loop(1, count, send, 0)

    send_small(1)

    def arrived_a1(i, carry):
        a1_in(i).wait()
        ga_in(i).wait()
        return carry

    lax.fori_loop(0, blocks, arrived_a1, 0)

    def weight_grads(c, carry):
        columns = pl.ds(pl.multiple_of(c * BLOCK, BLOCK), BLOCK)
        grads[columns, : 3 * local_width] = dot(wide_ref[:, columns], gqkv_ref[...], 0, 0)
        grads[columns, 3 * local_width :] = dot(ga_ref[:, columns], o_ref[...], 0, 0)
        return carry

    chunks = width // BLOCK
    whole[-2].wait()
    lax.fori_loop(0, chunks // 2, weight_grads, 0)
    rowsum2.cross(1)
    output_block(blocks - 1)
    lax.fori_loop(chunks // 2, chunks, weight_grads, 0)
    side = grads.shape[1] // 2

    def grads_view(way, step):
        return grads[
            place(sent_block(pos, way, step, count)), way * side : (way + 1) * side
        ]

    scatter2 = Scatter(grads_view, stage2, taken2, scatter2_sems, count)
    scatter2.begin()

    def layer_left(i, carry):
        layer.left(i)
        layer.arrived(i)
        return carry

    lax.fori_loop(0, blocks, layer_left, 0)
    result = Put(put_ref, tg_hbm, put2_sems)

    def norm_block(i):
        gn = rowsum2.total(i)
        own_in(i).wait()
        gh2_in(i).wait()
        unit, rate = normalized(own_ref[own_rows(i), :].astype(full_type))
        e = gn * vec_ref[2:3, :]
        inner = e - jnp.mean(e, axis=-1, keepdims=True)
        inner = inner - unit * jnp.mean(e * unit, axis=-1, keepdims=True)
        result.put(i, (gh_ref[own_rows(i), :] + rate * inner).astype(half_type))
        small_mine[2:3, :width] += jnp.sum(gn * unit, axis=0, keepdims=True)
        small_mine[3:4, :width] += jnp.sum(gn, axis=0, keepdims=True)

    def end_step(i, carry):
        @pl.when(i < blocks - 2)
        def _():
            norm_term(i + 2)

        norm_block(i)

        @pl.when(i < blocks - 2)
        def _():
            rowsum2.cross(i + 2)

        for t in range(per):
            hop = i * per + t + 1

            @pl.when(hop < hops)
            def _(hop=hop):
                scatter2.advance(hop)

        return carry

    lax.fori_loop(0, blocks, end_step, 0)
    send_small(0)
    terms_ready(hops)
    for way in range(2):
        for p, scatter in enumerate(scatters):
            dense_ref[way, :, p * part : (p + 1) * part] = scatter.total(way)
        total = scatter2.total(way)
        for k in range(2):
            sum_ref[2 * way + k] = total[:, k * local_width : (k + 1) * local_width]
    for kind in range(2):
        window = pl.ds(pl.multiple_of(me // fold * lanes, lanes), lanes)
        here = slice(lanes, lanes + local_width) if kind else slice(0, lanes)
        small_taken[me, :, here] = small_mine[:, width:] if kind else small_mine[:, window]

        def take(k, carry, kind=kind):
            source = (me + k) % count
            small_copy(kind, source, source).wait_recv()
            return carry

        lax.fori_loop(1, count, take, 0)
    total = small_taken[0]
    for j in range(1, count):
        total = total + small_taken[j]
    small_ref[...] = total
    pair = pltpu.make_async_remote_copy(
        src_ref=small_ref.at[:, pl.ds(0, lanes)],
        dst_ref=small_mate,
        send_sem=mate_sems.at[0],
        recv_sem=mate_sems.at[1],
        device_id=(me, mate),
        device_id_type=MESH,
    )
    pair.start()
    pair.wait()
    small_ref[:, :lanes] = total[:, :lanes] + small_mate[...]

    def result_left(i, carry):
        result.left(i)
        result.arrived(i)
        return carry

    lax.fori_loop(0, blocks, result_left, 0)
    for scatter in scatters + [scatter2]:
        scatter.finish()
    rowsum.finish(given=False)
    rowsum2.finish()
    for kind in range(2):

        def done(k, carry, kind=kind):
            small_copy(kind, me, (me + k) % count).wait_send()
            return carry

        lax.fori_loop(1, count, done, 0)


def permuted(x, owner, back):
    rows, width = x.shape
    count = owner.shape[0]
    order = jnp.argsort(owner) if back else owner
    return jnp.take(x.reshape(rows, count, -1), order, axis=1).reshape(rows, width)


def adamw_step(weight, first, second, grad, rate, decay):
    first_next = first_decay * first + (1.0 - first_decay) * grad
    second_next = second_decay * second + (1.0 - second_decay) * grad * grad
    first_hat = first_next / (1.0 - first_decay**STEP)
    second_hat = second_next / (1.0 - second_decay**STEP)
    update = first_hat / (jnp.sqrt(second_hat) + adam_epsilon) + decay * weight
    return (first_next, second_next, weight - rate * update)


def last_kernel(rates, owner_ref, *refs):
    count = owner_ref.shape[0]
    given, refs = refs[:5], refs[5:]
    layer, grad, weight_sum, dense_sum, small = given
    state, refs = refs[:15], refs[15:]
    results, outs = refs[:2], refs[2:]

    def step(k, grad, at=(Ellipsis,)):
        new = adamw_step(*(ref[at] for ref in state[3 * k : 3 * k + 3]), grad, *rates[k])
        for ref, value in zip(outs[3 * k : 3 * k + 3], new):
            ref[at] = value

    wide = layer.shape[1] // count
    if wide % LANES == 0:
        for j in range(count):
            natural = pl.ds(pl.multiple_of(owner_ref[j] * wide, wide), wide)
            for x, y in zip((layer, grad), results):
                y[:, natural] = x[:, j * wide : (j + 1) * wide]
    else:
        for x, y in zip((layer, grad), results):
            y[...] = x[...]
    step(0, weight_sum[0:3])
    step(1, weight_sum[3])
    ratio, local_width = state[6].shape[2:]
    for r in range(ratio):
        step(
            2,
            dense_sum[:, :, r * local_width : (r + 1) * local_width],
            (slice(None), slice(None), r, slice(None)),
        )
    me = lax.axis_index("dp")
    lanes = small.shape[1] - local_width

    def chosen(x, start, size):
        row = lax.broadcasted_iota(jnp.int32, (x.shape[1], size), 0)
        column = lax.broadcasted_iota(jnp.int32, (x.shape[1], size), 1)
        pick = jnp.where(row == column + start, 1.0, 0.0).astype(half_type)
        return sum(dot(part.astype(half_type), pick) for part in three_parts(x))

    narrow, wide = state[9].shape[1], state[12].shape[1]
    step(3, chosen(small[:, lanes:], owner_ref[me] * narrow, narrow)[: 1 + ratio])
    step(4, chosen(small[:, :lanes], me % (lanes // wide) * wide, wide)[:6])


def last(owner, layer_output, tokens_grad, weight_sum, dense_sum, small_sum, *state):
    steps = 4 if dense_sum.shape[1] % 128 == 0 else 1
    rates = (
        (matrix_rate, matrix_decay),
        (output_rate, matrix_decay),
        (matrix_rate, matrix_decay),
        (bias_rate, 0.0),
        (vector_rate, 0.0),
    )

    def spec(x, dim):
        shape = tuple(n // steps if k == dim else n for k, n in enumerate(x.shape))
        return pl.BlockSpec(shape, lambda i, *_: tuple(i if k == dim else 0 for k in range(x.ndim)))

    dims = [0, 0, 1, 1, None] + [1] * 3 + [0] * 3 + [1] * 3 + [None] * 6
    operands = (layer_output, tokens_grad, weight_sum, dense_sum, small_sum) + state
    specs = [spec(x, dim) for x, dim in zip(operands, dims)]
    outs = operands[:2] + state
    return pl.pallas_call(
        functools.partial(last_kernel, rates),
        out_shape=[jax.ShapeDtypeStruct(x.shape, x.dtype) for x in outs],
        grid_spec=pltpu.PrefetchScalarGridSpec(
            num_scalar_prefetch=1, grid=(steps,), in_specs=specs, out_specs=specs[:2] + specs[5:]
        ),
        compiler_params=pltpu.CompilerParams(vmem_limit_bytes=60 * 2**20),
    )(owner, *operands)


def call(kernel, collective, outs, scratch, operands, spaces, limit=62):
    spec = {
        "s": pl.BlockSpec(memory_space=pltpu.SMEM),
        "v": pl.BlockSpec(memory_space=pltpu.VMEM),
        "h": pl.BlockSpec(memory_space=pl.ANY),
    }
    return pl.pallas_call(
        kernel,
        out_shape=[jax.ShapeDtypeStruct(shape, dtype) for shape, dtype in outs],
        in_specs=[spec[c] for c in spaces[0]],
        out_specs=[spec[c] for c in spaces[1]],
        scratch_shapes=scratch,
        compiler_params=pltpu.CompilerParams(
            collective_id=collective, has_side_effects=True, vmem_limit_bytes=limit * 2**20
        ),
    )(*operands)


def dma(*shape):
    return pltpu.SemaphoreType.DMA(shape)


def local(
    tokens,
    lengths,
    owner,
    attend_master,
    attend_first,
    attend_second,
    output_master,
    output_first,
    output_second,
    dense_master,
    dense_first,
    dense_second,
    bias_master,
    bias_first,
    bias_second,
    vector_master,
    vector_first,
    vector_second,
    cotangent,
):
    count = owner.shape[0]
    rows, width = tokens.shape
    local_width = output_master.shape[1]
    ratio = dense_master.shape[2]
    hidden = ratio * local_width
    heads = local_width // HD
    blocks = rows // BLOCK
    half = BLOCK // 2
    wide = width // count
    lanes = max(LANES, wide)
    tok, cot = tokens, cotangent
    if wide % LANES:
        tok, cot = (permuted(x, owner, False) for x in (tokens, cotangent))
    row_sum = [pltpu.VMEM((blocks, half, width), half_type)] * 3
    two_terms = pltpu.VMEM((2, BLOCK, width), half_type)
    heads_shape = (heads, rows, LANES)
    small = (8, lanes + local_width)
    a1, ga, h2, own, qb, ka, va, o, w, gh2, down, up, dn, goa, kt, vec, gbias, gvec = call(
        functools.partial(front_kernel, count),
        0,
        [
            ((rows, width), half_type),
            ((rows, width), half_type),
            ((rows // 2, width), full_type),
            ((rows // 2, width), half_type),
            (heads_shape, half_type),
            (heads_shape, half_type),
            (heads_shape, half_type),
            ((rows, local_width), half_type),
            ((width, 3 * local_width), half_type),
            ((rows // 2, width), full_type),
            ((rows, width), half_type),
            ((width, hidden), full_type),
            ((width, hidden), full_type),
            (heads_shape, half_type),
            ((local_width, rows), half_type),
            ((8, width), full_type),
            ((8, hidden), full_type),
            ((8, width), full_type),
        ],
        [
            pltpu.VMEM((rows // 2, width), half_type),
            *[pltpu.VMEM(heads_shape, half_type)] * 3,
            pltpu.VMEM((rows, local_width), half_type),
            pltpu.VMEM((width, 3 * local_width), half_type),
            pltpu.VMEM((width, width), half_type),
            pltpu.VMEM((rows // 2, width), full_type),
            pltpu.VMEM((rows, width), half_type),
            *[pltpu.VMEM((rows, hidden), half_type)] * 2,
            pltpu.VMEM((2, BLOCK, hidden), full_type),
            *[pltpu.VMEM((rows, width), half_type)] * 2,
            pltpu.VMEM((2, width, hidden), half_type),
            pltpu.VMEM((rows, width), half_type),
            pltpu.VMEM(heads_shape, half_type),
            pltpu.VMEM((local_width, rows), half_type),
            pltpu.VMEM((8, local_width), full_type),
            pltpu.VMEM((1, hidden), full_type),
            pltpu.VMEM(small, full_type),
            pltpu.VMEM((count,) + small, full_type),
            pltpu.VMEM((blocks, half, width), half_type),
            two_terms,
            *row_sum,
            dma(6, 4, count // 2),
            dma(2, count),
            dma(6, count),
            dma(6, blocks),
            dma(4, blocks),
            dma(2, blocks),
            dma(2, blocks),
            dma(8, blocks),
            dma(7),
            dma(2, width // BLOCK),
        ],
        (
            lengths, owner, tok, cot, attend_master, output_master, dense_master, vector_master,
            bias_master,
        ),
        ("sshhvvvvv", "h" * 15 + "vvv"),
    )
    pieces = 2
    row_blocks = pltpu.VMEM((blocks, half, width), half_type)
    row_slots = pltpu.VMEM((min(3, blocks), half, width), half_type)
    part, side = hidden // pieces, 2 * local_width
    layer_output, tokens_grad, dense_sum, weight_sum, small_sum = call(
        functools.partial(back_kernel, count),
        1,
        [
            ((rows, width), half_type),
            ((rows, width), half_type),
            ((2, wide, hidden), full_type),
            ((4, wide, local_width), full_type),
            ((8, lanes + local_width), full_type),
        ],
        [
            pltpu.VMEM((rows, width), half_type),
            pltpu.VMEM((rows, local_width), half_type),
            *[pltpu.VMEM(heads_shape, half_type)] * 3,
            pltpu.VMEM((width, 3 * local_width), half_type),
            pltpu.VMEM((rows, width), half_type),
            pltpu.VMEM((rows // 2, width), full_type),
            pltpu.VMEM((rows // 2, width), half_type),
            pltpu.VMEM(heads_shape, half_type),
            pltpu.VMEM((local_width, rows), half_type),
            pltpu.VMEM((local_width, rows), full_type),
            pltpu.VMEM((rows, 3 * local_width), half_type),
            pltpu.VMEM((rows // 2, width), half_type),
            row_blocks,
            row_slots,
            row_blocks,
            two_terms,
            row_blocks,
            row_slots,
            row_blocks,
            pltpu.VMEM((2, 2, wide, hidden), full_type),
            pltpu.VMEM((pieces, 2, 2, wide, part), half_type),
            pltpu.VMEM((pieces, 2, count - 1, wide, part), half_type),
            pltpu.VMEM((width, 4 * local_width), full_type),
            pltpu.VMEM((2, 2, wide, side), half_type),
            pltpu.VMEM((2, count - 1, wide, side), half_type),
            pltpu.VMEM((8, width + local_width), full_type),
            pltpu.VMEM((count, 8, lanes + local_width), full_type),
            pltpu.VMEM((8, lanes), full_type),
            dma(4, blocks),
            dma(4, blocks),
            dma(3, blocks),
            dma(3, blocks),
            dma(pieces, 4, count - 1),
            dma(4, count - 1),
            dma(4, count),
            dma(2),
            dma(6, blocks),
            dma(2, 2),
            dma(7),
        ],
        (ga, o, qb, ka, va, goa, kt, w, up, dn, down, h2, gh2, own, a1, vec, gbias, gvec),
        ("h" * 15 + "vvv", "hhvvv"),
    )
    if wide % LANES:
        layer_output, tokens_grad = (permuted(x, owner, True) for x in (layer_output, tokens_grad))
    return tuple(
        last(
            owner, layer_output, tokens_grad, weight_sum, dense_sum, small_sum,
            attend_master, attend_first, attend_second,
            output_master, output_first, output_second,
            dense_master, dense_first, dense_second,
            bias_master, bias_first, bias_second,
            vector_master, vector_first, vector_second,
        )
    )


def solution(mesh):
    return jax.shard_map(
        local,
        mesh=mesh,
        in_specs=(
            P("dp", None),
            P("dp", None),
            P(),
            P(None, "dp", "tensor"),
            P(None, "dp", "tensor"),
            P(None, "dp", "tensor"),
            P("dp", "tensor"),
            P("dp", "tensor"),
            P("dp", "tensor"),
            P(None, "dp", None, "tensor"),
            P(None, "dp", None, "tensor"),
            P(None, "dp", None, "tensor"),
            P(None, ("tensor", "dp")),
            P(None, ("tensor", "dp")),
            P(None, ("tensor", "dp")),
            P(None, "dp"),
            P(None, "dp"),
            P(None, "dp"),
            P("dp", None),
        ),
        out_specs=(
            P("dp", None),
            P("dp", None),
            P(None, "dp", "tensor"),
            P(None, "dp", "tensor"),
            P(None, "dp", "tensor"),
            P("dp", "tensor"),
            P("dp", "tensor"),
            P("dp", "tensor"),
            P(None, "dp", None, "tensor"),
            P(None, "dp", None, "tensor"),
            P(None, "dp", None, "tensor"),
            P(None, ("tensor", "dp")),
            P(None, ("tensor", "dp")),
            P(None, ("tensor", "dp")),
            P(None, "dp"),
            P(None, "dp"),
            P(None, "dp"),
        ),
        check_vma=False,
    )
```

```python
import functools

import jax
import jax.numpy as jnp
from jax import lax
from jax.experimental import pallas as pl
from jax.experimental.pallas import tpu as pltpu
from jax.sharding import PartitionSpec as P

HD = 64
STEP = 10
LANES = 128
BLOCK = 256
MESH = pl.DeviceIdType.MESH
BIG = 2.0**50

norm_epsilon = 1e-06
first_decay = 0.9
second_decay = 0.95
adam_epsilon = 1e-08
matrix_rate = 0.1
output_rate = 0.5
bias_rate = 0.5
vector_rate = 1.0
matrix_decay = 0.05

half_type = jnp.bfloat16
full_type = jnp.float32


def dot(left, right, left_dim=1, right_dim=0):
    return lax.dot_general(
        left, right, (((left_dim,), (right_dim,)), ((), ())), preferred_element_type=full_type
    )


def ring_pos(place, count):
    column = place % 2
    row = place // 2
    return row * (1 - column) + (count - 1 - row) * column


def ring_at(pos, count):
    near = (pos + 2 * count) % count
    down = near // (count // 2)
    return 2 * near * (1 - down) + (2 * count - 1 - 2 * near) * down


def normalized(x):
    center = jnp.mean(x, axis=-1, keepdims=True)
    offset = x - center
    spread = jnp.mean(offset * offset, axis=-1, keepdims=True)
    rate = lax.rsqrt(spread + norm_epsilon)
    return offset * rate, rate


class Gather:
    def __init__(self, view, width, sems, count):
        self.view, self.width, self.sems, self.count = view, width, sems, count
        self.steps = count // 2
        self.pos = ring_pos(lax.axis_index("dp"), count)
        self.tensor = lax.axis_index("tensor")

    def _copy(self, way, step, hops):
        sign = 1 - 2 * way
        part = (0, self.width)
        if step == self.steps - 1:
            part = (way * (self.width // 2), self.width // 2)
        block = self.view(ring_at(self.pos - sign * hops, self.count), *part)
        return pltpu.make_async_remote_copy(
            src_ref=block,
            dst_ref=block,
            send_sem=self.sems.at[2 * way, step],
            recv_sem=self.sems.at[2 * way + 1, step],
            device_id=(ring_at(self.pos + sign, self.count), self.tensor),
            device_id_type=MESH,
        )

    def advance(self, step):
        if step:
            for way in range(2):
                self._copy(way, step - 1, step).wait_recv()
        if step < self.steps:
            for way in range(2):
                self._copy(way, step, step).start()

    def sent(self):
        for step in range(self.steps):
            for way in range(2):
                self._copy(way, step, step).wait_send()


class RowSum:
    def __init__(self, term, given, sent, crossed, sems, first=0):
        self.term, self.given, self.sent_ref, self.crossed = term, given, sent, crossed
        self.slots, self.sent_slots, self.blocks = term.shape[0], sent.shape[0], given.shape[0]
        self.sems, self.first = sems, first
        self.half = given.shape[1]
        self.dp, tensor = lax.axis_index("dp"), lax.axis_index("tensor")
        self.core = tensor % 2
        self.mate = tensor - tensor % 2 + (tensor + 1) % 2
        self.other = (tensor + 2) % 4

    def rows(self, core):
        return pl.ds(pl.multiple_of(core * self.half, self.half), self.half)

    def _give(self, i):
        return pltpu.make_async_remote_copy(
            src_ref=self.term.at[i % self.slots, self.rows(1 - self.core), :],
            dst_ref=self.given.at[i],
            send_sem=self.sems.at[0, i],
            recv_sem=self.sems.at[1, i],
            device_id=(self.dp, self.mate),
            device_id_type=MESH,
        )

    def _cross(self, i):
        return pltpu.make_async_remote_copy(
            src_ref=self.sent_ref.at[i % self.sent_slots],
            dst_ref=self.crossed.at[i],
            send_sem=self.sems.at[2, i],
            recv_sem=self.sems.at[3, i],
            device_id=(self.dp, self.other),
            device_id_type=MESH,
        )

    def free(self, i):
        if self.slots < self.blocks:

            @pl.when(i >= self.slots)
            def _():
                self._give(i - self.slots).wait_send()

    def give(self, i):
        self._give(i).start()

    def cross(self, i):
        self._give(i).wait_recv()
        mine = self.term[i % self.slots, self.rows(self.core), :].astype(full_type)
        if self.sent_slots < self.blocks:

            @pl.when(i >= self.sent_slots + self.first)
            def _():
                self._cross(i - self.sent_slots).wait_send()

        total = mine + self.given[i].astype(full_type)
        self.sent_ref[i % self.sent_slots] = total.astype(half_type)
        self._cross(i).start()

    def total(self, i):
        if self.first:

            @pl.when(i >= self.first)
            def _():
                self._cross(i).wait_recv()

        else:
            self._cross(i).wait_recv()
        mine = self.sent_ref[i % self.sent_slots].astype(full_type)
        return mine + self.crossed[i].astype(full_type)

    def ready(self, i):
        self._cross(i).wait_recv()

    def gone(self):
        def given(i, carry):
            self._give(i).wait_send()
            return carry

        lax.fori_loop(max(self.blocks - self.slots, self.first), self.blocks, given, 0)

    def finish(self, given=True):
        if given:
            self.gone()

        def crossed(i, carry):
            self._cross(i).wait_send()
            return carry

        lax.fori_loop(max(self.blocks - self.sent_slots, self.first), self.blocks, crossed, 0)


class Share:
    def __init__(self, ref, sems):
        self.ref, self.sems = ref, sems
        self.dp, tensor = lax.axis_index("dp"), lax.axis_index("tensor")
        self.core = tensor % 2
        self.mate = tensor - tensor % 2 + (tensor + 1) % 2

    def rows(self, i, core):
        half = BLOCK // 2
        return pl.ds(pl.multiple_of(i * BLOCK + core * half, half), half)

    def _copy(self, i, core):
        piece = self.ref.at[self.rows(i, core), :]
        return pltpu.make_async_remote_copy(
            src_ref=piece,
            dst_ref=piece,
            send_sem=self.sems.at[0, i],
            recv_sem=self.sems.at[1, i],
            device_id=(self.dp, self.mate),
            device_id_type=MESH,
        )

    def put(self, i, value):
        self.ref[self.rows(i, self.core), :] = value
        self._copy(i, self.core).start()

    def arrived(self, i):
        self._copy(i, 1 - self.core).wait_recv()

    def finish(self, blocks):
        def done(i, carry):
            self._copy(i, self.core).wait_send()
            return carry

        lax.fori_loop(0, blocks, done, 0)


def greet(peers):
    barrier = pltpu.get_barrier_semaphore()
    for peer in peers:
        pl.semaphore_signal(barrier, inc=1, device_id=peer, device_id_type=MESH)
    return lambda: pl.semaphore_wait(barrier, len(peers))


def tensor_peers():
    dp, tensor = lax.axis_index("dp"), lax.axis_index("tensor")
    return [(dp, tensor - tensor % 2 + (tensor + 1) % 2), (dp, (tensor + 2) % 4)]


def ring_peers(count):
    dp, tensor = lax.axis_index("dp"), lax.axis_index("tensor")
    pos = ring_pos(dp, count)
    return [(ring_at(pos + 1, count), tensor), (ring_at(pos - 1, count), tensor)]


def dp_peers(count):
    dp, tensor = lax.axis_index("dp"), lax.axis_index("tensor")
    return [((dp + k) % count, tensor) for k in range(1, count)]


def three_parts(x):
    high = x.astype(half_type).astype(full_type)
    middle = (x - high).astype(half_type).astype(full_type)
    return high, middle, x - high - middle


def gelu_parts(z):
    phi = 0.5 + 0.5 * lax.erf(z * (0.5**0.5))
    slope = phi + z * (jnp.exp(-0.5 * z * z) * (2.0 * 3.141592653589793) ** -0.5)
    return z * phi, slope


def fetch(source, target, sems):
    def copy(i):
        rows = pl.ds(pl.multiple_of(i * BLOCK, BLOCK), BLOCK)
        return pltpu.make_async_copy(source.at[rows, :], target.at[rows, :], sems.at[i])

    return copy


def stored_order(x, owner_ref):
    count = owner_ref.shape[0]
    wide = x.shape[1] // count
    if wide % LANES:
        return x
    parts = []
    for j in range(count):
        total = None
        for n in range(count):
            term = x[:, n * wide : (n + 1) * wide] * jnp.where(owner_ref[j] == n, 1.0, 0.0)
            total = term if total is None else total + term
        parts.append(total)
    return jnp.concatenate(parts, axis=1)


def front_kernel(
    count, len_ref, owner_ref, tok_hbm, cot_hbm, att_ref, out_ref, dense_ref, vector_ref, split_ref,
    a1_hbm, ga_hbm, h2_hbm, own_hbm, qa_hbm, ka_hbm, va_hbm, o_hbm, w_hbm, gh2_hbm, down_hbm,
    up_hbm, dn_hbm, goa_hbm, kt_hbm, first_hbm, vec_ref, gbias_ref, gvec_ref,
    own_ref, qa_ref, ka_ref, va_ref, o_ref, w_ref, wo_ref, gh2_ref, down_ref, ul_ref, gz_ref, made,
    norm_ref, cot_ref, wd_ref, ga_ref, goa_ref, kt_ref, bias_ref, b1_ref, small_ref, smalls,
    mixed_ref, term2, given2, sent2, crossed2, given3, sent3, crossed3,
    gather_sems, small_sems, spread_sems, mixed_sems, sum2_sems, share_sems, put_sems, local_sems,
    whole_sems, made_sems, sum3_sems,
):
    me, tensor = lax.axis_index("dp"), lax.axis_index("tensor")
    total_rows, width = norm_ref.shape
    local_width = out_ref.shape[1]
    ratio = dense_ref.shape[2]
    wide = width // count
    slots = len_ref.shape[1]
    heads = local_width // HD
    blocks = total_rows // BLOCK
    half = BLOCK // 2
    lanes = small_ref.shape[1] - local_width
    fold = lanes // wide
    steps = count // 2
    core = tensor % 2
    mate = tensor - core + 1 - core
    other, across = (tensor + 2) % 4, (mate + 2) % 4

    greeted = greet(tensor_peers() + [(me, across)] + dp_peers(count))
    tokens_in = fetch(tok_hbm, norm_ref, local_sems.at[0])
    cot_in = fetch(cot_hbm, cot_ref, local_sems.at[1])
    a1_out = fetch(norm_ref, a1_hbm, local_sems.at[2])
    for i in range(blocks):
        tokens_in(i).start()
    for i in range(blocks):
        cot_in(i).start()
    mine = pl.ds(pl.multiple_of(me * wide, wide), wide)
    for row in range(3):
        w_ref[mine, row * local_width : (row + 1) * local_width] = att_ref[row].astype(half_type)

    def columns_of(index, low=0, size=local_width):
        return pl.ds(pl.multiple_of(index * local_width + low, LANES), size)

    wo_ref[mine, columns_of(tensor)] = out_ref[...].astype(half_type)

    small_ref[...] = jnp.zeros_like(small_ref)
    vectors = vector_ref[...].astype(half_type)
    if fold == 1:
        small_ref[0:6, :lanes] = vectors.astype(full_type)
    else:
        row = lax.broadcasted_iota(jnp.int32, (wide, lanes), 0)
        column = lax.broadcasted_iota(jnp.int32, (wide, lanes), 1)
        spread = jnp.where(column == row + me % fold * wide, 1.0, 0.0).astype(half_type)
        small_ref[0:6, :lanes] = dot(vectors, spread)
    narrow = split_ref.shape[1]
    row = lax.broadcasted_iota(jnp.int32, (narrow, local_width), 0)
    column = lax.broadcasted_iota(jnp.int32, (narrow, local_width), 1)
    spread = jnp.where(column == row + owner_ref[me] * narrow, 1.0, 0.0).astype(half_type)
    small_ref[0 : 1 + ratio, lanes:] = dot(split_ref[...].astype(half_type), spread)
    smalls[me] = small_ref[...]
    greeted()

    def place(block):
        return pl.ds(pl.multiple_of(block * wide, wide), wide)

    def small_copy(source, peer):
        return pltpu.make_async_remote_copy(
            src_ref=small_ref,
            dst_ref=smalls.at[source],
            send_sem=small_sems.at[0, peer],
            recv_sem=small_sems.at[1, source],
            device_id=(peer, tensor),
            device_id_type=MESH,
        )

    def send_small(k, carry):
        small_copy(me, (me + k) % count).start()
        return carry

    lax.fori_loop(1, count, send_small, 0)

    def attend_view(row):
        return lambda block, low, size: w_ref.at[
            place(block), pl.ds(row * local_width + low, size)
        ]

    def dense_view(row):
        return lambda block, low, size: wd_ref.at[row, place(block), pl.ds(low, size)]

    attend = [Gather(attend_view(row), local_width, gather_sems.at[row], count) for row in range(3)]
    attend.append(
        Gather(
            lambda block, low, size: wo_ref.at[place(block), columns_of(tensor, low, size)],
            local_width, gather_sems.at[3], count,
        )
    )
    dense = [
        Gather(dense_view(row), ratio * local_width, gather_sems.at[4 + row], count)
        for row in range(2)
    ]
    for piece in attend:
        piece.advance(0)

    def spread(kind, block, source, target):
        piece = wo_ref.at[place(block), columns_of(source)]
        return pltpu.make_async_remote_copy(
            src_ref=piece,
            dst_ref=piece,
            send_sem=spread_sems.at[2 * kind, block],
            recv_sem=spread_sems.at[2 * kind + 1, block],
            device_id=(me, target),
            device_id_type=MESH,
        )

    def spread_step(step):
        pos = attend[3].pos
        hops = {0: [0], steps: [steps]}.get(step, [step, -step])
        for hop in hops:
            block = ring_at(pos - hop, count)
            spread(0, block, tensor, mate).start()
            spread(1, block, tensor, other).start()

    spread_step(0)
    for row in range(2):
        for r in range(ratio):
            wd_ref[row, mine, r * local_width : (r + 1) * local_width] = dense_ref[
                row, :, r, :
            ].astype(half_type)

    def take_small(k, carry):
        source = (me + k) % count
        small_copy(source, source).wait_recv()
        return carry

    lax.fori_loop(1, count, take_small, 0)
    bias = smalls[0, :, lanes:]
    for j in range(1, count):
        bias = bias + smalls[j, :, lanes:]
    bias_ref[...] = bias
    for r in range(ratio):
        b1_ref[:, r * local_width : (r + 1) * local_width] = bias[1 + r : 2 + r, :]
    for window in range(width // lanes):
        piece = smalls[window * fold, :, :lanes]
        for j in range(window * fold + 1, (window + 1) * fold):
            piece = piece + smalls[j, :, :lanes]
        vec_ref[:, window * lanes : (window + 1) * lanes] = piece

    def norm_rows(i, carry):
        tokens_in(i).wait()
        rows = pl.ds(pl.multiple_of(i * BLOCK, BLOCK), BLOCK)
        x = stored_order(norm_ref[rows, :].astype(full_type), owner_ref)
        norm_ref[rows, :] = x.astype(half_type)
        here = pl.ds(pl.multiple_of(i * BLOCK + core * half, half), half)
        own_ref[pl.ds(pl.multiple_of(i * half, half), half), :] = norm_ref[here, :]
        unit, _ = normalized(x)
        norm_ref[rows, :] = (unit * vec_ref[2:3, :] + vec_ref[3:4, :]).astype(half_type)
        a1_out(i).start()
        cot_in(i).wait()
        cot_ref[rows, :] = stored_order(cot_ref[rows, :].astype(full_type), owner_ref).astype(
            half_type
        )
        return carry

    done = 0
    for step in range(1, steps + 1):
        for piece in attend:
            piece.advance(step)
        spread_step(step)
        if step == steps - 1:
            for piece in dense:
                piece.advance(0)
        upto = min(blocks, -(-blocks * step // steps))
        if upto > done:
            lax.fori_loop(done, upto, norm_rows, 0)
        done = max(done, upto)

    pumps = [(piece, step) for step in range(1, steps + 1) for piece in dense]

    def pump(slot):
        for k, (piece, step) in enumerate(pumps):
            if min(blocks + 1, (14 * k + 9) // 10 * 8 // len(pumps)) == slot:
                piece.advance(step)

    lane = lax.broadcasted_iota(jnp.int32, (BLOCK, LANES), 1)
    low_half = lane < HD
    spot = lane % HD

    def project(i, carry):
        row = pl.multiple_of(i * BLOCK, BLOCK)
        rows = pl.ds(row, BLOCK)
        a1 = norm_ref[rows, :]
        qkv = dot(a1, w_ref[...])
        q, k, v = (qkv[:, part * local_width : (part + 1) * local_width] for part in range(3))
        q = (q + bias_ref[0:1, :]).astype(half_type).astype(full_type) * HD**-0.5
        index = row + lax.broadcasted_iota(jnp.int32, (BLOCK, LANES), 0)
        segment = jnp.zeros((BLOCK, LANES), jnp.int32)
        end = 0
        for slot in range(slots):
            end = end + len_ref[0, slot]
            segment = segment + jnp.where(index >= end, 1, 0)
        same = spot == segment
        inside = spot <= slots
        q_mark = jnp.where(inside & ~same, -BIG, 0.0)
        k_mark = jnp.where(same, BIG, jnp.where((spot > slots) & (spot <= slots + 3), 1.0, 0.0))
        for head in range(heads):
            pair = slice(head // 2 * LANES, head // 2 * LANES + LANES)
            own = low_half if head % 2 == 0 else ~low_half
            qa_ref[head, rows, :] = jnp.where(own, q[:, pair], q_mark).astype(half_type)
            ka_ref[head, rows, :] = jnp.where(own, k[:, pair], k_mark).astype(half_type)
            va_ref[head, rows, :] = jnp.where(own, v[:, pair], 1.0).astype(half_type)
        return carry

    lax.fori_loop(0, blocks, project, 0)
    pump(0)

    def forward(block, carry):
        spread(1, block, other, other).wait_recv()
        spread(2, block, other, mate).start()
        return carry

    lax.fori_loop(0, count, forward, 0)

    def a1_left(i, carry):
        a1_out(i).wait()
        return carry

    lax.fori_loop(0, blocks, a1_left, 0)
    gbias_ref[...] = jnp.zeros_like(gbias_ref)
    gvec_ref[...] = jnp.zeros_like(gvec_ref)

    share = Share(norm_ref, share_sems)

    def mixed_copy(kind, i, source, target, half_rows):
        rows = pl.ds(pl.multiple_of(i * BLOCK + half_rows * half, half), half)
        return pltpu.make_async_remote_copy(
            src_ref=o_ref.at[rows, :],
            dst_ref=mixed_ref.at[i, :, columns_of(source)],
            send_sem=mixed_sems.at[2 * kind, i],
            recv_sem=mixed_sems.at[2 * kind + 1, i],
            device_id=(me, target),
            device_id_type=MESH,
        )

    peers = ((0, mate, 1 - core), (1, other, core), (2, across, 1 - core))

    def h2_out(i):
        own = pl.ds(pl.multiple_of(i * half, half), half)
        return pltpu.make_async_copy(gh2_ref.at[own, :], h2_hbm.at[own, :], local_sems.at[3, i])

    def attend_block(i):
        rows = pl.ds(pl.multiple_of(i * BLOCK, BLOCK), BLOCK)
        for head in range(heads):
            query = qa_ref[head, rows, :]
            scores = dot(query, ka_ref[head], 1, 1)
            top = jnp.max(scores, axis=1, keepdims=True)
            weights = jnp.exp(scores - top).astype(half_type)
            mixed = dot(weights, va_ref[head])
            turned = pltpu.roll(mixed, HD, 1)
            own = low_half if head % 2 == 0 else ~low_half
            log_total = three_parts(top + jnp.log(jnp.where(own, turned, mixed)))
            marked = query.astype(full_type)
            for part in range(3):
                marked = jnp.where(~own & (spot == slots + 1 + part), -log_total[part], marked)
            qa_ref[head, rows, :] = marked.astype(half_type)
            out = mixed / turned
            if head % 2 == 0:
                before = out
            else:
                pair = slice(head // 2 * LANES, head // 2 * LANES + LANES)
                o_ref[rows, pair] = jnp.where(low_half, before, out).astype(half_type)
        for kind, peer, half_rows in peers[1:] + peers[:1]:
            mixed_copy(kind, i, tensor, peer, half_rows).start()
        here = pl.ds(pl.multiple_of(i * BLOCK + core * half, half), half)
        mixed_ref[i, :, columns_of(tensor)] = o_ref[here, :]

    def norm_block(i):
        own = pl.ds(pl.multiple_of(i * half, half), half)
        for kind, peer, _ in peers:
            mixed_copy(kind, i, peer, peer, 0).wait_recv()
        attn = dot(mixed_ref[i], wo_ref[...], 1, 1)
        hidden = own_ref[own, :].astype(full_type) + attn + vec_ref[0:1, :]
        gh2_ref[own, :] = hidden
        h2_out(i).start()
        unit, _ = normalized(hidden)
        share.put(i, (unit * vec_ref[4:5, :] + vec_ref[5:6, :]).astype(half_type))

    behind = min(2, blocks)

    def attend_step(i, carry):
        attend_block(i)
        for slot in range(1, blocks + 1):

            @pl.when(i == slot - 1)
            def _(slot=slot):
                pump(slot)

        @pl.when(i == behind)
        def _():
            def spread_in(block, carry):
                spread(0, block, mate, mate).wait_recv()
                spread(2, block, across, mate).wait_recv()
                return carry

            lax.fori_loop(0, count, spread_in, 0)

        @pl.when(i >= behind)
        def _():
            norm_block(i - behind)

        return carry

    lax.fori_loop(0, blocks, attend_step, 0)

    def norm_step(i, carry):
        norm_block(i)
        return carry

    lax.fori_loop(blocks - behind, blocks, norm_step, 0)
    pump(blocks + 1)

    whole = [
        pltpu.make_async_copy(source, target, whole_sems.at[k])
        for k, (source, target) in enumerate(
            (
                (own_ref, own_hbm), (qa_ref, qa_hbm), (ka_ref, ka_hbm), (va_ref, va_hbm),
                (o_ref, o_hbm), (w_ref, w_hbm),
            )
        )
    ]
    for copy in whole:
        copy.start()
    down_out = fetch(down_ref, down_hbm, local_sems.at[5])

    def gh2_out(i):
        own = pl.ds(pl.multiple_of(i * half, half), half)
        return pltpu.make_async_copy(gh2_ref.at[own, :], gh2_hbm.at[own, :], local_sems.at[6, i])

    rowsum2 = RowSum(term2, given2, sent2, crossed2, sum2_sems)

    share2 = Share(ga_ref, put_sems)
    ga_out = fetch(ga_ref, ga_hbm, local_sems.at[4])

    def goa_out(i):
        rows = pl.ds(pl.multiple_of(i * BLOCK, BLOCK), BLOCK)
        return pltpu.make_async_copy(
            goa_ref.at[:, rows, :], goa_hbm.at[:, rows, :], local_sems.at[7, i]
        )

    def prepare(i):
        share2.arrived(i)
        ga_out(i).start()
        rows = pl.ds(pl.multiple_of(i * BLOCK, BLOCK), BLOCK)
        go = dot(ga_ref[rows, :], wo_ref[:, columns_of(tensor)]).astype(half_type).astype(full_type)
        both = go * o_ref[rows, :].astype(full_type)
        for head in range(heads):
            pair = slice(head // 2 * LANES, head // 2 * LANES + LANES)
            own = low_half if head % 2 == 0 else ~low_half
            inner = jnp.sum(jnp.where(own, both[:, pair], 0.0), axis=1, keepdims=True)
            filled = jnp.where(own, go[:, pair], 0.0)
            for k, value in enumerate(three_parts(inner)):
                filled = jnp.where(~own & (spot == k), -value, filled)
            goa_ref[head, rows, :] = filled.astype(half_type)
            if head % 2 == 0:
                before = ka_ref[head, rows, :].astype(full_type)
            else:
                k = jnp.where(low_half, before, ka_ref[head, rows, :].astype(full_type))
                kt_ref[pair, rows] = k.T.astype(half_type)
        goa_out(i).start()

    def mlp_block(i):
        rows = pl.ds(pl.multiple_of(i * BLOCK, BLOCK), BLOCK)
        share.arrived(i)
        a2 = norm_ref[rows, :]
        gy = cot_ref[rows, :]
        u, slope = gelu_parts(dot(a2, wd_ref[0]) + b1_ref[...])
        ul = u.astype(half_type)
        gz = (dot(gy, wd_ref[1]) * slope).astype(half_type)
        rowsum2.free(i)
        term2[i % term2.shape[0]] = dot(gz, wd_ref[0], 1, 1).astype(half_type)
        rowsum2.give(i)
        gbias_ref[0:1, :] += jnp.sum(gz.astype(full_type), axis=0, keepdims=True)
        ul_ref[rows, :] = ul
        gz_ref[rows, :] = gz
        down_ref[rows, :] = dot(ul, wd_ref[1], 1, 1).astype(half_type)
        down_out(i).start()
        rowsum2.cross(i)

    chunks = width // BLOCK

    def made_out(kind, c):
        rows = pl.ds(pl.multiple_of(c * BLOCK, BLOCK), BLOCK)
        target = (up_hbm, dn_hbm)[kind].at[rows, :]
        return pltpu.make_async_copy(made.at[kind], target, made_sems.at[kind, c])

    def weight_grads(c):
        columns = pl.ds(pl.multiple_of(c * BLOCK, BLOCK), BLOCK)
        for kind, (left, right) in enumerate(((norm_ref, gz_ref), (cot_ref, ul_ref))):

            @pl.when(c >= 1)
            def _(kind=kind):
                made_out(kind, c - 1).wait()

            made[kind] = dot(left[:, columns], right[...], 0, 0)
            made_out(kind, c).start()

    def back_block(i):
        own = pl.ds(pl.multiple_of(i * half, half), half)
        gn = rowsum2.total(i)
        h2_out(i).wait()
        unit, rate = normalized(gh2_ref[own, :])
        e = gn * vec_ref[4:5, :]
        inner = e - jnp.mean(e, axis=-1, keepdims=True)
        inner = inner - unit * jnp.mean(e * unit, axis=-1, keepdims=True)
        gy = cot_ref[share.rows(i, core), :].astype(full_type)
        gh = gy + rate * inner
        gh2_ref[own, :] = gh
        gh2_out(i).start()
        share2.put(i, gh.astype(half_type))
        gvec_ref[0:1, :] += jnp.sum(gh, axis=0, keepdims=True)
        gvec_ref[1:2, :] += jnp.sum(gy, axis=0, keepdims=True)
        gvec_ref[4:5, :] += jnp.sum(gn * unit, axis=0, keepdims=True)
        gvec_ref[5:6, :] += jnp.sum(gn, axis=0, keepdims=True)

    def mlp_step(i, carry):
        mlp_block(i)
        return carry

    lax.fori_loop(0, blocks, mlp_step, 0)
    rowsum3 = RowSum(
        down_ref.reshape(blocks, BLOCK, width), given3, sent3, crossed3, sum3_sems
    )
    rowsum3.give(0)

    late = max(blocks + 2, chunks)

    def tail_step(i, carry):
        @pl.when(i < blocks)
        def _():
            back_block(i)

        @pl.when((i >= 2) & (i < blocks + 2))
        def _():
            prepare(i - 2)

        @pl.when(i < chunks)
        def _():
            weight_grads(i)

        @pl.when(i == 0)
        def _():
            rowsum3.cross(0)

        return carry

    lax.fori_loop(0, late, tail_step, 0)
    kt_out = pltpu.make_async_copy(kt_ref, kt_hbm, whole_sems.at[len(whole)])
    kt_out.start()
    for kind in range(2):
        made_out(kind, chunks - 1).wait()
    rowsum3.ready(0)
    first_out = [
        pltpu.make_async_copy(ref.at[0], first_hbm.at[k], whole_sems.at[len(whole) + 1 + k])
        for k, ref in enumerate((sent3, crossed3))
    ]
    for copy in first_out:
        copy.start()

    def copied(i, carry):
        down_out(i).wait()
        gh2_out(i).wait()
        ga_out(i).wait()
        goa_out(i).wait()
        return carry

    lax.fori_loop(0, blocks, copied, 0)
    for copy in whole + [kt_out] + first_out:
        copy.wait()
    for piece in attend + dense:
        piece.sent()
    rowsum2.finish()
    rowsum3.finish()
    share.finish(blocks)
    share2.finish(blocks)

    def spread_out(block, carry):
        spread(0, block, tensor, mate).wait_send()
        spread(1, block, tensor, other).wait_send()
        spread(2, block, other, mate).wait_send()
        return carry

    lax.fori_loop(0, count, spread_out, 0)

    def mixed_out(i, carry):
        for kind, peer, half_rows in peers:
            mixed_copy(kind, i, tensor, peer, half_rows).wait_send()
        return carry

    lax.fori_loop(0, blocks, mixed_out, 0)

    def sent_small(k, carry):
        small_copy(me, (me + k) % count).wait_send()
        return carry

    lax.fori_loop(1, count, sent_small, 0)


class Scatter:
    def __init__(self, view, stage, taken, sems, count):
        self.view, self.stage, self.taken = view, stage, taken
        self.sems, self.count = sems, count
        self.slots = stage.shape[1]
        self.pos = ring_pos(lax.axis_index("dp"), count)
        self.tensor = lax.axis_index("tensor")

    def _copy(self, way, step):
        sign = 1 - 2 * way
        return pltpu.make_async_remote_copy(
            src_ref=self.stage.at[way, step % self.slots],
            dst_ref=self.taken.at[way, step],
            send_sem=self.sems.at[2 * way, step],
            recv_sem=self.sems.at[2 * way + 1, step],
            device_id=(ring_at(self.pos + sign, self.count), self.tensor),
            device_id_type=MESH,
        )

    def begin(self):
        for way in range(2):
            self.stage[way, 0] = self.view(way, 0).astype(half_type)
            self._copy(way, 0).start()

    def advance(self, step):
        for way in range(2):
            self._copy(way, step - 1).wait_recv()
            total = self.taken[way, step - 1].astype(full_type) + self.view(way, step)

            @pl.when(step >= self.slots)
            def _(way=way):
                self._copy(way, step - self.slots).wait_send()

            self.stage[way, step % self.slots] = total.astype(half_type)
            self._copy(way, step).start()

    def total(self, way):
        last = self.count - 2
        self._copy(way, last).wait_recv()
        return self.taken[way, last].astype(full_type) + self.view(way, last + 1)

    def finish(self):
        for step in range(max(self.count - 1 - self.slots, 0), self.count - 1):
            for way in range(2):
                self._copy(way, step).wait_send()


def sent_block(pos, way, step, count):
    return ring_at(pos - (1 - 2 * way) * (1 + step), count)


class Put:
    def __init__(self, held, result, sems):
        self.held, self.result, self.sems = held, result, sems
        self.half = held.shape[0] // sems.shape[1]
        self.dp, tensor = lax.axis_index("dp"), lax.axis_index("tensor")
        self.core = tensor % 2
        self.mate = tensor - tensor % 2 + (tensor + 1) % 2

    def own(self, i):
        return pl.ds(pl.multiple_of(i * self.half, self.half), self.half)

    def _rows(self, i, core):
        return pl.ds(pl.multiple_of((2 * i + core) * self.half, self.half), self.half)

    def _here(self, i):
        target = self.result.at[self._rows(i, self.core), :]
        return pltpu.make_async_copy(self.held.at[self.own(i), :], target, self.sems.at[0, i])

    def _there(self, i, core):
        return pltpu.make_async_remote_copy(
            src_ref=self.held.at[self.own(i), :],
            dst_ref=self.result.at[self._rows(i, core), :],
            send_sem=self.sems.at[1, i],
            recv_sem=self.sems.at[2, i],
            device_id=(self.dp, self.mate),
            device_id_type=MESH,
        )

    def put(self, i, value):
        self.held[self.own(i), :] = value
        self._here(i).start()
        self._there(i, self.core).start()

    def left(self, i):
        self._here(i).wait()
        self._there(i, self.core).wait_send()

    def arrived(self, i):
        self._there(i, 1 - self.core).wait_recv()


def back_kernel(
    count, ga_hbm, o_hbm, qb_hbm, ka_hbm, va_hbm, goa_hbm, kt_hbm, w_hbm, up_hbm, dn_hbm, down_hbm,
    h2_hbm, gh2_hbm, own_hbm, a1_hbm, first_hbm, vec_ref, gbias_ref, gvec_ref,
    layer_hbm, tg_hbm, dense_ref, sum_ref, small_ref,
    ga_ref, o_ref, qb_ref, ka_ref, va_ref, w_ref, wide_ref, gh_ref, own_ref, goa_ref, kt_ref, gqt_ref, gqkv_ref, put_ref,
    given, sent, crossed, term2, given2, sent2, crossed2,
    terms, stage, taken, grads, stage2, taken2, small_mine, small_taken, small_mate,
    sum_sems, sum2_sems, put_sems, put2_sems, scatter_sems, scatter2_sems, small_sems, mate_sems,
    local_sems, terms_sems, whole_sems,
):
    total_rows, width = ga_ref.shape
    local_width = o_ref.shape[1]
    heads = local_width // HD
    blocks = total_rows // BLOCK
    half = BLOCK // 2
    wide = width // count
    hops = count - 1
    lanes = small_ref.shape[1] - local_width
    fold = lanes // wide
    me, tensor = lax.axis_index("dp"), lax.axis_index("tensor")
    mate = tensor - tensor % 2 + (tensor + 1) % 2
    pos = ring_pos(me, count)
    greeted = greet(tensor_peers() + dp_peers(count))

    def own_rows(i):
        return pl.ds(pl.multiple_of(i * half, half), half)

    def place(block):
        return pl.ds(pl.multiple_of(block * wide, wide), wide)

    def own_fetch(source, target, sems):
        return lambda i: pltpu.make_async_copy(
            source.at[own_rows(i), :], target.at[own_rows(i), :], sems.at[i]
        )

    ga_in = fetch(ga_hbm, ga_ref, local_sems.at[0])
    down_in = fetch(down_hbm, wide_ref, local_sems.at[1])
    a1_in = fetch(a1_hbm, wide_ref, local_sems.at[2])
    h2_in = own_fetch(h2_hbm, gh_ref, local_sems.at[3])
    gh2_in = own_fetch(gh2_hbm, gh_ref, local_sems.at[4])
    own_in = own_fetch(own_hbm, own_ref, local_sems.at[5])

    def term_in(way, step):
        rows = place(sent_block(pos, way, step, count))
        source = (up_hbm, dn_hbm)[way].at[rows, :]
        return pltpu.make_async_copy(
            source, terms.at[way, step % 2], terms_sems.at[way, step % 2]
        )

    def each(copy):
        def start(i, carry):
            copy(i).start()
            return carry

        lax.fori_loop(0, blocks, start, 0)

    for step in range(2):
        for way in range(2):
            term_in(way, step).start()
    whole = [
        pltpu.make_async_copy(source, target, whole_sems.at[k])
        for k, (source, target) in enumerate(
            (
                (qb_hbm, qb_ref), (ka_hbm, ka_ref), (va_hbm, va_ref), (goa_hbm, goa_ref),
                (kt_hbm, kt_ref), (first_hbm.at[0], sent.at[0]), (first_hbm.at[1], crossed.at[0]),
                (o_hbm, o_ref), (w_hbm, w_ref),
            )
        )
    ]
    for copy in whole[:-4]:
        copy.start()
    each(down_in)
    for copy in whole[-4:-2]:
        copy.start()
    each(h2_in)
    for copy in whole[-2:]:
        copy.start()
    each(ga_in)
    each(own_in)
    small_mine[:, :width] = gvec_ref[...]
    ratio = gbias_ref.shape[1] // local_width
    for r in range(ratio):
        small_mine[1 + r : 2 + r, width:] = gbias_ref[0:1, r * local_width : (r + 1) * local_width]
    small_mine[1 + ratio :, width:] = jnp.zeros((7 - ratio, local_width), full_type)
    greeted()

    pieces = stage.shape[0]
    part = terms.shape[3] // pieces

    def term_view(piece):
        columns = slice(piece * part, (piece + 1) * part)
        return lambda way, step: terms[way, step % 2, :, columns]

    scatters = [
        Scatter(term_view(p), stage.at[p], taken.at[p], scatter_sems.at[p], count)
        for p in range(pieces)
    ]

    def terms_ready(step):
        for way in range(2):
            term_in(way, step).wait()

    def terms_next(step):
        @pl.when(step <= hops)
        def _():
            for way in range(2):
                term_in(way, step).start()

    rowsum = RowSum(wide_ref.reshape(blocks, BLOCK, width), given, sent, crossed, sum_sems, 1)
    layer = Put(put_ref, layer_hbm, put_sems)
    terms_ready(0)
    for scatter in scatters:
        scatter.begin()
    terms_next(2)

    lane = lax.broadcasted_iota(jnp.int32, (BLOCK, LANES), 1)
    low_half = lane < HD
    gqt_ref[...] = jnp.zeros_like(gqt_ref)
    down_in(0).wait()
    for i in range(1, 3):
        down_in(i).wait()
        rowsum.give(i)
    for copy in whole[:-2]:
        copy.wait()

    def output_block(i):
        h2_in(i).wait()
        total = gh_ref[own_rows(i), :] + rowsum.total(i) + vec_ref[1:2, :]
        layer.put(i, total.astype(half_type))
        gh2_in(i).start()

    per = -(-hops // blocks)

    def between(j, piece):
        if piece == 0:

            @pl.when(j >= 1)
            def _():
                output_block(j - 1)

            @pl.when(j < blocks - 3)
            def _():
                down_in(j + 3).wait()
                rowsum.give(j + 3)

            @pl.when(j < blocks - 1)
            def _():
                rowsum.cross(j + 1)

        for t in range(per):
            hop = j * per + t

            @pl.when((hop >= 1) & (hop < hops))
            def _(hop=hop):
                if piece == 0:
                    terms_ready(hop)
                scatters[piece].advance(hop)
                if piece == pieces - 1:
                    terms_next(hop + 2)

    def keys_block(j, carry):
        rows = pl.ds(pl.multiple_of(j * BLOCK, BLOCK), BLOCK)
        for head in range(heads):
            scores = dot(ka_ref[head, rows, :], qb_ref[head], 1, 1)
            probs = jnp.exp(scores)
            gp = dot(va_ref[head, rows, :], goa_ref[head], 1, 1)
            gs = (probs * gp).astype(half_type)
            gv = dot(probs.astype(half_type), goa_ref[head])
            gk = dot(gs, qb_ref[head])
            own = slice(head * HD, head * HD + HD)
            gqt_ref[own, :] += dot(kt_ref[own, rows], gs)
            if head % 2 == 0:
                gk_even, gv_even = gk, gv
            else:
                for k, value in ((1, (gk_even, gk)), (2, (gv_even, gv))):
                    base = k * local_width + head // 2 * LANES
                    gqkv_ref[rows, base : base + LANES] = jnp.where(low_half, *value).astype(
                        half_type
                    )
            if (head + 1) * pieces % heads == 0:
                between(j, (head + 1) * pieces // heads - 1)
        return carry

    lax.fori_loop(0, blocks, keys_block, 0)

    def turn(i, carry):
        rows = pl.ds(pl.multiple_of(i * BLOCK, BLOCK), BLOCK)
        gqkv_ref[rows, :local_width] = (gqt_ref[:, rows].T * HD**-0.5).astype(half_type)
        return carry

    rowsum2 = RowSum(term2, given2, sent2, crossed2, sum2_sems)

    def norm_term(i):
        rows = pl.ds(pl.multiple_of(i * BLOCK, BLOCK), BLOCK)
        rowsum2.free(i)
        term2[i % term2.shape[0]] = dot(gqkv_ref[rows, :], w_ref[...], 1, 1).astype(half_type)
        rowsum2.give(i)

    turn(0, 0)
    whole[-1].wait()
    norm_term(0)
    rowsum.gone()
    each(a1_in)
    turn(1, 0)
    norm_term(1)
    rowsum2.cross(0)
    lax.fori_loop(2, blocks, turn, 0)
    ones = jnp.ones((8, total_rows), half_type)
    bias_query = dot(ones, gqkv_ref[:, :local_width])
    small_mine[0:1, width:] = bias_query[0:1, :]

    def small_copy(kind, source, peer):
        window = pl.ds(pl.multiple_of(peer // fold * lanes, lanes), lanes)
        return pltpu.make_async_remote_copy(
            src_ref=small_mine.at[:, pl.ds(width, local_width) if kind else window],
            dst_ref=small_taken.at[source, :, pl.ds(lanes, local_width) if kind else pl.ds(0, lanes)],
            send_sem=small_sems.at[2 * kind, peer],
            recv_sem=small_sems.at[2 * kind + 1, source],
            device_id=(peer, tensor),
            device_id_type=MESH,
        )

    def send_small(kind):
        def send(k, carry):
            small_copy(kind, me, (me + k) % count).start()
            return carry

        lax.fori_loop(1, count, send, 0)

    send_small(1)

    def arrived_a1(i, carry):
        a1_in(i).wait()
        ga_in(i).wait()
        return carry

    lax.fori_loop(0, blocks, arrived_a1, 0)

    def weight_grads(c, carry):
        columns = pl.ds(pl.multiple_of(c * BLOCK, BLOCK), BLOCK)
        grads[columns, : 3 * local_width] = dot(wide_ref[:, columns], gqkv_ref[...], 0, 0)
        grads[columns, 3 * local_width :] = dot(ga_ref[:, columns], o_ref[...], 0, 0)
        return carry

    chunks = width // BLOCK
    whole[-2].wait()
    rowsum2.cross(1)
    lax.fori_loop(0, chunks, weight_grads, 0)
    side = grads.shape[1] // 2

    def grads_view(way, step):
        return grads[
            place(sent_block(pos, way, step, count)), way * side : (way + 1) * side
        ]

    scatter2 = Scatter(grads_view, stage2, taken2, scatter2_sems, count)
    scatter2.begin()
    output_block(blocks - 1)

    def layer_left(i, carry):
        layer.left(i)
        layer.arrived(i)
        return carry

    lax.fori_loop(0, blocks, layer_left, 0)
    result = Put(put_ref, tg_hbm, put2_sems)

    def norm_block(i):
        gn = rowsum2.total(i)
        own_in(i).wait()
        gh2_in(i).wait()
        unit, rate = normalized(own_ref[own_rows(i), :].astype(full_type))
        e = gn * vec_ref[2:3, :]
        inner = e - jnp.mean(e, axis=-1, keepdims=True)
        inner = inner - unit * jnp.mean(e * unit, axis=-1, keepdims=True)
        result.put(i, (gh_ref[own_rows(i), :] + rate * inner).astype(half_type))
        small_mine[2:3, :width] += jnp.sum(gn * unit, axis=0, keepdims=True)
        small_mine[3:4, :width] += jnp.sum(gn, axis=0, keepdims=True)

    def end_step(i, carry):
        @pl.when(i < blocks - 2)
        def _():
            norm_term(i + 2)

        norm_block(i)

        @pl.when(i < blocks - 2)
        def _():
            rowsum2.cross(i + 2)

        for t in range(per):
            hop = i * per + t + 1

            @pl.when(hop < hops)
            def _(hop=hop):
                scatter2.advance(hop)

        return carry

    lax.fori_loop(0, blocks, end_step, 0)
    send_small(0)
    terms_ready(hops)
    for way in range(2):
        for p, scatter in enumerate(scatters):
            dense_ref[way, :, p * part : (p + 1) * part] = scatter.total(way)
        total = scatter2.total(way)
        for k in range(2):
            sum_ref[2 * way + k] = total[:, k * local_width : (k + 1) * local_width]
    for kind in range(2):
        window = pl.ds(pl.multiple_of(me // fold * lanes, lanes), lanes)
        here = slice(lanes, lanes + local_width) if kind else slice(0, lanes)
        small_taken[me, :, here] = small_mine[:, width:] if kind else small_mine[:, window]

        def take(k, carry, kind=kind):
            source = (me + k) % count
            small_copy(kind, source, source).wait_recv()
            return carry

        lax.fori_loop(1, count, take, 0)
    total = small_taken[0]
    for j in range(1, count):
        total = total + small_taken[j]
    small_ref[...] = total
    pair = pltpu.make_async_remote_copy(
        src_ref=small_ref.at[:, pl.ds(0, lanes)],
        dst_ref=small_mate,
        send_sem=mate_sems.at[0],
        recv_sem=mate_sems.at[1],
        device_id=(me, mate),
        device_id_type=MESH,
    )
    pair.start()
    pair.wait()
    small_ref[:, :lanes] = total[:, :lanes] + small_mate[...]

    def result_left(i, carry):
        result.left(i)
        result.arrived(i)
        return carry

    lax.fori_loop(0, blocks, result_left, 0)
    for scatter in scatters + [scatter2]:
        scatter.finish()
    rowsum.finish(given=False)
    rowsum2.finish()
    for kind in range(2):

        def done(k, carry, kind=kind):
            small_copy(kind, me, (me + k) % count).wait_send()
            return carry

        lax.fori_loop(1, count, done, 0)


def permuted(x, owner, back):
    rows, width = x.shape
    count = owner.shape[0]
    order = jnp.argsort(owner) if back else owner
    return jnp.take(x.reshape(rows, count, -1), order, axis=1).reshape(rows, width)


def adamw_step(weight, first, second, grad, rate, decay):
    first_next = first_decay * first + (1.0 - first_decay) * grad
    second_next = second_decay * second + (1.0 - second_decay) * grad * grad
    first_hat = first_next / (1.0 - first_decay**STEP)
    second_hat = second_next / (1.0 - second_decay**STEP)
    update = first_hat / (jnp.sqrt(second_hat) + adam_epsilon) + decay * weight
    return (first_next, second_next, weight - rate * update)


def last_kernel(rates, owner_ref, *refs):
    count = owner_ref.shape[0]
    given, refs = refs[:5], refs[5:]
    layer, grad, weight_sum, dense_sum, small = given
    state, refs = refs[:15], refs[15:]
    results, outs = refs[:2], refs[2:]

    def step(k, grad, at=(Ellipsis,)):
        new = adamw_step(*(ref[at] for ref in state[3 * k : 3 * k + 3]), grad, *rates[k])
        for ref, value in zip(outs[3 * k : 3 * k + 3], new):
            ref[at] = value

    wide = layer.shape[1] // count
    if wide % LANES == 0:
        for j in range(count):
            natural = pl.ds(pl.multiple_of(owner_ref[j] * wide, wide), wide)
            for x, y in zip((layer, grad), results):
                y[:, natural] = x[:, j * wide : (j + 1) * wide]
    else:
        for x, y in zip((layer, grad), results):
            y[...] = x[...]
    step(0, weight_sum[0:3])
    step(1, weight_sum[3])
    ratio, local_width = state[6].shape[2:]
    for r in range(ratio):
        step(
            2,
            dense_sum[:, :, r * local_width : (r + 1) * local_width],
            (slice(None), slice(None), r, slice(None)),
        )
    me = lax.axis_index("dp")
    lanes = small.shape[1] - local_width

    def chosen(x, start, size):
        row = lax.broadcasted_iota(jnp.int32, (x.shape[1], size), 0)
        column = lax.broadcasted_iota(jnp.int32, (x.shape[1], size), 1)
        pick = jnp.where(row == column + start, 1.0, 0.0).astype(half_type)
        return sum(dot(part.astype(half_type), pick) for part in three_parts(x))

    narrow, wide = state[9].shape[1], state[12].shape[1]
    step(3, chosen(small[:, lanes:], owner_ref[me] * narrow, narrow)[: 1 + ratio])
    step(4, chosen(small[:, :lanes], me % (lanes // wide) * wide, wide)[:6])


def last(owner, layer_output, tokens_grad, weight_sum, dense_sum, small_sum, *state):
    steps = 4 if dense_sum.shape[1] % 128 == 0 else 1
    rates = (
        (matrix_rate, matrix_decay),
        (output_rate, matrix_decay),
        (matrix_rate, matrix_decay),
        (bias_rate, 0.0),
        (vector_rate, 0.0),
    )

    def spec(x, dim):
        shape = tuple(n // steps if k == dim else n for k, n in enumerate(x.shape))
        return pl.BlockSpec(shape, lambda i, *_: tuple(i if k == dim else 0 for k in range(x.ndim)))

    dims = [0, 0, 1, 1, None] + [1] * 3 + [0] * 3 + [1] * 3 + [None] * 6
    operands = (layer_output, tokens_grad, weight_sum, dense_sum, small_sum) + state
    specs = [spec(x, dim) for x, dim in zip(operands, dims)]
    outs = operands[:2] + state
    return pl.pallas_call(
        functools.partial(last_kernel, rates),
        out_shape=[jax.ShapeDtypeStruct(x.shape, x.dtype) for x in outs],
        grid_spec=pltpu.PrefetchScalarGridSpec(
            num_scalar_prefetch=1, grid=(steps,), in_specs=specs, out_specs=specs[:2] + specs[5:]
        ),
        compiler_params=pltpu.CompilerParams(vmem_limit_bytes=60 * 2**20),
    )(owner, *operands)


def call(kernel, collective, outs, scratch, operands, spaces, limit=62):
    spec = {
        "s": pl.BlockSpec(memory_space=pltpu.SMEM),
        "v": pl.BlockSpec(memory_space=pltpu.VMEM),
        "h": pl.BlockSpec(memory_space=pl.ANY),
    }
    return pl.pallas_call(
        kernel,
        out_shape=[jax.ShapeDtypeStruct(shape, dtype) for shape, dtype in outs],
        in_specs=[spec[c] for c in spaces[0]],
        out_specs=[spec[c] for c in spaces[1]],
        scratch_shapes=scratch,
        compiler_params=pltpu.CompilerParams(
            collective_id=collective, has_side_effects=True, vmem_limit_bytes=limit * 2**20
        ),
    )(*operands)


def dma(*shape):
    return pltpu.SemaphoreType.DMA(shape)


def local(
    tokens,
    lengths,
    owner,
    attend_master,
    attend_first,
    attend_second,
    output_master,
    output_first,
    output_second,
    dense_master,
    dense_first,
    dense_second,
    bias_master,
    bias_first,
    bias_second,
    vector_master,
    vector_first,
    vector_second,
    cotangent,
):
    count = owner.shape[0]
    rows, width = tokens.shape
    local_width = output_master.shape[1]
    ratio = dense_master.shape[2]
    hidden = ratio * local_width
    heads = local_width // HD
    blocks = rows // BLOCK
    half = BLOCK // 2
    wide = width // count
    lanes = max(LANES, wide)
    tok, cot = tokens, cotangent
    if wide % LANES:
        tok, cot = (permuted(x, owner, False) for x in (tokens, cotangent))
    row_sum = [pltpu.VMEM((blocks, half, width), half_type)] * 3
    two_terms = pltpu.VMEM((2, BLOCK, width), half_type)
    heads_shape = (heads, rows, LANES)
    small = (8, lanes + local_width)
    a1, ga, h2, own, qb, ka, va, o, w, gh2, down, up, dn, goa, kt, first, vec, gbias, gvec = call(
        functools.partial(front_kernel, count),
        0,
        [
            ((rows, width), half_type),
            ((rows, width), half_type),
            ((rows // 2, width), full_type),
            ((rows // 2, width), half_type),
            (heads_shape, half_type),
            (heads_shape, half_type),
            (heads_shape, half_type),
            ((rows, local_width), half_type),
            ((width, 3 * local_width), half_type),
            ((rows // 2, width), full_type),
            ((rows, width), half_type),
            ((width, hidden), full_type),
            ((width, hidden), full_type),
            (heads_shape, half_type),
            ((local_width, rows), half_type),
            ((2, half, width), half_type),
            ((8, width), full_type),
            ((8, hidden), full_type),
            ((8, width), full_type),
        ],
        [
            pltpu.VMEM((rows // 2, width), half_type),
            *[pltpu.VMEM(heads_shape, half_type)] * 3,
            pltpu.VMEM((rows, local_width), half_type),
            pltpu.VMEM((width, 3 * local_width), half_type),
            pltpu.VMEM((width, width), half_type),
            pltpu.VMEM((rows // 2, width), full_type),
            pltpu.VMEM((rows, width), half_type),
            *[pltpu.VMEM((rows, hidden), half_type)] * 2,
            pltpu.VMEM((2, BLOCK, hidden), full_type),
            *[pltpu.VMEM((rows, width), half_type)] * 2,
            pltpu.VMEM((2, width, hidden), half_type),
            pltpu.VMEM((rows, width), half_type),
            pltpu.VMEM(heads_shape, half_type),
            pltpu.VMEM((local_width, rows), half_type),
            pltpu.VMEM((8, local_width), full_type),
            pltpu.VMEM((1, hidden), full_type),
            pltpu.VMEM(small, full_type),
            pltpu.VMEM((count,) + small, full_type),
            pltpu.VMEM((blocks, half, width), half_type),
            two_terms,
            *row_sum,
            *[pltpu.VMEM((1, half, width), half_type)] * 3,
            dma(6, 4, count // 2),
            dma(2, count),
            dma(6, count),
            dma(6, blocks),
            dma(4, blocks),
            dma(2, blocks),
            dma(2, blocks),
            dma(8, blocks),
            dma(9),
            dma(2, width // BLOCK),
            dma(4, 1),
        ],
        (
            lengths, owner, tok, cot, attend_master, output_master, dense_master, vector_master,
            bias_master,
        ),
        ("sshhvvvvv", "h" * 16 + "vvv"),
    )
    pieces = 2
    row_blocks = pltpu.VMEM((blocks, half, width), half_type)
    row_slots = pltpu.VMEM((min(3, blocks), half, width), half_type)
    part, side = hidden // pieces, 2 * local_width
    layer_output, tokens_grad, dense_sum, weight_sum, small_sum = call(
        functools.partial(back_kernel, count),
        1,
        [
            ((rows, width), half_type),
            ((rows, width), half_type),
            ((2, wide, hidden), full_type),
            ((4, wide, local_width), full_type),
            ((8, lanes + local_width), full_type),
        ],
        [
            pltpu.VMEM((rows, width), half_type),
            pltpu.VMEM((rows, local_width), half_type),
            *[pltpu.VMEM(heads_shape, half_type)] * 3,
            pltpu.VMEM((width, 3 * local_width), half_type),
            pltpu.VMEM((rows, width), half_type),
            pltpu.VMEM((rows // 2, width), full_type),
            pltpu.VMEM((rows // 2, width), half_type),
            pltpu.VMEM(heads_shape, half_type),
            pltpu.VMEM((local_width, rows), half_type),
            pltpu.VMEM((local_width, rows), full_type),
            pltpu.VMEM((rows, 3 * local_width), half_type),
            pltpu.VMEM((rows // 2, width), half_type),
            row_blocks,
            row_slots,
            row_blocks,
            two_terms,
            row_blocks,
            row_slots,
            row_blocks,
            pltpu.VMEM((2, 2, wide, hidden), full_type),
            pltpu.VMEM((pieces, 2, 2, wide, part), half_type),
            pltpu.VMEM((pieces, 2, count - 1, wide, part), half_type),
            pltpu.VMEM((width, 4 * local_width), full_type),
            pltpu.VMEM((2, 2, wide, side), half_type),
            pltpu.VMEM((2, count - 1, wide, side), half_type),
            pltpu.VMEM((8, width + local_width), full_type),
            pltpu.VMEM((count, 8, lanes + local_width), full_type),
            pltpu.VMEM((8, lanes), full_type),
            dma(4, blocks),
            dma(4, blocks),
            dma(3, blocks),
            dma(3, blocks),
            dma(pieces, 4, count - 1),
            dma(4, count - 1),
            dma(4, count),
            dma(2),
            dma(6, blocks),
            dma(2, 2),
            dma(9),
        ],
        (
            ga, o, qb, ka, va, goa, kt, w, up, dn, down, h2, gh2, own, a1, first, vec, gbias,
            gvec,
        ),
        ("h" * 16 + "vvv", "hhvvv"),
    )
    if wide % LANES:
        layer_output, tokens_grad = (permuted(x, owner, True) for x in (layer_output, tokens_grad))
    return tuple(
        last(
            owner, layer_output, tokens_grad, weight_sum, dense_sum, small_sum,
            attend_master, attend_first, attend_second,
            output_master, output_first, output_second,
            dense_master, dense_first, dense_second,
            bias_master, bias_first, bias_second,
            vector_master, vector_first, vector_second,
        )
    )


def solution(mesh):
    return jax.shard_map(
        local,
        mesh=mesh,
        in_specs=(
            P("dp", None),
            P("dp", None),
            P(),
            P(None, "dp", "tensor"),
            P(None, "dp", "tensor"),
            P(None, "dp", "tensor"),
            P("dp", "tensor"),
            P("dp", "tensor"),
            P("dp", "tensor"),
            P(None, "dp", None, "tensor"),
            P(None, "dp", None, "tensor"),
            P(None, "dp", None, "tensor"),
            P(None, ("tensor", "dp")),
            P(None, ("tensor", "dp")),
            P(None, ("tensor", "dp")),
            P(None, "dp"),
            P(None, "dp"),
            P(None, "dp"),
            P("dp", None),
        ),
        out_specs=(
            P("dp", None),
            P("dp", None),
            P(None, "dp", "tensor"),
            P(None, "dp", "tensor"),
            P(None, "dp", "tensor"),
            P("dp", "tensor"),
            P("dp", "tensor"),
            P("dp", "tensor"),
            P(None, "dp", None, "tensor"),
            P(None, "dp", None, "tensor"),
            P(None, "dp", None, "tensor"),
            P(None, ("tensor", "dp")),
            P(None, ("tensor", "dp")),
            P(None, ("tensor", "dp")),
            P(None, "dp"),
            P(None, "dp"),
            P(None, "dp"),
        ),
        check_vma=False,
    )
```

```python
import functools

import jax
import jax.numpy as jnp
from jax import lax
from jax.experimental import pallas as pl
from jax.experimental.pallas import tpu as pltpu
from jax.sharding import PartitionSpec as P

HD = 64
STEP = 10
LANES = 128
BLOCK = 256
MESH = pl.DeviceIdType.MESH
BIG = 2.0**50

norm_epsilon = 1e-06
first_decay = 0.9
second_decay = 0.95
adam_epsilon = 1e-08
matrix_rate = 0.1
output_rate = 0.5
bias_rate = 0.5
vector_rate = 1.0
matrix_decay = 0.05

half_type = jnp.bfloat16
full_type = jnp.float32


def dot(left, right, left_dim=1, right_dim=0):
    return lax.dot_general(
        left, right, (((left_dim,), (right_dim,)), ((), ())), preferred_element_type=full_type
    )


def ring_pos(place, count):
    column = place % 2
    row = place // 2
    return row * (1 - column) + (count - 1 - row) * column


def ring_at(pos, count):
    near = (pos + 2 * count) % count
    down = near // (count // 2)
    return 2 * near * (1 - down) + (2 * count - 1 - 2 * near) * down


def normalized(x):
    center = jnp.mean(x, axis=-1, keepdims=True)
    offset = x - center
    spread = jnp.mean(offset * offset, axis=-1, keepdims=True)
    rate = lax.rsqrt(spread + norm_epsilon)
    return offset * rate, rate


class Gather:
    def __init__(self, view, width, sems, count):
        self.view, self.width, self.sems, self.count = view, width, sems, count
        self.steps = count // 2
        self.pos = ring_pos(lax.axis_index("dp"), count)
        self.tensor = lax.axis_index("tensor")

    def _copy(self, way, step, hops):
        sign = 1 - 2 * way
        part = (0, self.width)
        if step == self.steps - 1:
            part = (way * (self.width // 2), self.width // 2)
        block = self.view(ring_at(self.pos - sign * hops, self.count), *part)
        return pltpu.make_async_remote_copy(
            src_ref=block,
            dst_ref=block,
            send_sem=self.sems.at[2 * way, step],
            recv_sem=self.sems.at[2 * way + 1, step],
            device_id=(ring_at(self.pos + sign, self.count), self.tensor),
            device_id_type=MESH,
        )

    def advance(self, step):
        if step:
            for way in range(2):
                self._copy(way, step - 1, step).wait_recv()
        if step < self.steps:
            for way in range(2):
                self._copy(way, step, step).start()

    def sent(self):
        for step in range(self.steps):
            for way in range(2):
                self._copy(way, step, step).wait_send()


class RowSum:
    def __init__(self, term, given, sent, crossed, sems, first=0):
        self.term, self.given, self.sent_ref, self.crossed = term, given, sent, crossed
        self.slots, self.sent_slots, self.blocks = term.shape[0], sent.shape[0], given.shape[0]
        self.sems, self.first = sems, first
        self.half = given.shape[1]
        self.dp, tensor = lax.axis_index("dp"), lax.axis_index("tensor")
        self.core = tensor % 2
        self.mate = tensor - tensor % 2 + (tensor + 1) % 2
        self.other = (tensor + 2) % 4

    def rows(self, core):
        return pl.ds(pl.multiple_of(core * self.half, self.half), self.half)

    def _give(self, i):
        return pltpu.make_async_remote_copy(
            src_ref=self.term.at[i % self.slots, self.rows(1 - self.core), :],
            dst_ref=self.given.at[i],
            send_sem=self.sems.at[0, i],
            recv_sem=self.sems.at[1, i],
            device_id=(self.dp, self.mate),
            device_id_type=MESH,
        )

    def _cross(self, i):
        return pltpu.make_async_remote_copy(
            src_ref=self.sent_ref.at[i % self.sent_slots],
            dst_ref=self.crossed.at[i],
            send_sem=self.sems.at[2, i],
            recv_sem=self.sems.at[3, i],
            device_id=(self.dp, self.other),
            device_id_type=MESH,
        )

    def free(self, i):
        if self.slots < self.blocks:

            @pl.when(i >= self.slots)
            def _():
                self._give(i - self.slots).wait_send()

    def give(self, i):
        self._give(i).start()

    def cross(self, i):
        self._give(i).wait_recv()
        mine = self.term[i % self.slots, self.rows(self.core), :].astype(full_type)
        if self.sent_slots < self.blocks:

            @pl.when(i >= self.sent_slots + self.first)
            def _():
                self._cross(i - self.sent_slots).wait_send()

        total = mine + self.given[i].astype(full_type)
        self.sent_ref[i % self.sent_slots] = total.astype(half_type)
        self._cross(i).start()

    def total(self, i):
        if self.first:

            @pl.when(i >= self.first)
            def _():
                self._cross(i).wait_recv()

        else:
            self._cross(i).wait_recv()
        mine = self.sent_ref[i % self.sent_slots].astype(full_type)
        return mine + self.crossed[i].astype(full_type)

    def ready(self, i):
        self._cross(i).wait_recv()

    def gone(self):
        def given(i, carry):
            self._give(i).wait_send()
            return carry

        lax.fori_loop(max(self.blocks - self.slots, self.first), self.blocks, given, 0)

    def finish(self, given=True):
        if given:
            self.gone()

        def crossed(i, carry):
            self._cross(i).wait_send()
            return carry

        lax.fori_loop(max(self.blocks - self.sent_slots, self.first), self.blocks, crossed, 0)


class Share:
    def __init__(self, ref, sems):
        self.ref, self.sems = ref, sems
        self.dp, tensor = lax.axis_index("dp"), lax.axis_index("tensor")
        self.core = tensor % 2
        self.mate = tensor - tensor % 2 + (tensor + 1) % 2

    def rows(self, i, core):
        half = BLOCK // 2
        return pl.ds(pl.multiple_of(i * BLOCK + core * half, half), half)

    def _copy(self, i, core):
        piece = self.ref.at[self.rows(i, core), :]
        return pltpu.make_async_remote_copy(
            src_ref=piece,
            dst_ref=piece,
            send_sem=self.sems.at[0, i],
            recv_sem=self.sems.at[1, i],
            device_id=(self.dp, self.mate),
            device_id_type=MESH,
        )

    def put(self, i, value):
        self.ref[self.rows(i, self.core), :] = value
        self._copy(i, self.core).start()

    def arrived(self, i):
        self._copy(i, 1 - self.core).wait_recv()

    def finish(self, blocks):
        def done(i, carry):
            self._copy(i, self.core).wait_send()
            return carry

        lax.fori_loop(0, blocks, done, 0)


def greet(peers):
    barrier = pltpu.get_barrier_semaphore()
    for peer in peers:
        pl.semaphore_signal(barrier, inc=1, device_id=peer, device_id_type=MESH)
    return lambda: pl.semaphore_wait(barrier, len(peers))


def tensor_peers():
    dp, tensor = lax.axis_index("dp"), lax.axis_index("tensor")
    return [(dp, tensor - tensor % 2 + (tensor + 1) % 2), (dp, (tensor + 2) % 4)]


def ring_peers(count):
    dp, tensor = lax.axis_index("dp"), lax.axis_index("tensor")
    pos = ring_pos(dp, count)
    return [(ring_at(pos + 1, count), tensor), (ring_at(pos - 1, count), tensor)]


def dp_peers(count):
    dp, tensor = lax.axis_index("dp"), lax.axis_index("tensor")
    return [((dp + k) % count, tensor) for k in range(1, count)]


def three_parts(x):
    high = x.astype(half_type).astype(full_type)
    middle = (x - high).astype(half_type).astype(full_type)
    return high, middle, x - high - middle


def gelu_parts(z):
    phi = 0.5 + 0.5 * lax.erf(z * (0.5**0.5))
    slope = phi + z * (jnp.exp(-0.5 * z * z) * (2.0 * 3.141592653589793) ** -0.5)
    return z * phi, slope


def fetch(source, target, sems):
    def copy(i):
        rows = pl.ds(pl.multiple_of(i * BLOCK, BLOCK), BLOCK)
        return pltpu.make_async_copy(source.at[rows, :], target.at[rows, :], sems.at[i])

    return copy


def stored_order(x, owner_ref):
    count = owner_ref.shape[0]
    wide = x.shape[1] // count
    if wide % LANES:
        return x
    parts = []
    for j in range(count):
        total = None
        for n in range(count):
            term = x[:, n * wide : (n + 1) * wide] * jnp.where(owner_ref[j] == n, 1.0, 0.0)
            total = term if total is None else total + term
        parts.append(total)
    return jnp.concatenate(parts, axis=1)


def front_kernel(
    count, len_ref, owner_ref, tok_hbm, cot_hbm, att_ref, out_ref, dense_ref, vector_ref, split_ref,
    a1_hbm, ga_hbm, h2_hbm, own_hbm, qa_hbm, ka_hbm, va_hbm, o_hbm, w_hbm, gh2_hbm, down_hbm,
    up_hbm, dn_hbm, goa_hbm, kt_hbm, first_hbm, vec_ref, gbias_ref, gvec_ref,
    own_ref, qa_ref, ka_ref, va_ref, o_ref, w_ref, wo_ref, gh2_ref, down_ref, ul_ref, gz_ref, made,
    norm_ref, cot_ref, wd_ref, ga_ref, goa_ref, kt_ref, bias_ref, b1_ref, small_ref, smalls,
    mixed_ref, term2, given2, sent2, crossed2, given3, sent3, crossed3,
    gather_sems, small_sems, spread_sems, mixed_sems, sum2_sems, share_sems, put_sems, local_sems,
    whole_sems, made_sems, sum3_sems,
):
    me, tensor = lax.axis_index("dp"), lax.axis_index("tensor")
    total_rows, width = norm_ref.shape
    local_width = out_ref.shape[1]
    ratio = dense_ref.shape[2]
    wide = width // count
    slots = len_ref.shape[1]
    heads = local_width // HD
    blocks = total_rows // BLOCK
    half = BLOCK // 2
    lanes = small_ref.shape[1] - local_width
    fold = lanes // wide
    steps = count // 2
    core = tensor % 2
    mate = tensor - core + 1 - core
    other, across = (tensor + 2) % 4, (mate + 2) % 4

    greeted = greet(tensor_peers() + [(me, across)] + dp_peers(count))
    tokens_in = fetch(tok_hbm, norm_ref, local_sems.at[0])
    cot_in = fetch(cot_hbm, cot_ref, local_sems.at[1])
    a1_out = fetch(norm_ref, a1_hbm, local_sems.at[2])
    for i in range(blocks):
        tokens_in(i).start()
    for i in range(blocks):
        cot_in(i).start()
    mine = pl.ds(pl.multiple_of(me * wide, wide), wide)
    for row in range(3):
        w_ref[mine, row * local_width : (row + 1) * local_width] = att_ref[row].astype(half_type)

    def columns_of(index, low=0, size=local_width):
        return pl.ds(pl.multiple_of(index * local_width + low, LANES), size)

    wo_ref[mine, columns_of(tensor)] = out_ref[...].astype(half_type)

    small_ref[...] = jnp.zeros_like(small_ref)
    vectors = vector_ref[...].astype(half_type)
    if fold == 1:
        small_ref[0:6, :lanes] = vectors.astype(full_type)
    else:
        row = lax.broadcasted_iota(jnp.int32, (wide, lanes), 0)
        column = lax.broadcasted_iota(jnp.int32, (wide, lanes), 1)
        spread = jnp.where(column == row + me % fold * wide, 1.0, 0.0).astype(half_type)
        small_ref[0:6, :lanes] = dot(vectors, spread)
    narrow = split_ref.shape[1]
    row = lax.broadcasted_iota(jnp.int32, (narrow, local_width), 0)
    column = lax.broadcasted_iota(jnp.int32, (narrow, local_width), 1)
    spread = jnp.where(column == row + owner_ref[me] * narrow, 1.0, 0.0).astype(half_type)
    small_ref[0 : 1 + ratio, lanes:] = dot(split_ref[...].astype(half_type), spread)
    smalls[me] = small_ref[...]
    greeted()

    def place(block):
        return pl.ds(pl.multiple_of(block * wide, wide), wide)

    def small_copy(source, peer):
        return pltpu.make_async_remote_copy(
            src_ref=small_ref,
            dst_ref=smalls.at[source],
            send_sem=small_sems.at[0, peer],
            recv_sem=small_sems.at[1, source],
            device_id=(peer, tensor),
            device_id_type=MESH,
        )

    def send_small(k, carry):
        small_copy(me, (me + k) % count).start()
        return carry

    lax.fori_loop(1, count, send_small, 0)

    def attend_view(row):
        return lambda block, low, size: w_ref.at[
            place(block), pl.ds(row * local_width + low, size)
        ]

    def dense_view(row):
        return lambda block, low, size: wd_ref.at[row, place(block), pl.ds(low, size)]

    attend = [Gather(attend_view(row), local_width, gather_sems.at[row], count) for row in range(3)]
    attend.append(
        Gather(
            lambda block, low, size: wo_ref.at[place(block), columns_of(tensor, low, size)],
            local_width, gather_sems.at[3], count,
        )
    )
    dense = [
        Gather(dense_view(row), ratio * local_width, gather_sems.at[4 + row], count)
        for row in range(2)
    ]
    for piece in attend:
        piece.advance(0)

    def spread(kind, block, source, target):
        piece = wo_ref.at[place(block), columns_of(source)]
        return pltpu.make_async_remote_copy(
            src_ref=piece,
            dst_ref=piece,
            send_sem=spread_sems.at[2 * kind, block],
            recv_sem=spread_sems.at[2 * kind + 1, block],
            device_id=(me, target),
            device_id_type=MESH,
        )

    def spread_step(step):
        pos = attend[3].pos
        hops = {0: [0], steps: [steps]}.get(step, [step, -step])
        for hop in hops:
            block = ring_at(pos - hop, count)
            spread(0, block, tensor, mate).start()
            spread(1, block, tensor, other).start()

    spread_step(0)
    for row in range(2):
        for r in range(ratio):
            wd_ref[row, mine, r * local_width : (r + 1) * local_width] = dense_ref[
                row, :, r, :
            ].astype(half_type)

    def take_small(k, carry):
        source = (me + k) % count
        small_copy(source, source).wait_recv()
        return carry

    lax.fori_loop(1, count, take_small, 0)
    bias = smalls[0, :, lanes:]
    for j in range(1, count):
        bias = bias + smalls[j, :, lanes:]
    bias_ref[...] = bias
    for r in range(ratio):
        b1_ref[:, r * local_width : (r + 1) * local_width] = bias[1 + r : 2 + r, :]
    for window in range(width // lanes):
        piece = smalls[window * fold, :, :lanes]
        for j in range(window * fold + 1, (window + 1) * fold):
            piece = piece + smalls[j, :, :lanes]
        vec_ref[:, window * lanes : (window + 1) * lanes] = piece

    def norm_rows(i, carry):
        tokens_in(i).wait()
        rows = pl.ds(pl.multiple_of(i * BLOCK, BLOCK), BLOCK)
        x = stored_order(norm_ref[rows, :].astype(full_type), owner_ref)
        norm_ref[rows, :] = x.astype(half_type)
        here = pl.ds(pl.multiple_of(i * BLOCK + core * half, half), half)
        own_ref[pl.ds(pl.multiple_of(i * half, half), half), :] = norm_ref[here, :]
        unit, _ = normalized(x)
        norm_ref[rows, :] = (unit * vec_ref[2:3, :] + vec_ref[3:4, :]).astype(half_type)
        a1_out(i).start()
        cot_in(i).wait()
        cot_ref[rows, :] = stored_order(cot_ref[rows, :].astype(full_type), owner_ref).astype(
            half_type
        )
        return carry

    done = 0
    for step in range(1, steps + 1):
        for piece in attend:
            piece.advance(step)
        spread_step(step)
        if step == steps - 1:
            for piece in dense:
                piece.advance(0)
        upto = min(blocks, -(-blocks * step // steps))
        if upto > done:
            lax.fori_loop(done, upto, norm_rows, 0)
        done = max(done, upto)

    pumps = [(piece, step) for step in range(1, steps + 1) for piece in dense]

    def pump(slot):
        for k, (piece, step) in enumerate(pumps):
            if min(blocks + 1, (14 * k + 9) // 10 * 8 // len(pumps)) == slot:
                piece.advance(step)

    lane = lax.broadcasted_iota(jnp.int32, (BLOCK, LANES), 1)
    low_half = lane < HD
    spot = lane % HD

    def project(i, carry):
        row = pl.multiple_of(i * BLOCK, BLOCK)
        rows = pl.ds(row, BLOCK)
        a1 = norm_ref[rows, :]
        qkv = dot(a1, w_ref[...])
        q, k, v = (qkv[:, part * local_width : (part + 1) * local_width] for part in range(3))
        q = (q + bias_ref[0:1, :]).astype(half_type).astype(full_type) * HD**-0.5
        index = row + lax.broadcasted_iota(jnp.int32, (BLOCK, LANES), 0)
        segment = jnp.zeros((BLOCK, LANES), jnp.int32)
        end = 0
        for slot in range(slots):
            end = end + len_ref[0, slot]
            segment = segment + jnp.where(index >= end, 1, 0)
        same = spot == segment
        inside = spot <= slots
        q_mark = jnp.where(inside & ~same, -BIG, 0.0)
        k_mark = jnp.where(same, BIG, jnp.where((spot > slots) & (spot <= slots + 3), 1.0, 0.0))
        for head in range(heads):
            pair = slice(head // 2 * LANES, head // 2 * LANES + LANES)
            own = low_half if head % 2 == 0 else ~low_half
            qa_ref[head, rows, :] = jnp.where(own, q[:, pair], q_mark).astype(half_type)
            ka_ref[head, rows, :] = jnp.where(own, k[:, pair], k_mark).astype(half_type)
            va_ref[head, rows, :] = jnp.where(own, v[:, pair], 1.0).astype(half_type)
        return carry

    lax.fori_loop(0, blocks, project, 0)
    pump(0)

    def forward(block, carry):
        spread(1, block, other, other).wait_recv()
        spread(2, block, other, mate).start()
        return carry

    lax.fori_loop(0, count, forward, 0)

    def a1_left(i, carry):
        a1_out(i).wait()
        return carry

    lax.fori_loop(0, blocks, a1_left, 0)
    gbias_ref[...] = jnp.zeros_like(gbias_ref)
    gvec_ref[...] = jnp.zeros_like(gvec_ref)

    share = Share(norm_ref, share_sems)

    def mixed_copy(kind, i, source, target, half_rows):
        rows = pl.ds(pl.multiple_of(i * BLOCK + half_rows * half, half), half)
        return pltpu.make_async_remote_copy(
            src_ref=o_ref.at[rows, :],
            dst_ref=mixed_ref.at[i, :, columns_of(source)],
            send_sem=mixed_sems.at[2 * kind, i],
            recv_sem=mixed_sems.at[2 * kind + 1, i],
            device_id=(me, target),
            device_id_type=MESH,
        )

    peers = ((0, mate, 1 - core), (1, other, core), (2, across, 1 - core))

    def h2_out(i):
        own = pl.ds(pl.multiple_of(i * half, half), half)
        return pltpu.make_async_copy(gh2_ref.at[own, :], h2_hbm.at[own, :], local_sems.at[3, i])

    def attend_block(i):
        rows = pl.ds(pl.multiple_of(i * BLOCK, BLOCK), BLOCK)
        for head in range(heads):
            query = qa_ref[head, rows, :]
            scores = dot(query, ka_ref[head], 1, 1)
            top = jnp.max(scores, axis=1, keepdims=True)
            weights = jnp.exp(scores - top).astype(half_type)
            mixed = dot(weights, va_ref[head])
            turned = pltpu.roll(mixed, HD, 1)
            own = low_half if head % 2 == 0 else ~low_half
            log_total = three_parts(top + jnp.log(jnp.where(own, turned, mixed)))
            marked = query.astype(full_type)
            for part in range(3):
                marked = jnp.where(~own & (spot == slots + 1 + part), -log_total[part], marked)
            qa_ref[head, rows, :] = marked.astype(half_type)
            out = mixed / turned
            if head % 2 == 0:
                before = out
            else:
                pair = slice(head // 2 * LANES, head // 2 * LANES + LANES)
                o_ref[rows, pair] = jnp.where(low_half, before, out).astype(half_type)
        for kind, peer, half_rows in peers[1:] + peers[:1]:
            mixed_copy(kind, i, tensor, peer, half_rows).start()
        here = pl.ds(pl.multiple_of(i * BLOCK + core * half, half), half)
        mixed_ref[i, :, columns_of(tensor)] = o_ref[here, :]

    def norm_block(i):
        own = pl.ds(pl.multiple_of(i * half, half), half)
        for kind, peer, _ in peers:
            mixed_copy(kind, i, peer, peer, 0).wait_recv()
        attn = dot(mixed_ref[i], wo_ref[...], 1, 1)
        hidden = own_ref[own, :].astype(full_type) + attn + vec_ref[0:1, :]
        gh2_ref[own, :] = hidden
        h2_out(i).start()
        unit, _ = normalized(hidden)
        share.put(i, (unit * vec_ref[4:5, :] + vec_ref[5:6, :]).astype(half_type))

    behind = min(2, blocks)

    def attend_step(i, carry):
        attend_block(i)
        for slot in range(1, blocks + 1):

            @pl.when(i == slot - 1)
            def _(slot=slot):
                pump(slot)

        @pl.when(i == behind)
        def _():
            def spread_in(block, carry):
                spread(0, block, mate, mate).wait_recv()
                spread(2, block, across, mate).wait_recv()
                return carry

            lax.fori_loop(0, count, spread_in, 0)

        @pl.when(i >= behind)
        def _():
            norm_block(i - behind)

        return carry

    lax.fori_loop(0, blocks, attend_step, 0)

    def norm_step(i, carry):
        norm_block(i)
        return carry

    lax.fori_loop(blocks - behind, blocks, norm_step, 0)
    pump(blocks + 1)

    whole = [
        pltpu.make_async_copy(source, target, whole_sems.at[k])
        for k, (source, target) in enumerate(
            (
                (own_ref, own_hbm), (qa_ref, qa_hbm), (ka_ref, ka_hbm), (va_ref, va_hbm),
                (o_ref, o_hbm), (w_ref, w_hbm),
            )
        )
    ]
    for copy in whole:
        copy.start()
    down_out = fetch(down_ref, down_hbm, local_sems.at[5])

    def gh2_out(i):
        own = pl.ds(pl.multiple_of(i * half, half), half)
        return pltpu.make_async_copy(gh2_ref.at[own, :], gh2_hbm.at[own, :], local_sems.at[6, i])

    rowsum2 = RowSum(term2, given2, sent2, crossed2, sum2_sems)

    share2 = Share(ga_ref, put_sems)
    ga_out = fetch(ga_ref, ga_hbm, local_sems.at[4])

    def goa_out(i):
        rows = pl.ds(pl.multiple_of(i * BLOCK, BLOCK), BLOCK)
        return pltpu.make_async_copy(
            goa_ref.at[:, rows, :], goa_hbm.at[:, rows, :], local_sems.at[7, i]
        )

    def prepare(i):
        share2.arrived(i)
        ga_out(i).start()
        rows = pl.ds(pl.multiple_of(i * BLOCK, BLOCK), BLOCK)
        go = dot(ga_ref[rows, :], wo_ref[:, columns_of(tensor)]).astype(half_type).astype(full_type)
        both = go * o_ref[rows, :].astype(full_type)
        for head in range(heads):
            pair = slice(head // 2 * LANES, head // 2 * LANES + LANES)
            own = low_half if head % 2 == 0 else ~low_half
            inner = jnp.sum(jnp.where(own, both[:, pair], 0.0), axis=1, keepdims=True)
            filled = jnp.where(own, go[:, pair], 0.0)
            for k, value in enumerate(three_parts(inner)):
                filled = jnp.where(~own & (spot == k), -value, filled)
            goa_ref[head, rows, :] = filled.astype(half_type)
            if head % 2 == 0:
                before = ka_ref[head, rows, :].astype(full_type)
            else:
                k = jnp.where(low_half, before, ka_ref[head, rows, :].astype(full_type))
                kt_ref[pair, rows] = k.T.astype(half_type)
        goa_out(i).start()

    def mlp_block(i):
        rows = pl.ds(pl.multiple_of(i * BLOCK, BLOCK), BLOCK)
        share.arrived(i)
        a2 = norm_ref[rows, :]
        gy = cot_ref[rows, :]
        u, slope = gelu_parts(dot(a2, wd_ref[0]) + b1_ref[...])
        ul = u.astype(half_type)
        gz = (dot(gy, wd_ref[1]) * slope).astype(half_type)
        rowsum2.free(i)
        term2[i % term2.shape[0]] = dot(gz, wd_ref[0], 1, 1).astype(half_type)
        rowsum2.give(i)
        gbias_ref[0:1, :] += jnp.sum(gz.astype(full_type), axis=0, keepdims=True)
        ul_ref[rows, :] = ul
        gz_ref[rows, :] = gz
        down_ref[rows, :] = dot(ul, wd_ref[1], 1, 1).astype(half_type)
        down_out(i).start()
        rowsum2.cross(i)

    chunks = width // BLOCK

    def made_out(kind, c):
        rows = pl.ds(pl.multiple_of(c * BLOCK, BLOCK), BLOCK)
        target = (up_hbm, dn_hbm)[kind].at[rows, :]
        return pltpu.make_async_copy(made.at[kind], target, made_sems.at[kind, c])

    def weight_grads(c):
        columns = pl.ds(pl.multiple_of(c * BLOCK, BLOCK), BLOCK)
        for kind, (left, right) in enumerate(((norm_ref, gz_ref), (cot_ref, ul_ref))):

            @pl.when(c >= 1)
            def _(kind=kind):
                made_out(kind, c - 1).wait()

            made[kind] = dot(left[:, columns], right[...], 0, 0)
            made_out(kind, c).start()

    def back_block(i):
        own = pl.ds(pl.multiple_of(i * half, half), half)
        gn = rowsum2.total(i)
        h2_out(i).wait()
        unit, rate = normalized(gh2_ref[own, :])
        e = gn * vec_ref[4:5, :]
        inner = e - jnp.mean(e, axis=-1, keepdims=True)
        inner = inner - unit * jnp.mean(e * unit, axis=-1, keepdims=True)
        gy = cot_ref[share.rows(i, core), :].astype(full_type)
        gh = gy + rate * inner
        gh2_ref[own, :] = gh
        gh2_out(i).start()
        share2.put(i, gh.astype(half_type))
        gvec_ref[0:1, :] += jnp.sum(gh, axis=0, keepdims=True)
        gvec_ref[1:2, :] += jnp.sum(gy, axis=0, keepdims=True)
        gvec_ref[4:5, :] += jnp.sum(gn * unit, axis=0, keepdims=True)
        gvec_ref[5:6, :] += jnp.sum(gn, axis=0, keepdims=True)

    def mlp_step(i, carry):
        mlp_block(i)
        return carry

    lax.fori_loop(0, blocks, mlp_step, 0)
    rowsum3 = RowSum(
        down_ref.reshape(blocks, BLOCK, width), given3, sent3, crossed3, sum3_sems
    )
    rowsum3.give(0)

    late = max(blocks + 2, chunks)

    def tail_step(i, carry):
        @pl.when(i < blocks)
        def _():
            back_block(i)

        @pl.when((i >= 2) & (i < blocks + 2))
        def _():
            prepare(i - 2)

        @pl.when(i < chunks)
        def _():
            weight_grads(i)

        @pl.when(i == 0)
        def _():
            rowsum3.cross(0)

        return carry

    lax.fori_loop(0, late, tail_step, 0)
    kt_out = pltpu.make_async_copy(kt_ref, kt_hbm, whole_sems.at[len(whole)])
    kt_out.start()
    for kind in range(2):
        made_out(kind, chunks - 1).wait()
    rowsum3.ready(0)
    first_out = [
        pltpu.make_async_copy(ref.at[0], first_hbm.at[k], whole_sems.at[len(whole) + 1 + k])
        for k, ref in enumerate((sent3, crossed3))
    ]
    for copy in first_out:
        copy.start()

    def copied(i, carry):
        down_out(i).wait()
        gh2_out(i).wait()
        ga_out(i).wait()
        goa_out(i).wait()
        return carry

    lax.fori_loop(0, blocks, copied, 0)
    for copy in whole + [kt_out] + first_out:
        copy.wait()
    for piece in attend + dense:
        piece.sent()
    rowsum2.finish()
    rowsum3.finish()
    share.finish(blocks)
    share2.finish(blocks)

    def spread_out(block, carry):
        spread(0, block, tensor, mate).wait_send()
        spread(1, block, tensor, other).wait_send()
        spread(2, block, other, mate).wait_send()
        return carry

    lax.fori_loop(0, count, spread_out, 0)

    def mixed_out(i, carry):
        for kind, peer, half_rows in peers:
            mixed_copy(kind, i, tensor, peer, half_rows).wait_send()
        return carry

    lax.fori_loop(0, blocks, mixed_out, 0)

    def sent_small(k, carry):
        small_copy(me, (me + k) % count).wait_send()
        return carry

    lax.fori_loop(1, count, sent_small, 0)


class Scatter:
    def __init__(self, view, stage, taken, sems, count):
        self.view, self.stage, self.taken = view, stage, taken
        self.sems, self.count = sems, count
        self.slots = stage.shape[1]
        self.pos = ring_pos(lax.axis_index("dp"), count)
        self.tensor = lax.axis_index("tensor")

    def _copy(self, way, step):
        sign = 1 - 2 * way
        return pltpu.make_async_remote_copy(
            src_ref=self.stage.at[way, step % self.slots],
            dst_ref=self.taken.at[way, step],
            send_sem=self.sems.at[2 * way, step],
            recv_sem=self.sems.at[2 * way + 1, step],
            device_id=(ring_at(self.pos + sign, self.count), self.tensor),
            device_id_type=MESH,
        )

    def begin(self):
        for way in range(2):
            self.stage[way, 0] = self.view(way, 0).astype(half_type)
            self._copy(way, 0).start()

    def advance(self, step):
        for way in range(2):
            self._copy(way, step - 1).wait_recv()
            total = self.taken[way, step - 1].astype(full_type) + self.view(way, step)

            @pl.when(step >= self.slots)
            def _(way=way):
                self._copy(way, step - self.slots).wait_send()

            self.stage[way, step % self.slots] = total.astype(half_type)
            self._copy(way, step).start()

    def total(self, way):
        last = self.count - 2
        self._copy(way, last).wait_recv()
        return self.taken[way, last].astype(full_type) + self.view(way, last + 1)

    def finish(self):
        for step in range(max(self.count - 1 - self.slots, 0), self.count - 1):
            for way in range(2):
                self._copy(way, step).wait_send()


def sent_block(pos, way, step, count):
    return ring_at(pos - (1 - 2 * way) * (1 + step), count)


class Put:
    def __init__(self, held, result, sems):
        self.held, self.result, self.sems = held, result, sems
        self.half = held.shape[0] // sems.shape[1]
        self.dp, tensor = lax.axis_index("dp"), lax.axis_index("tensor")
        self.core = tensor % 2
        self.mate = tensor - tensor % 2 + (tensor + 1) % 2

    def own(self, i):
        return pl.ds(pl.multiple_of(i * self.half, self.half), self.half)

    def _rows(self, i, core):
        return pl.ds(pl.multiple_of((2 * i + core) * self.half, self.half), self.half)

    def _here(self, i):
        target = self.result.at[self._rows(i, self.core), :]
        return pltpu.make_async_copy(self.held.at[self.own(i), :], target, self.sems.at[0, i])

    def _there(self, i, core):
        return pltpu.make_async_remote_copy(
            src_ref=self.held.at[self.own(i), :],
            dst_ref=self.result.at[self._rows(i, core), :],
            send_sem=self.sems.at[1, i],
            recv_sem=self.sems.at[2, i],
            device_id=(self.dp, self.mate),
            device_id_type=MESH,
        )

    def put(self, i, value):
        self.held[self.own(i), :] = value
        self._here(i).start()
        self._there(i, self.core).start()

    def left(self, i):
        self._here(i).wait()
        self._there(i, self.core).wait_send()

    def arrived(self, i):
        self._there(i, 1 - self.core).wait_recv()


def back_kernel(
    count, ga_hbm, o_hbm, qb_hbm, ka_hbm, va_hbm, goa_hbm, kt_hbm, w_hbm, up_hbm, dn_hbm, down_hbm,
    h2_hbm, gh2_hbm, own_hbm, a1_hbm, first_hbm, vec_ref, gbias_ref, gvec_ref,
    layer_hbm, tg_hbm, dense_ref, sum_ref, small_ref,
    ga_ref, o_ref, qb_ref, ka_ref, va_ref, w_ref, wide_ref, gh_ref, own_ref, goa_ref, kt_ref, gqt_ref, gqkv_ref, put_ref,
    given, sent, crossed, term2, given2, sent2, crossed2,
    terms, stage, taken, grads, stage2, taken2, small_mine, small_taken, small_mate,
    sum_sems, sum2_sems, put_sems, put2_sems, scatter_sems, scatter2_sems, small_sems, mate_sems,
    local_sems, terms_sems, whole_sems,
):
    total_rows, width = ga_ref.shape
    local_width = o_ref.shape[1]
    heads = local_width // HD
    blocks = total_rows // BLOCK
    half = BLOCK // 2
    wide = width // count
    hops = count - 1
    lanes = small_ref.shape[1] - local_width
    fold = lanes // wide
    me, tensor = lax.axis_index("dp"), lax.axis_index("tensor")
    mate = tensor - tensor % 2 + (tensor + 1) % 2
    pos = ring_pos(me, count)
    greeted = greet(tensor_peers() + dp_peers(count))

    def own_rows(i):
        return pl.ds(pl.multiple_of(i * half, half), half)

    def place(block):
        return pl.ds(pl.multiple_of(block * wide, wide), wide)

    def own_fetch(source, target, sems):
        return lambda i: pltpu.make_async_copy(
            source.at[own_rows(i), :], target.at[own_rows(i), :], sems.at[i]
        )

    ga_in = fetch(ga_hbm, ga_ref, local_sems.at[0])
    down_in = fetch(down_hbm, wide_ref, local_sems.at[1])
    a1_in = fetch(a1_hbm, wide_ref, local_sems.at[2])
    h2_in = own_fetch(h2_hbm, gh_ref, local_sems.at[3])
    gh2_in = own_fetch(gh2_hbm, gh_ref, local_sems.at[4])
    own_in = own_fetch(own_hbm, own_ref, local_sems.at[5])

    def term_in(way, step):
        rows = place(sent_block(pos, way, step, count))
        source = (up_hbm, dn_hbm)[way].at[rows, :]
        return pltpu.make_async_copy(
            source, terms.at[way, step % 2], terms_sems.at[way, step % 2]
        )

    def each(copy):
        def start(i, carry):
            copy(i).start()
            return carry

        lax.fori_loop(0, blocks, start, 0)

    for step in range(2):
        for way in range(2):
            term_in(way, step).start()
    whole = [
        pltpu.make_async_copy(source, target, whole_sems.at[k])
        for k, (source, target) in enumerate(
            (
                (qb_hbm, qb_ref), (ka_hbm, ka_ref), (va_hbm, va_ref), (goa_hbm, goa_ref),
                (kt_hbm, kt_ref), (first_hbm.at[0], sent.at[0]), (first_hbm.at[1], crossed.at[0]),
                (o_hbm, o_ref), (w_hbm, w_ref),
            )
        )
    ]
    for copy in whole[:-4]:
        copy.start()
    each(down_in)
    for copy in whole[-4:-2]:
        copy.start()
    each(h2_in)
    for copy in whole[-2:]:
        copy.start()
    each(ga_in)
    each(own_in)
    small_mine[:, :width] = gvec_ref[...]
    ratio = gbias_ref.shape[1] // local_width
    for r in range(ratio):
        small_mine[1 + r : 2 + r, width:] = gbias_ref[0:1, r * local_width : (r + 1) * local_width]
    small_mine[1 + ratio :, width:] = jnp.zeros((7 - ratio, local_width), full_type)
    greeted()

    pieces = stage.shape[0]
    part = terms.shape[3] // pieces

    def term_view(piece):
        columns = slice(piece * part, (piece + 1) * part)
        return lambda way, step: terms[way, step % 2, :, columns]

    scatters = [
        Scatter(term_view(p), stage.at[p], taken.at[p], scatter_sems.at[p], count)
        for p in range(pieces)
    ]

    def terms_ready(step):
        for way in range(2):
            term_in(way, step).wait()

    def terms_next(step):
        @pl.when(step <= hops)
        def _():
            for way in range(2):
                term_in(way, step).start()

    rowsum = RowSum(wide_ref.reshape(blocks, BLOCK, width), given, sent, crossed, sum_sems, 1)
    layer = Put(put_ref, layer_hbm, put_sems)
    terms_ready(0)
    for scatter in scatters:
        scatter.begin()
    terms_next(2)

    lane = lax.broadcasted_iota(jnp.int32, (BLOCK, LANES), 1)
    low_half = lane < HD
    gqt_ref[...] = jnp.zeros_like(gqt_ref)
    down_in(0).wait()
    for i in range(1, 3):
        down_in(i).wait()
        rowsum.give(i)
    for copy in whole[:-2]:
        copy.wait()

    def output_block(i):
        h2_in(i).wait()
        total = gh_ref[own_rows(i), :] + rowsum.total(i) + vec_ref[1:2, :]
        layer.put(i, total.astype(half_type))
        gh2_in(i).start()

    per = -(-hops // blocks)

    def between(j, piece):
        if piece == 0:

            @pl.when(j >= 1)
            def _():
                output_block(j - 1)

            @pl.when(j < blocks - 3)
            def _():
                down_in(j + 3).wait()
                rowsum.give(j + 3)

            @pl.when(j < blocks - 1)
            def _():
                rowsum.cross(j + 1)

        for t in range(per):
            hop = j * per + t

            @pl.when((hop >= 1) & (hop < hops))
            def _(hop=hop):
                if piece == 0:
                    terms_ready(hop)
                scatters[piece].advance(hop)
                if piece == pieces - 1:
                    terms_next(hop + 2)

    def keys_block(j, carry):
        rows = pl.ds(pl.multiple_of(j * BLOCK, BLOCK), BLOCK)
        for head in range(heads):
            scores = dot(ka_ref[head, rows, :], qb_ref[head], 1, 1)
            probs = jnp.exp(scores)
            gp = dot(va_ref[head, rows, :], goa_ref[head], 1, 1)
            gs = (probs * gp).astype(half_type)
            gv = dot(probs.astype(half_type), goa_ref[head])
            gk = dot(gs, qb_ref[head])
            own = slice(head * HD, head * HD + HD)
            gqt_ref[own, :] += dot(kt_ref[own, rows], gs)
            if head % 2 == 0:
                gk_even, gv_even = gk, gv
            else:
                for k, value in ((1, (gk_even, gk)), (2, (gv_even, gv))):
                    base = k * local_width + head // 2 * LANES
                    gqkv_ref[rows, base : base + LANES] = jnp.where(low_half, *value).astype(
                        half_type
                    )
            if (head + 1) * pieces % heads == 0:
                between(j, (head + 1) * pieces // heads - 1)
        return carry

    lax.fori_loop(0, blocks, keys_block, 0)

    def turn(i, carry):
        rows = pl.ds(pl.multiple_of(i * BLOCK, BLOCK), BLOCK)
        gqkv_ref[rows, :local_width] = (gqt_ref[:, rows].T * HD**-0.5).astype(half_type)
        return carry

    rowsum2 = RowSum(term2, given2, sent2, crossed2, sum2_sems)

    def norm_term(i):
        rows = pl.ds(pl.multiple_of(i * BLOCK, BLOCK), BLOCK)
        rowsum2.free(i)
        term2[i % term2.shape[0]] = dot(gqkv_ref[rows, :], w_ref[...], 1, 1).astype(half_type)
        rowsum2.give(i)

    turn(0, 0)
    whole[-1].wait()
    norm_term(0)
    rowsum.gone()
    each(a1_in)
    turn(1, 0)
    norm_term(1)
    rowsum2.cross(0)
    lax.fori_loop(2, blocks, turn, 0)
    ones = jnp.ones((8, total_rows), half_type)
    bias_query = dot(ones, gqkv_ref[:, :local_width])
    small_mine[0:1, width:] = bias_query[0:1, :]

    def small_copy(kind, source, peer):
        window = pl.ds(pl.multiple_of(peer // fold * lanes, lanes), lanes)
        return pltpu.make_async_remote_copy(
            src_ref=small_mine.at[:, pl.ds(width, local_width) if kind else window],
            dst_ref=small_taken.at[source, :, pl.ds(lanes, local_width) if kind else pl.ds(0, lanes)],
            send_sem=small_sems.at[2 * kind, peer],
            recv_sem=small_sems.at[2 * kind + 1, source],
            device_id=(peer, tensor),
            device_id_type=MESH,
        )

    def send_small(kind):
        def send(k, carry):
            small_copy(kind, me, (me + k) % count).start()
            return carry

        lax.fori_loop(1, count, send, 0)

    send_small(1)

    def arrived_a1(i, carry):
        a1_in(i).wait()
        ga_in(i).wait()
        return carry

    lax.fori_loop(0, blocks, arrived_a1, 0)

    def weight_grads(c, carry):
        columns = pl.ds(pl.multiple_of(c * BLOCK, BLOCK), BLOCK)
        grads[columns, : 3 * local_width] = dot(wide_ref[:, columns], gqkv_ref[...], 0, 0)
        grads[columns, 3 * local_width :] = dot(ga_ref[:, columns], o_ref[...], 0, 0)
        return carry

    chunks = width // BLOCK
    whole[-2].wait()
    rowsum2.cross(1)
    lax.fori_loop(0, chunks, weight_grads, 0)
    side = grads.shape[1] // 2

    def grads_view(way, step):
        return grads[
            place(sent_block(pos, way, step, count)), way * side : (way + 1) * side
        ]

    scatter2 = Scatter(grads_view, stage2, taken2, scatter2_sems, count)
    scatter2.begin()
    output_block(blocks - 1)

    def layer_left(i, carry):
        layer.left(i)
        layer.arrived(i)
        return carry

    lax.fori_loop(0, blocks, layer_left, 0)
    result = Put(put_ref, tg_hbm, put2_sems)

    def norm_block(i):
        gn = rowsum2.total(i)
        own_in(i).wait()
        gh2_in(i).wait()
        unit, rate = normalized(own_ref[own_rows(i), :].astype(full_type))
        e = gn * vec_ref[2:3, :]
        inner = e - jnp.mean(e, axis=-1, keepdims=True)
        inner = inner - unit * jnp.mean(e * unit, axis=-1, keepdims=True)
        result.put(i, (gh_ref[own_rows(i), :] + rate * inner).astype(half_type))
        small_mine[2:3, :width] += jnp.sum(gn * unit, axis=0, keepdims=True)
        small_mine[3:4, :width] += jnp.sum(gn, axis=0, keepdims=True)

    def end_step(i, carry):
        @pl.when(i < blocks - 2)
        def _():
            norm_term(i + 2)

        norm_block(i)

        @pl.when(i < blocks - 2)
        def _():
            rowsum2.cross(i + 2)

        for t in range(per):
            hop = i * per + t + 1

            @pl.when(hop < hops)
            def _(hop=hop):
                scatter2.advance(hop)

        return carry

    lax.fori_loop(0, blocks, end_step, 0)
    send_small(0)
    terms_ready(hops)
    for way in range(2):
        for p, scatter in enumerate(scatters):
            total = scatter.total(way)
            for r in range(part // local_width):
                dense_ref[way, :, p * part // local_width + r, :] = total[
                    :, r * local_width : (r + 1) * local_width
                ]
        total = scatter2.total(way)
        for k in range(2):
            sum_ref[2 * way + k] = total[:, k * local_width : (k + 1) * local_width]
    for kind in range(2):
        window = pl.ds(pl.multiple_of(me // fold * lanes, lanes), lanes)
        here = slice(lanes, lanes + local_width) if kind else slice(0, lanes)
        small_taken[me, :, here] = small_mine[:, width:] if kind else small_mine[:, window]

        def take(k, carry, kind=kind):
            source = (me + k) % count
            small_copy(kind, source, source).wait_recv()
            return carry

        lax.fori_loop(1, count, take, 0)
    total = small_taken[0]
    for j in range(1, count):
        total = total + small_taken[j]
    small_ref[...] = total
    pair = pltpu.make_async_remote_copy(
        src_ref=small_ref.at[:, pl.ds(0, lanes)],
        dst_ref=small_mate,
        send_sem=mate_sems.at[0],
        recv_sem=mate_sems.at[1],
        device_id=(me, mate),
        device_id_type=MESH,
    )
    pair.start()
    pair.wait()
    small_ref[:, :lanes] = total[:, :lanes] + small_mate[...]

    def result_left(i, carry):
        result.left(i)
        result.arrived(i)
        return carry

    lax.fori_loop(0, blocks, result_left, 0)
    for scatter in scatters + [scatter2]:
        scatter.finish()
    rowsum.finish(given=False)
    rowsum2.finish()
    for kind in range(2):

        def done(k, carry, kind=kind):
            small_copy(kind, me, (me + k) % count).wait_send()
            return carry

        lax.fori_loop(1, count, done, 0)


def permuted(x, owner, back):
    rows, width = x.shape
    count = owner.shape[0]
    order = jnp.argsort(owner) if back else owner
    return jnp.take(x.reshape(rows, count, -1), order, axis=1).reshape(rows, width)


def adamw_step(weight, first, second, grad, rate, decay):
    first_next = first_decay * first + (1.0 - first_decay) * grad
    second_next = second_decay * second + (1.0 - second_decay) * grad * grad
    first_hat = first_next / (1.0 - first_decay**STEP)
    second_hat = second_next / (1.0 - second_decay**STEP)
    update = first_hat / (jnp.sqrt(second_hat) + adam_epsilon) + decay * weight
    return (first_next, second_next, weight - rate * update)


def last_kernel(rates, owner_ref, *refs):
    count = owner_ref.shape[0]
    given, refs = refs[:5], refs[5:]
    layer, grad, weight_sum, dense_sum, small = given
    state, refs = refs[:15], refs[15:]
    results, outs = refs[:2], refs[2:]

    def step(k, grad, at=(Ellipsis,)):
        new = adamw_step(*(ref[at] for ref in state[3 * k : 3 * k + 3]), grad, *rates[k])
        for ref, value in zip(outs[3 * k : 3 * k + 3], new):
            ref[at] = value

    wide = layer.shape[1] // count
    if wide % LANES == 0:
        for j in range(count):
            natural = pl.ds(pl.multiple_of(owner_ref[j] * wide, wide), wide)
            for x, y in zip((layer, grad), results):
                y[:, natural] = x[:, j * wide : (j + 1) * wide]
    else:
        for x, y in zip((layer, grad), results):
            y[...] = x[...]
    step(0, weight_sum[0:3])
    step(1, weight_sum[3])
    step(2, dense_sum[...])
    ratio, local_width = state[6].shape[2:]
    me = lax.axis_index("dp")
    lanes = small.shape[1] - local_width

    def chosen(x, start, size):
        row = lax.broadcasted_iota(jnp.int32, (x.shape[1], size), 0)
        column = lax.broadcasted_iota(jnp.int32, (x.shape[1], size), 1)
        pick = jnp.where(row == column + start, 1.0, 0.0).astype(half_type)
        return sum(dot(part.astype(half_type), pick) for part in three_parts(x))

    narrow, wide = state[9].shape[1], state[12].shape[1]
    step(3, chosen(small[:, lanes:], owner_ref[me] * narrow, narrow)[: 1 + ratio])
    step(4, chosen(small[:, :lanes], me % (lanes // wide) * wide, wide)[:6])


def last(owner, layer_output, tokens_grad, weight_sum, dense_sum, small_sum, *state):
    steps = 4 if dense_sum.shape[1] % 128 == 0 else 1
    rates = (
        (matrix_rate, matrix_decay),
        (output_rate, matrix_decay),
        (matrix_rate, matrix_decay),
        (bias_rate, 0.0),
        (vector_rate, 0.0),
    )

    def spec(x, dim):
        shape = tuple(n // steps if k == dim else n for k, n in enumerate(x.shape))
        return pl.BlockSpec(shape, lambda i, *_: tuple(i if k == dim else 0 for k in range(x.ndim)))

    dims = [0, 0, 1, 1, None] + [1] * 3 + [0] * 3 + [1] * 3 + [None] * 6
    operands = (layer_output, tokens_grad, weight_sum, dense_sum, small_sum) + state
    specs = [spec(x, dim) for x, dim in zip(operands, dims)]
    outs = operands[:2] + state
    return pl.pallas_call(
        functools.partial(last_kernel, rates),
        out_shape=[jax.ShapeDtypeStruct(x.shape, x.dtype) for x in outs],
        grid_spec=pltpu.PrefetchScalarGridSpec(
            num_scalar_prefetch=1, grid=(steps,), in_specs=specs, out_specs=specs[:2] + specs[5:]
        ),
        compiler_params=pltpu.CompilerParams(vmem_limit_bytes=60 * 2**20),
    )(owner, *operands)


def call(kernel, collective, outs, scratch, operands, spaces, limit=62):
    spec = {
        "s": pl.BlockSpec(memory_space=pltpu.SMEM),
        "v": pl.BlockSpec(memory_space=pltpu.VMEM),
        "h": pl.BlockSpec(memory_space=pl.ANY),
    }
    return pl.pallas_call(
        kernel,
        out_shape=[jax.ShapeDtypeStruct(shape, dtype) for shape, dtype in outs],
        in_specs=[spec[c] for c in spaces[0]],
        out_specs=[spec[c] for c in spaces[1]],
        scratch_shapes=scratch,
        compiler_params=pltpu.CompilerParams(
            collective_id=collective, has_side_effects=True, vmem_limit_bytes=limit * 2**20
        ),
    )(*operands)


def dma(*shape):
    return pltpu.SemaphoreType.DMA(shape)


def local(
    tokens,
    lengths,
    owner,
    attend_master,
    attend_first,
    attend_second,
    output_master,
    output_first,
    output_second,
    dense_master,
    dense_first,
    dense_second,
    bias_master,
    bias_first,
    bias_second,
    vector_master,
    vector_first,
    vector_second,
    cotangent,
):
    count = owner.shape[0]
    rows, width = tokens.shape
    local_width = output_master.shape[1]
    ratio = dense_master.shape[2]
    hidden = ratio * local_width
    heads = local_width // HD
    blocks = rows // BLOCK
    half = BLOCK // 2
    wide = width // count
    lanes = max(LANES, wide)
    tok, cot = tokens, cotangent
    if wide % LANES:
        tok, cot = (permuted(x, owner, False) for x in (tokens, cotangent))
    row_sum = [pltpu.VMEM((blocks, half, width), half_type)] * 3
    two_terms = pltpu.VMEM((2, BLOCK, width), half_type)
    heads_shape = (heads, rows, LANES)
    small = (8, lanes + local_width)
    a1, ga, h2, own, qb, ka, va, o, w, gh2, down, up, dn, goa, kt, first, vec, gbias, gvec = call(
        functools.partial(front_kernel, count),
        0,
        [
            ((rows, width), half_type),
            ((rows, width), half_type),
            ((rows // 2, width), full_type),
            ((rows // 2, width), half_type),
            (heads_shape, half_type),
            (heads_shape, half_type),
            (heads_shape, half_type),
            ((rows, local_width), half_type),
            ((width, 3 * local_width), half_type),
            ((rows // 2, width), full_type),
            ((rows, width), half_type),
            ((width, hidden), full_type),
            ((width, hidden), full_type),
            (heads_shape, half_type),
            ((local_width, rows), half_type),
            ((2, half, width), half_type),
            ((8, width), full_type),
            ((8, hidden), full_type),
            ((8, width), full_type),
        ],
        [
            pltpu.VMEM((rows // 2, width), half_type),
            *[pltpu.VMEM(heads_shape, half_type)] * 3,
            pltpu.VMEM((rows, local_width), half_type),
            pltpu.VMEM((width, 3 * local_width), half_type),
            pltpu.VMEM((width, width), half_type),
            pltpu.VMEM((rows // 2, width), full_type),
            pltpu.VMEM((rows, width), half_type),
            *[pltpu.VMEM((rows, hidden), half_type)] * 2,
            pltpu.VMEM((2, BLOCK, hidden), full_type),
            *[pltpu.VMEM((rows, width), half_type)] * 2,
            pltpu.VMEM((2, width, hidden), half_type),
            pltpu.VMEM((rows, width), half_type),
            pltpu.VMEM(heads_shape, half_type),
            pltpu.VMEM((local_width, rows), half_type),
            pltpu.VMEM((8, local_width), full_type),
            pltpu.VMEM((1, hidden), full_type),
            pltpu.VMEM(small, full_type),
            pltpu.VMEM((count,) + small, full_type),
            pltpu.VMEM((blocks, half, width), half_type),
            two_terms,
            *row_sum,
            *[pltpu.VMEM((1, half, width), half_type)] * 3,
            dma(6, 4, count // 2),
            dma(2, count),
            dma(6, count),
            dma(6, blocks),
            dma(4, blocks),
            dma(2, blocks),
            dma(2, blocks),
            dma(8, blocks),
            dma(9),
            dma(2, width // BLOCK),
            dma(4, 1),
        ],
        (
            lengths, owner, tok, cot, attend_master, output_master, dense_master, vector_master,
            bias_master,
        ),
        ("sshhvvvvv", "h" * 16 + "vvv"),
    )
    pieces = 2
    row_blocks = pltpu.VMEM((blocks, half, width), half_type)
    row_slots = pltpu.VMEM((min(3, blocks), half, width), half_type)
    part, side = hidden // pieces, 2 * local_width
    layer_output, tokens_grad, dense_sum, weight_sum, small_sum = call(
        functools.partial(back_kernel, count),
        1,
        [
            ((rows, width), half_type),
            ((rows, width), half_type),
            (dense_master.shape, full_type),
            ((4, wide, local_width), full_type),
            ((8, lanes + local_width), full_type),
        ],
        [
            pltpu.VMEM((rows, width), half_type),
            pltpu.VMEM((rows, local_width), half_type),
            *[pltpu.VMEM(heads_shape, half_type)] * 3,
            pltpu.VMEM((width, 3 * local_width), half_type),
            pltpu.VMEM((rows, width), half_type),
            pltpu.VMEM((rows // 2, width), full_type),
            pltpu.VMEM((rows // 2, width), half_type),
            pltpu.VMEM(heads_shape, half_type),
            pltpu.VMEM((local_width, rows), half_type),
            pltpu.VMEM((local_width, rows), full_type),
            pltpu.VMEM((rows, 3 * local_width), half_type),
            pltpu.VMEM((rows // 2, width), half_type),
            row_blocks,
            row_slots,
            row_blocks,
            two_terms,
            row_blocks,
            row_slots,
            row_blocks,
            pltpu.VMEM((2, 2, wide, hidden), full_type),
            pltpu.VMEM((pieces, 2, 2, wide, part), half_type),
            pltpu.VMEM((pieces, 2, count - 1, wide, part), half_type),
            pltpu.VMEM((width, 4 * local_width), full_type),
            pltpu.VMEM((2, 2, wide, side), half_type),
            pltpu.VMEM((2, count - 1, wide, side), half_type),
            pltpu.VMEM((8, width + local_width), full_type),
            pltpu.VMEM((count, 8, lanes + local_width), full_type),
            pltpu.VMEM((8, lanes), full_type),
            dma(4, blocks),
            dma(4, blocks),
            dma(3, blocks),
            dma(3, blocks),
            dma(pieces, 4, count - 1),
            dma(4, count - 1),
            dma(4, count),
            dma(2),
            dma(6, blocks),
            dma(2, 2),
            dma(9),
        ],
        (
            ga, o, qb, ka, va, goa, kt, w, up, dn, down, h2, gh2, own, a1, first, vec, gbias,
            gvec,
        ),
        ("h" * 16 + "vvv", "hhvvv"),
    )
    if wide % LANES:
        layer_output, tokens_grad = (permuted(x, owner, True) for x in (layer_output, tokens_grad))
    return tuple(
        last(
            owner, layer_output, tokens_grad, weight_sum, dense_sum, small_sum,
            attend_master, attend_first, attend_second,
            output_master, output_first, output_second,
            dense_master, dense_first, dense_second,
            bias_master, bias_first, bias_second,
            vector_master, vector_first, vector_second,
        )
    )


def solution(mesh):
    return jax.shard_map(
        local,
        mesh=mesh,
        in_specs=(
            P("dp", None),
            P("dp", None),
            P(),
            P(None, "dp", "tensor"),
            P(None, "dp", "tensor"),
            P(None, "dp", "tensor"),
            P("dp", "tensor"),
            P("dp", "tensor"),
            P("dp", "tensor"),
            P(None, "dp", None, "tensor"),
            P(None, "dp", None, "tensor"),
            P(None, "dp", None, "tensor"),
            P(None, ("tensor", "dp")),
            P(None, ("tensor", "dp")),
            P(None, ("tensor", "dp")),
            P(None, "dp"),
            P(None, "dp"),
            P(None, "dp"),
            P("dp", None),
        ),
        out_specs=(
            P("dp", None),
            P("dp", None),
            P(None, "dp", "tensor"),
            P(None, "dp", "tensor"),
            P(None, "dp", "tensor"),
            P("dp", "tensor"),
            P("dp", "tensor"),
            P("dp", "tensor"),
            P(None, "dp", None, "tensor"),
            P(None, "dp", None, "tensor"),
            P(None, "dp", None, "tensor"),
            P(None, ("tensor", "dp")),
            P(None, ("tensor", "dp")),
            P(None, ("tensor", "dp")),
            P(None, "dp"),
            P(None, "dp"),
            P(None, "dp"),
        ),
        check_vma=False,
    )
```
